32 devices in a mesh: cols: 8 (over z, y), rows: 4 (over x, core).
Axes of the slice: x: 2, y: 2, z: 4, core: 2. Of those that a mesh axis runs over, the one named last changes fastest.
Arguments:
- observed: float32 [1024, 8192], P('rows', 'cols'), may hold values from -14 to 14
- class_map: int32 [1024, 8192], P('rows', 'cols'), may hold values from 0 to 3
- class_weights: float32 [4], replicated, may hold values from 0.5 to 8
- blur_kernel: float32 [3, 3], replicated, may hold values from 0.02 to 0.25
Outputs:
- solution: float32 [1024, 8192], P('rows', 'cols')
- residual: float32 [1024, 8192], P('rows', 'cols')
The draws below stay inside these ranges and needn't reach their ends.
All inputs are finite; a program needn't handle non-finite values.
Results may differ from the reference program's by a relative error of at most 0.0003.
Values sent between devices are 32-bit elements; how exact they have to be, the bound alone decides.
No kernel may reach another device: no remote copies, remote signals or barrier semaphores. Data moves between devices by JAX's collectives and lax.ppermute only.
A program may use at most 128 MiB of HBM per device.

```python
import math
import jax
import jax.numpy as jnp

COARSE = 8
SWEEPS = 8
ITERS = 2
CLASSES = 4
HEIGHT = 1024
BAND_LEN = 8192


def draw_observed(key, part):
    key_base, key_rows, key_cols = jax.random.split(key, 3)
    row_scale = jnp.exp(jax.random.uniform(key_rows, (HEIGHT, 1), jnp.float32) * (0.5 * math.log(10.0)))
    col_scale = jnp.exp(jax.random.uniform(key_cols, (1, BAND_LEN), jnp.float32) * (0.5 * math.log(10.0)))
    base = jnp.clip(jax.random.normal(key_base, (HEIGHT, BAND_LEN), jnp.float32), -4.0, 4.0)
    return (base * row_scale * col_scale / 3.0).astype(jnp.float32)


def touch_ends(values, key, smallest, largest):
    longest = values.shape.index(max(values.shape))
    spots = []
    for shift in (0, 1):
        where = [jax.random.randint(jax.random.fold_in(key, axis), (), 0, length) for axis, length in enumerate(values.shape)]
        where[longest] = (where[longest] + shift) % values.shape[longest]
        spots.append(tuple(where))
    return values.at[spots[0]].set(smallest).at[spots[1]].set(largest)


def setup_inputs(seed: int = 0) -> dict:
    key_of = jax.random.split(jax.random.key(seed), 5)
    return {
        "observed": draw_observed(jax.random.fold_in(key_of[4], 71), 0),
        "class_map": touch_ends(jax.random.randint(key_of[1], (HEIGHT, BAND_LEN), 0, CLASSES), jax.random.fold_in(key_of[1], 1), 0, CLASSES - 1).astype(jnp.int32),
        "class_weights": jnp.clip(jnp.exp(jax.random.uniform(key_of[2], (CLASSES,), jnp.float32, math.log(0.5), math.log(8.0))), 0.5, 8.0),
        "blur_kernel": jnp.clip(jnp.exp(jax.random.uniform(key_of[3], (3, 3), jnp.float32, math.log(0.02), math.log(0.25))), 0.02, 0.25),
    }


OMEGA = 0.8


def blurred(padded, kernel):
    height = padded.shape[0] - 2
    breadth = padded.shape[1] - 2
    summed = jnp.zeros((height, breadth), jnp.float32)
    for across in range(3):
        for along in range(3):
            summed = summed + kernel[across, along] * padded[across:across + height, along:along + breadth]
    return summed


def adjoint(padded, kernel):
    height = padded.shape[0] - 2
    breadth = padded.shape[1] - 2
    summed = jnp.zeros((height, breadth), jnp.float32)
    for across in range(3):
        for along in range(3):
            summed = summed + kernel[across, along] * padded[2 - across:2 - across + height, 2 - along:2 - along + breadth]
    return summed


def edge_weights(cond_pad):
    center = cond_pad[1:-1, 1:-1]
    return (0.5 * (center + cond_pad[1:-1, 2:]), 0.5 * (center + cond_pad[1:-1, :-2]),
            0.5 * (center + cond_pad[:-2, 1:-1]), 0.5 * (center + cond_pad[2:, 1:-1]))


def laplace(padded, edge_set):
    east, west, north, south = edge_set
    center = padded[1:-1, 1:-1]
    return ((east + west + north + south) * center - east * padded[1:-1, 2:] - west * padded[1:-1, :-2]
            - north * padded[:-2, 1:-1] - south * padded[2:, 1:-1])


def coarse_weights(edge_set, kernel):
    east, west, north, south = edge_set
    blocks_down = east.shape[0] // COARSE
    blocks_across = east.shape[1] // COARSE
    c_east = east[:, COARSE - 1::COARSE].reshape(blocks_down, COARSE, blocks_across).sum(axis=1)
    c_west = west[:, 0::COARSE].reshape(blocks_down, COARSE, blocks_across).sum(axis=1)
    c_north = north[0::COARSE, :].reshape(blocks_down, blocks_across, COARSE).sum(axis=2)
    c_south = south[COARSE - 1::COARSE, :].reshape(blocks_down, blocks_across, COARSE).sum(axis=2)
    c_diag = COARSE * COARSE * jnp.square(jnp.sum(kernel)) + c_east + c_west + c_north + c_south
    return jnp.stack([c_east, c_west, c_north, c_south, c_diag])


def jacobi(source, coarse_table, widen):
    c_east, c_west, c_north, c_south, c_diag = coarse_table[0], coarse_table[1], coarse_table[2], coarse_table[3], coarse_table[4]
    iterate = OMEGA * source / c_diag
    for repeat in range(SWEEPS - 1):
        padded = widen(iterate)
        applied = (c_diag * iterate - c_east * padded[1:-1, 2:] - c_west * padded[1:-1, :-2]
                   - c_north * padded[:-2, 1:-1] - c_south * padded[2:, 1:-1])
        iterate = iterate + OMEGA * (source - applied) / c_diag
    return iterate


def pad_zero(field):
    return jnp.pad(field, 1)


def reference(observed, class_map, class_weights, blur_kernel):
    conductance = jnp.zeros(observed.shape, jnp.float32)
    for class_id in range(CLASSES):
        conductance = conductance + jnp.where(class_map == class_id, class_weights[class_id], 0.0)
    edge_set = edge_weights(jnp.pad(conductance, 1))
    right_side = adjoint(jnp.pad(observed, 1), blur_kernel)
    fine_diag = jnp.sum(blur_kernel * blur_kernel) + edge_set[0] + edge_set[1] + edge_set[2] + edge_set[3]
    coarse_table = coarse_weights(edge_set, blur_kernel)
    blocks_down = HEIGHT // COARSE
    blocks_across = BAND_LEN // COARSE

    def precondition(residual):
        source = residual.reshape(blocks_down, COARSE, blocks_across, COARSE).sum(axis=(1, 3))
        coarse = jacobi(source, coarse_table, pad_zero)
        spread = jnp.broadcast_to(coarse[:, None, :, None], (blocks_down, COARSE, blocks_across, COARSE))
        return residual / fine_diag + spread.reshape(HEIGHT, BAND_LEN)

    def apply_operator(field):
        padded = jnp.pad(field, 1)
        image = blurred(padded, blur_kernel)
        return adjoint(jnp.pad(image, 1), blur_kernel) + laplace(padded, edge_set)

    solution = jnp.zeros(observed.shape, jnp.float32)
    residual = right_side
    precond = precondition(residual)
    gamma_now = jnp.sum(residual * precond)
    direction = precond
    for iteration in range(ITERS):
        product_field = apply_operator(direction)
        step_size = gamma_now / jnp.sum(direction * product_field)
        solution = solution + step_size * direction
        residual = residual - step_size * product_field
        if iteration + 1 < ITERS:
            precond = precondition(residual)
            gamma_next = jnp.sum(residual * precond)
            direction = precond + (gamma_next / gamma_now) * direction
            gamma_now = gamma_next
    return solution, residual
```

```python
import functools

import jax
import jax.numpy as jnp
from jax import lax
from jax.experimental import pallas as pl
from jax.experimental.pallas import tpu as pltpu
from jax.sharding import PartitionSpec as P

COARSE = 8
SWEEPS = 8
CLASSES = 4
OMEGA = 0.8

LANES = 128
HALF = LANES // 2
EDGE = 8
STRIP = 2 * EDGE
AXES = ("cols", "rows")
LIMIT = 40 * 1024 * 1024


VMEM = pl.BlockSpec(memory_space=pltpu.VMEM)
SMEM = pl.BlockSpec(memory_space=pltpu.SMEM)
HBM = pl.BlockSpec(memory_space=pltpu.HBM)


def params():
    return pltpu.CompilerParams(vmem_limit_bytes=LIMIT)


def floats(*shapes):
    return [jax.ShapeDtypeStruct(shape, jnp.float32) for shape in shapes]


def place():
    at_col, at_row = lax.axis_index("cols"), lax.axis_index("rows")
    n_cols, n_rows = lax.axis_size("cols"), lax.axis_size("rows")
    return at_col, at_row, n_cols, n_rows


def has_sides():
    at_col, at_row, n_cols, n_rows = place()
    flag = lambda test: jnp.where(test, 1.0, 0.0).astype(jnp.float32)
    return (
        flag(at_row > 0),
        flag(at_row < n_rows - 1),
        flag(at_col < n_cols - 1),
        flag(at_col > 0),
    )


def iota(shape, dim):
    return lax.broadcasted_iota(jnp.int32, shape, dim)


def cell_of(pixel, tiles):
    turn = (tiles + 1) * LANES
    return jnp.where(pixel < turn - HALF, pixel >> 3, ((pixel - turn) >> 3) & (2 * LANES - 1))


def gather_matrix(tiles):
    shape = ((tiles + 1) * LANES, 2 * LANES)
    hit = cell_of(iota(shape, 0), tiles) == iota(shape, 1)
    return jnp.where(hit, 1.0, 0.0).astype(jnp.bfloat16)


def spread_matrix(tiles):
    shape = (2 * LANES, (tiles + 1) * LANES)
    hit = cell_of(iota(shape, 1), tiles) == iota(shape, 0)
    return jnp.where(hit, 1.0, 0.0).astype(jnp.bfloat16)


def split_dot(field, matrix):
    rows = field.shape[0]
    high = field.astype(jnp.bfloat16)
    low = (field - high.astype(jnp.float32)).astype(jnp.bfloat16)
    both = jnp.dot(
        jnp.concatenate([high, low], axis=0), matrix, preferred_element_type=jnp.float32
    )
    return both[:rows] + both[rows:]


def roll(field, by, axis):
    return pltpu.roll(field, by % field.shape[axis], axis)


def load(ref, at, rows=STRIP):
    return [ref[t, pl.ds(at, rows), :] for t in range(ref.shape[0])]


def store(ref, at, strip):
    for t, part in enumerate(strip):
        ref[t, pl.ds(at, part.shape[0]), :] = part


def wide(ref, at, rows):
    return jnp.concatenate(load(ref, at, rows), axis=1)


def from_west(strip):
    lane = iota(strip[0].shape, 1)
    turned = [roll(part, 1, 1) for part in strip]
    return [jnp.where(lane == 0, turned[t - 1], turned[t]) for t in range(len(strip))]


def from_east(strip):
    lane = iota(strip[0].shape, 1)
    turned = [roll(part, -1, 1) for part in strip]
    count = len(strip)
    return [
        jnp.where(lane == LANES - 1, turned[(t + 1) % count], turned[t]) for t in range(count)
    ]


def read_taps(taps):
    return [[taps[a, b] for b in range(3)] for a in range(3)]


def tap_total(taps, power):
    return sum(tap * tap if power == 2 else tap for line in taps for tap in line)


def conv(ref, at, taps, flip):
    if flip:
        taps = [line[::-1] for line in taps[::-1]]
    above, here, below = load(ref, at - 1), load(ref, at), load(ref, at + 1)
    sums = [[], [], []]
    for t in range(len(here)):
        for b in range(3):
            sums[b].append(
                taps[0][b] * above[t] + taps[1][b] * here[t] + taps[2][b] * below[t]
            )
    west, east = from_west(sums[0]), from_east(sums[2])
    return [sums[1][t] + west[t] + east[t] for t in range(len(here))]


def laplace(ref, east_ref, south_ref, at):
    above, here, below = load(ref, at - 1), load(ref, at), load(ref, at + 1)
    east, south, north = load(east_ref, at), load(south_ref, at), load(south_ref, at - 1)
    beside = from_east(here)
    flux = [east[t] * (here[t] - beside[t]) for t in range(len(here))]
    back = from_west(flux)
    return here, [
        flux[t]
        - back[t]
        + south[t] * (here[t] - below[t])
        - north[t] * (above[t] - here[t])
        for t in range(len(here))
    ]


def spread_strip(spread, index):
    top, bottom = load(spread, 2 * index + EDGE - 1, 1), load(spread, 2 * index + EDGE, 1)
    shape = (EDGE, LANES)
    return [
        jnp.concatenate([jnp.broadcast_to(a, shape), jnp.broadcast_to(b, shape)], axis=0)
        for a, b in zip(top, bottom)
    ]


def side_lanes(has_e, has_w):
    return jnp.where(iota((STRIP, LANES), 1) < HALF, has_e, has_w)


def mask_rows(ref, has_n, has_s):
    last = ref.shape[1] - 2 * EDGE
    ref[:, EDGE : 2 * EDGE, :] = ref[:, EDGE : 2 * EDGE, :] * has_n
    ref[:, last : last + EDGE, :] = ref[:, last : last + EDGE, :] * has_s


def clear_pads(*refs):
    for ref in refs:
        empty = jnp.zeros((ref.shape[0], EDGE, LANES), jnp.float32)
        ref[:, :EDGE, :] = empty
        ref[:, ref.shape[1] - EDGE :, :] = empty


def product_sum(one, two, count, keep_top=None, keep_bottom=None):
    total = one[0] * two[0]
    for t in range(1, count):
        total = total + one[t] * two[t]
    top, bottom = total[:EDGE], total[EDGE:]
    if keep_top is not None:
        top, bottom = top * keep_top, bottom * keep_bottom
    return top + bottom


def strip_at(index):
    return pl.multiple_of(EDGE + STRIP * index, EDGE)


def jacobi(source, east, south, factor):
    west = roll(east, 1, 1)
    north = roll(south, 1, 0)
    iterate = factor * source
    for _ in range(SWEEPS - 1):
        around = (
            source
            + east * roll(iterate, -1, 1)
            + west * roll(iterate, 1, 1)
            + south * roll(iterate, -1, 0)
            + north * roll(iterate, 1, 0)
        )
        iterate = (1.0 - OMEGA) * iterate + factor * around
    return iterate


def in_pair_order(at, for_before, for_after):
    even = at % 2 == 0
    return jnp.where(even, for_after, for_before), jnp.where(even, for_before, for_after)


def pack_kernel(
    tiles,
    down,
    obs_in,
    class_in,
    weight_in,
    taps_in,
    obs_ref,
    cond_ref,
    coarse_ref,
    send_a,
    send_b,
    classes,
    weights,
    taps,
    sums,
    message,
    obs_sem,
    class_sem,
    small_sem,
):
    height = down * COARSE
    window = down + 2 * EDGE
    own = pl.ds(2 * EDGE, height)
    small = [
        pltpu.make_async_copy(weight_in, weights, small_sem.at[0]),
        pltpu.make_async_copy(taps_in, taps, small_sem.at[1]),
    ]
    moves = []
    for t in range(tiles):
        lanes = pl.ds(t * LANES, LANES)
        moves.append(
            (
                pltpu.make_async_copy(class_in.at[:, lanes], classes.at[t], class_sem.at[t]),
                pltpu.make_async_copy(
                    obs_in.at[:, lanes], obs_ref.at[t, own, :], obs_sem.at[t]
                ),
            )
        )
    for copy in small:
        copy.start()
    for pair in moves:
        for copy in pair:
            copy.start()
    sums[...] = jnp.zeros_like(sums)
    matrix = gather_matrix(tiles)
    for copy in small:
        copy.wait()
    values = [weights[class_id] for class_id in range(CLASSES)]
    fields = (obs_ref, cond_ref)
    for t in range(tiles):
        for copy in moves[t]:
            copy.wait()
        kind = classes[t]
        level = jnp.where(
            kind < 2,
            jnp.where(kind == 0, values[0], values[1]),
            jnp.where(kind == 2, values[2], values[3]),
        )
        cond_ref[t, own, :] = level
        for which, ref in enumerate(fields):
            picked = [
                ref[t, pl.ds(2 * EDGE + k, down, stride=COARSE), :] for k in range(COARSE)
            ]
            sums[3 * which, t, EDGE : EDGE + down, :] = sum(picked[1:], picked[0])
            sums[3 * which + 1, t, EDGE : EDGE + down, :] = picked[0]
            sums[3 * which + 2, t, EDGE : EDGE + down, :] = picked[-1]

    halves = height // LANES
    for which, ref in enumerate(fields):
        for slot, t, begin in ((0, 0, 0), (1, tiles - 1, LANES - EDGE)):
            turned = jnp.transpose(ref[t, own, :])[begin : begin + EDGE]
            for half in range(halves):
                at = (which * halves + half) * EDGE
                message[slot, at : at + EDGE, :] = turned[:, half * LANES : (half + 1) * LANES]
    taps = read_taps(taps)
    whole = lambda index: wide(sums.at[index], 0, window)
    full, head, tail = whole(0), whole(1), whole(2)
    by_tap = [full - head + roll(head, -1, 0), full, full - tail + roll(tail, 1, 0)]
    across = [sum(taps[a][b] * by_tap[a] for a in range(3)) for b in range(3)]
    source = across[1] + roll(across[0], -1, 1) + roll(across[2], 1, 1)
    full, head, tail = whole(3), whole(4), whole(5)
    last = (iota(full.shape, 1) & (COARSE - 1)) == COARSE - 1
    east = jnp.where(last, 0.5 * (full + roll(full, -1, 1)), 0.0)
    south = 0.5 * (tail + roll(head, -1, 0))
    cells = split_dot(jnp.concatenate([source, east, south], axis=0), matrix)
    source, east, south = cells[:window], cells[window : 2 * window], cells[2 * window :]
    around = east + roll(east, 1, 1) + south + roll(south, 1, 0)
    parts = [source, east, south, around]
    for index, part in enumerate(parts):
        coarse_ref[index] = part
    spare = jnp.zeros((2 * LANES - 4 * window, 2 * LANES), jnp.float32)
    stack = jnp.concatenate(parts + [spare], axis=0)
    left = jnp.transpose(stack[:, :LANES])
    right = jnp.transpose(stack[:, LANES:])
    base = 2 * halves * EDGE
    for slot, pieces in (
        (0, (left[:EDGE], right[LANES - EDGE :])),
        (1, (left[LANES - EDGE :], right[:EDGE])),
    ):
        for index, piece in enumerate(pieces):
            for half in range(2):
                at = base + (2 * index + half) * EDGE
                message[slot, at : at + EDGE, :] = piece[:, half * LANES : (half + 1) * LANES]
    send_a[...], send_b[...] = in_pair_order(place()[0], message[0], message[1])


def pack(observed, class_map, class_weights, taps):
    height, breadth = observed.shape
    tiles, down = breadth // LANES, height // COARSE
    window = down + 2 * EDGE
    field = (tiles + 1, height + 4 * EDGE, LANES)
    strip = ((2 * (height // LANES) + 4) * EDGE, LANES)
    return pl.pallas_call(
        functools.partial(pack_kernel, tiles, down),
        in_specs=[HBM] * 4,
        out_specs=[VMEM] * 5,
        out_shape=floats(field, field, (4, window, 2 * LANES), strip, strip),
        scratch_shapes=[
            pltpu.VMEM((tiles, height, LANES), jnp.int32),
            pltpu.SMEM(class_weights.shape, jnp.float32),
            pltpu.SMEM(taps.shape, jnp.float32),
            pltpu.VMEM((6, tiles + 1, window, LANES), jnp.float32),
            pltpu.VMEM((2,) + strip, jnp.float32),
            pltpu.SemaphoreType.DMA((tiles,)),
            pltpu.SemaphoreType.DMA((tiles,)),
            pltpu.SemaphoreType.DMA((2,)),
        ],
        compiler_params=params(),
        name="pack_east_west",
    )(observed, class_map, class_weights, taps)


def middle_kernel(
    tiles, down, got_a, got_b, coarse_in, obs_ref, cond_ref, side_ref, coarse_ref, send_a, send_b, message
):
    height = down * COARSE
    halves = height // LANES
    at_col, at_row, _, _ = place()
    from_e, from_w = in_pair_order(at_col, got_b[...], got_a[...])
    gap = jnp.zeros((LANES - 2 * EDGE, LANES), jnp.float32)

    def turned(low, high):
        return jnp.transpose(jnp.concatenate([low, gap, high], axis=0))

    for which in range(2):
        for half in range(halves):
            at = (which * halves + half) * EDGE
            side_ref[which, half * LANES : (half + 1) * LANES, :] = turned(
                from_e[at : at + EDGE], from_w[at : at + EDGE]
            )
    base = 2 * halves * EDGE

    def piece(strip, index, half):
        at = base + (2 * index + half) * EDGE
        return strip[at : at + EDGE]

    left = [turned(piece(from_w, 1, half), piece(from_e, 1, half)) for half in range(2)]
    right = [turned(piece(from_e, 0, half), piece(from_w, 0, half)) for half in range(2)]
    left = jnp.concatenate(left, axis=0)
    right = jnp.concatenate(right, axis=0)
    window = down + 2 * EDGE
    for index in range(4):
        rows = slice(index * window, (index + 1) * window)
        coarse_ref[index, :, :LANES] = coarse_in[index, :, :LANES] + left[rows]
        coarse_ref[index, :, LANES:] = coarse_in[index, :, LANES:] + right[rows]
    for slot, side_at, coarse_at in ((0, 0, 0), (1, height - EDGE, window - 2 * EDGE)):
        for which, field in enumerate((obs_ref, cond_ref)):
            for t in range(tiles + 1):
                at = (which * (tiles + 1) + t) * EDGE
                if t < tiles:
                    begin = 2 * EDGE + side_at
                    message[slot, at : at + EDGE, :] = field[t, begin : begin + EDGE, :]
                else:
                    message[slot, at : at + EDGE, :] = side_ref[
                        which, side_at : side_at + EDGE, :
                    ]
        for index in range(4):
            for half in range(2):
                at = 2 * (tiles + 1) * EDGE + (2 * index + half) * 2 * EDGE
                message[slot, at : at + 2 * EDGE, :] = coarse_ref[
                    index, coarse_at : coarse_at + 2 * EDGE, half * LANES : (half + 1) * LANES
                ]
    send_a[...], send_b[...] = in_pair_order(at_row, message[0], message[1])


def middle(got_a, got_b, coarse, obs, cond):
    tiles, height = obs.shape[0] - 1, obs.shape[1] - 4 * EDGE
    down = height // COARSE
    long = (2 * (tiles + 1) * EDGE + 16 * EDGE, LANES)
    return pl.pallas_call(
        functools.partial(middle_kernel, tiles, down),
        in_specs=[VMEM] * 5,
        out_specs=[VMEM] * 4,
        out_shape=floats((2, height, LANES), coarse.shape, long, long),
        scratch_shapes=[pltpu.VMEM((2,) + long, jnp.float32)],
        compiler_params=params(),
        name="pack_north_south",
    )(got_a, got_b, coarse, obs, cond)


def first_kernel(
    tiles,
    down,
    taps,
    obs_in,
    cond_in,
    side_ref,
    got_a,
    got_b,
    coarse_in,
    obs,
    cond,
    res_ref,
    p_ref,
    q_ref,
    east_ref,
    south_ref,
    inv_ref,
    table_ref,
    own_ref,
    chunk_ref,
    dots_ref,
    image,
    spread,
):
    height = down * COARSE
    window = down + 2 * EDGE
    strips = height // STRIP + 1
    at_col, at_row, n_cols, n_rows = place()
    has_n, has_s, has_e, has_w = has_sides()
    from_s, from_n = in_pair_order(at_row, got_b[...], got_a[...])
    clear_pads(obs, cond, p_ref, image, res_ref, q_ref, east_ref, south_ref, inv_ref)
    for which, field in enumerate((obs, cond)):
        field[tiles, 2 * EDGE : 2 * EDGE + height, :] = side_ref[which]
        for t in range(tiles + 1):
            at = (which * (tiles + 1) + t) * EDGE
            field[t, EDGE : 2 * EDGE, :] = from_n[at : at + EDGE]
            field[t, 2 * EDGE + height : 3 * EDGE + height, :] = from_s[at : at + EDGE]

    base = 2 * (tiles + 1) * EDGE

    def joined(index):
        def part(strip):
            at = [base + (2 * index + half) * 2 * EDGE for half in range(2)]
            return jnp.concatenate([strip[a : a + 2 * EDGE] for a in at], axis=1)

        gap = jnp.zeros((window - 4 * EDGE, 2 * LANES), jnp.float32)
        return coarse_in[index] + jnp.concatenate([part(from_n), gap, part(from_s)], axis=0)

    source, east, south, around = [joined(index) for index in range(4)]
    row = iota(source.shape, 0)
    lane = iota(source.shape, 1)
    inside = jnp.where(row < EDGE, has_n, jnp.where(row < window - EDGE, 1.0, has_s))
    inside = inside * jnp.where(
        lane < LANES, 1.0, jnp.where(lane < LANES + HALF, has_e, has_w)
    )
    taps = read_taps(taps)
    total = tap_total(taps, 1)
    factor = inside * OMEGA / (COARSE * COARSE * total * total + around)
    table_ref[0] = east
    table_ref[1] = south
    table_ref[2] = factor
    cells = split_dot(jacobi(source, east, south, factor), spread_matrix(tiles))
    for t in range(tiles + 1):
        spread[t] = cells[:, t * LANES : (t + 1) * LANES]

    squares = tap_total(taps, 2)
    sides = side_lanes(has_e, has_w)

    def keeps(index):
        return jnp.where(index > 0, 1.0, 0.0), jnp.where(index < strips - 1, 1.0, 0.0)

    def start(index, total):
        at = strip_at(index)
        above, here, below = load(cond, at - 1), load(cond, at), load(cond, at + 1)
        right = from_east(here)
        span = range(tiles + 1)
        to_e = [0.5 * (here[t] + right[t]) for t in span]
        to_w = from_west(to_e)
        to_s = [0.5 * (here[t] + below[t]) for t in span]
        inverse = [
            1.0 / (squares + to_e[t] + to_w[t] + to_s[t] + 0.5 * (here[t] + above[t]))
            for t in span
        ]
        inverse[tiles] = inverse[tiles] * sides
        residual = conv(obs, at, taps, True)
        cells = spread_strip(spread, index)
        direction = [residual[t] * inverse[t] + cells[t] for t in span]
        store(east_ref, at, to_e)
        store(south_ref, at, to_s)
        store(inv_ref, at, inverse)
        store(res_ref, at, residual)
        store(p_ref, at, direction)
        return total + product_sum(residual, direction, tiles, *keeps(index))

    def blur(index, _):
        at = strip_at(index)
        blurred = conv(p_ref, at, taps, False)
        blurred[tiles] = blurred[tiles] * sides
        store(image, at, blurred)
        return 0

    def finish(index, total):
        at = strip_at(index)
        here, pulled = laplace(p_ref, east_ref, south_ref, at)
        back = conv(image, at, taps, True)
        product = [back[t] + pulled[t] for t in range(tiles + 1)]
        store(q_ref, at, product)
        return total + product_sum(here, product, tiles, *keeps(index))

    nothing = jnp.zeros((EDGE, LANES), jnp.float32)
    dots_ref[0] = lax.fori_loop(0, strips, start, nothing)
    mask_rows(inv_ref, has_n, has_s)
    mask_rows(p_ref, has_n, has_s)
    lax.fori_loop(0, strips, blur, 0)
    mask_rows(image, has_n, has_s)
    dots_ref[1] = lax.fori_loop(0, strips, finish, nothing)

    shape = (tiles * LANES, LANES)
    matrix = jnp.where(iota(shape, 0) >> 3 == iota(shape, 1), 1.0, 0.0).astype(jnp.bfloat16)
    flat = []
    for t in range(tiles):
        picked = [
            q_ref[t, pl.ds(2 * EDGE + k, down, stride=COARSE), :] for k in range(COARSE)
        ]
        flat.append(sum(picked[1:], picked[0]))
    own = split_dot(jnp.concatenate(flat, axis=1), matrix)
    own_ref[...] = own
    spare = jnp.zeros((LANES - down, LANES), jnp.float32)
    turned = jnp.transpose(jnp.concatenate([own, spare], axis=0))
    chunk_ref[...] = jnp.zeros_like(chunk_ref)
    for down_by in (-1, 0, 1):
        for right_by in (-1, 0, 1):
            if down_by == 0 and right_by == 0:
                continue
            if down_by == 0:
                piece = turned[:EDGE] if right_by < 0 else turned[LANES - EDGE :]
            else:
                piece = own[:EDGE] if down_by < 0 else own[down - EDGE :]
            to_row, to_col = at_row + down_by, at_col + right_by

            @pl.when((to_row >= 0) & (to_row < n_rows) & (to_col >= 0) & (to_col < n_cols))
            def _(piece=piece, to_row=to_row, to_col=to_col):
                chunk_ref[to_col * n_rows + to_row] = piece


def first(taps, obs, cond, side, got_a, got_b, coarse):
    field = obs.shape
    tiles, height = field[0] - 1, field[1] - 4 * EDGE
    down = height // COARSE
    window = down + 2 * EDGE
    count = lax.axis_size("cols") * lax.axis_size("rows")
    shapes = [field] * 8 + [
        (3, window, 2 * LANES),
        (down, LANES),
        (count, EDGE, LANES),
        (2, EDGE, LANES),
    ]
    return pl.pallas_call(
        functools.partial(first_kernel, tiles, down),
        in_specs=[SMEM] + [VMEM] * 6,
        out_specs=[VMEM] * len(shapes),
        out_shape=floats(*shapes),
        input_output_aliases={1: 0, 2: 1},
        scratch_shapes=[
            pltpu.VMEM(field, jnp.float32),
            pltpu.VMEM((tiles + 1, window, LANES), jnp.float32),
        ],
        compiler_params=params(),
        name="first_direction",
    )(taps, obs, cond, side, got_a, got_b, coarse)[2:]


def second_kernel(
    tiles,
    down,
    taps,
    got_ref,
    own_ref,
    table_ref,
    q_ref,
    east_ref,
    south_ref,
    inv_ref,
    dots_in,
    w_ref,
    v_ref,
    out_ref,
    image,
    spread,
):
    height = down * COARSE
    strips = height // STRIP + 1
    has_n, has_s, has_e, has_w = has_sides()
    at_col, at_row, n_cols, n_rows = place()
    me = at_col * n_rows + at_row

    def got(down_by, right_by):
        to_row, to_col = at_row + down_by, at_col + right_by
        there = (to_row >= 0) & (to_row < n_rows) & (to_col >= 0) & (to_col < n_cols)
        return got_ref[jnp.where(there, to_col * n_rows + to_row, me)]

    low = iota((EDGE, LANES), 1) < HALF
    gap = jnp.zeros((LANES - 2 * EDGE, LANES), jnp.float32)
    beside = jnp.transpose(jnp.concatenate([got(0, 1), gap, got(0, -1)], axis=0))[:down]
    source = jnp.concatenate(
        [
            jnp.concatenate([got(-1, 0), jnp.where(low, got(-1, 1), got(-1, -1))], axis=1),
            jnp.concatenate([own_ref[...], beside], axis=1),
            jnp.concatenate([got(1, 0), jnp.where(low, got(1, 1), got(1, -1))], axis=1),
        ],
        axis=0,
    )
    cells = jacobi(source, table_ref[0], table_ref[1], table_ref[2])
    cells = split_dot(cells, spread_matrix(tiles))
    for t in range(tiles + 1):
        spread[t] = cells[:, t * LANES : (t + 1) * LANES]
    clear_pads(w_ref, image, v_ref)
    sides = side_lanes(has_e, has_w)
    taps = read_taps(taps)

    def start(index, _):
        at = strip_at(index)
        field, inverse = load(q_ref, at), load(inv_ref, at)
        cells = spread_strip(spread, index)
        store(w_ref, at, [field[t] * inverse[t] + cells[t] for t in range(tiles + 1)])
        return 0

    def blur(index, _):
        at = strip_at(index)
        blurred = conv(w_ref, at, taps, False)
        blurred[tiles] = blurred[tiles] * sides
        store(image, at, blurred)
        return 0

    def finish(index, totals):
        at = pl.multiple_of(2 * EDGE + STRIP * index, EDGE)
        here, pulled = laplace(w_ref, east_ref, south_ref, at)
        back = conv(image, at, taps, True)
        product = [back[t] + pulled[t] for t in range(tiles + 1)]
        field = load(q_ref, at)
        store(v_ref, at, product)
        return (
            totals[0] + product_sum(field, here, tiles),
            totals[1] + product_sum(here, product, tiles),
        )

    nothing = jnp.zeros((EDGE, LANES), jnp.float32)
    lax.fori_loop(0, strips, start, 0)
    lax.fori_loop(0, strips, blur, 0)
    mask_rows(image, has_n, has_s)
    dot_qw, dot_wv = lax.fori_loop(0, strips - 1, finish, (nothing, nothing))
    line = jnp.zeros((1, LANES), jnp.float32)
    at_lane = iota((1, LANES), 1)
    for index, part in enumerate((dots_in[0], dots_in[1], dot_qw, dot_wv)):
        line = line + jnp.where(at_lane == index, jnp.sum(part), 0.0)
    for index in range(out_ref.shape[0]):
        out_ref[index] = line


def second(taps, got, own, table, q, east, south, inv, dots):
    tiles, height = q.shape[0] - 1, q.shape[1] - 4 * EDGE
    down = height // COARSE
    window = down + 2 * EDGE
    return pl.pallas_call(
        functools.partial(second_kernel, tiles, down),
        in_specs=[SMEM] + [VMEM] * 8,
        out_specs=[VMEM] * 3,
        out_shape=floats(q.shape, q.shape, (got.shape[0], 1, LANES)),
        scratch_shapes=[
            pltpu.VMEM(q.shape, jnp.float32),
            pltpu.VMEM((tiles + 1, window, LANES), jnp.float32),
        ],
        compiler_params=params(),
        name="second_direction",
    )(taps, got, own, table, q, east, south, inv, dots)


def combine_kernel(
    tiles, height, sums_ref, p_ref, w_ref, r_ref, q_ref, v_ref, sol_out, res_out, sol, res, sem
):
    line = sums_ref[0]
    for index in range(1, sums_ref.shape[0]):
        line = line + sums_ref[index]
    lane = iota((1, LANES), 1)
    pick = lambda index: jnp.sum(jnp.where(lane == index, line, 0.0), axis=1, keepdims=True)
    rp, pq, qw, wv = [pick(index) for index in range(4)]
    step = rp / pq
    rp_next = step * step * qw - rp
    ratio = rp_next / rp
    lead = 1.0 + ratio
    curvature = lead * lead * pq - 2.0 * lead * step * qw + step * step * wv
    step_next = rp_next / curvature
    on_p = jnp.broadcast_to(step + step_next * lead, (STRIP, LANES))
    on_w = jnp.broadcast_to(step_next * step, (STRIP, LANES))

    def copies(index):
        rows = pl.ds(pl.multiple_of(index * STRIP, STRIP), STRIP)
        return (
            pltpu.make_async_copy(sol.at[rows, :], sol_out.at[rows, :], sem.at[0, index]),
            pltpu.make_async_copy(res.at[rows, :], res_out.at[rows, :], sem.at[1, index]),
        )

    def work(index, _):
        at = pl.multiple_of(index * STRIP, STRIP)
        p, w, r, q, v = [
            load(ref, at + 2 * EDGE) for ref in (p_ref, w_ref, r_ref, q_ref, v_ref)
        ]
        one = [on_p * p[t] - on_w * w[t] for t in range(tiles)]
        two = [r[t] - on_p * q[t] + on_w * v[t] for t in range(tiles)]
        for t in range(tiles):
            sol[pl.ds(at, STRIP), t * LANES : (t + 1) * LANES] = one[t]
            res[pl.ds(at, STRIP), t * LANES : (t + 1) * LANES] = two[t]
        for copy in copies(index):
            copy.start()
        return 0

    def settle(index, _):
        for copy in copies(index):
            copy.wait()
        return 0

    lax.fori_loop(0, height // STRIP, work, 0)
    lax.fori_loop(0, height // STRIP, settle, 0)


def combine(sums, p, w, r, q, v):
    tiles, height = q.shape[0] - 1, q.shape[1] - 4 * EDGE
    shape = (height, tiles * LANES)
    return pl.pallas_call(
        functools.partial(combine_kernel, tiles, height),
        in_specs=[VMEM] * 6,
        out_specs=[HBM] * 2,
        out_shape=floats(shape, shape),
        scratch_shapes=[
            pltpu.VMEM(shape, jnp.float32),
            pltpu.VMEM(shape, jnp.float32),
            pltpu.SemaphoreType.DMA((2, height // STRIP)),
        ],
        compiler_params=params(),
        name="combine",
    )(sums, p, w, r, q, v)


def exchange(send_a, send_b, axis):
    count = lax.axis_size(axis)

    def pairs(begin):
        return [
            pair for i in range(begin, count - 1, 2) for pair in ((i, i + 1), (i + 1, i))
        ]

    return lax.ppermute(send_a, axis, pairs(0)), lax.ppermute(send_b, axis, pairs(1))


def body(observed, class_map, class_weights, blur_kernel):
    obs, cond, coarse, send_a, send_b = pack(observed, class_map, class_weights, blur_kernel)
    got_a, got_b = exchange(send_a, send_b, "cols")
    side, coarse, send_a, send_b = middle(got_a, got_b, coarse, obs, cond)
    got_a, got_b = exchange(send_a, send_b, "rows")
    r, p, q, east, south, inv, table, own, chunk, dots = first(
        blur_kernel, obs, cond, side, got_a, got_b, coarse
    )
    got = lax.all_to_all(chunk, AXES, 0, 0, tiled=True)
    w, v, line = second(blur_kernel, got, own, table, q, east, south, inv, dots)
    sums = lax.all_to_all(line, AXES, 0, 0, tiled=True)
    return tuple(combine(sums, p, w, r, q, v))


def solution(mesh):
    return jax.shard_map(
        body,
        mesh=mesh,
        in_specs=(P("rows", "cols"), P("rows", "cols"), P(), P()),
        out_specs=(P("rows", "cols"), P("rows", "cols")),
        check_vma=False,
    )
```

```python
import functools

import jax
import jax.numpy as jnp
from jax import lax
from jax.experimental import pallas as pl
from jax.experimental.pallas import tpu as pltpu
from jax.sharding import PartitionSpec as P

COARSE = 8
SWEEPS = 8
CLASSES = 4
OMEGA = 0.8

LANES = 128
HALF = LANES // 2
EDGE = 8
STRIP = 2 * EDGE
AXES = ("cols", "rows")
LIMIT = 40 * 1024 * 1024


VMEM = pl.BlockSpec(memory_space=pltpu.VMEM)
SMEM = pl.BlockSpec(memory_space=pltpu.SMEM)
HBM = pl.BlockSpec(memory_space=pltpu.HBM)


def params():
    return pltpu.CompilerParams(vmem_limit_bytes=LIMIT)


def in_hbm(array):
    return pltpu.with_memory_space_constraint(array, pltpu.HBM)


def floats(*shapes):
    return [jax.ShapeDtypeStruct(shape, jnp.float32) for shape in shapes]


def place():
    at_col, at_row = lax.axis_index("cols"), lax.axis_index("rows")
    n_cols, n_rows = lax.axis_size("cols"), lax.axis_size("rows")
    return at_col, at_row, n_cols, n_rows


def has_sides():
    at_col, at_row, n_cols, n_rows = place()
    flag = lambda test: jnp.where(test, 1.0, 0.0).astype(jnp.float32)
    return (
        flag(at_row > 0),
        flag(at_row < n_rows - 1),
        flag(at_col < n_cols - 1),
        flag(at_col > 0),
    )


def iota(shape, dim):
    return lax.broadcasted_iota(jnp.int32, shape, dim)


def cell_of(pixel, tiles):
    turn = (tiles + 1) * LANES
    return jnp.where(pixel < turn - HALF, pixel >> 3, ((pixel - turn) >> 3) & (2 * LANES - 1))


def gather_matrix(tiles):
    shape = ((tiles + 1) * LANES, 2 * LANES)
    hit = cell_of(iota(shape, 0), tiles) == iota(shape, 1)
    return jnp.where(hit, 1.0, 0.0).astype(jnp.bfloat16)


def spread_matrix(tiles):
    shape = (2 * LANES, (tiles + 1) * LANES)
    hit = cell_of(iota(shape, 1), tiles) == iota(shape, 0)
    return jnp.where(hit, 1.0, 0.0).astype(jnp.bfloat16)


def split_dot(field, matrix):
    rows = field.shape[0]
    high = field.astype(jnp.bfloat16)
    low = (field - high.astype(jnp.float32)).astype(jnp.bfloat16)
    both = jnp.dot(
        jnp.concatenate([high, low], axis=0), matrix, preferred_element_type=jnp.float32
    )
    return both[:rows] + both[rows:]


def roll(field, by, axis):
    return pltpu.roll(field, by % field.shape[axis], axis)


def load(ref, at, rows=STRIP):
    return [ref[t, pl.ds(at, rows), :] for t in range(ref.shape[0])]


def store(ref, at, strip):
    for t, part in enumerate(strip):
        ref[t, pl.ds(at, part.shape[0]), :] = part


def wide(ref, at, rows):
    return jnp.concatenate(load(ref, at, rows), axis=1)


def from_west(strip):
    lane = iota(strip[0].shape, 1)
    turned = [roll(part, 1, 1) for part in strip]
    return [jnp.where(lane == 0, turned[t - 1], turned[t]) for t in range(len(strip))]


def from_east(strip):
    lane = iota(strip[0].shape, 1)
    turned = [roll(part, -1, 1) for part in strip]
    count = len(strip)
    return [
        jnp.where(lane == LANES - 1, turned[(t + 1) % count], turned[t]) for t in range(count)
    ]


def read_taps(taps):
    return [[taps[a, b] for b in range(3)] for a in range(3)]


def tap_total(taps, power):
    return sum(tap * tap if power == 2 else tap for line in taps for tap in line)


def tap_sums(ref, at, taps, flip):
    if flip:
        taps = [line[::-1] for line in taps[::-1]]
    above, here, below = load(ref, at - 1), load(ref, at), load(ref, at + 1)
    sums = [[], [], []]
    for t in range(len(here)):
        for b in range(3):
            sums[b].append(
                taps[0][b] * above[t] + taps[1][b] * here[t] + taps[2][b] * below[t]
            )
    return sums


def conv(ref, at, taps, flip):
    sums = tap_sums(ref, at, taps, flip)
    west, east = from_west(sums[0]), from_east(sums[2])
    return [sums[1][t] + west[t] + east[t] for t in range(len(west))]


def operate(ref, image, east_ref, south_ref, at, taps):
    above, here, below = load(ref, at - 1), load(ref, at), load(ref, at + 1)
    east, south, north = load(east_ref, at), load(south_ref, at), load(south_ref, at - 1)
    sums = tap_sums(image, at, taps, True)
    span = range(len(here))
    beside = from_east(here)
    flux = [east[t] * (here[t] - beside[t]) for t in span]
    from_left = from_west([sums[0][t] - flux[t] for t in span])
    from_right = from_east(sums[2])
    return here, [
        sums[1][t]
        + flux[t]
        + from_left[t]
        + from_right[t]
        + south[t] * (here[t] - below[t])
        - north[t] * (above[t] - here[t])
        for t in span
    ]


def begin(obs, cond, at, taps, sides):
    above, here, below = load(cond, at - 1), load(cond, at), load(cond, at + 1)
    span = range(len(here))
    right = from_east(here)
    east = [here[t] + right[t] for t in span]
    west = from_west(east)
    south = [here[t] + below[t] for t in span]
    squares = tap_total(taps, 2)
    inverse = [
        1.0 / (squares + east[t] + west[t] + south[t] + (here[t] + above[t])) for t in span
    ]
    inverse[-1] = inverse[-1] * sides
    return east, south, inverse, conv(obs, at, taps, True)


def spread_strip(spread, index):
    top, bottom = load(spread, 2 * index + EDGE - 1, 1), load(spread, 2 * index + EDGE, 1)
    shape = (EDGE, LANES)
    return [
        jnp.concatenate([jnp.broadcast_to(a, shape), jnp.broadcast_to(b, shape)], axis=0)
        for a, b in zip(top, bottom)
    ]


def side_lanes(has_e, has_w):
    return jnp.where(iota((STRIP, LANES), 1) < HALF, has_e, has_w)


def mask_rows(ref, has_n, has_s):
    last = ref.shape[1] - 2 * EDGE
    ref[:, EDGE : 2 * EDGE, :] = ref[:, EDGE : 2 * EDGE, :] * has_n
    ref[:, last : last + EDGE, :] = ref[:, last : last + EDGE, :] * has_s


def clear_pads(*refs):
    for ref in refs:
        empty = jnp.zeros((ref.shape[0], EDGE, LANES), jnp.float32)
        ref[:, :EDGE, :] = empty
        ref[:, ref.shape[1] - EDGE :, :] = empty


def product_sum(one, two, count, keep_top=None, keep_bottom=None):
    total = one[0] * two[0]
    for t in range(1, count):
        total = total + one[t] * two[t]
    top, bottom = total[:EDGE], total[EDGE:]
    if keep_top is not None:
        top, bottom = top * keep_top, bottom * keep_bottom
    return top + bottom


def sweep(count, group, body, carry):
    def some(first_index, width, carry):
        stores = []
        for offset in range(width):
            more, carry = body(first_index + offset, carry)
            stores += more
        for ref, at, strip in stores:
            store(ref, at, strip)
        return carry

    steps = count // group
    carry = lax.fori_loop(0, steps, lambda step, c: some(step * group, group, c), carry)
    left = count - steps * group
    return some(steps * group, left, carry) if left else carry


def strip_at(index):
    return pl.multiple_of(EDGE + STRIP * index, EDGE)


def jacobi(source, table):
    factor, east, west, south, north = table
    source = factor * source
    iterate = source
    for _ in range(SWEEPS - 1):
        across = east * roll(iterate, -1, 1) + west * roll(iterate, 1, 1)
        along = south * roll(iterate, -1, 0) + north * roll(iterate, 1, 0)
        iterate = ((1.0 - OMEGA) * iterate + source) + (across + along)
    return iterate


def in_pair_order(at, for_before, for_after):
    even = at % 2 == 0
    return jnp.where(even, for_after, for_before), jnp.where(even, for_before, for_after)


def reader(tiles_here, refs, scratch, obs, cond, down):
    obs_in, class_in, weight_in, taps_in = refs
    classes, weights, taps, sums, obs_sem, class_sem, small_sem = scratch
    own = pl.ds(2 * EDGE, down * COARSE)
    small = [
        pltpu.make_async_copy(weight_in, weights, small_sem.at[0]),
        pltpu.make_async_copy(taps_in, taps, small_sem.at[1]),
    ]
    moves = []
    for slot, t in enumerate(tiles_here):
        lanes = pl.ds(t * LANES, LANES)
        moves.append(
            (
                pltpu.make_async_copy(class_in.at[:, lanes], classes.at[slot], class_sem.at[slot]),
                pltpu.make_async_copy(
                    obs_in.at[:, lanes], obs.at[slot, own, :], obs_sem.at[slot]
                ),
            )
        )
    for copy in small:
        copy.start()
    for pair in moves:
        for copy in pair:
            copy.start()
    sums[...] = jnp.zeros_like(sums)

    def settle(slot):
        if slot == 0:
            for copy in small:
                copy.wait()
        for copy in moves[slot]:
            copy.wait()
        values = [0.5 * weights[class_id] for class_id in range(CLASSES)]
        kind = classes[slot]
        cond[slot, own, :] = jnp.where(
            kind < 2,
            jnp.where(kind == 0, values[0], values[1]),
            jnp.where(kind == 2, values[2], values[3]),
        )
        for which, ref in enumerate((obs, cond)):
            picked = [
                ref[slot, pl.ds(2 * EDGE + k, down, stride=COARSE), :] for k in range(COARSE)
            ]
            sums[3 * which, slot, EDGE : EDGE + down, :] = sum(picked[1:], picked[0])
            sums[3 * which + 1, slot, EDGE : EDGE + down, :] = picked[0]
            sums[3 * which + 2, slot, EDGE : EDGE + down, :] = picked[-1]

    return settle


def reader_scratch(tiles, height, window, class_weights, taps):
    return [
        pltpu.VMEM((tiles, height, LANES), jnp.int32),
        pltpu.SMEM(class_weights.shape, jnp.float32),
        pltpu.SMEM(taps.shape, jnp.float32),
        pltpu.VMEM((6, tiles + 1, window, LANES), jnp.float32),
        pltpu.SemaphoreType.DMA((tiles,)),
        pltpu.SemaphoreType.DMA((tiles,)),
        pltpu.SemaphoreType.DMA((2,)),
    ]


def coarse_parts(sums, taps, matrix):
    window = sums.shape[2]
    whole = lambda index: wide(sums.at[index], 0, window)
    full, head, tail = whole(0), whole(1), whole(2)
    by_tap = [full - head + roll(head, -1, 0), full, full - tail + roll(tail, 1, 0)]
    across = [sum(taps[a][b] * by_tap[a] for a in range(3)) for b in range(3)]
    source = across[1] + roll(across[0], -1, 1) + roll(across[2], 1, 1)
    full, head, tail = whole(3), whole(4), whole(5)
    last = (iota(full.shape, 1) & (COARSE - 1)) == COARSE - 1
    east = jnp.where(last, full + roll(full, -1, 1), 0.0)
    south = tail + roll(head, -1, 0)
    cells = split_dot(jnp.concatenate([source, east, south], axis=0), matrix)
    source, east, south = cells[:window], cells[window : 2 * window], cells[2 * window :]
    around = east + roll(east, 1, 1) + south + roll(south, 1, 0)
    return [source, east, south, around]


def edge_kernel(tiles, down, *refs):
    arguments, (send_a, send_b), (obs, cond, message, *scratch) = refs[:4], refs[4:6], refs[6:]
    height = down * COARSE
    halves = height // LANES
    window = down + 2 * EDGE
    settle = reader((0, tiles - 1), arguments, scratch, obs, cond, down)
    matrix = gather_matrix(2)
    for slot, begin_row in ((0, 0), (1, LANES - EDGE)):
        settle(slot)
        for which, ref in enumerate((obs, cond)):
            turned = jnp.transpose(ref[slot, 2 * EDGE : 2 * EDGE + height, :])
            turned = turned[begin_row : begin_row + EDGE]
            for half in range(halves):
                at = (which * halves + half) * EDGE
                message[slot, at : at + EDGE, :] = turned[:, half * LANES : (half + 1) * LANES]
    parts = coarse_parts(scratch[3], read_taps(scratch[2]), matrix)
    spare = jnp.zeros((2 * LANES - 4 * window, 2 * LANES), jnp.float32)
    stack = jnp.concatenate(parts + [spare], axis=0)
    left = jnp.transpose(stack[:, :LANES])
    right = jnp.transpose(stack[:, LANES:])
    base = 2 * halves * EDGE
    past = 2 * LANES // COARSE
    for slot, pieces in (
        (0, (left[:EDGE], right[LANES - EDGE :])),
        (1, (left[past - EDGE : past], left[past : past + EDGE])),
    ):
        for index, piece in enumerate(pieces):
            for half in range(2):
                at = base + (2 * index + half) * EDGE
                message[slot, at : at + EDGE, :] = piece[:, half * LANES : (half + 1) * LANES]
    send_a[...], send_b[...] = in_pair_order(place()[0], message[0], message[1])


def edge(observed, class_map, class_weights, taps):
    height, breadth = observed.shape
    tiles, down = breadth // LANES, height // COARSE
    window = down + 2 * EDGE
    field = (3, height + 4 * EDGE, LANES)
    strip = ((2 * (height // LANES) + 4) * EDGE, LANES)
    return pl.pallas_call(
        functools.partial(edge_kernel, tiles, down),
        in_specs=[HBM] * 4,
        out_specs=[VMEM] * 2,
        out_shape=floats(strip, strip),
        scratch_shapes=[
            pltpu.VMEM(field, jnp.float32),
            pltpu.VMEM(field, jnp.float32),
            pltpu.VMEM((2,) + strip, jnp.float32),
        ]
        + reader_scratch(2, height, window, class_weights, taps),
        compiler_params=params(),
        name="pack_east_west",
    )(*[in_hbm(array) for array in (observed, class_map, class_weights, taps)])


def pack_kernel(tiles, down, *refs):
    arguments, (obs, cond, coarse_ref), scratch = refs[:4], refs[5:8], refs[8:]
    settle = reader(range(tiles), arguments, scratch, obs, cond, down)
    matrix = gather_matrix(tiles)
    for t in range(tiles):
        settle(t)
    for index, part in enumerate(coarse_parts(scratch[3], read_taps(scratch[2]), matrix)):
        coarse_ref[index] = part


def pack(observed, class_map, class_weights, taps, after):
    height, breadth = observed.shape
    tiles, down = breadth // LANES, height // COARSE
    window = down + 2 * EDGE
    field = (tiles + 1, height + 4 * EDGE, LANES)
    pixels = height * breadth
    return pl.pallas_call(
        functools.partial(pack_kernel, tiles, down),
        in_specs=[HBM] * 4 + [VMEM],
        out_specs=[VMEM] * 3,
        out_shape=floats(field, field, (4, window, 2 * LANES)),
        scratch_shapes=reader_scratch(tiles, height, window, class_weights, taps),
        compiler_params=params(),
        cost_estimate=pl.CostEstimate(
            flops=20 * pixels, bytes_accessed=16 * pixels, transcendentals=0
        ),
        name="pack_all",
    )(*[in_hbm(array) for array in (observed, class_map, class_weights, taps)], after)


def middle_kernel(
    tiles,
    down,
    got_b,
    got_a,
    coarse_in,
    obs_in,
    cond_in,
    obs,
    cond,
    coarse_ref,
    send_a,
    send_b,
    message,
):
    height = down * COARSE
    halves = height // LANES
    at_col, at_row, _, _ = place()
    from_e, from_w = in_pair_order(at_col, got_b[...], got_a[...])
    gap = jnp.zeros((LANES - 2 * EDGE, LANES), jnp.float32)

    def turned(low, high):
        return jnp.transpose(jnp.concatenate([low, gap, high], axis=0))

    for which, field in enumerate((obs, cond)):
        for half in range(halves):
            at = (which * halves + half) * EDGE
            begin_row = 2 * EDGE + half * LANES
            field[tiles, begin_row : begin_row + LANES, :] = turned(
                from_e[at : at + EDGE], from_w[at : at + EDGE]
            )
    base = 2 * halves * EDGE

    def piece(strip, index, half):
        at = base + (2 * index + half) * EDGE
        return strip[at : at + EDGE]

    left = [turned(piece(from_w, 1, half), piece(from_e, 1, half)) for half in range(2)]
    right = [turned(piece(from_e, 0, half), piece(from_w, 0, half)) for half in range(2)]
    left = jnp.concatenate(left, axis=0)
    right = jnp.concatenate(right, axis=0)
    window = down + 2 * EDGE
    for index in range(4):
        rows = slice(index * window, (index + 1) * window)
        coarse_ref[index, :, :LANES] = coarse_in[index, :, :LANES] + left[rows]
        coarse_ref[index, :, LANES:] = coarse_in[index, :, LANES:] + right[rows]
    for slot, begin_row, coarse_at in (
        (0, 2 * EDGE, 0),
        (1, EDGE + height, window - 2 * EDGE),
    ):
        for which, field in enumerate((obs, cond)):
            for t in range(tiles + 1):
                at = (which * (tiles + 1) + t) * EDGE
                message[slot, at : at + EDGE, :] = field[t, begin_row : begin_row + EDGE, :]
        for index in range(4):
            for half in range(2):
                at = 2 * (tiles + 1) * EDGE + (2 * index + half) * 2 * EDGE
                message[slot, at : at + 2 * EDGE, :] = coarse_ref[
                    index, coarse_at : coarse_at + 2 * EDGE, half * LANES : (half + 1) * LANES
                ]
    send_a[...], send_b[...] = in_pair_order(at_row, message[0], message[1])


def middle(got_a, got_b, coarse, obs, cond):
    tiles, height = obs.shape[0] - 1, obs.shape[1] - 4 * EDGE
    down = height // COARSE
    long = (2 * (tiles + 1) * EDGE + 16 * EDGE, LANES)
    return pl.pallas_call(
        functools.partial(middle_kernel, tiles, down),
        in_specs=[VMEM] * 5,
        out_specs=[VMEM] * 5,
        out_shape=floats(obs.shape, cond.shape, coarse.shape, long, long),
        input_output_aliases={3: 0, 4: 1},
        scratch_shapes=[pltpu.VMEM((2,) + long, jnp.float32)],
        compiler_params=params(),
        name="pack_north_south",
    )(got_b, got_a, coarse, obs, cond)


def inner_kernel(tiles, taps, obs, cond, res_ref, east_ref, south_ref, inv_ref, spread_ref):
    strips = (obs.shape[1] - 2 * EDGE) // STRIP
    _, _, has_e, has_w = has_sides()
    clear_pads(east_ref, south_ref)
    spread_ref[...] = spread_matrix(tiles)
    taps = read_taps(taps)
    sides = side_lanes(has_e, has_w)

    def work(index, _):
        at = strip_at(index + 1)
        fields = begin(obs, cond, at, taps, sides)
        return [
            (ref, at, strip)
            for ref, strip in zip((east_ref, south_ref, inv_ref, res_ref), fields)
        ], 0

    sweep(strips - 2, 1, work, 0)


def inner(taps, obs, cond):
    field = obs.shape
    tiles = field[0] - 1
    pixels = field[0] * field[1] * field[2]
    return pl.pallas_call(
        functools.partial(inner_kernel, tiles),
        in_specs=[SMEM] + [VMEM] * 2,
        out_specs=[VMEM] * 5,
        out_shape=floats(field, field, field, field)
        + [jax.ShapeDtypeStruct((2 * LANES, (tiles + 1) * LANES), jnp.bfloat16)],
        compiler_params=params(),
        cost_estimate=pl.CostEstimate(
            flops=45 * pixels, bytes_accessed=24 * pixels, transcendentals=0
        ),
        name="inner_strips",
    )(taps, obs, cond)


def first_kernel(
    tiles,
    down,
    taps,
    obs_in,
    cond_in,
    res_in,
    east_in,
    south_in,
    inv_in,
    got_b,
    got_a,
    coarse_in,
    matrix,
    obs,
    cond,
    res_ref,
    east_ref,
    south_ref,
    inv_ref,
    p_ref,
    q_ref,
    table_ref,
    own_ref,
    chunk_ref,
    dots_ref,
    image,
    spread,
):
    height = down * COARSE
    window = down + 2 * EDGE
    strips = height // STRIP + 1
    at_col, at_row, n_cols, n_rows = place()
    has_n, has_s, has_e, has_w = has_sides()
    from_s, from_n = in_pair_order(at_row, got_b[...], got_a[...])
    clear_pads(obs, cond, p_ref, image)
    for which, field in enumerate((obs, cond)):
        for t in range(tiles + 1):
            at = (which * (tiles + 1) + t) * EDGE
            field[t, EDGE : 2 * EDGE, :] = from_n[at : at + EDGE]
            field[t, 2 * EDGE + height : 3 * EDGE + height, :] = from_s[at : at + EDGE]

    base = 2 * (tiles + 1) * EDGE

    def joined(index):
        def part(strip):
            at = [base + (2 * index + half) * 2 * EDGE for half in range(2)]
            return jnp.concatenate([strip[a : a + 2 * EDGE] for a in at], axis=1)

        gap = jnp.zeros((window - 4 * EDGE, 2 * LANES), jnp.float32)
        return coarse_in[index] + jnp.concatenate([part(from_n), gap, part(from_s)], axis=0)

    source, east, south, around = [joined(index) for index in range(4)]
    row = iota(source.shape, 0)
    lane = iota(source.shape, 1)
    inside = jnp.where(row < EDGE, has_n, jnp.where(row < window - EDGE, 1.0, has_s))
    inside = inside * jnp.where(
        lane < LANES, 1.0, jnp.where(lane < LANES + HALF, has_e, has_w)
    )
    taps = read_taps(taps)
    total = tap_total(taps, 1)
    factor = inside * OMEGA / (COARSE * COARSE * total * total + around)
    weights = (east, roll(east, 1, 1), south, roll(south, 1, 0))
    table = [factor] + [factor * weight for weight in weights]
    for index, part in enumerate(table):
        table_ref[index] = part
    cells = split_dot(jacobi(source, table), matrix[...])
    for t in range(tiles + 1):
        spread[t] = cells[:, t * LANES : (t + 1) * LANES]

    sides = side_lanes(has_e, has_w)
    for index in (0, strips - 1):
        at = EDGE + STRIP * index
        fields = begin(obs, cond, at, taps, sides)
        for ref, strip in zip((east_ref, south_ref, inv_ref, res_ref), fields):
            store(ref, at, strip)
    mask_rows(inv_ref, has_n, has_s)

    def keeps(index):
        return jnp.where(index > 0, 1.0, 0.0), jnp.where(index < strips - 1, 1.0, 0.0)

    def start(index, total):
        at = strip_at(index)
        residual, inverse = load(res_ref, at), load(inv_ref, at)
        cells = spread_strip(spread, index)
        direction = [residual[t] * inverse[t] + cells[t] for t in range(tiles + 1)]
        return [(p_ref, at, direction)], total + product_sum(
            residual, direction, tiles, *keeps(index)
        )

    def blur(index, _):
        at = strip_at(index)
        blurred = conv(p_ref, at, taps, False)
        blurred[tiles] = blurred[tiles] * sides
        return [(image, at, blurred)], 0

    def finish(index, total):
        at = strip_at(index)
        here, product = operate(p_ref, image, east_ref, south_ref, at, taps)
        return [(q_ref, at, product)], total + product_sum(here, product, tiles, *keeps(index))

    nothing = jnp.zeros((EDGE, LANES), jnp.float32)
    dots_ref[0] = sweep(strips, 2, start, nothing)
    sweep(strips, 2, blur, 0)
    mask_rows(image, has_n, has_s)
    dots_ref[1] = sweep(strips, 2, finish, nothing)

    shape = (tiles * LANES, LANES)
    matrix = jnp.where(iota(shape, 0) >> 3 == iota(shape, 1), 1.0, 0.0).astype(jnp.bfloat16)
    flat = []
    for t in range(tiles):
        picked = [
            q_ref[t, pl.ds(2 * EDGE + k, down, stride=COARSE), :] for k in range(COARSE)
        ]
        flat.append(sum(picked[1:], picked[0]))
    own = split_dot(jnp.concatenate(flat, axis=1), matrix)
    own_ref[...] = own
    spare = jnp.zeros((LANES - down, LANES), jnp.float32)
    turned = jnp.transpose(jnp.concatenate([own, spare], axis=0))
    chunk_ref[...] = jnp.zeros_like(chunk_ref)
    for down_by in (-1, 0, 1):
        for right_by in (-1, 0, 1):
            if down_by == 0 and right_by == 0:
                continue
            if down_by == 0:
                piece = turned[:EDGE] if right_by < 0 else turned[LANES - EDGE :]
            else:
                piece = own[:EDGE] if down_by < 0 else own[down - EDGE :]
            to_row, to_col = at_row + down_by, at_col + right_by

            @pl.when((to_row >= 0) & (to_row < n_rows) & (to_col >= 0) & (to_col < n_cols))
            def _(piece=piece, to_row=to_row, to_col=to_col):
                chunk_ref[to_col * n_rows + to_row] = piece


def first(taps, fields, got_a, got_b, coarse, matrix):
    field = fields[0].shape
    tiles, height = field[0] - 1, field[1] - 4 * EDGE
    down = height // COARSE
    window = down + 2 * EDGE
    count = lax.axis_size("cols") * lax.axis_size("rows")
    shapes = [field] * 8 + [
        (5, window, 2 * LANES),
        (down, LANES),
        (count, EDGE, LANES),
        (2, EDGE, LANES),
    ]
    return pl.pallas_call(
        functools.partial(first_kernel, tiles, down),
        in_specs=[SMEM] + [VMEM] * 10,
        out_specs=[VMEM] * len(shapes),
        out_shape=floats(*shapes),
        input_output_aliases={index + 1: index for index in range(6)},
        scratch_shapes=[
            pltpu.VMEM(field, jnp.float32),
            pltpu.VMEM((tiles + 1, window, LANES), jnp.float32),
        ],
        compiler_params=params(),
        name="first_direction",
    )(taps, *fields, got_b, got_a, coarse, matrix)[2:]


def second_kernel(
    tiles,
    down,
    taps,
    got_ref,
    own_ref,
    table_ref,
    q_ref,
    east_ref,
    south_ref,
    inv_ref,
    dots_in,
    matrix,
    w_ref,
    v_ref,
    out_ref,
    image,
    spread,
):
    height = down * COARSE
    strips = height // STRIP + 1
    has_n, has_s, has_e, has_w = has_sides()
    at_col, at_row, n_cols, n_rows = place()
    me = at_col * n_rows + at_row

    def got(down_by, right_by):
        to_row, to_col = at_row + down_by, at_col + right_by
        there = (to_row >= 0) & (to_row < n_rows) & (to_col >= 0) & (to_col < n_cols)
        return got_ref[jnp.where(there, to_col * n_rows + to_row, me)]

    low = iota((EDGE, LANES), 1) < HALF
    gap = jnp.zeros((LANES - 2 * EDGE, LANES), jnp.float32)
    beside = jnp.transpose(jnp.concatenate([got(0, 1), gap, got(0, -1)], axis=0))[:down]
    source = jnp.concatenate(
        [
            jnp.concatenate([got(-1, 0), jnp.where(low, got(-1, 1), got(-1, -1))], axis=1),
            jnp.concatenate([own_ref[...], beside], axis=1),
            jnp.concatenate([got(1, 0), jnp.where(low, got(1, 1), got(1, -1))], axis=1),
        ],
        axis=0,
    )
    cells = jacobi(source, [table_ref[index] for index in range(5)])
    cells = split_dot(cells, matrix[...])
    for t in range(tiles + 1):
        spread[t] = cells[:, t * LANES : (t + 1) * LANES]
    clear_pads(w_ref, image)
    sides = side_lanes(has_e, has_w)
    taps = read_taps(taps)

    def start(index, _):
        at = strip_at(index)
        field, inverse = load(q_ref, at), load(inv_ref, at)
        cells = spread_strip(spread, index)
        return [(w_ref, at, [field[t] * inverse[t] + cells[t] for t in range(tiles + 1)])], 0

    def blur(index, _):
        at = strip_at(index)
        blurred = conv(w_ref, at, taps, False)
        blurred[tiles] = blurred[tiles] * sides
        return [(image, at, blurred)], 0

    def finish(index, totals):
        at = pl.multiple_of(2 * EDGE + STRIP * index, EDGE)
        here, product = operate(w_ref, image, east_ref, south_ref, at, taps)
        field = load(q_ref, at)
        return [(v_ref, at, product[:tiles])], (
            totals[0] + product_sum(field, here, tiles),
            totals[1] + product_sum(here, product, tiles),
        )

    nothing = jnp.zeros((EDGE, LANES), jnp.float32)
    sweep(strips, 2, start, 0)
    sweep(strips, 2, blur, 0)
    mask_rows(image, has_n, has_s)
    dot_qw, dot_wv = sweep(strips - 1, 2, finish, (nothing, nothing))
    line = jnp.zeros((1, LANES), jnp.float32)
    block = iota((1, LANES), 1) // (LANES // 4)
    for index, part in enumerate((dots_in[0], dots_in[1], dot_qw, dot_wv)):
        part = jnp.sum(part, axis=0, keepdims=True)
        part = part + roll(part, LANES // 2, 1)
        part = part + roll(part, LANES // 4, 1)
        line = jnp.where(block == index, part, line)
    for index in range(out_ref.shape[0]):
        out_ref[index] = line


def second(taps, got, own, table, q, east, south, inv, dots, matrix):
    tiles, height = q.shape[0] - 1, q.shape[1] - 4 * EDGE
    down = height // COARSE
    window = down + 2 * EDGE
    count = lax.axis_size("cols") * lax.axis_size("rows")
    return pl.pallas_call(
        functools.partial(second_kernel, tiles, down),
        in_specs=[SMEM] + [VMEM] * 9,
        out_specs=[VMEM] * 3,
        out_shape=floats(q.shape, q.shape, (count, 1, LANES)),
        scratch_shapes=[
            pltpu.VMEM(q.shape, jnp.float32),
            pltpu.VMEM((tiles + 1, window, LANES), jnp.float32),
        ],
        compiler_params=params(),
        name="second_direction",
    )(taps, got, own, table, q, east, south, inv, dots, matrix)


def combine_kernel(
    tiles, height, sums_ref, p_ref, w_ref, r_ref, q_ref, v_ref, sol_out, res_out, sol, res, sem
):
    line = sums_ref[0]
    for index in range(1, sums_ref.shape[0]):
        line = line + sums_ref[index]
    block = iota((1, LANES), 1) // (LANES // 4)
    pick = lambda index: jnp.sum(jnp.where(block == index, line, 0.0), axis=1, keepdims=True)
    rp, pq, qw, wv = [pick(index) for index in range(4)]
    step = rp / pq
    rp_next = step * step * qw - rp
    ratio = rp_next / rp
    lead = 1.0 + ratio
    curvature = lead * lead * pq - 2.0 * lead * step * qw + step * step * wv
    step_next = rp_next / curvature
    on_p = jnp.broadcast_to(step + step_next * lead, (STRIP, LANES))
    on_w = jnp.broadcast_to(step_next * step, (STRIP, LANES))

    def copies(index):
        rows = pl.ds(pl.multiple_of(index * STRIP, STRIP), STRIP)
        return (
            pltpu.make_async_copy(sol.at[rows, :], sol_out.at[rows, :], sem.at[0, index]),
            pltpu.make_async_copy(res.at[rows, :], res_out.at[rows, :], sem.at[1, index]),
        )

    def work(index, _):
        at = pl.multiple_of(index * STRIP, STRIP)
        p, w, r, q, v = [
            load(ref, at + 2 * EDGE) for ref in (p_ref, w_ref, r_ref, q_ref, v_ref)
        ]
        one = [on_p * p[t] - on_w * w[t] for t in range(tiles)]
        two = [r[t] - on_p * q[t] + on_w * v[t] for t in range(tiles)]
        for t in range(tiles):
            sol[pl.ds(at, STRIP), t * LANES : (t + 1) * LANES] = one[t]
            res[pl.ds(at, STRIP), t * LANES : (t + 1) * LANES] = two[t]
        for copy in copies(index):
            copy.start()
        return 0

    def settle(index, _):
        for copy in copies(index):
            copy.wait()
        return 0

    lax.fori_loop(0, height // STRIP, work, 0)
    lax.fori_loop(0, height // STRIP, settle, 0)


def combine(sums, p, w, r, q, v):
    tiles, height = q.shape[0] - 1, q.shape[1] - 4 * EDGE
    shape = (height, tiles * LANES)
    return pl.pallas_call(
        functools.partial(combine_kernel, tiles, height),
        in_specs=[VMEM] * 6,
        out_specs=[HBM] * 2,
        out_shape=floats(shape, shape),
        scratch_shapes=[
            pltpu.VMEM(shape, jnp.float32),
            pltpu.VMEM(shape, jnp.float32),
            pltpu.SemaphoreType.DMA((2, height // STRIP)),
        ],
        compiler_params=params(),
        name="combine",
    )(sums, p, w, r, q, v)


def exchange(send_a, send_b, axis):
    count = lax.axis_size(axis)

    def pairs(begin):
        return [
            pair for i in range(begin, count - 1, 2) for pair in ((i, i + 1), (i + 1, i))
        ]

    got_b = lax.ppermute(send_b, axis, pairs(1))
    got_a = lax.ppermute(send_a, axis, pairs(0))
    return got_a, got_b


def body(observed, class_map, class_weights, blur_kernel):
    arguments = (observed, class_map, class_weights, blur_kernel)
    send_a, send_b = edge(*arguments)
    got_a, got_b = exchange(send_a, send_b, "cols")
    obs, cond, coarse = pack(*arguments, send_a)
    obs, cond, coarse, send_a, send_b = middle(got_a, got_b, coarse, obs, cond)
    got_a, got_b = exchange(send_a, send_b, "rows")
    r, east, south, inv, matrix = inner(blur_kernel, obs, cond)
    fields = (obs, cond, r, east, south, inv)
    r, east, south, inv, p, q, table, own, chunk, dots = first(
        blur_kernel, fields, got_a, got_b, coarse, matrix
    )
    got = lax.all_to_all(chunk, AXES, 0, 0, tiled=True)
    w, v, line = second(blur_kernel, got, own, table, q, east, south, inv, dots, matrix)
    sums = lax.all_to_all(line, AXES, 0, 0, tiled=True)
    return tuple(combine(sums, p, w, r, q, v))


def solution(mesh):
    return jax.shard_map(
        body,
        mesh=mesh,
        in_specs=(P("rows", "cols"), P("rows", "cols"), P(), P()),
        out_specs=(P("rows", "cols"), P("rows", "cols")),
        check_vma=False,
    )
```

```python
import functools

import jax
import jax.numpy as jnp
from jax import lax
from jax.experimental import pallas as pl
from jax.experimental.pallas import tpu as pltpu
from jax.sharding import PartitionSpec as P

COARSE = 8
SWEEPS = 8
CLASSES = 4
OMEGA = 0.8

LANES = 128
HALF = LANES // 2
EDGE = 8
STRIP = 4 * EDGE
AXES = ("cols", "rows")
LIMIT = 40 * 1024 * 1024


VMEM = pl.BlockSpec(memory_space=pltpu.VMEM)
SMEM = pl.BlockSpec(memory_space=pltpu.SMEM)
HBM = pl.BlockSpec(memory_space=pltpu.HBM)


def params():
    return pltpu.CompilerParams(vmem_limit_bytes=LIMIT)


def in_hbm(array):
    return pltpu.with_memory_space_constraint(array, pltpu.HBM)


def floats(*shapes):
    return [jax.ShapeDtypeStruct(shape, jnp.float32) for shape in shapes]


def place():
    at_col, at_row = lax.axis_index("cols"), lax.axis_index("rows")
    n_cols, n_rows = lax.axis_size("cols"), lax.axis_size("rows")
    return at_col, at_row, n_cols, n_rows


def has_sides():
    at_col, at_row, n_cols, n_rows = place()
    flag = lambda test: jnp.where(test, 1.0, 0.0).astype(jnp.float32)
    return (
        flag(at_row > 0),
        flag(at_row < n_rows - 1),
        flag(at_col < n_cols - 1),
        flag(at_col > 0),
    )


def iota(shape, dim):
    return lax.broadcasted_iota(jnp.int32, shape, dim)


def cell_of(pixel, tiles):
    turn = (tiles + 1) * LANES
    return jnp.where(pixel < turn - HALF, pixel >> 3, ((pixel - turn) >> 3) & (2 * LANES - 1))


def gather_matrix(tiles):
    shape = ((tiles + 1) * LANES, 2 * LANES)
    hit = cell_of(iota(shape, 0), tiles) == iota(shape, 1)
    return jnp.where(hit, 1.0, 0.0).astype(jnp.bfloat16)


def split_dot(field, matrix):
    rows = field.shape[0]
    high = field.astype(jnp.bfloat16)
    low = (field - high.astype(jnp.float32)).astype(jnp.bfloat16)
    both = jnp.dot(
        jnp.concatenate([high, low], axis=0), matrix, preferred_element_type=jnp.float32
    )
    return both[:rows] + both[rows:]


def roll(field, by, axis):
    return pltpu.roll(field, by % field.shape[axis], axis)


def load(ref, at, rows=STRIP):
    return [ref[t, pl.ds(at, rows), :] for t in range(ref.shape[0])]


def store(ref, at, strip):
    for t, part in enumerate(strip):
        ref[t, pl.ds(at, part.shape[0]), :] = part


def wide(ref, at, rows):
    return jnp.concatenate(load(ref, at, rows), axis=1)


def read_taps(taps):
    return [[taps[a, b] for b in range(3)] for a in range(3)]


def tap_total(taps, power):
    return sum(tap * tap if power == 2 else tap for line in taps for tap in line)


def shifter(count, rows, make):
    make = functools.cache(make)
    west = functools.cache(lambda t: roll(make(t), 1, 1))
    east = functools.cache(lambda t: roll(make(t), -1, 1))

    def from_west(t):
        lane = iota((rows, LANES), 1)
        return jnp.where(lane == 0, west((t - 1) % count), west(t))

    def from_east(t):
        lane = iota((rows, LANES), 1)
        return jnp.where(lane == LANES - 1, east((t + 1) % count), east(t))

    return make, from_west, from_east


def reader_of(ref, at, rows=STRIP):
    return functools.cache(lambda t, by=0: ref[t, pl.ds(at + by, rows), :])


def tap_sum(field, taps, flip, b):
    if flip:
        taps = [line[::-1] for line in taps[::-1]]
    return lambda t: (
        taps[0][b] * field(t, -1) + taps[1][b] * field(t) + taps[2][b] * field(t, 1)
    )


def conv(ref, at, taps, flip, rows=STRIP):
    count = ref.shape[0]
    field = reader_of(ref, at, rows)
    sums = [tap_sum(field, taps, flip, b) for b in range(3)]
    _, from_west, _ = shifter(count, rows, sums[0])
    _, _, from_east = shifter(count, rows, sums[2])
    return lambda t: sums[1](t) + from_west(t) + from_east(t)


def operate(ref, image, east_ref, south_ref, at, taps):
    count = ref.shape[0]
    field, picture = reader_of(ref, at), reader_of(image, at)
    east, south = reader_of(east_ref, at), reader_of(south_ref, at)
    here, _, beside = shifter(count, STRIP, field)
    flux = functools.cache(lambda t: east(t) * (here(t) - beside(t)))
    sums = [tap_sum(picture, taps, True, b) for b in range(3)]
    _, from_west, _ = shifter(count, STRIP, lambda t: sums[0](t) - flux(t))
    _, _, from_east = shifter(count, STRIP, sums[2])

    def value(t):
        down = south(t) * (here(t) - field(t, 1)) - south(t, -1) * (field(t, -1) - here(t))
        return sums[1](t) + flux(t) + from_west(t) + from_east(t) + down

    return here, value


def begin(obs, cond, at, taps, sides, rows):
    count = cond.shape[0]
    level = reader_of(cond, at, rows)
    here, _, right = shifter(count, rows, level)
    east, west, _ = shifter(count, rows, lambda t: here(t) + right(t))
    squares = tap_total(taps, 2)
    residual = conv(obs, at, taps, True, rows)
    fields = [[], [], [], []]
    for t in range(count):
        south = here(t) + level(t, 1)
        diag = squares + east(t) + west(t) + south + (here(t) + level(t, -1))
        inverse = pl.reciprocal(diag, approx=True)
        inverse = inverse * (2.0 - diag * inverse)
        if t == count - 1:
            inverse = inverse * sides
        for strip, part in zip(fields, (east(t), south, inverse, residual(t))):
            strip.append(part)
    return fields


def pick_lanes(field, lanes):
    return jnp.take_along_axis(field, lanes, axis=1, mode="promise_in_bounds")


def spread_cells(cells, spread):
    tiles = spread.shape[0] - 1
    lane = iota((cells.shape[0], LANES), 1)
    for t in range(tiles):
        spread[t] = pick_lanes(cells[:, :LANES], (lane >> 3) + t * (LANES // COARSE))
    turn = jnp.where(lane < HALF, 0, LANES - LANES // COARSE)
    spread[tiles] = pick_lanes(cells[:, LANES:], (lane >> 3) + turn)


def cells_at(spread, at, rows, t):
    first = at // EDGE + EDGE - 2
    parts = [
        jnp.broadcast_to(spread[t, pl.ds(first + index, 1), :], (EDGE, LANES))
        for index in range(rows // EDGE)
    ]
    return jnp.concatenate(parts, axis=0)


def cell_sums(ref, tiles, down):
    lane = iota((down, LANES), 1)
    total = jnp.zeros((down, LANES), jnp.float32)
    for t in range(tiles):
        picked = [
            ref[t, pl.ds(2 * EDGE + k, down, stride=COARSE), :] for k in range(COARSE)
        ]
        part = sum(picked[1:], picked[0])
        for by in (1, 2, 4):
            part = part + roll(part, -by, 1)
        part = pick_lanes(part, (lane & (LANES // COARSE - 1)) * COARSE)
        total = jnp.where(lane // (LANES // COARSE) == t, part, total)
    return total


def side_lanes(has_e, has_w, rows=STRIP):
    return jnp.where(iota((rows, LANES), 1) < HALF, has_e, has_w)


def mask_rows(ref, has_n, has_s):
    last = ref.shape[1] - 2 * EDGE

    def work(t, _):
        for at, flag in ((EDGE, has_n), (last, has_s)):
            ref[t, at : at + EDGE, :] = ref[t, at : at + EDGE, :] * flag
        return 0

    lax.fori_loop(0, ref.shape[0], work, 0)


def clear_pads(*refs):
    def work(t, _):
        empty = jnp.zeros((EDGE, LANES), jnp.float32)
        for ref in refs:
            ref[t, :EDGE, :] = empty
            ref[t, ref.shape[1] - EDGE :, :] = empty
        return 0

    lax.fori_loop(0, refs[0].shape[0], work, 0)


def fold(total, flags=None):
    parts = [total[at : at + EDGE] for at in range(0, total.shape[0], EDGE)]
    if flags is not None:
        parts = [part * flag for part, flag in zip(parts, flags)]
    return sum(parts[1:], parts[0])


def sweep(first, last, body, carry):
    steps = -(-(last - first) // STRIP)

    def work(index, carry):
        start = first + index * STRIP
        at = pl.multiple_of(jnp.minimum(start, last - STRIP), EDGE)
        stores, carry = body(at, start, carry)
        for ref, strip in stores:
            store(ref, at, strip)
        return carry

    return lax.fori_loop(0, steps, work, carry)


def jacobi(source, table):
    source = table[0] * source

    def work(_, iterate):
        across = table[1] * roll(iterate, -1, 1) + table[2] * roll(iterate, 1, 1)
        along = table[3] * roll(iterate, -1, 0) + table[4] * roll(iterate, 1, 0)
        return ((1.0 - OMEGA) * iterate + source) + (across + along)

    return lax.fori_loop(0, SWEEPS - 1, work, source)


def in_pair_order(at, for_before, for_after):
    even = at % 2 == 0
    if callable(for_before):
        return (
            lambda index: jnp.where(even, for_after(index), for_before(index)),
            lambda index: jnp.where(even, for_before(index), for_after(index)),
        )
    return jnp.where(even, for_after, for_before), jnp.where(even, for_before, for_after)


def reader(tiles_here, refs, scratch, obs, cond, down):
    obs_in, class_in, weight_in, taps_in = refs
    classes, weights, taps, sums, obs_sem, class_sem, small_sem = scratch
    own = pl.ds(2 * EDGE, down * COARSE)
    small = [
        pltpu.make_async_copy(weight_in, weights, small_sem.at[0]),
        pltpu.make_async_copy(taps_in, taps, small_sem.at[1]),
    ]
    moves = []
    for slot, t in enumerate(tiles_here):
        lanes = pl.ds(t * LANES, LANES)
        moves.append(
            (
                pltpu.make_async_copy(class_in.at[:, lanes], classes.at[slot], class_sem.at[slot]),
                pltpu.make_async_copy(
                    obs_in.at[:, lanes], obs.at[slot, own, :], obs_sem.at[slot]
                ),
            )
        )
    for copy in small:
        copy.start()
    for pair in moves:
        for copy in pair:
            copy.start()
    sums[...] = jnp.zeros_like(sums)

    def settle(slot):
        if slot == 0:
            for copy in small:
                copy.wait()
        for copy in moves[slot]:
            copy.wait()
        values = [0.5 * weights[class_id] for class_id in range(CLASSES)]
        kind = classes[slot]
        cond[slot, own, :] = jnp.where(
            kind < 2,
            jnp.where(kind == 0, values[0], values[1]),
            jnp.where(kind == 2, values[2], values[3]),
        )
        for which, ref in enumerate((obs, cond)):
            picked = [
                ref[slot, pl.ds(2 * EDGE + k, down, stride=COARSE), :] for k in range(COARSE)
            ]
            sums[3 * which, slot, EDGE : EDGE + down, :] = sum(picked[1:], picked[0])
            sums[3 * which + 1, slot, EDGE : EDGE + down, :] = picked[0]
            sums[3 * which + 2, slot, EDGE : EDGE + down, :] = picked[-1]

    return settle


def reader_scratch(tiles, height, window, class_weights, taps):
    return [
        pltpu.VMEM((tiles, height, LANES), jnp.int32),
        pltpu.SMEM(class_weights.shape, jnp.float32),
        pltpu.SMEM(taps.shape, jnp.float32),
        pltpu.VMEM((6, tiles + 1, window, LANES), jnp.float32),
        pltpu.SemaphoreType.DMA((tiles,)),
        pltpu.SemaphoreType.DMA((tiles,)),
        pltpu.SemaphoreType.DMA((2,)),
    ]


def coarse_parts(sums, taps, matrix):
    window = sums.shape[2]
    whole = lambda index: wide(sums.at[index], 0, window)
    full, head, tail = whole(0), whole(1), whole(2)
    by_tap = [full - head + roll(head, -1, 0), full, full - tail + roll(tail, 1, 0)]
    across = [sum(taps[a][b] * by_tap[a] for a in range(3)) for b in range(3)]
    source = across[1] + roll(across[0], -1, 1) + roll(across[2], 1, 1)
    full, head, tail = whole(3), whole(4), whole(5)
    last = (iota(full.shape, 1) & (COARSE - 1)) == COARSE - 1
    east = jnp.where(last, full + roll(full, -1, 1), 0.0)
    south = tail + roll(head, -1, 0)
    cells = split_dot(jnp.concatenate([source, east, south], axis=0), matrix)
    source, east, south = cells[:window], cells[window : 2 * window], cells[2 * window :]
    around = east + roll(east, 1, 1) + south + roll(south, 1, 0)
    return [source, east, south, around]


def edge_kernel(tiles, down, *refs):
    arguments, (send_a, send_b), (obs, cond, message, *scratch) = refs[:4], refs[4:6], refs[6:]
    height = down * COARSE
    halves = height // LANES
    window = down + 2 * EDGE
    settle = reader((0, tiles - 1), arguments, scratch, obs, cond, down)
    matrix = gather_matrix(2)
    for slot, begin_row in ((0, 0), (1, LANES - EDGE)):
        settle(slot)
        for which, ref in enumerate((obs, cond)):
            turned = jnp.transpose(ref[slot, 2 * EDGE : 2 * EDGE + height, :])
            turned = turned[begin_row : begin_row + EDGE]
            for half in range(halves):
                at = (which * halves + half) * EDGE
                message[slot, at : at + EDGE, :] = turned[:, half * LANES : (half + 1) * LANES]
    parts = coarse_parts(scratch[3], read_taps(scratch[2]), matrix)
    spare = jnp.zeros((2 * LANES - 4 * window, 2 * LANES), jnp.float32)
    stack = jnp.concatenate(parts + [spare], axis=0)
    left = jnp.transpose(stack[:, :LANES])
    right = jnp.transpose(stack[:, LANES:])
    base = 2 * halves * EDGE
    past = 2 * LANES // COARSE
    for slot, pieces in (
        (0, (left[:EDGE], right[LANES - EDGE :])),
        (1, (left[past - EDGE : past], left[past : past + EDGE])),
    ):
        for index, piece in enumerate(pieces):
            for half in range(2):
                at = base + (2 * index + half) * EDGE
                message[slot, at : at + EDGE, :] = piece[:, half * LANES : (half + 1) * LANES]
    send_a[...], send_b[...] = in_pair_order(place()[0], message[0], message[1])


def edge(observed, class_map, class_weights, taps):
    height, breadth = observed.shape
    tiles, down = breadth // LANES, height // COARSE
    window = down + 2 * EDGE
    field = (3, height + 4 * EDGE, LANES)
    strip = ((2 * (height // LANES) + 4) * EDGE, LANES)
    return pl.pallas_call(
        functools.partial(edge_kernel, tiles, down),
        in_specs=[HBM] * 4,
        out_specs=[VMEM] * 2,
        out_shape=floats(strip, strip),
        scratch_shapes=[
            pltpu.VMEM(field, jnp.float32),
            pltpu.VMEM(field, jnp.float32),
            pltpu.VMEM((2,) + strip, jnp.float32),
        ]
        + reader_scratch(2, height, window, class_weights, taps),
        compiler_params=params(),
        name="pack_east_west",
    )(*[in_hbm(array) for array in (observed, class_map, class_weights, taps)])


def pack_kernel(tiles, down, *refs):
    arguments, (obs, cond, coarse_ref), scratch = refs[:4], refs[5:8], refs[8:]
    settle = reader(range(tiles), arguments, scratch, obs, cond, down)
    matrix = gather_matrix(tiles)
    for t in range(tiles):
        settle(t)
    for index, part in enumerate(coarse_parts(scratch[3], read_taps(scratch[2]), matrix)):
        coarse_ref[index] = part


def pack(observed, class_map, class_weights, taps, after):
    height, breadth = observed.shape
    tiles, down = breadth // LANES, height // COARSE
    window = down + 2 * EDGE
    field = (tiles + 1, height + 4 * EDGE, LANES)
    pixels = height * breadth
    return pl.pallas_call(
        functools.partial(pack_kernel, tiles, down),
        in_specs=[HBM] * 4 + [VMEM],
        out_specs=[VMEM] * 3,
        out_shape=floats(field, field, (4, window, 2 * LANES)),
        scratch_shapes=reader_scratch(tiles, height, window, class_weights, taps),
        compiler_params=params(),
        cost_estimate=pl.CostEstimate(
            flops=20 * pixels, bytes_accessed=16 * pixels, transcendentals=0
        ),
        name="pack_all",
    )(*[in_hbm(array) for array in (observed, class_map, class_weights, taps)], after)


def merge_sides(parts):
    block = iota((EDGE, LANES), 1) // (2 * EDGE)
    merged = jnp.zeros((EDGE, LANES), jnp.float32)
    for index, part in enumerate(parts):
        merged = jnp.where(block == index, roll(part, (2 * index + 1) * EDGE, 1), merged)
    return merged


def split_sides(merged, count):
    lane = iota((EDGE, LANES), 1)
    outer = (lane < EDGE) | (lane >= LANES - EDGE)
    return [
        jnp.where(outer, roll(merged, -(2 * index + 1) * EDGE, 1), 0.0) for index in range(count)
    ]


def middle_kernel(
    tiles,
    down,
    got_b,
    got_a,
    coarse_in,
    obs_in,
    cond_in,
    obs,
    cond,
    coarse_ref,
    send_a,
    send_b,
    message,
):
    height = down * COARSE
    halves = height // LANES
    at_col, at_row, _, _ = place()
    from_e, from_w = in_pair_order(at_col, got_b[...], got_a[...])
    gap = jnp.zeros((LANES - 2 * EDGE, LANES), jnp.float32)

    def turned(low, high):
        return jnp.transpose(jnp.concatenate([low, gap, high], axis=0))

    for which, field in enumerate((obs, cond)):
        for half in range(halves):
            at = (which * halves + half) * EDGE
            begin_row = 2 * EDGE + half * LANES
            field[tiles, begin_row : begin_row + LANES, :] = turned(
                from_e[at : at + EDGE], from_w[at : at + EDGE]
            )
    base = 2 * halves * EDGE

    def piece(strip, index, half):
        at = base + (2 * index + half) * EDGE
        return strip[at : at + EDGE]

    left = [turned(piece(from_w, 1, half), piece(from_e, 1, half)) for half in range(2)]
    right = [turned(piece(from_e, 0, half), piece(from_w, 0, half)) for half in range(2)]
    left = jnp.concatenate(left, axis=0)
    right = jnp.concatenate(right, axis=0)
    window = down + 2 * EDGE
    for index in range(4):
        rows = slice(index * window, (index + 1) * window)
        coarse_ref[index, :, :LANES] = coarse_in[index, :, :LANES] + left[rows]
        coarse_ref[index, :, LANES:] = coarse_in[index, :, LANES:] + right[rows]
    fields = (obs, cond)
    for slot, begin_row, first_row, over_row in (
        (0, 2 * EDGE, EDGE, EDGE - 1),
        (1, EDGE + height, window - 2 * EDGE, window - EDGE),
    ):
        pieces = [field[t, begin_row : begin_row + EDGE, :] for field in fields for t in range(tiles)]
        rows = slice(first_row, first_row + EDGE)
        pieces += [coarse_ref[index, rows, :LANES] for index in range(4)]
        beyond = [coarse_ref[index, rows, LANES:] for index in range(4)]
        beyond += [field[tiles, begin_row : begin_row + EDGE, :] for field in fields]
        pieces.append(merge_sides(beyond))
        pieces.append(
            jnp.concatenate(
                [
                    coarse_ref[index, over_row : over_row + 1, half * LANES : (half + 1) * LANES]
                    for index in range(4)
                    for half in range(2)
                ],
                axis=0,
            )
        )
        for index, piece in enumerate(pieces):
            message[slot, index] = piece
    send_a[...], send_b[...] = in_pair_order(at_row, message[0], message[1])


def middle(got_a, got_b, coarse, obs, cond):
    tiles, height = obs.shape[0] - 1, obs.shape[1] - 4 * EDGE
    down = height // COARSE
    long = (2 * tiles + 6, EDGE, LANES)
    return pl.pallas_call(
        functools.partial(middle_kernel, tiles, down),
        in_specs=[VMEM] * 5,
        out_specs=[VMEM] * 5,
        out_shape=floats(obs.shape, cond.shape, coarse.shape, long, long),
        input_output_aliases={3: 0, 4: 1},
        scratch_shapes=[pltpu.VMEM((2,) + long, jnp.float32)],
        compiler_params=params(),
        name="pack_north_south",
    )(got_b, got_a, coarse, obs, cond)


def inner_kernel(taps, obs, cond, res_ref, east_ref, south_ref, inv_ref):
    _, _, has_e, has_w = has_sides()
    clear_pads(east_ref, south_ref)
    taps = read_taps(taps)
    sides = side_lanes(has_e, has_w)

    def work(at, _, carry):
        fields = begin(obs, cond, at, taps, sides, STRIP)
        return list(zip((east_ref, south_ref, inv_ref, res_ref), fields)), carry

    sweep(3 * EDGE, obs.shape[1] - 3 * EDGE, work, 0)


def inner(taps, obs, cond):
    field = obs.shape
    pixels = field[0] * field[1] * field[2]
    return pl.pallas_call(
        inner_kernel,
        in_specs=[SMEM] + [VMEM] * 2,
        out_specs=[VMEM] * 4,
        out_shape=floats(field, field, field, field),
        compiler_params=params(),
        cost_estimate=pl.CostEstimate(
            flops=45 * pixels, bytes_accessed=24 * pixels, transcendentals=0
        ),
        name="inner_strips",
    )(taps, obs, cond)


def first_kernel(
    tiles,
    down,
    taps,
    obs_in,
    cond_in,
    res_in,
    east_in,
    south_in,
    inv_in,
    got_b,
    got_a,
    coarse_in,
    obs,
    cond,
    res_ref,
    east_ref,
    south_ref,
    inv_ref,
    p_ref,
    q_ref,
    table_ref,
    own_ref,
    chunk_ref,
    dots_ref,
    image,
    spread,
):
    height = down * COARSE
    window = down + 2 * EDGE
    at_col, at_row, n_cols, n_rows = place()
    has_n, has_s, has_e, has_w = has_sides()
    clear_pads(obs, cond, p_ref, image)
    from_s, from_n = in_pair_order(
        at_row, lambda index: got_b[index], lambda index: got_a[index]
    )

    def fill(t, _):
        for which, field in enumerate((obs, cond)):
            field[t, EDGE : 2 * EDGE, :] = from_n(which * tiles + t)
            field[t, 2 * EDGE + height : 3 * EDGE + height, :] = from_s(which * tiles + t)
        return 0

    lax.fori_loop(0, tiles, fill, 0)
    sides_n, sides_s = [split_sides(strip(2 * tiles + 4), 6) for strip in (from_n, from_s)]
    for which, field in enumerate((obs, cond)):
        field[tiles, EDGE : 2 * EDGE, :] = sides_n[4 + which]
        field[tiles, 2 * EDGE + height : 3 * EDGE + height, :] = sides_s[4 + which]

    def joined(index):
        def parts(strip, beyond):
            rows = jnp.concatenate([strip(2 * tiles + index), beyond[index]], axis=1)
            over = strip(2 * tiles + 5)
            over = [over[2 * index + half : 2 * index + half + 1] for half in range(2)]
            return rows, jnp.concatenate(over, axis=1)

        rows_n, over_n = parts(from_n, sides_n)
        rows_s, over_s = parts(from_s, sides_s)
        empty = jnp.zeros((EDGE - 1, 2 * LANES), jnp.float32)
        gap = jnp.zeros((window - 4 * EDGE, 2 * LANES), jnp.float32)
        return coarse_in[index] + jnp.concatenate(
            [rows_n, over_n, empty, gap, empty, over_s, rows_s], axis=0
        )

    source, east, south, around = [joined(index) for index in range(4)]
    row = iota(source.shape, 0)
    lane = iota(source.shape, 1)
    inside = jnp.where(row < EDGE, has_n, jnp.where(row < window - EDGE, 1.0, has_s))
    inside = inside * jnp.where(
        lane < LANES, 1.0, jnp.where(lane < LANES + HALF, has_e, has_w)
    )
    taps = read_taps(taps)
    total = tap_total(taps, 1)
    factor = inside * OMEGA / (COARSE * COARSE * total * total + around)
    weights = (east, roll(east, 1, 1), south, roll(south, 1, 0))
    table = [factor] + [factor * weight for weight in weights]
    for index, part in enumerate(table):
        table_ref[index] = part
    spread_cells(jacobi(source, table_ref), spread)

    end_rows = 2 * EDGE
    end_sides = side_lanes(has_e, has_w, end_rows)

    def ends(index, _):
        at = pl.multiple_of(EDGE + index * height, EDGE)
        fields = begin(obs, cond, at, taps, end_sides, end_rows)
        for ref, strip in zip((east_ref, south_ref, inv_ref, res_ref), fields):
            store(ref, at, strip)
        return 0

    lax.fori_loop(0, 2, ends, 0)
    mask_rows(inv_ref, has_n, has_s)
    sides = side_lanes(has_e, has_w)

    def flags(at, start):
        rows = [at + by for by in range(0, STRIP, EDGE)]
        first_row = jnp.maximum(start, 2 * EDGE)
        return [
            jnp.where((row >= first_row) & (row < 2 * EDGE + height), 1.0, 0.0) for row in rows
        ]

    def begin_p(at, start, total):
        residual, inverse = reader_of(res_ref, at), reader_of(inv_ref, at)
        strip = [
            residual(t) * inverse(t) + cells_at(spread, at, STRIP, t) for t in range(tiles + 1)
        ]
        terms = [residual(t) * strip[t] for t in range(tiles)]
        return [(p_ref, strip)], total + fold(sum(terms[1:], terms[0]), flags(at, start))

    def blur(at, _, carry):
        value = conv(p_ref, at, taps, False)
        return [(image, [value(t) for t in range(tiles)] + [value(tiles) * sides])], carry

    def finish(at, start, total):
        here, value = operate(p_ref, image, east_ref, south_ref, at, taps)
        product, term = [], 0.0
        for t in range(tiles + 1):
            product.append(value(t))
            if t < tiles:
                term = term + here(t) * product[t]
        return [(q_ref, product)], total + fold(term, flags(at, start))

    nothing = jnp.zeros((EDGE, LANES), jnp.float32)
    span = (EDGE, 3 * EDGE + height)
    dots_ref[0] = sweep(*span, begin_p, nothing)
    sweep(*span, blur, 0)
    mask_rows(image, has_n, has_s)
    dots_ref[1] = sweep(*span, finish, nothing)

    own = cell_sums(q_ref, tiles, down)
    own_ref[...] = own
    spare = jnp.zeros((LANES - down, LANES), jnp.float32)
    turned = jnp.transpose(jnp.concatenate([own, spare], axis=0))
    def empty(index, _):
        chunk_ref[index] = jnp.zeros((EDGE, LANES), jnp.float32)
        return 0

    lax.fori_loop(0, chunk_ref.shape[0], empty, 0)
    for down_by in (-1, 0, 1):
        for right_by in (-1, 0, 1):
            if down_by == 0 and right_by == 0:
                continue
            if down_by == 0:
                piece = turned[:EDGE] if right_by < 0 else turned[LANES - EDGE :]
            else:
                piece = own[:EDGE] if down_by < 0 else own[down - EDGE :]
            to_row, to_col = at_row + down_by, at_col + right_by

            @pl.when((to_row >= 0) & (to_row < n_rows) & (to_col >= 0) & (to_col < n_cols))
            def _(piece=piece, to_row=to_row, to_col=to_col):
                chunk_ref[to_col * n_rows + to_row] = piece


def first(taps, fields, got_a, got_b, coarse):
    field = fields[0].shape
    tiles, height = field[0] - 1, field[1] - 4 * EDGE
    down = height // COARSE
    window = down + 2 * EDGE
    count = lax.axis_size("cols") * lax.axis_size("rows")
    shapes = [field] * 8 + [
        (5, window, 2 * LANES),
        (down, LANES),
        (count, EDGE, LANES),
        (2, EDGE, LANES),
    ]
    return pl.pallas_call(
        functools.partial(first_kernel, tiles, down),
        in_specs=[SMEM] + [VMEM] * 9,
        out_specs=[VMEM] * len(shapes),
        out_shape=floats(*shapes),
        input_output_aliases={index + 1: index for index in range(6)},
        scratch_shapes=[
            pltpu.VMEM(field, jnp.float32),
            pltpu.VMEM((tiles + 1, window, LANES), jnp.float32),
        ],
        compiler_params=params(),
        name="first_direction",
    )(taps, *fields, got_b, got_a, coarse)[2:]


def second_kernel(
    tiles,
    down,
    taps,
    got_ref,
    own_ref,
    table_ref,
    q_ref,
    east_ref,
    south_ref,
    inv_ref,
    dots_in,
    w_ref,
    v_ref,
    out_ref,
    image,
    spread,
):
    height = down * COARSE
    has_n, has_s, has_e, has_w = has_sides()
    at_col, at_row, n_cols, n_rows = place()
    me = at_col * n_rows + at_row

    def got(down_by, right_by):
        to_row, to_col = at_row + down_by, at_col + right_by
        there = (to_row >= 0) & (to_row < n_rows) & (to_col >= 0) & (to_col < n_cols)
        return got_ref[jnp.where(there, to_col * n_rows + to_row, me)]

    low = iota((EDGE, LANES), 1) < HALF
    gap = jnp.zeros((LANES - 2 * EDGE, LANES), jnp.float32)
    beside = jnp.transpose(jnp.concatenate([got(0, 1), gap, got(0, -1)], axis=0))[:down]
    source = jnp.concatenate(
        [
            jnp.concatenate([got(-1, 0), jnp.where(low, got(-1, 1), got(-1, -1))], axis=1),
            jnp.concatenate([own_ref[...], beside], axis=1),
            jnp.concatenate([got(1, 0), jnp.where(low, got(1, 1), got(1, -1))], axis=1),
        ],
        axis=0,
    )
    spread_cells(jacobi(source, table_ref), spread)
    clear_pads(w_ref, image)
    sides = side_lanes(has_e, has_w)
    taps = read_taps(taps)

    def begin_w(at, _, carry):
        field, inverse = reader_of(q_ref, at), reader_of(inv_ref, at)
        strip = [
            field(t) * inverse(t) + cells_at(spread, at, STRIP, t) for t in range(tiles + 1)
        ]
        return [(w_ref, strip)], carry

    def blur(at, _, carry):
        value = conv(w_ref, at, taps, False)
        return [(image, [value(t) for t in range(tiles)] + [value(tiles) * sides])], carry

    def finish(at, _, totals):
        here, value = operate(w_ref, image, east_ref, south_ref, at, taps)
        field = reader_of(q_ref, at)
        product, terms = [], [0.0, 0.0]
        for t in range(tiles):
            product.append(value(t))
            terms = [terms[0] + field(t) * here(t), terms[1] + here(t) * product[t]]
        return [(v_ref, product)], tuple(
            total + fold(term) for total, term in zip(totals, terms)
        )

    nothing = jnp.zeros((EDGE, LANES), jnp.float32)
    span = (EDGE, 3 * EDGE + height)
    sweep(*span, begin_w, 0)
    sweep(*span, blur, 0)
    mask_rows(image, has_n, has_s)
    dot_qw, dot_wv = sweep(2 * EDGE, 2 * EDGE + height, finish, (nothing, nothing))
    line = jnp.zeros((1, LANES), jnp.float32)
    block = iota((1, LANES), 1) // (LANES // 4)
    for index, part in enumerate((dots_in[0], dots_in[1], dot_qw, dot_wv)):
        part = jnp.sum(part, axis=0, keepdims=True)
        part = part + roll(part, LANES // 2, 1)
        part = part + roll(part, LANES // 4, 1)
        line = jnp.where(block == index, part, line)
    for index in range(out_ref.shape[0]):
        out_ref[index] = line


def second(taps, got, own, table, q, east, south, inv, dots):
    tiles, height = q.shape[0] - 1, q.shape[1] - 4 * EDGE
    down = height // COARSE
    window = down + 2 * EDGE
    count = lax.axis_size("cols") * lax.axis_size("rows")
    return pl.pallas_call(
        functools.partial(second_kernel, tiles, down),
        in_specs=[SMEM] + [VMEM] * 8,
        out_specs=[VMEM] * 3,
        out_shape=floats(q.shape, q.shape, (count, 1, LANES)),
        scratch_shapes=[
            pltpu.VMEM(q.shape, jnp.float32),
            pltpu.VMEM((tiles + 1, window, LANES), jnp.float32),
        ],
        compiler_params=params(),
        name="second_direction",
    )(taps, got, own, table, q, east, south, inv, dots)


def combine_kernel(
    tiles, height, sums_ref, p_ref, w_ref, r_ref, q_ref, v_ref, sol_out, res_out, sol, res, sem
):
    line = sums_ref[0]
    for index in range(1, sums_ref.shape[0]):
        line = line + sums_ref[index]
    block = iota((1, LANES), 1) // (LANES // 4)
    pick = lambda index: jnp.sum(jnp.where(block == index, line, 0.0), axis=1, keepdims=True)
    rp, pq, qw, wv = [pick(index) for index in range(4)]
    step = rp / pq
    rp_next = step * step * qw - rp
    ratio = rp_next / rp
    lead = 1.0 + ratio
    curvature = lead * lead * pq - 2.0 * lead * step * qw + step * step * wv
    step_next = rp_next / curvature
    on_p = jnp.broadcast_to(step + step_next * lead, (STRIP, LANES))
    on_w = jnp.broadcast_to(step_next * step, (STRIP, LANES))

    def copies(index):
        rows = pl.ds(pl.multiple_of(index * STRIP, STRIP), STRIP)
        return (
            pltpu.make_async_copy(sol.at[rows, :], sol_out.at[rows, :], sem.at[0, index]),
            pltpu.make_async_copy(res.at[rows, :], res_out.at[rows, :], sem.at[1, index]),
        )

    def work(index, _):
        at = pl.multiple_of(index * STRIP, STRIP)
        p, w, r, q, v = [
            load(ref, at + 2 * EDGE) for ref in (p_ref, w_ref, r_ref, q_ref, v_ref)
        ]
        one = [on_p * p[t] - on_w * w[t] for t in range(tiles)]
        two = [r[t] - on_p * q[t] + on_w * v[t] for t in range(tiles)]
        for t in range(tiles):
            sol[pl.ds(at, STRIP), t * LANES : (t + 1) * LANES] = one[t]
            res[pl.ds(at, STRIP), t * LANES : (t + 1) * LANES] = two[t]
        for copy in copies(index):
            copy.start()
        return 0

    def settle(index, _):
        for copy in copies(index):
            copy.wait()
        return 0

    lax.fori_loop(0, height // STRIP, work, 0)
    lax.fori_loop(0, height // STRIP, settle, 0)


def combine(sums, p, w, r, q, v):
    tiles, height = q.shape[0] - 1, q.shape[1] - 4 * EDGE
    shape = (height, tiles * LANES)
    return pl.pallas_call(
        functools.partial(combine_kernel, tiles, height),
        in_specs=[VMEM] * 6,
        out_specs=[HBM] * 2,
        out_shape=floats(shape, shape),
        scratch_shapes=[
            pltpu.VMEM(shape, jnp.float32),
            pltpu.VMEM(shape, jnp.float32),
            pltpu.SemaphoreType.DMA((2, height // STRIP)),
        ],
        compiler_params=params(),
        name="combine",
    )(sums, p, w, r, q, v)


def exchange(send_a, send_b, axis):
    count = lax.axis_size(axis)

    def pairs(begin):
        return [
            pair for i in range(begin, count - 1, 2) for pair in ((i, i + 1), (i + 1, i))
        ]

    got_b = lax.ppermute(send_b, axis, pairs(1))
    got_a = lax.ppermute(send_a, axis, pairs(0))
    return got_a, got_b


def body(observed, class_map, class_weights, blur_kernel):
    arguments = (observed, class_map, class_weights, blur_kernel)
    send_a, send_b = edge(*arguments)
    got_a, got_b = exchange(send_a, send_b, "cols")
    obs, cond, coarse = pack(*arguments, send_a)
    obs, cond, coarse, send_a, send_b = middle(got_a, got_b, coarse, obs, cond)
    got_a, got_b = exchange(send_a, send_b, "rows")
    r, east, south, inv = inner(blur_kernel, obs, cond)
    fields = (obs, cond, r, east, south, inv)
    r, east, south, inv, p, q, table, own, chunk, dots = first(
        blur_kernel, fields, got_a, got_b, coarse
    )
    got = lax.all_to_all(chunk, AXES, 0, 0, tiled=True)
    w, v, line = second(blur_kernel, got, own, table, q, east, south, inv, dots)
    sums = lax.all_to_all(line, AXES, 0, 0, tiled=True)
    return tuple(combine(sums, p, w, r, q, v))


def solution(mesh):
    return jax.shard_map(
        body,
        mesh=mesh,
        in_specs=(P("rows", "cols"), P("rows", "cols"), P(), P()),
        out_specs=(P("rows", "cols"), P("rows", "cols")),
        check_vma=False,
    )
```

```python
import functools

import jax
import jax.numpy as jnp
from jax import lax
from jax.experimental import pallas as pl
from jax.experimental.pallas import tpu as pltpu
from jax.sharding import PartitionSpec as P

COARSE = 8
SWEEPS = 8
CLASSES = 4
OMEGA = 0.8

LANES = 128
HALF = LANES // 2
EDGE = 8
STRIP = 2 * EDGE
GROUP = 2
CHUNK = 32
AXES = ("cols", "rows")
LIMIT = 40 * 1024 * 1024


VMEM = pl.BlockSpec(memory_space=pltpu.VMEM)
SMEM = pl.BlockSpec(memory_space=pltpu.SMEM)
HBM = pl.BlockSpec(memory_space=pltpu.HBM)


def params():
    return pltpu.CompilerParams(vmem_limit_bytes=LIMIT)


def in_hbm(array):
    return pltpu.with_memory_space_constraint(array, pltpu.HBM)


def floats(*shapes):
    return [jax.ShapeDtypeStruct(shape, jnp.float32) for shape in shapes]


def place():
    at_col, at_row = lax.axis_index("cols"), lax.axis_index("rows")
    n_cols, n_rows = lax.axis_size("cols"), lax.axis_size("rows")
    return at_col, at_row, n_cols, n_rows


def has_sides():
    at_col, at_row, n_cols, n_rows = place()
    flag = lambda test: jnp.where(test, 1.0, 0.0).astype(jnp.float32)
    return (
        flag(at_row > 0),
        flag(at_row < n_rows - 1),
        flag(at_col < n_cols - 1),
        flag(at_col > 0),
    )


def iota(shape, dim):
    return lax.broadcasted_iota(jnp.int32, shape, dim)


def cell_of(pixel, tiles):
    turn = (tiles + 1) * LANES
    return jnp.where(pixel < turn - HALF, pixel >> 3, ((pixel - turn) >> 3) & (2 * LANES - 1))


def gather_matrix(tiles):
    shape = ((tiles + 1) * LANES, 2 * LANES)
    hit = cell_of(iota(shape, 0), tiles) == iota(shape, 1)
    return jnp.where(hit, 1.0, 0.0).astype(jnp.bfloat16)


def split_dot(field, matrix):
    rows = field.shape[0]
    high = field.astype(jnp.bfloat16)
    low = (field - high.astype(jnp.float32)).astype(jnp.bfloat16)
    both = jnp.dot(
        jnp.concatenate([high, low], axis=0), matrix, preferred_element_type=jnp.float32
    )
    return both[:rows] + both[rows:]


def roll(field, by, axis):
    return pltpu.roll(field, by % field.shape[axis], axis)


def load(ref, at, rows=STRIP):
    return [ref[t, pl.ds(at, rows), :] for t in range(ref.shape[0])]


def store(ref, at, strip):
    for t, part in enumerate(strip):
        ref[t, pl.ds(at, part.shape[0]), :] = part


def wide(ref, at, rows):
    return jnp.concatenate(load(ref, at, rows), axis=1)


def read_taps(taps):
    return [[taps[a, b] for b in range(3)] for a in range(3)]


def tap_total(taps, power):
    return sum(tap * tap if power == 2 else tap for line in taps for tap in line)


def from_west(strip):
    lane = iota(strip[0].shape, 1)
    turned = [roll(part, 1, 1) for part in strip]
    return [jnp.where(lane == 0, turned[t - 1], turned[t]) for t in range(len(strip))]


def from_east(strip):
    lane = iota(strip[0].shape, 1)
    turned = [roll(part, -1, 1) for part in strip]
    count = len(strip)
    return [
        jnp.where(lane == LANES - 1, turned[(t + 1) % count], turned[t]) for t in range(count)
    ]


def tap_sums(ref, at, taps, flip):
    if flip:
        taps = [line[::-1] for line in taps[::-1]]
    above, here, below = load(ref, at - 1), load(ref, at), load(ref, at + 1)
    sums = [[], [], []]
    for t in range(len(here)):
        for b in range(3):
            sums[b].append(
                taps[0][b] * above[t] + taps[1][b] * here[t] + taps[2][b] * below[t]
            )
    return sums


def conv(ref, at, taps, flip):
    sums = tap_sums(ref, at, taps, flip)
    west, east = from_west(sums[0]), from_east(sums[2])
    return [sums[1][t] + west[t] + east[t] for t in range(len(west))]


def operate(ref, image, east_ref, south_ref, at, taps):
    above, here, below = load(ref, at - 1), load(ref, at), load(ref, at + 1)
    east, south, north = load(east_ref, at), load(south_ref, at), load(south_ref, at - 1)
    sums = tap_sums(image, at, taps, True)
    span = range(len(here))
    beside = from_east(here)
    flux = [east[t] * (here[t] - beside[t]) for t in span]
    from_left = from_west([sums[0][t] - flux[t] for t in span])
    from_right = from_east(sums[2])
    return here, [
        sums[1][t]
        + flux[t]
        + from_left[t]
        + from_right[t]
        + south[t] * (here[t] - below[t])
        - north[t] * (above[t] - here[t])
        for t in span
    ]


def begin(obs, cond, at, taps, sides):
    above, here, below = load(cond, at - 1), load(cond, at), load(cond, at + 1)
    span = range(len(here))
    right = from_east(here)
    east = [here[t] + right[t] for t in span]
    west = from_west(east)
    south = [here[t] + below[t] for t in span]
    squares = tap_total(taps, 2)
    diag = [squares + east[t] + west[t] + south[t] + (here[t] + above[t]) for t in span]
    inverse = [pl.reciprocal(part, approx=True) for part in diag]
    inverse = [inverse[t] * (2.0 - diag[t] * inverse[t]) for t in span]
    inverse[-1] = inverse[-1] * sides
    return east, south, inverse, conv(obs, at, taps, True)


def pick_lanes(field, lanes):
    return jnp.take_along_axis(field, lanes, axis=1, mode="promise_in_bounds")


def spread_cells(cells, spread):
    tiles = spread.shape[0] - 1
    lane = iota((cells.shape[0], LANES), 1)
    for t in range(tiles):
        spread[t] = pick_lanes(cells[:, :LANES], (lane >> 3) + t * (LANES // COARSE))
    turn = jnp.where(lane < HALF, 0, LANES - LANES // COARSE)
    spread[tiles] = pick_lanes(cells[:, LANES:], (lane >> 3) + turn)


def cells_at(spread, at):
    first = at // EDGE + EDGE - 2
    rows = [load(spread, first + index, 1) for index in range(STRIP // EDGE)]
    return [
        jnp.concatenate([jnp.broadcast_to(row, (EDGE, LANES)) for row in parts], axis=0)
        for parts in zip(*rows)
    ]


def cell_sums(ref, tiles, down):
    lane = iota((down, LANES), 1)
    total = jnp.zeros((down, LANES), jnp.float32)
    for t in range(tiles):
        picked = [
            ref[t, pl.ds(2 * EDGE + k, down, stride=COARSE), :] for k in range(COARSE)
        ]
        part = sum(picked[1:], picked[0])
        for by in (1, 2, 4):
            part = part + roll(part, -by, 1)
        part = pick_lanes(part, (lane & (LANES // COARSE - 1)) * COARSE)
        total = jnp.where(lane // (LANES // COARSE) == t, part, total)
    return total


def side_lanes(has_e, has_w):
    return jnp.where(iota((STRIP, LANES), 1) < HALF, has_e, has_w)


def mask_rows(ref, has_n, has_s):
    last = ref.shape[1] - 2 * EDGE

    def work(t, _):
        for at, flag in ((EDGE, has_n), (last, has_s)):
            ref[t, at : at + EDGE, :] = ref[t, at : at + EDGE, :] * flag
        return 0

    lax.fori_loop(0, ref.shape[0], work, 0)


def clear_pads(*refs):
    def work(t, _):
        empty = jnp.zeros((EDGE, LANES), jnp.float32)
        for ref in refs:
            ref[t, :EDGE, :] = empty
            ref[t, ref.shape[1] - EDGE :, :] = empty
        return 0

    lax.fori_loop(0, refs[0].shape[0], work, 0)


def product_sum(one, two, count, flags=None):
    total = one[0] * two[0]
    for t in range(1, count):
        total = total + one[t] * two[t]
    return fold(total, flags)


def fold(total, flags=None):
    parts = [total[at : at + EDGE] for at in range(0, total.shape[0], EDGE)]
    if flags is not None:
        parts = [part * flag for part, flag in zip(parts, flags)]
    return sum(parts[1:], parts[0])


def sweep(first, last, body, carry):
    width = GROUP * STRIP
    steps = -(-(last - first) // width)

    def work(index, carry):
        start = first + index * width
        at = pl.multiple_of(jnp.minimum(start, last - width), EDGE)
        pending = []
        for by in range(0, width, STRIP):
            stores, carry = body(at + by, start, carry)
            pending += [(ref, at + by, strip) for ref, strip in stores]
        for ref, row, strip in pending:
            store(ref, row, strip)
        return carry

    return lax.fori_loop(0, steps, work, carry)


def jacobi(source, table):
    source = table[0] * source

    def work(_, iterate):
        across = table[1] * roll(iterate, -1, 1) + table[2] * roll(iterate, 1, 1)
        along = table[3] * roll(iterate, -1, 0) + table[4] * roll(iterate, 1, 0)
        return ((1.0 - OMEGA) * iterate + source) + (across + along)

    return lax.fori_loop(0, SWEEPS - 1, work, source)


def in_pair_order(at, for_before, for_after):
    even = at % 2 == 0
    if callable(for_before):
        return (
            lambda index: jnp.where(even, for_after(index), for_before(index)),
            lambda index: jnp.where(even, for_before(index), for_after(index)),
        )
    return jnp.where(even, for_after, for_before), jnp.where(even, for_before, for_after)


def reader(tiles_here, refs, scratch, obs, cond, down):
    obs_in, class_in, weight_in, taps_in = refs
    classes, weights, taps, sums, obs_sem, class_sem, small_sem = scratch
    own = pl.ds(2 * EDGE, down * COARSE)
    small = [
        pltpu.make_async_copy(weight_in, weights, small_sem.at[0]),
        pltpu.make_async_copy(taps_in, taps, small_sem.at[1]),
    ]
    moves = []
    for slot, t in enumerate(tiles_here):
        lanes = pl.ds(t * LANES, LANES)
        moves.append(
            (
                pltpu.make_async_copy(class_in.at[:, lanes], classes.at[slot], class_sem.at[slot]),
                pltpu.make_async_copy(
                    obs_in.at[:, lanes], obs.at[slot, own, :], obs_sem.at[slot]
                ),
            )
        )
    for copy in small:
        copy.start()
    for pair in moves:
        for copy in pair:
            copy.start()
    sums[...] = jnp.zeros_like(sums)

    def settle(slot):
        if slot == 0:
            for copy in small:
                copy.wait()
        for copy in moves[slot]:
            copy.wait()
        values = [0.5 * weights[class_id] for class_id in range(CLASSES)]
        kind = classes[slot]
        cond[slot, own, :] = jnp.where(
            kind < 2,
            jnp.where(kind == 0, values[0], values[1]),
            jnp.where(kind == 2, values[2], values[3]),
        )
        for which, ref in enumerate((obs, cond)):
            picked = [
                ref[slot, pl.ds(2 * EDGE + k, down, stride=COARSE), :] for k in range(COARSE)
            ]
            sums[3 * which, slot, EDGE : EDGE + down, :] = sum(picked[1:], picked[0])
            sums[3 * which + 1, slot, EDGE : EDGE + down, :] = picked[0]
            sums[3 * which + 2, slot, EDGE : EDGE + down, :] = picked[-1]

    return settle


def reader_scratch(tiles, height, window, class_weights, taps):
    return [
        pltpu.VMEM((tiles, height, LANES), jnp.int32),
        pltpu.SMEM(class_weights.shape, jnp.float32),
        pltpu.SMEM(taps.shape, jnp.float32),
        pltpu.VMEM((6, tiles + 1, window, LANES), jnp.float32),
        pltpu.SemaphoreType.DMA((tiles,)),
        pltpu.SemaphoreType.DMA((tiles,)),
        pltpu.SemaphoreType.DMA((2,)),
    ]


def coarse_parts(sums, taps, matrix):
    window = sums.shape[2]
    whole = lambda index: wide(sums.at[index], 0, window)
    full, head, tail = whole(0), whole(1), whole(2)
    by_tap = [full - head + roll(head, -1, 0), full, full - tail + roll(tail, 1, 0)]
    across = [sum(taps[a][b] * by_tap[a] for a in range(3)) for b in range(3)]
    source = across[1] + roll(across[0], -1, 1) + roll(across[2], 1, 1)
    full, head, tail = whole(3), whole(4), whole(5)
    last = (iota(full.shape, 1) & (COARSE - 1)) == COARSE - 1
    east = jnp.where(last, full + roll(full, -1, 1), 0.0)
    south = tail + roll(head, -1, 0)
    cells = split_dot(jnp.concatenate([source, east, south], axis=0), matrix)
    source, east, south = cells[:window], cells[window : 2 * window], cells[2 * window :]
    around = east + roll(east, 1, 1) + south + roll(south, 1, 0)
    return [source, east, south, around]


def edge_kernel(tiles, down, *refs):
    arguments, (send_a, send_b), (obs, cond, message, *scratch) = refs[:4], refs[4:6], refs[6:]
    height = down * COARSE
    halves = height // LANES
    window = down + 2 * EDGE
    settle = reader((0, tiles - 1), arguments, scratch, obs, cond, down)
    matrix = gather_matrix(2)
    for slot, begin_row in ((0, 0), (1, LANES - EDGE)):
        settle(slot)
        for which, ref in enumerate((obs, cond)):
            turned = jnp.transpose(ref[slot, 2 * EDGE : 2 * EDGE + height, :])
            turned = turned[begin_row : begin_row + EDGE]
            for half in range(halves):
                at = (which * halves + half) * EDGE
                message[slot, at : at + EDGE, :] = turned[:, half * LANES : (half + 1) * LANES]
    parts = coarse_parts(scratch[3], read_taps(scratch[2]), matrix)
    spare = jnp.zeros((2 * LANES - 4 * window, 2 * LANES), jnp.float32)
    stack = jnp.concatenate(parts + [spare], axis=0)
    left = jnp.transpose(stack[:, :LANES])
    right = jnp.transpose(stack[:, LANES:])
    base = 2 * halves * EDGE
    past = 2 * LANES // COARSE
    for slot, pieces in (
        (0, (left[:EDGE], right[LANES - EDGE :])),
        (1, (left[past - EDGE : past], left[past : past + EDGE])),
    ):
        for index, piece in enumerate(pieces):
            for half in range(2):
                at = base + (2 * index + half) * EDGE
                message[slot, at : at + EDGE, :] = piece[:, half * LANES : (half + 1) * LANES]
    send_a[...], send_b[...] = in_pair_order(place()[0], message[0], message[1])


def edge(observed, class_map, class_weights, taps):
    height, breadth = observed.shape
    tiles, down = breadth // LANES, height // COARSE
    window = down + 2 * EDGE
    field = (3, height + 4 * EDGE, LANES)
    strip = ((2 * (height // LANES) + 4) * EDGE, LANES)
    return pl.pallas_call(
        functools.partial(edge_kernel, tiles, down),
        in_specs=[HBM] * 4,
        out_specs=[VMEM] * 2,
        out_shape=floats(strip, strip),
        scratch_shapes=[
            pltpu.VMEM(field, jnp.float32),
            pltpu.VMEM(field, jnp.float32),
            pltpu.VMEM((2,) + strip, jnp.float32),
        ]
        + reader_scratch(2, height, window, class_weights, taps),
        compiler_params=params(),
        name="pack_east_west",
    )(*[in_hbm(array) for array in (observed, class_map, class_weights, taps)])


def pack_kernel(tiles, down, *refs):
    arguments, (obs, cond, coarse_ref), scratch = refs[:4], refs[5:8], refs[8:]
    settle = reader(range(tiles), arguments, scratch, obs, cond, down)
    matrix = gather_matrix(tiles)
    for t in range(tiles):
        settle(t)
    for index, part in enumerate(coarse_parts(scratch[3], read_taps(scratch[2]), matrix)):
        coarse_ref[index] = part


def pack(observed, class_map, class_weights, taps, after):
    height, breadth = observed.shape
    tiles, down = breadth // LANES, height // COARSE
    window = down + 2 * EDGE
    field = (tiles + 1, height + 4 * EDGE, LANES)
    pixels = height * breadth
    return pl.pallas_call(
        functools.partial(pack_kernel, tiles, down),
        in_specs=[HBM] * 4 + [VMEM],
        out_specs=[VMEM] * 3,
        out_shape=floats(field, field, (4, window, 2 * LANES)),
        scratch_shapes=reader_scratch(tiles, height, window, class_weights, taps),
        compiler_params=params(),
        cost_estimate=pl.CostEstimate(
            flops=20 * pixels, bytes_accessed=16 * pixels, transcendentals=0
        ),
        name="pack_all",
    )(*[in_hbm(array) for array in (observed, class_map, class_weights, taps)], after)


def merge_sides(parts):
    block = iota((EDGE, LANES), 1) // (2 * EDGE)
    merged = jnp.zeros((EDGE, LANES), jnp.float32)
    for index, part in enumerate(parts):
        merged = jnp.where(block == index, roll(part, (2 * index + 1) * EDGE, 1), merged)
    return merged


def split_sides(merged, count):
    lane = iota((EDGE, LANES), 1)
    outer = (lane < EDGE) | (lane >= LANES - EDGE)
    return [
        jnp.where(outer, roll(merged, -(2 * index + 1) * EDGE, 1), 0.0) for index in range(count)
    ]


def middle_kernel(
    tiles,
    down,
    got_b,
    got_a,
    coarse_in,
    obs_in,
    cond_in,
    obs,
    cond,
    coarse_ref,
    send_a,
    send_b,
    message,
):
    height = down * COARSE
    halves = height // LANES
    at_col, at_row, _, _ = place()
    from_e, from_w = in_pair_order(at_col, got_b[...], got_a[...])
    gap = jnp.zeros((LANES - 2 * EDGE, LANES), jnp.float32)

    def turned(low, high):
        return jnp.transpose(jnp.concatenate([low, gap, high], axis=0))

    for which, field in enumerate((obs, cond)):
        for half in range(halves):
            at = (which * halves + half) * EDGE
            begin_row = 2 * EDGE + half * LANES
            field[tiles, begin_row : begin_row + LANES, :] = turned(
                from_e[at : at + EDGE], from_w[at : at + EDGE]
            )
    base = 2 * halves * EDGE

    def piece(strip, index, half):
        at = base + (2 * index + half) * EDGE
        return strip[at : at + EDGE]

    left = [turned(piece(from_w, 1, half), piece(from_e, 1, half)) for half in range(2)]
    right = [turned(piece(from_e, 0, half), piece(from_w, 0, half)) for half in range(2)]
    left = jnp.concatenate(left, axis=0)
    right = jnp.concatenate(right, axis=0)
    window = down + 2 * EDGE
    for index in range(4):
        rows = slice(index * window, (index + 1) * window)
        coarse_ref[index, :, :LANES] = coarse_in[index, :, :LANES] + left[rows]
        coarse_ref[index, :, LANES:] = coarse_in[index, :, LANES:] + right[rows]
    fields = (obs, cond)
    for slot, begin_row, first_row, over_row in (
        (0, 2 * EDGE, EDGE, EDGE - 1),
        (1, EDGE + height, window - 2 * EDGE, window - EDGE),
    ):
        pieces = [field[t, begin_row : begin_row + EDGE, :] for field in fields for t in range(tiles)]
        rows = slice(first_row, first_row + EDGE)
        pieces += [coarse_ref[index, rows, :LANES] for index in range(4)]
        beyond = [coarse_ref[index, rows, LANES:] for index in range(4)]
        beyond += [field[tiles, begin_row : begin_row + EDGE, :] for field in fields]
        pieces.append(merge_sides(beyond))
        pieces.append(
            jnp.concatenate(
                [
                    coarse_ref[index, over_row : over_row + 1, half * LANES : (half + 1) * LANES]
                    for index in range(4)
                    for half in range(2)
                ],
                axis=0,
            )
        )
        for index, piece in enumerate(pieces):
            message[slot, index] = piece
    send_a[...], send_b[...] = in_pair_order(at_row, message[0], message[1])


def middle(got_a, got_b, coarse, obs, cond):
    tiles, height = obs.shape[0] - 1, obs.shape[1] - 4 * EDGE
    down = height // COARSE
    long = (2 * tiles + 6, EDGE, LANES)
    return pl.pallas_call(
        functools.partial(middle_kernel, tiles, down),
        in_specs=[VMEM] * 5,
        out_specs=[VMEM] * 5,
        out_shape=floats(obs.shape, cond.shape, coarse.shape, long, long),
        input_output_aliases={3: 0, 4: 1},
        scratch_shapes=[pltpu.VMEM((2,) + long, jnp.float32)],
        compiler_params=params(),
        name="pack_north_south",
    )(got_b, got_a, coarse, obs, cond)


def inner_kernel(taps, obs, cond, res_ref, east_ref, south_ref, inv_ref):
    _, _, has_e, has_w = has_sides()
    clear_pads(east_ref, south_ref)
    taps = read_taps(taps)
    sides = side_lanes(has_e, has_w)

    def work(at, _, carry):
        fields = begin(obs, cond, at, taps, sides)
        return list(zip((east_ref, south_ref, inv_ref, res_ref), fields)), carry

    sweep(3 * EDGE, obs.shape[1] - 3 * EDGE, work, 0)


def inner(taps, obs, cond):
    field = obs.shape
    pixels = field[0] * field[1] * field[2]
    return pl.pallas_call(
        inner_kernel,
        in_specs=[SMEM] + [VMEM] * 2,
        out_specs=[VMEM] * 4,
        out_shape=floats(field, field, field, field),
        compiler_params=params(),
        cost_estimate=pl.CostEstimate(
            flops=45 * pixels, bytes_accessed=24 * pixels, transcendentals=0
        ),
        name="inner_strips",
    )(taps, obs, cond)


def first_kernel(
    tiles,
    down,
    taps,
    obs_in,
    cond_in,
    res_in,
    east_in,
    south_in,
    inv_in,
    got_b,
    got_a,
    coarse_in,
    obs,
    cond,
    res_ref,
    east_ref,
    south_ref,
    inv_ref,
    p_ref,
    q_ref,
    table_ref,
    own_ref,
    chunk_ref,
    dots_ref,
    image,
    spread,
):
    height = down * COARSE
    window = down + 2 * EDGE
    at_col, at_row, n_cols, n_rows = place()
    has_n, has_s, has_e, has_w = has_sides()
    clear_pads(obs, cond, p_ref, image)
    from_s, from_n = in_pair_order(
        at_row, lambda index: got_b[index], lambda index: got_a[index]
    )

    def fill(t, _):
        for which, field in enumerate((obs, cond)):
            field[t, EDGE : 2 * EDGE, :] = from_n(which * tiles + t)
            field[t, 2 * EDGE + height : 3 * EDGE + height, :] = from_s(which * tiles + t)
        return 0

    lax.fori_loop(0, tiles, fill, 0)
    sides_n, sides_s = [split_sides(strip(2 * tiles + 4), 6) for strip in (from_n, from_s)]
    for which, field in enumerate((obs, cond)):
        field[tiles, EDGE : 2 * EDGE, :] = sides_n[4 + which]
        field[tiles, 2 * EDGE + height : 3 * EDGE + height, :] = sides_s[4 + which]

    def joined(index):
        def parts(strip, beyond):
            rows = jnp.concatenate([strip(2 * tiles + index), beyond[index]], axis=1)
            over = strip(2 * tiles + 5)
            over = [over[2 * index + half : 2 * index + half + 1] for half in range(2)]
            return rows, jnp.concatenate(over, axis=1)

        rows_n, over_n = parts(from_n, sides_n)
        rows_s, over_s = parts(from_s, sides_s)
        empty = jnp.zeros((EDGE - 1, 2 * LANES), jnp.float32)
        gap = jnp.zeros((window - 4 * EDGE, 2 * LANES), jnp.float32)
        return coarse_in[index] + jnp.concatenate(
            [rows_n, over_n, empty, gap, empty, over_s, rows_s], axis=0
        )

    source, east, south, around = [joined(index) for index in range(4)]
    row = iota(source.shape, 0)
    lane = iota(source.shape, 1)
    inside = jnp.where(row < EDGE, has_n, jnp.where(row < window - EDGE, 1.0, has_s))
    inside = inside * jnp.where(
        lane < LANES, 1.0, jnp.where(lane < LANES + HALF, has_e, has_w)
    )
    taps = read_taps(taps)
    total = tap_total(taps, 1)
    factor = inside * OMEGA / (COARSE * COARSE * total * total + around)
    weights = (east, roll(east, 1, 1), south, roll(south, 1, 0))
    table = [factor] + [factor * weight for weight in weights]
    for index, part in enumerate(table):
        table_ref[index] = part
    spread_cells(jacobi(source, table_ref), spread)

    sides = side_lanes(has_e, has_w)

    def ends(index, _):
        at = pl.multiple_of(EDGE + index * height, EDGE)
        fields = begin(obs, cond, at, taps, sides)
        for ref, strip in zip((east_ref, south_ref, inv_ref, res_ref), fields):
            store(ref, at, strip)
        return 0

    lax.fori_loop(0, 2, ends, 0)
    mask_rows(inv_ref, has_n, has_s)

    def flags(at, start):
        rows = [at + by for by in range(0, STRIP, EDGE)]
        first_row = jnp.maximum(start, 2 * EDGE)
        return [
            jnp.where((row >= first_row) & (row < 2 * EDGE + height), 1.0, 0.0) for row in rows
        ]

    def begin_p(at, start, total):
        residual, inverse, cells = load(res_ref, at), load(inv_ref, at), cells_at(spread, at)
        strip = [residual[t] * inverse[t] + cells[t] for t in range(tiles + 1)]
        return [(p_ref, strip)], total + product_sum(residual, strip, tiles, flags(at, start))

    def blur(at, _, carry):
        strip = conv(p_ref, at, taps, False)
        strip[tiles] = strip[tiles] * sides
        return [(image, strip)], carry

    def finish(at, start, total):
        here, product = operate(p_ref, image, east_ref, south_ref, at, taps)
        return [(q_ref, product)], total + product_sum(here, product, tiles, flags(at, start))

    nothing = jnp.zeros((EDGE, LANES), jnp.float32)
    span = (EDGE, 3 * EDGE + height)
    dots_ref[0] = sweep(*span, begin_p, nothing)
    sweep(*span, blur, 0)
    mask_rows(image, has_n, has_s)
    dots_ref[1] = sweep(*span, finish, nothing)

    own = cell_sums(q_ref, tiles, down)
    own_ref[...] = own
    spare = jnp.zeros((LANES - down, LANES), jnp.float32)
    turned = jnp.transpose(jnp.concatenate([own, spare], axis=0))
    def empty(index, _):
        chunk_ref[index] = jnp.zeros((EDGE, LANES), jnp.float32)
        return 0

    lax.fori_loop(0, chunk_ref.shape[0], empty, 0)
    for down_by in (-1, 0, 1):
        for right_by in (-1, 0, 1):
            if down_by == 0 and right_by == 0:
                continue
            if down_by == 0:
                piece = turned[:EDGE] if right_by < 0 else turned[LANES - EDGE :]
            else:
                piece = own[:EDGE] if down_by < 0 else own[down - EDGE :]
            to_row, to_col = at_row + down_by, at_col + right_by

            @pl.when((to_row >= 0) & (to_row < n_rows) & (to_col >= 0) & (to_col < n_cols))
            def _(piece=piece, to_row=to_row, to_col=to_col):
                chunk_ref[to_col * n_rows + to_row] = piece


def first(taps, fields, got_a, got_b, coarse):
    field = fields[0].shape
    tiles, height = field[0] - 1, field[1] - 4 * EDGE
    down = height // COARSE
    window = down + 2 * EDGE
    count = lax.axis_size("cols") * lax.axis_size("rows")
    shapes = [field] * 8 + [
        (5, window, 2 * LANES),
        (down, LANES),
        (count, EDGE, LANES),
        (2, EDGE, LANES),
    ]
    return pl.pallas_call(
        functools.partial(first_kernel, tiles, down),
        in_specs=[SMEM] + [VMEM] * 9,
        out_specs=[VMEM] * len(shapes),
        out_shape=floats(*shapes),
        input_output_aliases={index + 1: index for index in range(6)},
        scratch_shapes=[
            pltpu.VMEM(field, jnp.float32),
            pltpu.VMEM((tiles + 1, window, LANES), jnp.float32),
        ],
        compiler_params=params(),
        name="first_direction",
    )(taps, *fields, got_b, got_a, coarse)[2:]


def second_kernel(
    tiles,
    down,
    taps,
    got_ref,
    own_ref,
    table_ref,
    q_ref,
    east_ref,
    south_ref,
    inv_ref,
    dots_in,
    w_ref,
    v_ref,
    out_ref,
    image,
    spread,
):
    height = down * COARSE
    has_n, has_s, has_e, has_w = has_sides()
    at_col, at_row, n_cols, n_rows = place()
    me = at_col * n_rows + at_row

    def got(down_by, right_by):
        to_row, to_col = at_row + down_by, at_col + right_by
        there = (to_row >= 0) & (to_row < n_rows) & (to_col >= 0) & (to_col < n_cols)
        return got_ref[jnp.where(there, to_col * n_rows + to_row, me)]

    low = iota((EDGE, LANES), 1) < HALF
    gap = jnp.zeros((LANES - 2 * EDGE, LANES), jnp.float32)
    beside = jnp.transpose(jnp.concatenate([got(0, 1), gap, got(0, -1)], axis=0))[:down]
    source = jnp.concatenate(
        [
            jnp.concatenate([got(-1, 0), jnp.where(low, got(-1, 1), got(-1, -1))], axis=1),
            jnp.concatenate([own_ref[...], beside], axis=1),
            jnp.concatenate([got(1, 0), jnp.where(low, got(1, 1), got(1, -1))], axis=1),
        ],
        axis=0,
    )
    spread_cells(jacobi(source, table_ref), spread)
    clear_pads(w_ref, image)
    sides = side_lanes(has_e, has_w)
    taps = read_taps(taps)

    def begin_w(at, _, carry):
        field, inverse, cells = load(q_ref, at), load(inv_ref, at), cells_at(spread, at)
        return [(w_ref, [field[t] * inverse[t] + cells[t] for t in range(tiles + 1)])], carry

    def blur(at, _, carry):
        strip = conv(w_ref, at, taps, False)
        strip[tiles] = strip[tiles] * sides
        return [(image, strip)], carry

    def finish(at, _, totals):
        here, product = operate(w_ref, image, east_ref, south_ref, at, taps)
        field = load(q_ref, at)
        return [(v_ref, product[:tiles])], (
            totals[0] + product_sum(field, here, tiles),
            totals[1] + product_sum(here, product, tiles),
        )

    nothing = jnp.zeros((EDGE, LANES), jnp.float32)
    span = (EDGE, 3 * EDGE + height)
    sweep(*span, begin_w, 0)
    sweep(*span, blur, 0)
    mask_rows(image, has_n, has_s)
    dot_qw, dot_wv = sweep(2 * EDGE, 2 * EDGE + height, finish, (nothing, nothing))
    line = jnp.zeros((1, LANES), jnp.float32)
    block = iota((1, LANES), 1) // (LANES // 4)
    for index, part in enumerate((dots_in[0], dots_in[1], dot_qw, dot_wv)):
        part = jnp.sum(part, axis=0, keepdims=True)
        part = part + roll(part, LANES // 2, 1)
        part = part + roll(part, LANES // 4, 1)
        line = jnp.where(block == index, part, line)
    for index in range(out_ref.shape[0]):
        out_ref[index] = line


def second(taps, got, own, table, q, east, south, inv, dots):
    tiles, height = q.shape[0] - 1, q.shape[1] - 4 * EDGE
    down = height // COARSE
    window = down + 2 * EDGE
    count = lax.axis_size("cols") * lax.axis_size("rows")
    return pl.pallas_call(
        functools.partial(second_kernel, tiles, down),
        in_specs=[SMEM] + [VMEM] * 8,
        out_specs=[VMEM] * 3,
        out_shape=floats(q.shape, q.shape, (count, 1, LANES)),
        scratch_shapes=[
            pltpu.VMEM(q.shape, jnp.float32),
            pltpu.VMEM((tiles + 1, window, LANES), jnp.float32),
        ],
        compiler_params=params(),
        name="second_direction",
    )(taps, got, own, table, q, east, south, inv, dots)


def combine_kernel(
    tiles, height, sums_ref, p_ref, w_ref, r_ref, q_ref, v_ref, sol_out, res_out, sol, res, sem
):
    line = sums_ref[0]
    for index in range(1, sums_ref.shape[0]):
        line = line + sums_ref[index]
    block = iota((1, LANES), 1) // (LANES // 4)
    pick = lambda index: jnp.sum(jnp.where(block == index, line, 0.0), axis=1, keepdims=True)
    rp, pq, qw, wv = [pick(index) for index in range(4)]
    step = rp / pq
    rp_next = step * step * qw - rp
    ratio = rp_next / rp
    lead = 1.0 + ratio
    curvature = lead * lead * pq - 2.0 * lead * step * qw + step * step * wv
    step_next = rp_next / curvature
    on_p = jnp.broadcast_to(step + step_next * lead, (CHUNK, LANES))
    on_w = jnp.broadcast_to(step_next * step, (CHUNK, LANES))

    def copies(index):
        rows = pl.ds(pl.multiple_of(index * CHUNK, CHUNK), CHUNK)
        return (
            pltpu.make_async_copy(sol.at[rows, :], sol_out.at[rows, :], sem.at[0, index]),
            pltpu.make_async_copy(res.at[rows, :], res_out.at[rows, :], sem.at[1, index]),
        )

    def work(index, _):
        at = pl.multiple_of(index * CHUNK, CHUNK)
        p, w, r, q, v = [
            load(ref, at + 2 * EDGE, CHUNK) for ref in (p_ref, w_ref, r_ref, q_ref, v_ref)
        ]
        one = [on_p * p[t] - on_w * w[t] for t in range(tiles)]
        two = [r[t] - on_p * q[t] + on_w * v[t] for t in range(tiles)]
        for t in range(tiles):
            sol[pl.ds(at, CHUNK), t * LANES : (t + 1) * LANES] = one[t]
            res[pl.ds(at, CHUNK), t * LANES : (t + 1) * LANES] = two[t]
        for copy in copies(index):
            copy.start()
        return 0

    def settle(index, _):
        for copy in copies(index):
            copy.wait()
        return 0

    lax.fori_loop(0, height // CHUNK, work, 0)
    lax.fori_loop(0, height // CHUNK, settle, 0)


def combine(sums, p, w, r, q, v):
    tiles, height = q.shape[0] - 1, q.shape[1] - 4 * EDGE
    shape = (height, tiles * LANES)
    return pl.pallas_call(
        functools.partial(combine_kernel, tiles, height),
        in_specs=[VMEM] * 6,
        out_specs=[HBM] * 2,
        out_shape=floats(shape, shape),
        scratch_shapes=[
            pltpu.VMEM(shape, jnp.float32),
            pltpu.VMEM(shape, jnp.float32),
            pltpu.SemaphoreType.DMA((2, height // CHUNK)),
        ],
        compiler_params=params(),
        name="combine",
    )(sums, p, w, r, q, v)


def exchange(send_a, send_b, axis):
    count = lax.axis_size(axis)

    def pairs(begin):
        return [
            pair for i in range(begin, count - 1, 2) for pair in ((i, i + 1), (i + 1, i))
        ]

    got_b = lax.ppermute(send_b, axis, pairs(1))
    got_a = lax.ppermute(send_a, axis, pairs(0))
    return got_a, got_b


def body(observed, class_map, class_weights, blur_kernel):
    arguments = (observed, class_map, class_weights, blur_kernel)
    send_a, send_b = edge(*arguments)
    got_a, got_b = exchange(send_a, send_b, "cols")
    obs, cond, coarse = pack(*arguments, send_a)
    obs, cond, coarse, send_a, send_b = middle(got_a, got_b, coarse, obs, cond)
    got_a, got_b = exchange(send_a, send_b, "rows")
    r, east, south, inv = inner(blur_kernel, obs, cond)
    fields = (obs, cond, r, east, south, inv)
    r, east, south, inv, p, q, table, own, chunk, dots = first(
        blur_kernel, fields, got_a, got_b, coarse
    )
    got = lax.all_to_all(chunk, AXES, 0, 0, tiled=True)
    w, v, line = second(blur_kernel, got, own, table, q, east, south, inv, dots)
    sums = lax.all_to_all(line, AXES, 0, 0, tiled=True)
    return tuple(combine(sums, p, w, r, q, v))


def solution(mesh):
    return jax.shard_map(
        body,
        mesh=mesh,
        in_specs=(P("rows", "cols"), P("rows", "cols"), P(), P()),
        out_specs=(P("rows", "cols"), P("rows", "cols")),
        check_vma=False,
    )
```

```python
import functools

import jax
import jax.numpy as jnp
from jax import lax
from jax.experimental import pallas as pl
from jax.experimental.pallas import tpu as pltpu
from jax.sharding import PartitionSpec as P

COARSE = 8
SWEEPS = 8
CLASSES = 4
OMEGA = 0.8

LANES = 128
HALF = LANES // 2
EDGE = 8
STRIP = 2 * EDGE
GROUP = 2
CHUNK = 32
AXES = ("cols", "rows")
LIMIT = 40 * 1024 * 1024


VMEM = pl.BlockSpec(memory_space=pltpu.VMEM)
SMEM = pl.BlockSpec(memory_space=pltpu.SMEM)
HBM = pl.BlockSpec(memory_space=pltpu.HBM)


def params():
    return pltpu.CompilerParams(vmem_limit_bytes=LIMIT)


def in_hbm(array):
    return pltpu.with_memory_space_constraint(array, pltpu.HBM)


def floats(*shapes):
    return [jax.ShapeDtypeStruct(shape, jnp.float32) for shape in shapes]


def place():
    at_col, at_row = lax.axis_index("cols"), lax.axis_index("rows")
    n_cols, n_rows = lax.axis_size("cols"), lax.axis_size("rows")
    return at_col, at_row, n_cols, n_rows


def has_sides():
    at_col, at_row, n_cols, n_rows = place()
    flag = lambda test: jnp.where(test, 1.0, 0.0).astype(jnp.float32)
    return (
        flag(at_row > 0),
        flag(at_row < n_rows - 1),
        flag(at_col < n_cols - 1),
        flag(at_col > 0),
    )


def iota(shape, dim):
    return lax.broadcasted_iota(jnp.int32, shape, dim)


def cell_of(pixel, tiles):
    turn = (tiles + 1) * LANES
    return jnp.where(pixel < turn - HALF, pixel >> 3, ((pixel - turn) >> 3) & (2 * LANES - 1))


def gather_matrix(tiles):
    shape = ((tiles + 1) * LANES, 2 * LANES)
    hit = cell_of(iota(shape, 0), tiles) == iota(shape, 1)
    return jnp.where(hit, 1.0, 0.0).astype(jnp.bfloat16)


def split_dot(field, matrix):
    rows = field.shape[0]
    high = field.astype(jnp.bfloat16)
    low = (field - high.astype(jnp.float32)).astype(jnp.bfloat16)
    both = jnp.dot(
        jnp.concatenate([high, low], axis=0), matrix, preferred_element_type=jnp.float32
    )
    return both[:rows] + both[rows:]


def roll(field, by, axis):
    return pltpu.roll(field, by % field.shape[axis], axis)


def load(ref, at, rows=STRIP):
    return [ref[t, pl.ds(at, rows), :] for t in range(ref.shape[0])]


def store(ref, at, strip):
    for t, part in enumerate(strip):
        ref[t, pl.ds(at, part.shape[0]), :] = part


def wide(ref, at, rows):
    return jnp.concatenate(load(ref, at, rows), axis=1)


def read_taps(taps):
    return [[taps[a, b] for b in range(3)] for a in range(3)]


def tap_total(taps, power):
    return sum(tap * tap if power == 2 else tap for line in taps for tap in line)


def from_west(strip):
    lane = iota(strip[0].shape, 1)
    turned = [roll(part, 1, 1) for part in strip]
    return [jnp.where(lane == 0, turned[t - 1], turned[t]) for t in range(len(strip))]


def from_east(strip):
    lane = iota(strip[0].shape, 1)
    turned = [roll(part, -1, 1) for part in strip]
    count = len(strip)
    return [
        jnp.where(lane == LANES - 1, turned[(t + 1) % count], turned[t]) for t in range(count)
    ]


def tap_sums(ref, at, taps, flip):
    if flip:
        taps = [line[::-1] for line in taps[::-1]]
    above, here, below = load(ref, at - 1), load(ref, at), load(ref, at + 1)
    sums = [[], [], []]
    for t in range(len(here)):
        for b in range(3):
            sums[b].append(
                taps[0][b] * above[t] + taps[1][b] * here[t] + taps[2][b] * below[t]
            )
    return sums


def conv(ref, at, taps, flip):
    sums = tap_sums(ref, at, taps, flip)
    west, east = from_west(sums[0]), from_east(sums[2])
    return [sums[1][t] + west[t] + east[t] for t in range(len(west))]


def operate(ref, image, east_ref, south_ref, at, taps):
    above, here, below = load(ref, at - 1), load(ref, at), load(ref, at + 1)
    east, south, north = load(east_ref, at), load(south_ref, at), load(south_ref, at - 1)
    sums = tap_sums(image, at, taps, True)
    span = range(len(here))
    beside = from_east(here)
    flux = [east[t] * (here[t] - beside[t]) for t in span]
    from_left = from_west([sums[0][t] - flux[t] for t in span])
    from_right = from_east(sums[2])
    return here, [
        sums[1][t]
        + flux[t]
        + from_left[t]
        + from_right[t]
        + south[t] * (here[t] - below[t])
        - north[t] * (above[t] - here[t])
        for t in span
    ]


def begin(obs, cond, at, taps, sides):
    above, here, below = load(cond, at - 1), load(cond, at), load(cond, at + 1)
    span = range(len(here))
    right = from_east(here)
    east = [here[t] + right[t] for t in span]
    west = from_west(east)
    south = [here[t] + below[t] for t in span]
    squares = tap_total(taps, 2)
    diag = [squares + east[t] + west[t] + south[t] + (here[t] + above[t]) for t in span]
    inverse = [pl.reciprocal(part, approx=True) for part in diag]
    inverse = [inverse[t] * (2.0 - diag[t] * inverse[t]) for t in span]
    inverse[-1] = inverse[-1] * sides
    return east, south, inverse, conv(obs, at, taps, True)


def pick_lanes(field, lanes):
    return jnp.take_along_axis(field, lanes, axis=1, mode="promise_in_bounds")


def spread_cells(cells, spread):
    tiles = spread.shape[0] - 1
    lane = iota((cells.shape[0], LANES), 1)
    for t in range(tiles):
        spread[t] = pick_lanes(cells[:, :LANES], (lane >> 3) + t * (LANES // COARSE))
    turn = jnp.where(lane < HALF, 0, LANES - LANES // COARSE)
    spread[tiles] = pick_lanes(cells[:, LANES:], (lane >> 3) + turn)


def cells_at(spread, at):
    first = at // EDGE + EDGE - 2
    rows = [load(spread, first + index, 1) for index in range(STRIP // EDGE)]
    return [
        jnp.concatenate([jnp.broadcast_to(row, (EDGE, LANES)) for row in parts], axis=0)
        for parts in zip(*rows)
    ]


def cell_sums(ref, tiles, down):
    lane = iota((down, LANES), 1)
    total = jnp.zeros((down, LANES), jnp.float32)
    for t in range(tiles):
        picked = [
            ref[t, pl.ds(2 * EDGE + k, down, stride=COARSE), :] for k in range(COARSE)
        ]
        part = sum(picked[1:], picked[0])
        for by in (1, 2, 4):
            part = part + roll(part, -by, 1)
        part = pick_lanes(part, (lane & (LANES // COARSE - 1)) * COARSE)
        total = jnp.where(lane // (LANES // COARSE) == t, part, total)
    return total


def side_lanes(has_e, has_w):
    return jnp.where(iota((STRIP, LANES), 1) < HALF, has_e, has_w)


def mask_rows(ref, has_n, has_s):
    last = ref.shape[1] - 2 * EDGE
    for at, flag in ((EDGE, has_n), (last, has_s)):
        ref[:, at : at + EDGE, :] = ref[:, at : at + EDGE, :] * flag


def clear_pads(*refs):
    empty = jnp.zeros((refs[0].shape[0], EDGE, LANES), jnp.float32)
    for ref in refs:
        ref[:, :EDGE, :] = empty
        ref[:, ref.shape[1] - EDGE :, :] = empty


def product_sum(one, two, count, flags=None):
    total = one[0] * two[0]
    for t in range(1, count):
        total = total + one[t] * two[t]
    return fold(total, flags)


def fold(total, flags=None):
    parts = [total[at : at + EDGE] for at in range(0, total.shape[0], EDGE)]
    if flags is not None:
        parts = [part * flag for part, flag in zip(parts, flags)]
    return sum(parts[1:], parts[0])


def sweep(first, last, body, carry):
    width = GROUP * STRIP
    steps = -(-(last - first) // width)

    def work(index, carry):
        start = first + index * width
        at = pl.multiple_of(jnp.minimum(start, last - width), EDGE)
        pending = []
        for by in range(0, width, STRIP):
            stores, carry = body(at + by, start, carry)
            pending += [(ref, at + by, strip) for ref, strip in stores]
        for ref, row, strip in pending:
            store(ref, row, strip)
        return carry

    return lax.fori_loop(0, steps, work, carry)


def jacobi(source, table):
    factor, east, west, south, north = [table[index] for index in range(5)]
    source = factor * source
    iterate = source
    for _ in range(SWEEPS - 1):
        across = east * roll(iterate, -1, 1) + west * roll(iterate, 1, 1)
        along = south * roll(iterate, -1, 0) + north * roll(iterate, 1, 0)
        iterate = ((1.0 - OMEGA) * iterate + source) + (across + along)
    return iterate


def in_pair_order(at, for_before, for_after):
    even = at % 2 == 0
    if callable(for_before):
        return (
            lambda index: jnp.where(even, for_after(index), for_before(index)),
            lambda index: jnp.where(even, for_before(index), for_after(index)),
        )
    return jnp.where(even, for_after, for_before), jnp.where(even, for_before, for_after)


def reader(tiles_here, refs, scratch, obs, cond, down):
    obs_in, class_in, weight_in, taps_in = refs
    classes, weights, taps, sums, obs_sem, class_sem, small_sem = scratch
    own = pl.ds(2 * EDGE, down * COARSE)
    small = [
        pltpu.make_async_copy(weight_in, weights, small_sem.at[0]),
        pltpu.make_async_copy(taps_in, taps, small_sem.at[1]),
    ]
    moves = []
    for slot, t in enumerate(tiles_here):
        lanes = pl.ds(t * LANES, LANES)
        moves.append(
            (
                pltpu.make_async_copy(class_in.at[:, lanes], classes.at[slot], class_sem.at[slot]),
                pltpu.make_async_copy(
                    obs_in.at[:, lanes], obs.at[slot, own, :], obs_sem.at[slot]
                ),
            )
        )
    for copy in small:
        copy.start()
    for pair in moves:
        for copy in pair:
            copy.start()
    sums[...] = jnp.zeros_like(sums)

    def settle(slot):
        if slot == 0:
            for copy in small:
                copy.wait()
        for copy in moves[slot]:
            copy.wait()
        values = [0.5 * weights[class_id] for class_id in range(CLASSES)]
        kind = classes[slot]
        cond[slot, own, :] = jnp.where(
            kind < 2,
            jnp.where(kind == 0, values[0], values[1]),
            jnp.where(kind == 2, values[2], values[3]),
        )
        for which, ref in enumerate((obs, cond)):
            picked = [
                ref[slot, pl.ds(2 * EDGE + k, down, stride=COARSE), :] for k in range(COARSE)
            ]
            sums[3 * which, slot, EDGE : EDGE + down, :] = sum(picked[1:], picked[0])
            sums[3 * which + 1, slot, EDGE : EDGE + down, :] = picked[0]
            sums[3 * which + 2, slot, EDGE : EDGE + down, :] = picked[-1]

    return settle


def reader_scratch(tiles, height, window, class_weights, taps):
    return [
        pltpu.VMEM((tiles, height, LANES), jnp.int32),
        pltpu.SMEM(class_weights.shape, jnp.float32),
        pltpu.SMEM(taps.shape, jnp.float32),
        pltpu.VMEM((6, tiles + 1, window, LANES), jnp.float32),
        pltpu.SemaphoreType.DMA((tiles,)),
        pltpu.SemaphoreType.DMA((tiles,)),
        pltpu.SemaphoreType.DMA((2,)),
    ]


def coarse_parts(sums, taps, matrix):
    window = sums.shape[2]
    whole = lambda index: wide(sums.at[index], 0, window)
    full, head, tail = whole(0), whole(1), whole(2)
    by_tap = [full - head + roll(head, -1, 0), full, full - tail + roll(tail, 1, 0)]
    across = [sum(taps[a][b] * by_tap[a] for a in range(3)) for b in range(3)]
    source = across[1] + roll(across[0], -1, 1) + roll(across[2], 1, 1)
    full, head, tail = whole(3), whole(4), whole(5)
    last = (iota(full.shape, 1) & (COARSE - 1)) == COARSE - 1
    east = jnp.where(last, full + roll(full, -1, 1), 0.0)
    south = tail + roll(head, -1, 0)
    cells = split_dot(jnp.concatenate([source, east, south], axis=0), matrix)
    source, east, south = cells[:window], cells[window : 2 * window], cells[2 * window :]
    around = east + roll(east, 1, 1) + south + roll(south, 1, 0)
    return [source, east, south, around]


def edge_kernel(tiles, down, *refs):
    arguments, (send_a, send_b), (obs, cond, message, *scratch) = refs[:4], refs[4:6], refs[6:]
    height = down * COARSE
    halves = height // LANES
    window = down + 2 * EDGE
    settle = reader((0, tiles - 1), arguments, scratch, obs, cond, down)
    matrix = gather_matrix(2)
    for slot, begin_row in ((0, 0), (1, LANES - EDGE)):
        settle(slot)
        for which, ref in enumerate((obs, cond)):
            turned = jnp.transpose(ref[slot, 2 * EDGE : 2 * EDGE + height, :])
            turned = turned[begin_row : begin_row + EDGE]
            for half in range(halves):
                at = (which * halves + half) * EDGE
                message[slot, at : at + EDGE, :] = turned[:, half * LANES : (half + 1) * LANES]
    parts = coarse_parts(scratch[3], read_taps(scratch[2]), matrix)
    spare = jnp.zeros((2 * LANES - 4 * window, 2 * LANES), jnp.float32)
    stack = jnp.concatenate(parts + [spare], axis=0)
    left = jnp.transpose(stack[:, :LANES])
    right = jnp.transpose(stack[:, LANES:])
    base = 2 * halves * EDGE
    past = 2 * LANES // COARSE
    for slot, pieces in (
        (0, (left[:EDGE], right[LANES - EDGE :])),
        (1, (left[past - EDGE : past], left[past : past + EDGE])),
    ):
        for index, piece in enumerate(pieces):
            for half in range(2):
                at = base + (2 * index + half) * EDGE
                message[slot, at : at + EDGE, :] = piece[:, half * LANES : (half + 1) * LANES]
    send_a[...], send_b[...] = in_pair_order(place()[0], message[0], message[1])


def edge(observed, class_map, class_weights, taps):
    height, breadth = observed.shape
    tiles, down = breadth // LANES, height // COARSE
    window = down + 2 * EDGE
    field = (3, height + 4 * EDGE, LANES)
    strip = ((2 * (height // LANES) + 4) * EDGE, LANES)
    return pl.pallas_call(
        functools.partial(edge_kernel, tiles, down),
        in_specs=[HBM] * 4,
        out_specs=[VMEM] * 2,
        out_shape=floats(strip, strip),
        scratch_shapes=[
            pltpu.VMEM(field, jnp.float32),
            pltpu.VMEM(field, jnp.float32),
            pltpu.VMEM((2,) + strip, jnp.float32),
        ]
        + reader_scratch(2, height, window, class_weights, taps),
        compiler_params=params(),
        name="pack_east_west",
    )(*[in_hbm(array) for array in (observed, class_map, class_weights, taps)])


def pack_kernel(tiles, down, *refs):
    arguments, (obs, cond, coarse_ref), scratch = refs[:4], refs[5:8], refs[8:]
    settle = reader(range(tiles), arguments, scratch, obs, cond, down)
    matrix = gather_matrix(tiles)
    for t in range(tiles):
        settle(t)
    for index, part in enumerate(coarse_parts(scratch[3], read_taps(scratch[2]), matrix)):
        coarse_ref[index] = part


def pack(observed, class_map, class_weights, taps, after):
    height, breadth = observed.shape
    tiles, down = breadth // LANES, height // COARSE
    window = down + 2 * EDGE
    field = (tiles + 1, height + 4 * EDGE, LANES)
    pixels = height * breadth
    return pl.pallas_call(
        functools.partial(pack_kernel, tiles, down),
        in_specs=[HBM] * 4 + [VMEM],
        out_specs=[VMEM] * 3,
        out_shape=floats(field, field, (4, window, 2 * LANES)),
        scratch_shapes=reader_scratch(tiles, height, window, class_weights, taps),
        compiler_params=params(),
        cost_estimate=pl.CostEstimate(
            flops=20 * pixels, bytes_accessed=16 * pixels, transcendentals=0
        ),
        name="pack_all",
    )(*[in_hbm(array) for array in (observed, class_map, class_weights, taps)], after)


def merge_sides(parts):
    block = iota((EDGE, LANES), 1) // (2 * EDGE)
    merged = jnp.zeros((EDGE, LANES), jnp.float32)
    for index, part in enumerate(parts):
        merged = jnp.where(block == index, roll(part, (2 * index + 1) * EDGE, 1), merged)
    return merged


def split_sides(merged, count):
    lane = iota((EDGE, LANES), 1)
    outer = (lane < EDGE) | (lane >= LANES - EDGE)
    return [
        jnp.where(outer, roll(merged, -(2 * index + 1) * EDGE, 1), 0.0) for index in range(count)
    ]


def middle_kernel(
    tiles,
    down,
    got_b,
    got_a,
    coarse_in,
    obs_in,
    cond_in,
    obs,
    cond,
    coarse_ref,
    send_a,
    send_b,
    message,
):
    height = down * COARSE
    halves = height // LANES
    at_col, at_row, _, _ = place()
    from_e, from_w = in_pair_order(at_col, got_b[...], got_a[...])
    gap = jnp.zeros((LANES - 2 * EDGE, LANES), jnp.float32)

    def turned(low, high):
        return jnp.transpose(jnp.concatenate([low, gap, high], axis=0))

    for which, field in enumerate((obs, cond)):
        for half in range(halves):
            at = (which * halves + half) * EDGE
            begin_row = 2 * EDGE + half * LANES
            field[tiles, begin_row : begin_row + LANES, :] = turned(
                from_e[at : at + EDGE], from_w[at : at + EDGE]
            )
    base = 2 * halves * EDGE

    def piece(strip, index, half):
        at = base + (2 * index + half) * EDGE
        return strip[at : at + EDGE]

    left = [turned(piece(from_w, 1, half), piece(from_e, 1, half)) for half in range(2)]
    right = [turned(piece(from_e, 0, half), piece(from_w, 0, half)) for half in range(2)]
    left = jnp.concatenate(left, axis=0)
    right = jnp.concatenate(right, axis=0)
    window = down + 2 * EDGE
    for index in range(4):
        rows = slice(index * window, (index + 1) * window)
        coarse_ref[index, :, :LANES] = coarse_in[index, :, :LANES] + left[rows]
        coarse_ref[index, :, LANES:] = coarse_in[index, :, LANES:] + right[rows]
    fields = (obs, cond)
    for slot, begin_row, first_row, over_row in (
        (0, 2 * EDGE, EDGE, EDGE - 1),
        (1, EDGE + height, window - 2 * EDGE, window - EDGE),
    ):
        pieces = [field[t, begin_row : begin_row + EDGE, :] for field in fields for t in range(tiles)]
        rows = slice(first_row, first_row + EDGE)
        pieces += [coarse_ref[index, rows, :LANES] for index in range(4)]
        beyond = [coarse_ref[index, rows, LANES:] for index in range(4)]
        beyond += [field[tiles, begin_row : begin_row + EDGE, :] for field in fields]
        pieces.append(merge_sides(beyond))
        pieces.append(
            jnp.concatenate(
                [
                    coarse_ref[index, over_row : over_row + 1, half * LANES : (half + 1) * LANES]
                    for index in range(4)
                    for half in range(2)
                ],
                axis=0,
            )
        )
        for index, piece in enumerate(pieces):
            message[slot, index] = piece
    send_a[...], send_b[...] = in_pair_order(at_row, message[0], message[1])


def middle(got_a, got_b, coarse, obs, cond):
    tiles, height = obs.shape[0] - 1, obs.shape[1] - 4 * EDGE
    down = height // COARSE
    long = (2 * tiles + 6, EDGE, LANES)
    return pl.pallas_call(
        functools.partial(middle_kernel, tiles, down),
        in_specs=[VMEM] * 5,
        out_specs=[VMEM] * 5,
        out_shape=floats(obs.shape, cond.shape, coarse.shape, long, long),
        input_output_aliases={3: 0, 4: 1},
        scratch_shapes=[pltpu.VMEM((2,) + long, jnp.float32)],
        compiler_params=params(),
        name="pack_north_south",
    )(got_b, got_a, coarse, obs, cond)


def inner_kernel(taps, obs, cond, res_ref, east_ref, south_ref, inv_ref):
    _, _, has_e, has_w = has_sides()
    clear_pads(east_ref, south_ref)
    taps = read_taps(taps)
    sides = side_lanes(has_e, has_w)

    def work(at, _, carry):
        fields = begin(obs, cond, at, taps, sides)
        return list(zip((east_ref, south_ref, inv_ref, res_ref), fields)), carry

    sweep(3 * EDGE, obs.shape[1] - 3 * EDGE, work, 0)


def inner(taps, obs, cond):
    field = obs.shape
    pixels = field[0] * field[1] * field[2]
    return pl.pallas_call(
        inner_kernel,
        in_specs=[SMEM] + [VMEM] * 2,
        out_specs=[VMEM] * 4,
        out_shape=floats(field, field, field, field),
        compiler_params=params(),
        cost_estimate=pl.CostEstimate(
            flops=45 * pixels, bytes_accessed=24 * pixels, transcendentals=0
        ),
        name="inner_strips",
    )(taps, obs, cond)


def first_kernel(
    tiles,
    down,
    taps,
    obs_in,
    cond_in,
    res_in,
    east_in,
    south_in,
    inv_in,
    got_b,
    got_a,
    coarse_in,
    obs,
    cond,
    res_ref,
    east_ref,
    south_ref,
    inv_ref,
    p_ref,
    q_ref,
    table_ref,
    own_ref,
    chunk_ref,
    dots_ref,
    image,
    spread,
):
    height = down * COARSE
    window = down + 2 * EDGE
    at_col, at_row, n_cols, n_rows = place()
    has_n, has_s, has_e, has_w = has_sides()
    clear_pads(obs, cond, p_ref, image)
    from_s, from_n = in_pair_order(
        at_row, lambda index: got_b[index], lambda index: got_a[index]
    )

    for which, field in enumerate((obs, cond)):
        for t in range(tiles):
            field[t, EDGE : 2 * EDGE, :] = from_n(which * tiles + t)
            field[t, 2 * EDGE + height : 3 * EDGE + height, :] = from_s(which * tiles + t)
    sides_n, sides_s = [split_sides(strip(2 * tiles + 4), 6) for strip in (from_n, from_s)]
    for which, field in enumerate((obs, cond)):
        field[tiles, EDGE : 2 * EDGE, :] = sides_n[4 + which]
        field[tiles, 2 * EDGE + height : 3 * EDGE + height, :] = sides_s[4 + which]

    edge_row = iota((EDGE, 2 * LANES), 0)

    def joined(index):
        def over(strip, row):
            line = [
                jnp.broadcast_to(
                    strip((2 * tiles + 5, pl.ds(2 * index + half, 1))), (EDGE, LANES)
                )
                for half in range(2)
            ]
            return jnp.where(edge_row == row, jnp.concatenate(line, axis=1), 0.0)

        def rows(strip, beyond):
            return jnp.concatenate([strip(2 * tiles + index), beyond[index]], axis=1)

        parts = [coarse_in[index, at : at + EDGE, :] for at in range(0, window, EDGE)]
        parts[0] = parts[0] + rows(from_n, sides_n)
        parts[1] = parts[1] + over(from_n, 0)
        parts[-2] = parts[-2] + over(from_s, EDGE - 1)
        parts[-1] = parts[-1] + rows(from_s, sides_s)
        return jnp.concatenate(parts, axis=0)

    source, east, south, around = [joined(index) for index in range(4)]
    row = iota(source.shape, 0)
    lane = iota(source.shape, 1)
    inside = jnp.where(row < EDGE, has_n, jnp.where(row < window - EDGE, 1.0, has_s))
    inside = inside * jnp.where(
        lane < LANES, 1.0, jnp.where(lane < LANES + HALF, has_e, has_w)
    )
    taps = read_taps(taps)
    total = tap_total(taps, 1)
    factor = inside * OMEGA / (COARSE * COARSE * total * total + around)
    weights = (east, roll(east, 1, 1), south, roll(south, 1, 0))
    table = [factor] + [factor * weight for weight in weights]
    for index, part in enumerate(table):
        table_ref[index] = part
    sides = side_lanes(has_e, has_w)
    half = iota((STRIP, LANES), 0) // EDGE
    pending = []
    for index, known in ((0, has_n), (1, has_s)):
        at = EDGE + index * height
        fields = begin(obs, cond, at, taps, sides)
        flag = jnp.where(half == index, known, 1.0)
        fields = (*fields[:2], [part * flag for part in fields[2]], fields[3])
        pending += [
            (ref, at, strip)
            for ref, strip in zip((east_ref, south_ref, inv_ref, res_ref), fields)
        ]
    spread_cells(jacobi(source, table), spread)
    for ref, at, strip in pending:
        store(ref, at, strip)

    def flags(at, start):
        rows = [at + by for by in range(0, STRIP, EDGE)]
        first_row = jnp.maximum(start, 2 * EDGE)
        return [
            jnp.where((row >= first_row) & (row < 2 * EDGE + height), 1.0, 0.0) for row in rows
        ]

    def begin_p(at, start, total):
        residual, inverse, cells = load(res_ref, at), load(inv_ref, at), cells_at(spread, at)
        strip = [residual[t] * inverse[t] + cells[t] for t in range(tiles + 1)]
        return [(p_ref, strip)], total + product_sum(residual, strip, tiles, flags(at, start))

    def blur(at, _, carry):
        strip = conv(p_ref, at, taps, False)
        strip[tiles] = strip[tiles] * sides
        return [(image, strip)], carry

    def finish(at, start, total):
        here, product = operate(p_ref, image, east_ref, south_ref, at, taps)
        return [(q_ref, product)], total + product_sum(here, product, tiles, flags(at, start))

    nothing = jnp.zeros((EDGE, LANES), jnp.float32)
    span = (EDGE, 3 * EDGE + height)
    dots_ref[0] = sweep(*span, begin_p, nothing)
    sweep(*span, blur, 0)
    mask_rows(image, has_n, has_s)
    dots_ref[1] = sweep(*span, finish, nothing)

    own = cell_sums(q_ref, tiles, down)
    own_ref[...] = own
    spare = jnp.zeros((LANES - down, LANES), jnp.float32)
    turned = jnp.transpose(jnp.concatenate([own, spare], axis=0))
    chunk_ref[...] = jnp.zeros_like(chunk_ref)
    for down_by in (-1, 0, 1):
        for right_by in (-1, 0, 1):
            if down_by == 0 and right_by == 0:
                continue
            if down_by == 0:
                piece = turned[:EDGE] if right_by < 0 else turned[LANES - EDGE :]
            else:
                piece = own[:EDGE] if down_by < 0 else own[down - EDGE :]
            to_row, to_col = at_row + down_by, at_col + right_by

            @pl.when((to_row >= 0) & (to_row < n_rows) & (to_col >= 0) & (to_col < n_cols))
            def _(piece=piece, to_row=to_row, to_col=to_col):
                chunk_ref[to_col * n_rows + to_row] = piece


def first(taps, fields, got_a, got_b, coarse):
    field = fields[0].shape
    tiles, height = field[0] - 1, field[1] - 4 * EDGE
    down = height // COARSE
    window = down + 2 * EDGE
    count = lax.axis_size("cols") * lax.axis_size("rows")
    shapes = [field] * 8 + [
        (5, window, 2 * LANES),
        (down, LANES),
        (count, EDGE, LANES),
        (2, EDGE, LANES),
    ]
    return pl.pallas_call(
        functools.partial(first_kernel, tiles, down),
        in_specs=[SMEM] + [VMEM] * 9,
        out_specs=[VMEM] * len(shapes),
        out_shape=floats(*shapes),
        input_output_aliases={index + 1: index for index in range(6)},
        scratch_shapes=[
            pltpu.VMEM(field, jnp.float32),
            pltpu.VMEM((tiles + 1, window, LANES), jnp.float32),
        ],
        compiler_params=params(),
        name="first_direction",
    )(taps, *fields, got_b, got_a, coarse)[2:]


def second_kernel(
    tiles,
    down,
    taps,
    got_ref,
    own_ref,
    table_ref,
    q_ref,
    east_ref,
    south_ref,
    inv_ref,
    dots_in,
    w_ref,
    v_ref,
    out_ref,
    image,
    spread,
):
    height = down * COARSE
    has_n, has_s, has_e, has_w = has_sides()
    at_col, at_row, n_cols, n_rows = place()
    me = at_col * n_rows + at_row

    def got(down_by, right_by):
        to_row, to_col = at_row + down_by, at_col + right_by
        there = (to_row >= 0) & (to_row < n_rows) & (to_col >= 0) & (to_col < n_cols)
        return got_ref[jnp.where(there, to_col * n_rows + to_row, me)]

    low = iota((EDGE, LANES), 1) < HALF
    gap = jnp.zeros((LANES - 2 * EDGE, LANES), jnp.float32)
    beside = jnp.transpose(jnp.concatenate([got(0, 1), gap, got(0, -1)], axis=0))[:down]
    source = jnp.concatenate(
        [
            jnp.concatenate([got(-1, 0), jnp.where(low, got(-1, 1), got(-1, -1))], axis=1),
            jnp.concatenate([own_ref[...], beside], axis=1),
            jnp.concatenate([got(1, 0), jnp.where(low, got(1, 1), got(1, -1))], axis=1),
        ],
        axis=0,
    )
    spread_cells(jacobi(source, table_ref), spread)
    clear_pads(w_ref, image)
    sides = side_lanes(has_e, has_w)
    taps = read_taps(taps)

    def begin_w(at, _, carry):
        field, inverse, cells = load(q_ref, at), load(inv_ref, at), cells_at(spread, at)
        return [(w_ref, [field[t] * inverse[t] + cells[t] for t in range(tiles + 1)])], carry

    def blur(at, _, carry):
        strip = conv(w_ref, at, taps, False)
        strip[tiles] = strip[tiles] * sides
        return [(image, strip)], carry

    def finish(at, _, totals):
        here, product = operate(w_ref, image, east_ref, south_ref, at, taps)
        field = load(q_ref, at)
        return [(v_ref, product[:tiles])], (
            totals[0] + product_sum(field, here, tiles),
            totals[1] + product_sum(here, product, tiles),
        )

    nothing = jnp.zeros((EDGE, LANES), jnp.float32)
    span = (EDGE, 3 * EDGE + height)
    sweep(*span, begin_w, 0)
    sweep(*span, blur, 0)
    mask_rows(image, has_n, has_s)
    dot_qw, dot_wv = sweep(2 * EDGE, 2 * EDGE + height, finish, (nothing, nothing))
    line = jnp.zeros((1, LANES), jnp.float32)
    block = iota((1, LANES), 1) // (LANES // 4)
    for index, part in enumerate((dots_in[0], dots_in[1], dot_qw, dot_wv)):
        part = jnp.sum(part, axis=0, keepdims=True)
        part = part + roll(part, LANES // 2, 1)
        part = part + roll(part, LANES // 4, 1)
        line = jnp.where(block == index, part, line)
    for index in range(out_ref.shape[0]):
        out_ref[index] = line


def second(taps, got, own, table, q, east, south, inv, dots):
    tiles, height = q.shape[0] - 1, q.shape[1] - 4 * EDGE
    down = height // COARSE
    window = down + 2 * EDGE
    count = lax.axis_size("cols") * lax.axis_size("rows")
    return pl.pallas_call(
        functools.partial(second_kernel, tiles, down),
        in_specs=[SMEM] + [VMEM] * 8,
        out_specs=[VMEM] * 3,
        out_shape=floats(q.shape, q.shape, (count, 1, LANES)),
        scratch_shapes=[
            pltpu.VMEM(q.shape, jnp.float32),
            pltpu.VMEM((tiles + 1, window, LANES), jnp.float32),
        ],
        compiler_params=params(),
        name="second_direction",
    )(taps, got, own, table, q, east, south, inv, dots)


def combine_kernel(
    tiles, height, sums_ref, p_ref, w_ref, r_ref, q_ref, v_ref, sol_out, res_out, sol, res, sem
):
    line = sums_ref[0]
    for index in range(1, sums_ref.shape[0]):
        line = line + sums_ref[index]
    block = iota((1, LANES), 1) // (LANES // 4)
    pick = lambda index: jnp.sum(jnp.where(block == index, line, 0.0), axis=1, keepdims=True)
    rp, pq, qw, wv = [pick(index) for index in range(4)]
    step = rp / pq
    rp_next = step * step * qw - rp
    ratio = rp_next / rp
    lead = 1.0 + ratio
    curvature = lead * lead * pq - 2.0 * lead * step * qw + step * step * wv
    step_next = rp_next / curvature
    on_p = jnp.broadcast_to(step + step_next * lead, (CHUNK, LANES))
    on_w = jnp.broadcast_to(step_next * step, (CHUNK, LANES))

    def copies(index):
        rows = pl.ds(pl.multiple_of(index * CHUNK, CHUNK), CHUNK)
        return (
            pltpu.make_async_copy(sol.at[rows, :], sol_out.at[rows, :], sem.at[0, index]),
            pltpu.make_async_copy(res.at[rows, :], res_out.at[rows, :], sem.at[1, index]),
        )

    def work(index, _):
        at = pl.multiple_of(index * CHUNK, CHUNK)
        p, w, r, q, v = [
            load(ref, at + 2 * EDGE, CHUNK) for ref in (p_ref, w_ref, r_ref, q_ref, v_ref)
        ]
        one = [on_p * p[t] - on_w * w[t] for t in range(tiles)]
        two = [r[t] - on_p * q[t] + on_w * v[t] for t in range(tiles)]
        for t in range(tiles):
            sol[pl.ds(at, CHUNK), t * LANES : (t + 1) * LANES] = one[t]
            res[pl.ds(at, CHUNK), t * LANES : (t + 1) * LANES] = two[t]
        for copy in copies(index):
            copy.start()
        return 0

    def settle(index, _):
        for copy in copies(index):
            copy.wait()
        return 0

    lax.fori_loop(0, height // CHUNK, work, 0)
    lax.fori_loop(0, height // CHUNK, settle, 0)


def combine(sums, p, w, r, q, v):
    tiles, height = q.shape[0] - 1, q.shape[1] - 4 * EDGE
    shape = (height, tiles * LANES)
    return pl.pallas_call(
        functools.partial(combine_kernel, tiles, height),
        in_specs=[VMEM] * 6,
        out_specs=[HBM] * 2,
        out_shape=floats(shape, shape),
        scratch_shapes=[
            pltpu.VMEM(shape, jnp.float32),
            pltpu.VMEM(shape, jnp.float32),
            pltpu.SemaphoreType.DMA((2, height // CHUNK)),
        ],
        compiler_params=params(),
        name="combine",
    )(sums, p, w, r, q, v)


def exchange(send_a, send_b, axis):
    count = lax.axis_size(axis)

    def pairs(begin):
        return [
            pair for i in range(begin, count - 1, 2) for pair in ((i, i + 1), (i + 1, i))
        ]

    got_b = lax.ppermute(send_b, axis, pairs(1))
    got_a = lax.ppermute(send_a, axis, pairs(0))
    return got_a, got_b


def body(observed, class_map, class_weights, blur_kernel):
    arguments = (observed, class_map, class_weights, blur_kernel)
    send_a, send_b = edge(*arguments)
    got_a, got_b = exchange(send_a, send_b, "cols")
    obs, cond, coarse = pack(*arguments, send_a)
    obs, cond, coarse, send_a, send_b = middle(got_a, got_b, coarse, obs, cond)
    got_a, got_b = exchange(send_a, send_b, "rows")
    r, east, south, inv = inner(blur_kernel, obs, cond)
    fields = (obs, cond, r, east, south, inv)
    r, east, south, inv, p, q, table, own, chunk, dots = first(
        blur_kernel, fields, got_a, got_b, coarse
    )
    got = lax.all_to_all(chunk, AXES, 0, 0, tiled=True)
    w, v, line = second(blur_kernel, got, own, table, q, east, south, inv, dots)
    sums = lax.all_to_all(line, AXES, 0, 0, tiled=True)
    return tuple(combine(sums, p, w, r, q, v))


def solution(mesh):
    return jax.shard_map(
        body,
        mesh=mesh,
        in_specs=(P("rows", "cols"), P("rows", "cols"), P(), P()),
        out_specs=(P("rows", "cols"), P("rows", "cols")),
        check_vma=False,
    )
```

```python
import functools

import jax
import jax.numpy as jnp
from jax import lax
from jax.experimental import pallas as pl
from jax.experimental.pallas import tpu as pltpu
from jax.sharding import PartitionSpec as P

COARSE = 8
SWEEPS = 8
CLASSES = 4
OMEGA = 0.8

LANES = 128
HALF = LANES // 2
COLUMNS = LANES // COARSE
EDGE = 8
STRIP = 2 * EDGE
GROUP = 2
CHUNK = 32
AXES = ("cols", "rows")
LIMIT = 40 * 1024 * 1024


VMEM = pl.BlockSpec(memory_space=pltpu.VMEM)
SMEM = pl.BlockSpec(memory_space=pltpu.SMEM)
HBM = pl.BlockSpec(memory_space=pltpu.HBM)


def params():
    return pltpu.CompilerParams(vmem_limit_bytes=LIMIT)


def in_hbm(array):
    return pltpu.with_memory_space_constraint(array, pltpu.HBM)


def floats(*shapes):
    return [jax.ShapeDtypeStruct(shape, jnp.float32) for shape in shapes]


def place():
    at_col, at_row = lax.axis_index("cols"), lax.axis_index("rows")
    n_cols, n_rows = lax.axis_size("cols"), lax.axis_size("rows")
    return at_col, at_row, n_cols, n_rows


def has_sides():
    at_col, at_row, n_cols, n_rows = place()
    flag = lambda test: jnp.where(test, 1.0, 0.0).astype(jnp.float32)
    return (
        flag(at_row > 0),
        flag(at_row < n_rows - 1),
        flag(at_col < n_cols - 1),
        flag(at_col > 0),
    )


def iota(shape, dim):
    return lax.broadcasted_iota(jnp.int32, shape, dim)


def cell_of(pixel, tiles):
    turn = (tiles + 1) * LANES
    return jnp.where(pixel < turn - HALF, pixel >> 3, ((pixel - turn) >> 3) & (2 * LANES - 1))


def gather_matrix(tiles):
    shape = ((tiles + 1) * LANES, 2 * LANES)
    hit = cell_of(iota(shape, 0), tiles) == iota(shape, 1)
    return jnp.where(hit, 1.0, 0.0).astype(jnp.bfloat16)


def split_dot(field, matrix):
    rows = field.shape[0]
    high = field.astype(jnp.bfloat16)
    low = (field - high.astype(jnp.float32)).astype(jnp.bfloat16)
    both = jnp.dot(
        jnp.concatenate([high, low], axis=0), matrix, preferred_element_type=jnp.float32
    )
    return both[:rows] + both[rows:]


def roll(field, by, axis):
    return pltpu.roll(field, by % field.shape[axis], axis)


def load(ref, at, rows=STRIP):
    return [ref[t, pl.ds(at, rows), :] for t in range(ref.shape[0])]


def store(ref, at, strip):
    for t, part in enumerate(strip):
        ref[t, pl.ds(at, part.shape[0]), :] = part


def wide(ref, at, rows):
    return jnp.concatenate(load(ref, at, rows), axis=1)


def read_taps(taps):
    return [[taps[a, b] for b in range(3)] for a in range(3)]


def tap_total(taps, power):
    return sum(tap * tap if power == 2 else tap for line in taps for tap in line)


def from_west(strip):
    lane = iota(strip[0].shape, 1)
    last, halo = roll(strip[-2], 1, 1), roll(strip[-1], 1, 1)
    return [
        jnp.where(lane == 0, halo, last),
        *strip[:-2],
        jnp.where(lane == 0, last, halo),
    ]


def from_east(strip):
    lane = iota(strip[0].shape, 1)
    first, halo = roll(strip[0], -1, 1), roll(strip[-1], -1, 1)
    return [
        *strip[1:-1],
        jnp.where(lane == LANES - 1, halo, first),
        jnp.where(lane == LANES - 1, first, halo),
    ]


def swap_blocks(strip):
    strip = list(strip)
    block = iota(strip[0].shape, 1) // COLUMNS
    for apart in (1, 2, 4):
        low = (block & apart) == 0
        for one in range(COARSE):
            if one & apart:
                continue
            two = one + apart
            a, b = strip[one], strip[two]
            strip[one] = jnp.where(low, a, roll(b, COLUMNS * apart, 1))
            strip[two] = jnp.where(low, roll(a, -COLUMNS * apart, 1), b)
    return strip


def to_cells(strip):
    lane = iota(strip[0].shape, 1)
    turn = (lane % COLUMNS) * COARSE + lane // COLUMNS
    return swap_blocks([pick_lanes(part, turn) for part in strip])


def from_cells(strip):
    lane = iota(strip[0].shape, 1)
    turn = (lane % COARSE) * COLUMNS + lane // COARSE
    return [pick_lanes(part, turn) for part in swap_blocks(strip)]


def tap_sums(ref, at, taps, flip):
    if flip:
        taps = [line[::-1] for line in taps[::-1]]
    above, here, below = load(ref, at - 1), load(ref, at), load(ref, at + 1)
    sums = [[], [], []]
    for t in range(len(here)):
        for b in range(3):
            sums[b].append(
                taps[0][b] * above[t] + taps[1][b] * here[t] + taps[2][b] * below[t]
            )
    return sums


def conv(ref, at, taps, flip):
    sums = tap_sums(ref, at, taps, flip)
    west, east = from_west(sums[0]), from_east(sums[2])
    return [sums[1][t] + west[t] + east[t] for t in range(len(west))]


def operate(ref, image, east_ref, south_ref, at, taps):
    above, here, below = load(ref, at - 1), load(ref, at), load(ref, at + 1)
    east, south, north = load(east_ref, at), load(south_ref, at), load(south_ref, at - 1)
    sums = tap_sums(image, at, taps, True)
    span = range(len(here))
    beside = from_east(here)
    flux = [east[t] * (here[t] - beside[t]) for t in span]
    from_left = from_west([sums[0][t] - flux[t] for t in span])
    from_right = from_east(sums[2])
    return here, [
        sums[1][t]
        + flux[t]
        + from_left[t]
        + from_right[t]
        + south[t] * (here[t] - below[t])
        - north[t] * (above[t] - here[t])
        for t in span
    ]


def begin(obs, cond, at, taps, sides):
    above, here, below = load(cond, at - 1), load(cond, at), load(cond, at + 1)
    span = range(len(here))
    right = from_east(here)
    east = [here[t] + right[t] for t in span]
    west = from_west(east)
    south = [here[t] + below[t] for t in span]
    squares = tap_total(taps, 2)
    diag = [squares + east[t] + west[t] + south[t] + (here[t] + above[t]) for t in span]
    inverse = [pl.reciprocal(part, approx=True) for part in diag]
    inverse = [inverse[t] * (2.0 - diag[t] * inverse[t]) for t in span]
    inverse[-1] = inverse[-1] * sides
    return east, south, inverse, conv(obs, at, taps, True)


def pick_lanes(field, lanes):
    return jnp.take_along_axis(field, lanes, axis=1, mode="promise_in_bounds")


def spread_cells(cells, spread):
    spread[0] = cells[:, :LANES]
    lane = iota((cells.shape[0], LANES), 1)
    turn = jnp.where(lane < HALF, 0, LANES - COLUMNS)
    spread[1] = pick_lanes(cells[:, LANES:], lane // COARSE + turn)


def cells_at(spread, at):
    first = at // EDGE + EDGE - 2
    rows = [load(spread, first + index, 1) for index in range(STRIP // EDGE)]
    own, halo = [
        jnp.concatenate([jnp.broadcast_to(row, (EDGE, LANES)) for row in parts], axis=0)
        for parts in zip(*rows)
    ]
    return [own] * COARSE + [halo]


def cell_sums(ref, tiles, down):
    total = [
        sum(
            ref[t, pl.ds(2 * EDGE + k, down, stride=COARSE), :] for k in range(COARSE)
        )
        for t in range(tiles)
    ]
    return sum(total[1:], total[0])


def side_lanes(has_e, has_w):
    return jnp.where(iota((STRIP, LANES), 1) < HALF, has_e, has_w)


def mask_rows(ref, has_n, has_s):
    last = ref.shape[1] - 2 * EDGE
    for at, flag in ((EDGE, has_n), (last, has_s)):
        ref[:, at : at + EDGE, :] = ref[:, at : at + EDGE, :] * flag


def clear_pads(*refs):
    empty = jnp.zeros((refs[0].shape[0], EDGE, LANES), jnp.float32)
    for ref in refs:
        ref[:, :EDGE, :] = empty
        ref[:, ref.shape[1] - EDGE :, :] = empty


def product_sum(one, two, count, flags=None):
    total = one[0] * two[0]
    for t in range(1, count):
        total = total + one[t] * two[t]
    return fold(total, flags)


def fold(total, flags=None):
    parts = [total[at : at + EDGE] for at in range(0, total.shape[0], EDGE)]
    if flags is not None:
        parts = [part * flag for part, flag in zip(parts, flags)]
    return sum(parts[1:], parts[0])


def sweep(first, last, body, carry):
    width = GROUP * STRIP
    steps = -(-(last - first) // width)

    def work(index, carry):
        start = first + index * width
        at = pl.multiple_of(jnp.minimum(start, last - width), EDGE)
        pending = []
        for by in range(0, width, STRIP):
            stores, carry = body(at + by, start, carry)
            pending += [(ref, at + by, strip) for ref, strip in stores]
        for ref, row, strip in pending:
            store(ref, row, strip)
        return carry

    return lax.fori_loop(0, steps, work, carry)


def jacobi(source, table):
    factor, east, west, south, north = [table[index] for index in range(5)]
    source = factor * source
    iterate = source
    for _ in range(SWEEPS - 1):
        across = east * roll(iterate, -1, 1) + west * roll(iterate, 1, 1)
        along = south * roll(iterate, -1, 0) + north * roll(iterate, 1, 0)
        iterate = ((1.0 - OMEGA) * iterate + source) + (across + along)
    return iterate


def in_pair_order(at, for_before, for_after):
    even = at % 2 == 0
    if callable(for_before):
        return (
            lambda index: jnp.where(even, for_after(index), for_before(index)),
            lambda index: jnp.where(even, for_before(index), for_after(index)),
        )
    return jnp.where(even, for_after, for_before), jnp.where(even, for_before, for_after)


def reader(tiles_here, refs, scratch, obs, cond, down):
    obs_in, class_in, weight_in, taps_in = refs
    classes, weights, taps, sums, obs_sem, class_sem, small_sem = scratch
    own = pl.ds(2 * EDGE, down * COARSE)
    small = [
        pltpu.make_async_copy(weight_in, weights, small_sem.at[0]),
        pltpu.make_async_copy(taps_in, taps, small_sem.at[1]),
    ]
    moves = []
    for slot, t in enumerate(tiles_here):
        lanes = pl.ds(t * LANES, LANES)
        moves.append(
            (
                pltpu.make_async_copy(class_in.at[:, lanes], classes.at[slot], class_sem.at[slot]),
                pltpu.make_async_copy(
                    obs_in.at[:, lanes], obs.at[slot, own, :], obs_sem.at[slot]
                ),
            )
        )
    for copy in small:
        copy.start()
    for pair in moves:
        for copy in pair:
            copy.start()
    sums[...] = jnp.zeros_like(sums)

    def settle(slot):
        if slot == 0:
            for copy in small:
                copy.wait()
        for copy in moves[slot]:
            copy.wait()
        values = [0.5 * weights[class_id] for class_id in range(CLASSES)]
        kind = classes[slot]
        cond[slot, own, :] = jnp.where(
            kind < 2,
            jnp.where(kind == 0, values[0], values[1]),
            jnp.where(kind == 2, values[2], values[3]),
        )
        for which, ref in enumerate((obs, cond)):
            picked = [
                ref[slot, pl.ds(2 * EDGE + k, down, stride=COARSE), :] for k in range(COARSE)
            ]
            sums[3 * which, slot, EDGE : EDGE + down, :] = sum(picked[1:], picked[0])
            sums[3 * which + 1, slot, EDGE : EDGE + down, :] = picked[0]
            sums[3 * which + 2, slot, EDGE : EDGE + down, :] = picked[-1]

    return settle


def reader_scratch(tiles, height, window, class_weights, taps):
    return [
        pltpu.VMEM((tiles, height, LANES), jnp.int32),
        pltpu.SMEM(class_weights.shape, jnp.float32),
        pltpu.SMEM(taps.shape, jnp.float32),
        pltpu.VMEM((6, tiles + 1, window, LANES), jnp.float32),
        pltpu.SemaphoreType.DMA((tiles,)),
        pltpu.SemaphoreType.DMA((tiles,)),
        pltpu.SemaphoreType.DMA((2,)),
    ]


def coarse_parts(sums, taps, matrix):
    window = sums.shape[2]
    whole = lambda index: wide(sums.at[index], 0, window)
    full, head, tail = whole(0), whole(1), whole(2)
    by_tap = [full - head + roll(head, -1, 0), full, full - tail + roll(tail, 1, 0)]
    across = [sum(taps[a][b] * by_tap[a] for a in range(3)) for b in range(3)]
    source = across[1] + roll(across[0], -1, 1) + roll(across[2], 1, 1)
    full, head, tail = whole(3), whole(4), whole(5)
    last = (iota(full.shape, 1) & (COARSE - 1)) == COARSE - 1
    east = jnp.where(last, full + roll(full, -1, 1), 0.0)
    south = tail + roll(head, -1, 0)
    cells = split_dot(jnp.concatenate([source, east, south], axis=0), matrix)
    source, east, south = cells[:window], cells[window : 2 * window], cells[2 * window :]
    around = east + roll(east, 1, 1) + south + roll(south, 1, 0)
    return [source, east, south, around]


def edge_kernel(tiles, down, *refs):
    arguments, (send_a, send_b), (obs, cond, message, *scratch) = refs[:4], refs[4:6], refs[6:]
    height = down * COARSE
    halves = height // LANES
    window = down + 2 * EDGE
    settle = reader((0, tiles - 1), arguments, scratch, obs, cond, down)
    matrix = gather_matrix(2)
    for slot, begin_row in ((0, 0), (1, LANES - EDGE)):
        settle(slot)
        for which, ref in enumerate((obs, cond)):
            turned = jnp.transpose(ref[slot, 2 * EDGE : 2 * EDGE + height, :])
            turned = turned[begin_row : begin_row + EDGE]
            for half in range(halves):
                at = (which * halves + half) * EDGE
                message[slot, at : at + EDGE, :] = turned[:, half * LANES : (half + 1) * LANES]
    parts = coarse_parts(scratch[3], read_taps(scratch[2]), matrix)
    spare = jnp.zeros((2 * LANES - 4 * window, 2 * LANES), jnp.float32)
    stack = jnp.concatenate(parts + [spare], axis=0)
    left = jnp.transpose(stack[:, :LANES])
    right = jnp.transpose(stack[:, LANES:])
    base = 2 * halves * EDGE
    past = 2 * LANES // COARSE
    for slot, pieces in (
        (0, (left[:EDGE], right[LANES - EDGE :])),
        (1, (left[past - EDGE : past], left[past : past + EDGE])),
    ):
        for index, piece in enumerate(pieces):
            for half in range(2):
                at = base + (2 * index + half) * EDGE
                message[slot, at : at + EDGE, :] = piece[:, half * LANES : (half + 1) * LANES]
    send_a[...], send_b[...] = in_pair_order(place()[0], message[0], message[1])


def edge(observed, class_map, class_weights, taps):
    height, breadth = observed.shape
    tiles, down = breadth // LANES, height // COARSE
    window = down + 2 * EDGE
    field = (3, height + 4 * EDGE, LANES)
    strip = ((2 * (height // LANES) + 4) * EDGE, LANES)
    return pl.pallas_call(
        functools.partial(edge_kernel, tiles, down),
        in_specs=[HBM] * 4,
        out_specs=[VMEM] * 2,
        out_shape=floats(strip, strip),
        scratch_shapes=[
            pltpu.VMEM(field, jnp.float32),
            pltpu.VMEM(field, jnp.float32),
            pltpu.VMEM((2,) + strip, jnp.float32),
        ]
        + reader_scratch(2, height, window, class_weights, taps),
        compiler_params=params(),
        name="pack_east_west",
    )(*[in_hbm(array) for array in (observed, class_map, class_weights, taps)])


def pack_kernel(
    down,
    obs_in,
    class_in,
    weight_in,
    taps_in,
    _,
    obs,
    cond,
    coarse_ref,
    raw,
    classes,
    weights,
    taps,
    sums,
    row_sem,
    small_sem,
):
    tiles = COARSE
    window = down + 2 * EDGE
    small = [
        pltpu.make_async_copy(weight_in, weights, small_sem.at[0]),
        pltpu.make_async_copy(taps_in, taps, small_sem.at[1]),
    ]

    def copies(index):
        rows = pl.ds(pl.multiple_of(index * CHUNK, CHUNK), CHUNK)
        return (
            pltpu.make_async_copy(obs_in.at[rows, :], raw.at[rows, :], row_sem.at[0, index]),
            pltpu.make_async_copy(class_in.at[rows, :], classes.at[rows, :], row_sem.at[1, index]),
        )

    def request(index, _):
        for copy in copies(index):
            copy.start()
        return 0

    steps = raw.shape[0] // CHUNK
    for copy in small:
        copy.start()
    lax.fori_loop(0, steps, request, 0)
    sums[...] = jnp.zeros_like(sums)
    for copy in small:
        copy.wait()
    values = [0.5 * weights[class_id] for class_id in range(CLASSES)]

    def work(index, _):
        for copy in copies(index):
            copy.wait()
        at = pl.multiple_of(index * CHUNK, CHUNK)
        rows = pl.ds(at, CHUNK)
        level = []
        for t in range(tiles):
            kind = classes[rows, t * LANES : (t + 1) * LANES]
            level.append(
                jnp.where(
                    kind < 2,
                    jnp.where(kind == 0, values[0], values[1]),
                    jnp.where(kind == 2, values[2], values[3]),
                )
            )
        level = to_cells(level)
        field = to_cells([raw[rows, t * LANES : (t + 1) * LANES] for t in range(tiles)])
        store(cond, at + 2 * EDGE, level)
        store(obs, at + 2 * EDGE, field)
        return 0

    lax.fori_loop(0, steps, work, 0)
    for which, ref in enumerate((obs, cond)):
        for t in range(tiles):
            picked = [
                ref[t, pl.ds(2 * EDGE + k, down, stride=COARSE), :] for k in range(COARSE)
            ]
            sums[3 * which, t, EDGE : EDGE + down, :] = sum(picked[1:], picked[0])
            sums[3 * which + 1, t, EDGE : EDGE + down, :] = picked[0]
            sums[3 * which + 2, t, EDGE : EDGE + down, :] = picked[-1]

    taps = read_taps(taps)
    span = range(tiles + 1)
    together = lambda strip: sum(strip[1:tiles], strip[0])
    join = lambda own, beyond: jnp.concatenate([own, beyond], axis=1)
    full, head, tail = [load(sums.at[index], 0, window) for index in range(3)]
    by_tap = [
        [full[t] - head[t] + roll(head[t], -1, 0) for t in span],
        full,
        [full[t] - tail[t] + roll(tail[t], 1, 0) for t in span],
    ]
    across = [
        [sum(taps[a][b] * by_tap[a][t] for a in range(3)) for t in span] for b in range(3)
    ]
    right, left = from_east(across[0]), from_west(across[2])
    strip = [across[1][t] + right[t] + left[t] for t in span]
    source = join(together(strip), strip[tiles])
    full, head, tail = [load(sums.at[index], 0, window) for index in range(3, 6)]
    right = from_east(full)
    east = join(full[tiles - 1] + right[tiles - 1], right[tiles])
    south = together([tail[t] + roll(head[t], -1, 0) for t in span])
    south = join(south, jnp.zeros_like(south))
    around = east + roll(east, 1, 1) + south + roll(south, 1, 0)
    for index, part in enumerate((source, east, south, around)):
        coarse_ref[index] = part


def pack(observed, class_map, class_weights, taps, after):
    height, breadth = observed.shape
    tiles, down = breadth // LANES, height // COARSE
    window = down + 2 * EDGE
    field = (tiles + 1, height + 4 * EDGE, LANES)
    pixels = height * breadth
    return pl.pallas_call(
        functools.partial(pack_kernel, down),
        in_specs=[HBM] * 4 + [VMEM],
        out_specs=[VMEM] * 3,
        out_shape=floats(field, field, (4, window, 2 * LANES)),
        scratch_shapes=[
            pltpu.VMEM(observed.shape, jnp.float32),
            pltpu.VMEM(observed.shape, jnp.int32),
            pltpu.SMEM(class_weights.shape, jnp.float32),
            pltpu.SMEM(taps.shape, jnp.float32),
            pltpu.VMEM((6, tiles + 1, window, LANES), jnp.float32),
            pltpu.SemaphoreType.DMA((2, height // CHUNK)),
            pltpu.SemaphoreType.DMA((2,)),
        ],
        compiler_params=params(),
        cost_estimate=pl.CostEstimate(
            flops=20 * pixels, bytes_accessed=16 * pixels, transcendentals=0
        ),
        name="pack_all",
    )(*[in_hbm(array) for array in (observed, class_map, class_weights, taps)], after)


def merge_sides(parts):
    block = iota((EDGE, LANES), 1) // (2 * EDGE)
    merged = jnp.zeros((EDGE, LANES), jnp.float32)
    for index, part in enumerate(parts):
        merged = jnp.where(block == index, roll(part, (2 * index + 1) * EDGE, 1), merged)
    return merged


def split_sides(merged, count):
    lane = iota((EDGE, LANES), 1)
    outer = (lane < EDGE) | (lane >= LANES - EDGE)
    return [
        jnp.where(outer, roll(merged, -(2 * index + 1) * EDGE, 1), 0.0) for index in range(count)
    ]


def middle_kernel(
    tiles,
    down,
    got_b,
    got_a,
    coarse_in,
    obs_in,
    cond_in,
    obs,
    cond,
    coarse_ref,
    send_a,
    send_b,
    message,
):
    height = down * COARSE
    halves = height // LANES
    at_col, at_row, _, _ = place()
    from_e, from_w = in_pair_order(at_col, got_b[...], got_a[...])
    gap = jnp.zeros((LANES - 2 * EDGE, LANES), jnp.float32)

    def turned(low, high):
        return jnp.transpose(jnp.concatenate([low, gap, high], axis=0))

    for which, field in enumerate((obs, cond)):
        for half in range(halves):
            at = (which * halves + half) * EDGE
            begin_row = 2 * EDGE + half * LANES
            field[tiles, begin_row : begin_row + LANES, :] = turned(
                from_e[at : at + EDGE], from_w[at : at + EDGE]
            )
    base = 2 * halves * EDGE

    def piece(strip, index, half):
        at = base + (2 * index + half) * EDGE
        return strip[at : at + EDGE]

    left = [turned(piece(from_w, 1, half), piece(from_e, 1, half)) for half in range(2)]
    right = [turned(piece(from_e, 0, half), piece(from_w, 0, half)) for half in range(2)]
    left = jnp.concatenate(left, axis=0)
    right = jnp.concatenate(right, axis=0)
    window = down + 2 * EDGE
    for index in range(4):
        rows = slice(index * window, (index + 1) * window)
        coarse_ref[index, :, :LANES] = coarse_in[index, :, :LANES] + left[rows]
        coarse_ref[index, :, LANES:] = coarse_in[index, :, LANES:] + right[rows]
    fields = (obs, cond)
    for slot, begin_row, first_row, over_row in (
        (0, 2 * EDGE, EDGE, EDGE - 1),
        (1, EDGE + height, window - 2 * EDGE, window - EDGE),
    ):
        pieces = [field[t, begin_row : begin_row + EDGE, :] for field in fields for t in range(tiles)]
        rows = slice(first_row, first_row + EDGE)
        pieces += [coarse_ref[index, rows, :LANES] for index in range(4)]
        beyond = [coarse_ref[index, rows, LANES:] for index in range(4)]
        beyond += [field[tiles, begin_row : begin_row + EDGE, :] for field in fields]
        pieces.append(merge_sides(beyond))
        pieces.append(
            jnp.concatenate(
                [
                    coarse_ref[index, over_row : over_row + 1, half * LANES : (half + 1) * LANES]
                    for index in range(4)
                    for half in range(2)
                ],
                axis=0,
            )
        )
        for index, piece in enumerate(pieces):
            message[slot, index] = piece
    send_a[...], send_b[...] = in_pair_order(at_row, message[0], message[1])


def middle(got_a, got_b, coarse, obs, cond):
    tiles, height = obs.shape[0] - 1, obs.shape[1] - 4 * EDGE
    down = height // COARSE
    long = (2 * tiles + 6, EDGE, LANES)
    return pl.pallas_call(
        functools.partial(middle_kernel, tiles, down),
        in_specs=[VMEM] * 5,
        out_specs=[VMEM] * 5,
        out_shape=floats(obs.shape, cond.shape, coarse.shape, long, long),
        input_output_aliases={3: 0, 4: 1},
        scratch_shapes=[pltpu.VMEM((2,) + long, jnp.float32)],
        compiler_params=params(),
        name="pack_north_south",
    )(got_b, got_a, coarse, obs, cond)


def inner_kernel(taps, obs, cond, res_ref, east_ref, south_ref, inv_ref):
    _, _, has_e, has_w = has_sides()
    clear_pads(east_ref, south_ref)
    taps = read_taps(taps)
    sides = side_lanes(has_e, has_w)

    def work(at, _, carry):
        fields = begin(obs, cond, at, taps, sides)
        return list(zip((east_ref, south_ref, inv_ref, res_ref), fields)), carry

    sweep(3 * EDGE, obs.shape[1] - 3 * EDGE, work, 0)


def inner(taps, obs, cond):
    field = obs.shape
    pixels = field[0] * field[1] * field[2]
    return pl.pallas_call(
        inner_kernel,
        in_specs=[SMEM] + [VMEM] * 2,
        out_specs=[VMEM] * 4,
        out_shape=floats(field, field, field, field),
        compiler_params=params(),
        cost_estimate=pl.CostEstimate(
            flops=45 * pixels, bytes_accessed=24 * pixels, transcendentals=0
        ),
        name="inner_strips",
    )(taps, obs, cond)


def first_kernel(
    tiles,
    down,
    taps,
    obs_in,
    cond_in,
    res_in,
    east_in,
    south_in,
    inv_in,
    got_b,
    got_a,
    coarse_in,
    obs,
    cond,
    res_ref,
    east_ref,
    south_ref,
    inv_ref,
    p_ref,
    q_ref,
    table_ref,
    own_ref,
    chunk_ref,
    dots_ref,
    image,
    spread,
):
    height = down * COARSE
    window = down + 2 * EDGE
    at_col, at_row, n_cols, n_rows = place()
    has_n, has_s, has_e, has_w = has_sides()
    clear_pads(obs, cond, p_ref, image)
    from_s, from_n = in_pair_order(
        at_row, lambda index: got_b[index], lambda index: got_a[index]
    )

    for which, field in enumerate((obs, cond)):
        for t in range(tiles):
            field[t, EDGE : 2 * EDGE, :] = from_n(which * tiles + t)
            field[t, 2 * EDGE + height : 3 * EDGE + height, :] = from_s(which * tiles + t)
    sides_n, sides_s = [split_sides(strip(2 * tiles + 4), 6) for strip in (from_n, from_s)]
    for which, field in enumerate((obs, cond)):
        field[tiles, EDGE : 2 * EDGE, :] = sides_n[4 + which]
        field[tiles, 2 * EDGE + height : 3 * EDGE + height, :] = sides_s[4 + which]

    edge_row = iota((EDGE, 2 * LANES), 0)

    def joined(index):
        def over(strip, row):
            line = [
                jnp.broadcast_to(
                    strip((2 * tiles + 5, pl.ds(2 * index + half, 1))), (EDGE, LANES)
                )
                for half in range(2)
            ]
            return jnp.where(edge_row == row, jnp.concatenate(line, axis=1), 0.0)

        def rows(strip, beyond):
            return jnp.concatenate([strip(2 * tiles + index), beyond[index]], axis=1)

        parts = [coarse_in[index, at : at + EDGE, :] for at in range(0, window, EDGE)]
        parts[0] = parts[0] + rows(from_n, sides_n)
        parts[1] = parts[1] + over(from_n, 0)
        parts[-2] = parts[-2] + over(from_s, EDGE - 1)
        parts[-1] = parts[-1] + rows(from_s, sides_s)
        return jnp.concatenate(parts, axis=0)

    source, east, south, around = [joined(index) for index in range(4)]
    row = iota(source.shape, 0)
    lane = iota(source.shape, 1)
    inside = jnp.where(row < EDGE, has_n, jnp.where(row < window - EDGE, 1.0, has_s))
    inside = inside * jnp.where(
        lane < LANES, 1.0, jnp.where(lane < LANES + HALF, has_e, has_w)
    )
    taps = read_taps(taps)
    total = tap_total(taps, 1)
    factor = inside * OMEGA / (COARSE * COARSE * total * total + around)
    weights = (east, roll(east, 1, 1), south, roll(south, 1, 0))
    table = [factor] + [factor * weight for weight in weights]
    for index, part in enumerate(table):
        table_ref[index] = part
    sides = side_lanes(has_e, has_w)
    half = iota((STRIP, LANES), 0) // EDGE
    pending = []
    for index, known in ((0, has_n), (1, has_s)):
        at = EDGE + index * height
        fields = begin(obs, cond, at, taps, sides)
        flag = jnp.where(half == index, known, 1.0)
        fields = (*fields[:2], [part * flag for part in fields[2]], fields[3])
        pending += [
            (ref, at, strip)
            for ref, strip in zip((east_ref, south_ref, inv_ref, res_ref), fields)
        ]
    spread_cells(jacobi(source, table), spread)
    for ref, at, strip in pending:
        store(ref, at, strip)

    def flags(at, start):
        rows = [at + by for by in range(0, STRIP, EDGE)]
        first_row = jnp.maximum(start, 2 * EDGE)
        return [
            jnp.where((row >= first_row) & (row < 2 * EDGE + height), 1.0, 0.0) for row in rows
        ]

    def begin_p(at, start, total):
        residual, inverse, cells = load(res_ref, at), load(inv_ref, at), cells_at(spread, at)
        strip = [residual[t] * inverse[t] + cells[t] for t in range(tiles + 1)]
        return [(p_ref, strip)], total + product_sum(residual, strip, tiles, flags(at, start))

    def blur(at, _, carry):
        strip = conv(p_ref, at, taps, False)
        strip[tiles] = strip[tiles] * sides
        return [(image, strip)], carry

    def finish(at, start, total):
        here, product = operate(p_ref, image, east_ref, south_ref, at, taps)
        return [(q_ref, product)], total + product_sum(here, product, tiles, flags(at, start))

    nothing = jnp.zeros((EDGE, LANES), jnp.float32)
    span = (EDGE, 3 * EDGE + height)
    dots_ref[0] = sweep(*span, begin_p, nothing)
    sweep(*span, blur, 0)
    mask_rows(image, has_n, has_s)
    dots_ref[1] = sweep(*span, finish, nothing)

    own = cell_sums(q_ref, tiles, down)
    own_ref[...] = own
    spare = jnp.zeros((LANES - down, LANES), jnp.float32)
    turned = jnp.transpose(jnp.concatenate([own, spare], axis=0))
    chunk_ref[...] = jnp.zeros_like(chunk_ref)
    for down_by in (-1, 0, 1):
        for right_by in (-1, 0, 1):
            if down_by == 0 and right_by == 0:
                continue
            if down_by == 0:
                piece = turned[:EDGE] if right_by < 0 else turned[LANES - EDGE :]
            else:
                piece = own[:EDGE] if down_by < 0 else own[down - EDGE :]
            to_row, to_col = at_row + down_by, at_col + right_by

            @pl.when((to_row >= 0) & (to_row < n_rows) & (to_col >= 0) & (to_col < n_cols))
            def _(piece=piece, to_row=to_row, to_col=to_col):
                chunk_ref[to_col * n_rows + to_row] = piece


def first(taps, fields, got_a, got_b, coarse):
    field = fields[0].shape
    tiles, height = field[0] - 1, field[1] - 4 * EDGE
    down = height // COARSE
    window = down + 2 * EDGE
    count = lax.axis_size("cols") * lax.axis_size("rows")
    shapes = [field] * 8 + [
        (5, window, 2 * LANES),
        (down, LANES),
        (count, EDGE, LANES),
        (2, EDGE, LANES),
    ]
    return pl.pallas_call(
        functools.partial(first_kernel, tiles, down),
        in_specs=[SMEM] + [VMEM] * 9,
        out_specs=[VMEM] * len(shapes),
        out_shape=floats(*shapes),
        input_output_aliases={index + 1: index for index in range(6)},
        scratch_shapes=[
            pltpu.VMEM(field, jnp.float32),
            pltpu.VMEM((2, window, LANES), jnp.float32),
        ],
        compiler_params=params(),
        name="first_direction",
    )(taps, *fields, got_b, got_a, coarse)[2:]


def second_kernel(
    tiles,
    down,
    taps,
    got_ref,
    own_ref,
    table_ref,
    q_ref,
    east_ref,
    south_ref,
    inv_ref,
    dots_in,
    w_ref,
    v_ref,
    out_ref,
    image,
    spread,
):
    height = down * COARSE
    has_n, has_s, has_e, has_w = has_sides()
    at_col, at_row, n_cols, n_rows = place()
    me = at_col * n_rows + at_row

    def got(down_by, right_by):
        to_row, to_col = at_row + down_by, at_col + right_by
        there = (to_row >= 0) & (to_row < n_rows) & (to_col >= 0) & (to_col < n_cols)
        return got_ref[jnp.where(there, to_col * n_rows + to_row, me)]

    low = iota((EDGE, LANES), 1) < HALF
    gap = jnp.zeros((LANES - 2 * EDGE, LANES), jnp.float32)
    beside = jnp.transpose(jnp.concatenate([got(0, 1), gap, got(0, -1)], axis=0))[:down]
    source = jnp.concatenate(
        [
            jnp.concatenate([got(-1, 0), jnp.where(low, got(-1, 1), got(-1, -1))], axis=1),
            jnp.concatenate([own_ref[...], beside], axis=1),
            jnp.concatenate([got(1, 0), jnp.where(low, got(1, 1), got(1, -1))], axis=1),
        ],
        axis=0,
    )
    spread_cells(jacobi(source, table_ref), spread)
    clear_pads(w_ref, image)
    sides = side_lanes(has_e, has_w)
    taps = read_taps(taps)

    def begin_w(at, _, carry):
        field, inverse, cells = load(q_ref, at), load(inv_ref, at), cells_at(spread, at)
        return [(w_ref, [field[t] * inverse[t] + cells[t] for t in range(tiles + 1)])], carry

    def blur(at, _, carry):
        strip = conv(w_ref, at, taps, False)
        strip[tiles] = strip[tiles] * sides
        return [(image, strip)], carry

    def finish(at, _, totals):
        here, product = operate(w_ref, image, east_ref, south_ref, at, taps)
        field = load(q_ref, at)
        return [(v_ref, product[:tiles])], (
            totals[0] + product_sum(field, here, tiles),
            totals[1] + product_sum(here, product, tiles),
        )

    nothing = jnp.zeros((EDGE, LANES), jnp.float32)
    span = (EDGE, 3 * EDGE + height)
    sweep(*span, begin_w, 0)
    sweep(*span, blur, 0)
    mask_rows(image, has_n, has_s)
    dot_qw, dot_wv = sweep(2 * EDGE, 2 * EDGE + height, finish, (nothing, nothing))
    line = jnp.zeros((1, LANES), jnp.float32)
    block = iota((1, LANES), 1) // (LANES // 4)
    for index, part in enumerate((dots_in[0], dots_in[1], dot_qw, dot_wv)):
        part = jnp.sum(part, axis=0, keepdims=True)
        part = part + roll(part, LANES // 2, 1)
        part = part + roll(part, LANES // 4, 1)
        line = jnp.where(block == index, part, line)
    for index in range(out_ref.shape[0]):
        out_ref[index] = line


def second(taps, got, own, table, q, east, south, inv, dots):
    tiles, height = q.shape[0] - 1, q.shape[1] - 4 * EDGE
    down = height // COARSE
    window = down + 2 * EDGE
    count = lax.axis_size("cols") * lax.axis_size("rows")
    return pl.pallas_call(
        functools.partial(second_kernel, tiles, down),
        in_specs=[SMEM] + [VMEM] * 8,
        out_specs=[VMEM] * 3,
        out_shape=floats(q.shape, q.shape, (count, 1, LANES)),
        scratch_shapes=[
            pltpu.VMEM(q.shape, jnp.float32),
            pltpu.VMEM((2, window, LANES), jnp.float32),
        ],
        compiler_params=params(),
        name="second_direction",
    )(taps, got, own, table, q, east, south, inv, dots)


def combine_kernel(
    tiles, height, sums_ref, p_ref, w_ref, r_ref, q_ref, v_ref, sol_out, res_out, sol, res, sem
):
    line = sums_ref[0]
    for index in range(1, sums_ref.shape[0]):
        line = line + sums_ref[index]
    block = iota((1, LANES), 1) // (LANES // 4)
    pick = lambda index: jnp.sum(jnp.where(block == index, line, 0.0), axis=1, keepdims=True)
    rp, pq, qw, wv = [pick(index) for index in range(4)]
    step = rp / pq
    rp_next = step * step * qw - rp
    ratio = rp_next / rp
    lead = 1.0 + ratio
    curvature = lead * lead * pq - 2.0 * lead * step * qw + step * step * wv
    step_next = rp_next / curvature
    on_p = jnp.broadcast_to(step + step_next * lead, (CHUNK, LANES))
    on_w = jnp.broadcast_to(step_next * step, (CHUNK, LANES))

    def copies(index):
        rows = pl.ds(pl.multiple_of(index * CHUNK, CHUNK), CHUNK)
        return (
            pltpu.make_async_copy(sol.at[rows, :], sol_out.at[rows, :], sem.at[0, index]),
            pltpu.make_async_copy(res.at[rows, :], res_out.at[rows, :], sem.at[1, index]),
        )

    def work(index, _):
        at = pl.multiple_of(index * CHUNK, CHUNK)
        p, w, r, q, v = [
            load(ref, at + 2 * EDGE, CHUNK) for ref in (p_ref, w_ref, r_ref, q_ref, v_ref)
        ]
        one = from_cells([on_p * p[t] - on_w * w[t] for t in range(tiles)])
        two = from_cells([r[t] - on_p * q[t] + on_w * v[t] for t in range(tiles)])
        for t in range(tiles):
            sol[pl.ds(at, CHUNK), t * LANES : (t + 1) * LANES] = one[t]
            res[pl.ds(at, CHUNK), t * LANES : (t + 1) * LANES] = two[t]
        for copy in copies(index):
            copy.start()
        return 0

    def settle(index, _):
        for copy in copies(index):
            copy.wait()
        return 0

    lax.fori_loop(0, height // CHUNK, work, 0)
    lax.fori_loop(0, height // CHUNK, settle, 0)


def combine(sums, p, w, r, q, v):
    tiles, height = q.shape[0] - 1, q.shape[1] - 4 * EDGE
    shape = (height, tiles * LANES)
    return pl.pallas_call(
        functools.partial(combine_kernel, tiles, height),
        in_specs=[VMEM] * 6,
        out_specs=[HBM] * 2,
        out_shape=floats(shape, shape),
        scratch_shapes=[
            pltpu.VMEM(shape, jnp.float32),
            pltpu.VMEM(shape, jnp.float32),
            pltpu.SemaphoreType.DMA((2, height // CHUNK)),
        ],
        compiler_params=params(),
        name="combine",
    )(sums, p, w, r, q, v)


def exchange(send_a, send_b, axis):
    count = lax.axis_size(axis)

    def pairs(begin):
        return [
            pair for i in range(begin, count - 1, 2) for pair in ((i, i + 1), (i + 1, i))
        ]

    got_b = lax.ppermute(send_b, axis, pairs(1))
    got_a = lax.ppermute(send_a, axis, pairs(0))
    return got_a, got_b


def body(observed, class_map, class_weights, blur_kernel):
    arguments = (observed, class_map, class_weights, blur_kernel)
    send_a, send_b = edge(*arguments)
    got_a, got_b = exchange(send_a, send_b, "cols")
    obs, cond, coarse = pack(*arguments, send_a)
    obs, cond, coarse, send_a, send_b = middle(got_a, got_b, coarse, obs, cond)
    got_a, got_b = exchange(send_a, send_b, "rows")
    r, east, south, inv = inner(blur_kernel, obs, cond)
    fields = (obs, cond, r, east, south, inv)
    r, east, south, inv, p, q, table, own, chunk, dots = first(
        blur_kernel, fields, got_a, got_b, coarse
    )
    got = lax.all_to_all(chunk, AXES, 0, 0, tiled=True)
    w, v, line = second(blur_kernel, got, own, table, q, east, south, inv, dots)
    sums = lax.all_to_all(line, AXES, 0, 0, tiled=True)
    return tuple(combine(sums, p, w, r, q, v))


def solution(mesh):
    return jax.shard_map(
        body,
        mesh=mesh,
        in_specs=(P("rows", "cols"), P("rows", "cols"), P(), P()),
        out_specs=(P("rows", "cols"), P("rows", "cols")),
        check_vma=False,
    )
```

```python
import functools

import jax
import jax.numpy as jnp
from jax import lax
from jax.experimental import pallas as pl
from jax.experimental.pallas import tpu as pltpu
from jax.sharding import PartitionSpec as P

COARSE = 8
SWEEPS = 8
CLASSES = 4
OMEGA = 0.8

LANES = 128
HALF = LANES // 2
EDGE = 8
STRIP = 2 * EDGE
GROUP = 2
CHUNK = 32
AXES = ("cols", "rows")
LIMIT = 40 * 1024 * 1024


VMEM = pl.BlockSpec(memory_space=pltpu.VMEM)
SMEM = pl.BlockSpec(memory_space=pltpu.SMEM)
HBM = pl.BlockSpec(memory_space=pltpu.HBM)


def params():
    return pltpu.CompilerParams(vmem_limit_bytes=LIMIT)


def in_hbm(array):
    return pltpu.with_memory_space_constraint(array, pltpu.HBM)


def floats(*shapes):
    return [jax.ShapeDtypeStruct(shape, jnp.float32) for shape in shapes]


def place():
    at_col, at_row = lax.axis_index("cols"), lax.axis_index("rows")
    n_cols, n_rows = lax.axis_size("cols"), lax.axis_size("rows")
    return at_col, at_row, n_cols, n_rows


def has_sides():
    at_col, at_row, n_cols, n_rows = place()
    flag = lambda test: jnp.where(test, 1.0, 0.0).astype(jnp.float32)
    return (
        flag(at_row > 0),
        flag(at_row < n_rows - 1),
        flag(at_col < n_cols - 1),
        flag(at_col > 0),
    )


def iota(shape, dim):
    return lax.broadcasted_iota(jnp.int32, shape, dim)


def cell_of(pixel, tiles):
    turn = (tiles + 1) * LANES
    return jnp.where(pixel < turn - HALF, pixel >> 3, ((pixel - turn) >> 3) & (2 * LANES - 1))


def gather_matrix(tiles):
    shape = ((tiles + 1) * LANES, 2 * LANES)
    hit = cell_of(iota(shape, 0), tiles) == iota(shape, 1)
    return jnp.where(hit, 1.0, 0.0).astype(jnp.bfloat16)


def split_dot(field, matrix):
    rows = field.shape[0]
    high = field.astype(jnp.bfloat16)
    low = (field - high.astype(jnp.float32)).astype(jnp.bfloat16)
    both = jnp.dot(
        jnp.concatenate([high, low], axis=0), matrix, preferred_element_type=jnp.float32
    )
    return both[:rows] + both[rows:]


def roll(field, by, axis):
    return pltpu.roll(field, by % field.shape[axis], axis)


def load(ref, at, rows=STRIP):
    return [ref[t, pl.ds(at, rows), :] for t in range(ref.shape[0])]


def store(ref, at, strip):
    for t, part in enumerate(strip):
        ref[t, pl.ds(at, part.shape[0]), :] = part


def wide(ref, at, rows):
    return jnp.concatenate(load(ref, at, rows), axis=1)


def read_taps(taps):
    return [[taps[a, b] for b in range(3)] for a in range(3)]


def tap_total(taps, power):
    return sum(tap * tap if power == 2 else tap for line in taps for tap in line)


def from_west(strip):
    lane = iota(strip[0].shape, 1)
    turned = [roll(part, 1, 1) for part in strip]
    return [jnp.where(lane == 0, turned[t - 1], turned[t]) for t in range(len(strip))]


def from_east(strip):
    lane = iota(strip[0].shape, 1)
    turned = [roll(part, -1, 1) for part in strip]
    count = len(strip)
    return [
        jnp.where(lane == LANES - 1, turned[(t + 1) % count], turned[t]) for t in range(count)
    ]


def tap_sums(ref, at, taps, flip):
    if flip:
        taps = [line[::-1] for line in taps[::-1]]
    above, here, below = load(ref, at - 1), load(ref, at), load(ref, at + 1)
    sums = [[], [], []]
    for t in range(len(here)):
        for b in range(3):
            sums[b].append(
                taps[0][b] * above[t] + taps[1][b] * here[t] + taps[2][b] * below[t]
            )
    return sums


def conv(ref, at, taps, flip):
    sums = tap_sums(ref, at, taps, flip)
    west, east = from_west(sums[0]), from_east(sums[2])
    return [sums[1][t] + west[t] + east[t] for t in range(len(west))]


def operate(ref, image, east_ref, south_ref, at, taps):
    above, here, below = load(ref, at - 1), load(ref, at), load(ref, at + 1)
    east, south, north = load(east_ref, at), load(south_ref, at), load(south_ref, at - 1)
    sums = tap_sums(image, at, taps, True)
    span = range(len(here))
    beside = from_east(here)
    flux = [east[t] * (here[t] - beside[t]) for t in span]
    from_left = from_west([sums[0][t] - flux[t] for t in span])
    from_right = from_east(sums[2])
    return here, [
        sums[1][t]
        + flux[t]
        + from_left[t]
        + from_right[t]
        + south[t] * (here[t] - below[t])
        - north[t] * (above[t] - here[t])
        for t in span
    ]


def begin(obs, cond, at, taps, sides):
    above, here, below = load(cond, at - 1), load(cond, at), load(cond, at + 1)
    span = range(len(here))
    right = from_east(here)
    east = [here[t] + right[t] for t in span]
    west = from_west(east)
    south = [here[t] + below[t] for t in span]
    squares = tap_total(taps, 2)
    diag = [squares + east[t] + west[t] + south[t] + (here[t] + above[t]) for t in span]
    inverse = [pl.reciprocal(part, approx=True) for part in diag]
    inverse = [inverse[t] * (2.0 - diag[t] * inverse[t]) for t in span]
    inverse[-1] = inverse[-1] * sides
    residual = conv(obs, at, taps, True)
    return east, south, inverse, residual, [residual[t] * inverse[t] for t in span]


def pick_lanes(field, lanes):
    return jnp.take_along_axis(field, lanes, axis=1, mode="promise_in_bounds")


def spread_cells(cells, spread):
    tiles = spread.shape[0] - 1
    lane = iota((cells.shape[0], LANES), 1)
    for t in range(tiles):
        spread[t] = pick_lanes(cells[:, :LANES], (lane >> 3) + t * (LANES // COARSE))
    turn = jnp.where(lane < HALF, 0, LANES - LANES // COARSE)
    spread[tiles] = pick_lanes(cells[:, LANES:], (lane >> 3) + turn)


def cells_at(spread, at):
    first = at // EDGE + EDGE - 2
    rows = [load(spread, first + index, 1) for index in range(STRIP // EDGE)]
    return [
        jnp.concatenate([jnp.broadcast_to(row, (EDGE, LANES)) for row in parts], axis=0)
        for parts in zip(*rows)
    ]


def cell_sums(ref, tiles, down):
    lane = iota((down, LANES), 1)
    total = jnp.zeros((down, LANES), jnp.float32)
    for t in range(tiles):
        picked = [
            ref[t, pl.ds(2 * EDGE + k, down, stride=COARSE), :] for k in range(COARSE)
        ]
        part = sum(picked[1:], picked[0])
        for by in (1, 2, 4):
            part = part + roll(part, -by, 1)
        part = pick_lanes(part, (lane & (LANES // COARSE - 1)) * COARSE)
        total = jnp.where(lane // (LANES // COARSE) == t, part, total)
    return total


def side_lanes(has_e, has_w):
    return jnp.where(iota((STRIP, LANES), 1) < HALF, has_e, has_w)


def mask_rows(ref, has_n, has_s):
    last = ref.shape[1] - 2 * EDGE
    for at, flag in ((EDGE, has_n), (last, has_s)):
        ref[:, at : at + EDGE, :] = ref[:, at : at + EDGE, :] * flag


def clear_pads(*refs):
    empty = jnp.zeros((refs[0].shape[0], EDGE, LANES), jnp.float32)
    for ref in refs:
        ref[:, :EDGE, :] = empty
        ref[:, ref.shape[1] - EDGE :, :] = empty


def product_sum_rows(one, two, count):
    total = one[0] * two[0]
    for t in range(1, count):
        total = total + one[t] * two[t]
    return total


def product_sum(one, two, count, flags=None):
    return fold(product_sum_rows(one, two, count), flags)


def fold(total, flags=None):
    parts = [total[at : at + EDGE] for at in range(0, total.shape[0], EDGE)]
    if flags is not None:
        parts = [part * flag for part, flag in zip(parts, flags)]
    return sum(parts[1:], parts[0])


def sweep(first, last, body, carry):
    width = GROUP * STRIP
    steps = -(-(last - first) // width)

    def work(index, carry):
        start = first + index * width
        at = pl.multiple_of(jnp.minimum(start, last - width), EDGE)
        pending = []
        for by in range(0, width, STRIP):
            stores, carry = body(at + by, start, carry)
            pending += [(ref, at + by, strip) for ref, strip in stores]
        for ref, row, strip in pending:
            store(ref, row, strip)
        return carry

    return lax.fori_loop(0, steps, work, carry)


def jacobi(source, table, work):
    factor, east, west, south, north = [table[index] for index in range(5)]
    window = source.shape[0]
    source = factor * source
    iterate = source
    for sweep_index in range(SWEEPS - 1):
        place_ref = work.at[sweep_index % 2]
        for half in range(2):
            place_ref[half, EDGE : EDGE + window, :] = iterate[
                :, half * LANES : (half + 1) * LANES
            ]
        above, below = [
            jnp.concatenate(
                [place_ref[half, EDGE + by : EDGE + by + window, :] for half in range(2)], axis=1
            )
            for by in (-1, 1)
        ]
        across = east * roll(iterate, -1, 1) + west * roll(iterate, 1, 1)
        along = south * below + north * above
        iterate = ((1.0 - OMEGA) * iterate + source) + (across + along)
    return iterate


def clear_work(work):
    for buffer in range(2):
        clear_pads(work.at[buffer])


def in_pair_order(at, for_before, for_after):
    even = at % 2 == 0
    if callable(for_before):
        return (
            lambda index: jnp.where(even, for_after(index), for_before(index)),
            lambda index: jnp.where(even, for_before(index), for_after(index)),
        )
    return jnp.where(even, for_after, for_before), jnp.where(even, for_before, for_after)


def reader(tiles_here, refs, scratch, obs, cond, down):
    obs_in, class_in, weight_in, taps_in = refs
    classes, weights, taps, sums, obs_sem, class_sem, small_sem = scratch
    own = pl.ds(2 * EDGE, down * COARSE)
    small = [
        pltpu.make_async_copy(weight_in, weights, small_sem.at[0]),
        pltpu.make_async_copy(taps_in, taps, small_sem.at[1]),
    ]
    moves = []
    for slot, t in enumerate(tiles_here):
        lanes = pl.ds(t * LANES, LANES)
        moves.append(
            (
                pltpu.make_async_copy(class_in.at[:, lanes], classes.at[slot], class_sem.at[slot]),
                pltpu.make_async_copy(
                    obs_in.at[:, lanes], obs.at[slot, own, :], obs_sem.at[slot]
                ),
            )
        )
    for copy in small:
        copy.start()
    for pair in moves:
        for copy in pair:
            copy.start()
    sums[...] = jnp.zeros_like(sums)

    def settle(slot):
        if slot == 0:
            for copy in small:
                copy.wait()
        for copy in moves[slot]:
            copy.wait()
        values = [0.5 * weights[class_id] for class_id in range(CLASSES)]
        kind = classes[slot]
        cond[slot, own, :] = jnp.where(
            kind < 2,
            jnp.where(kind == 0, values[0], values[1]),
            jnp.where(kind == 2, values[2], values[3]),
        )
        for which, ref in enumerate((obs, cond)):
            picked = [
                ref[slot, pl.ds(2 * EDGE + k, down, stride=COARSE), :] for k in range(COARSE)
            ]
            cells = slice(2 * EDGE, 2 * EDGE + down)
            sums[3 * which, slot, cells, :] = sum(picked[1:], picked[0])
            sums[3 * which + 1, slot, cells, :] = picked[0]
            sums[3 * which + 2, slot, cells, :] = picked[-1]

    return settle


def reader_scratch(tiles, height, window, class_weights, taps):
    return [
        pltpu.VMEM((tiles, height, LANES), jnp.int32),
        pltpu.SMEM(class_weights.shape, jnp.float32),
        pltpu.SMEM(taps.shape, jnp.float32),
        pltpu.VMEM((6, tiles + 1, window + 2 * EDGE, LANES), jnp.float32),
        pltpu.SemaphoreType.DMA((tiles,)),
        pltpu.SemaphoreType.DMA((tiles,)),
        pltpu.SemaphoreType.DMA((2,)),
    ]


def coarse_parts(sums, taps, matrix):
    window = sums.shape[2] - 2 * EDGE
    whole = lambda index, by=0: wide(sums.at[index], EDGE + by, window)
    full = whole(0)
    by_tap = [full - whole(1) + whole(1, 1), full, full - whole(2) + whole(2, -1)]
    across = [sum(taps[a][b] * by_tap[a] for a in range(3)) for b in range(3)]
    source = across[1] + roll(across[0], -1, 1) + roll(across[2], 1, 1)
    full = whole(3)
    last = (iota(full.shape, 1) & (COARSE - 1)) == COARSE - 1
    east = jnp.where(last, full + roll(full, -1, 1), 0.0)
    south = whole(5) + whole(4, 1)
    cells = split_dot(jnp.concatenate([source, east, south], axis=0), matrix)
    source, east, south = cells[:window], cells[window : 2 * window], cells[2 * window :]
    around = east + roll(east, 1, 1) + south + roll(south, 1, 0)
    return [source, east, south, around]


def edge_kernel(tiles, down, *refs):
    arguments, (send_a, send_b), (obs, cond, message, *scratch) = refs[:4], refs[4:6], refs[6:]
    height = down * COARSE
    halves = height // LANES
    window = down + 2 * EDGE
    settle = reader((0, tiles - 1), arguments, scratch, obs, cond, down)
    matrix = gather_matrix(2)
    for slot, begin_row in ((0, 0), (1, LANES - EDGE)):
        settle(slot)
        for which, ref in enumerate((obs, cond)):
            turned = jnp.transpose(ref[slot, 2 * EDGE : 2 * EDGE + height, :])
            turned = turned[begin_row : begin_row + EDGE]
            for half in range(halves):
                at = (which * halves + half) * EDGE
                message[slot, at : at + EDGE, :] = turned[:, half * LANES : (half + 1) * LANES]
    parts = coarse_parts(scratch[3], read_taps(scratch[2]), matrix)
    spare = jnp.zeros((2 * LANES - 4 * window, 2 * LANES), jnp.float32)
    stack = jnp.concatenate(parts + [spare], axis=0)
    left = jnp.transpose(stack[:, :LANES])
    right = jnp.transpose(stack[:, LANES:])
    base = 2 * halves * EDGE
    past = 2 * LANES // COARSE
    for slot, pieces in (
        (0, (left[:EDGE], right[LANES - EDGE :])),
        (1, (left[past - EDGE : past], left[past : past + EDGE])),
    ):
        for index, piece in enumerate(pieces):
            for half in range(2):
                at = base + (2 * index + half) * EDGE
                message[slot, at : at + EDGE, :] = piece[:, half * LANES : (half + 1) * LANES]
    send_a[...], send_b[...] = in_pair_order(place()[0], message[0], message[1])


def edge(observed, class_map, class_weights, taps):
    height, breadth = observed.shape
    tiles, down = breadth // LANES, height // COARSE
    window = down + 2 * EDGE
    field = (3, height + 4 * EDGE, LANES)
    strip = ((2 * (height // LANES) + 4) * EDGE, LANES)
    return pl.pallas_call(
        functools.partial(edge_kernel, tiles, down),
        in_specs=[HBM] * 4,
        out_specs=[VMEM] * 2,
        out_shape=floats(strip, strip),
        scratch_shapes=[
            pltpu.VMEM(field, jnp.float32),
            pltpu.VMEM(field, jnp.float32),
            pltpu.VMEM((2,) + strip, jnp.float32),
        ]
        + reader_scratch(2, height, window, class_weights, taps),
        compiler_params=params(),
        name="pack_east_west",
    )(*[in_hbm(array) for array in (observed, class_map, class_weights, taps)])


def pack_kernel(tiles, down, *refs):
    arguments, (obs, cond, coarse_ref), scratch = refs[:4], refs[5:8], refs[8:]
    settle = reader(range(tiles), arguments, scratch, obs, cond, down)
    matrix = gather_matrix(tiles)
    for t in range(tiles):
        settle(t)
    for index, part in enumerate(coarse_parts(scratch[3], read_taps(scratch[2]), matrix)):
        coarse_ref[index] = part


def pack(observed, class_map, class_weights, taps, after):
    height, breadth = observed.shape
    tiles, down = breadth // LANES, height // COARSE
    window = down + 2 * EDGE
    field = (tiles + 1, height + 4 * EDGE, LANES)
    pixels = height * breadth
    return pl.pallas_call(
        functools.partial(pack_kernel, tiles, down),
        in_specs=[HBM] * 4 + [VMEM],
        out_specs=[VMEM] * 3,
        out_shape=floats(field, field, (4, window, 2 * LANES)),
        scratch_shapes=reader_scratch(tiles, height, window, class_weights, taps),
        compiler_params=params(),
        cost_estimate=pl.CostEstimate(
            flops=20 * pixels, bytes_accessed=16 * pixels, transcendentals=0
        ),
        name="pack_all",
    )(*[in_hbm(array) for array in (observed, class_map, class_weights, taps)], after)


def merge_sides(parts):
    block = iota((EDGE, LANES), 1) // (2 * EDGE)
    merged = jnp.zeros((EDGE, LANES), jnp.float32)
    for index, part in enumerate(parts):
        merged = jnp.where(block == index, roll(part, (2 * index + 1) * EDGE, 1), merged)
    return merged


def split_sides(merged, count):
    lane = iota((EDGE, LANES), 1)
    outer = (lane < EDGE) | (lane >= LANES - EDGE)
    return [
        jnp.where(outer, roll(merged, -(2 * index + 1) * EDGE, 1), 0.0) for index in range(count)
    ]


def middle_kernel(
    tiles,
    down,
    got_b,
    got_a,
    coarse_in,
    obs_in,
    cond_in,
    obs,
    cond,
    coarse_ref,
    send_a,
    send_b,
    message,
):
    height = down * COARSE
    halves = height // LANES
    at_col, at_row, _, _ = place()
    from_e, from_w = in_pair_order(at_col, got_b[...], got_a[...])
    gap = jnp.zeros((LANES - 2 * EDGE, LANES), jnp.float32)

    def turned(low, high):
        return jnp.transpose(jnp.concatenate([low, gap, high], axis=0))

    for which, field in enumerate((obs, cond)):
        for half in range(halves):
            at = (which * halves + half) * EDGE
            begin_row = 2 * EDGE + half * LANES
            field[tiles, begin_row : begin_row + LANES, :] = turned(
                from_e[at : at + EDGE], from_w[at : at + EDGE]
            )
    base = 2 * halves * EDGE

    def piece(strip, index, half):
        at = base + (2 * index + half) * EDGE
        return strip[at : at + EDGE]

    left = [turned(piece(from_w, 1, half), piece(from_e, 1, half)) for half in range(2)]
    right = [turned(piece(from_e, 0, half), piece(from_w, 0, half)) for half in range(2)]
    left = jnp.concatenate(left, axis=0)
    right = jnp.concatenate(right, axis=0)
    window = down + 2 * EDGE
    for index in range(4):
        rows = slice(index * window, (index + 1) * window)
        coarse_ref[index, :, :LANES] = coarse_in[index, :, :LANES] + left[rows]
        coarse_ref[index, :, LANES:] = coarse_in[index, :, LANES:] + right[rows]
    fields = (obs, cond)
    for slot, begin_row, first_row, over_row in (
        (0, 2 * EDGE, EDGE, EDGE - 1),
        (1, EDGE + height, window - 2 * EDGE, window - EDGE),
    ):
        pieces = [field[t, begin_row : begin_row + EDGE, :] for field in fields for t in range(tiles)]
        rows = slice(first_row, first_row + EDGE)
        pieces += [coarse_ref[index, rows, :LANES] for index in range(4)]
        beyond = [coarse_ref[index, rows, LANES:] for index in range(4)]
        beyond += [field[tiles, begin_row : begin_row + EDGE, :] for field in fields]
        pieces.append(merge_sides(beyond))
        pieces.append(
            jnp.concatenate(
                [
                    coarse_ref[index, over_row : over_row + 1, half * LANES : (half + 1) * LANES]
                    for index in range(4)
                    for half in range(2)
                ],
                axis=0,
            )
        )
        for index, piece in enumerate(pieces):
            message[slot, index] = piece
    send_a[...], send_b[...] = in_pair_order(at_row, message[0], message[1])


def middle(got_a, got_b, coarse, obs, cond):
    tiles, height = obs.shape[0] - 1, obs.shape[1] - 4 * EDGE
    down = height // COARSE
    long = (2 * tiles + 6, EDGE, LANES)
    return pl.pallas_call(
        functools.partial(middle_kernel, tiles, down),
        in_specs=[VMEM] * 5,
        out_specs=[VMEM] * 5,
        out_shape=floats(obs.shape, cond.shape, coarse.shape, long, long),
        input_output_aliases={3: 0, 4: 1},
        scratch_shapes=[pltpu.VMEM((2,) + long, jnp.float32)],
        compiler_params=params(),
        name="pack_north_south",
    )(got_b, got_a, coarse, obs, cond)


def inner_kernel(taps, obs, cond, res_ref, east_ref, south_ref, inv_ref, u_ref, dot_ref):
    _, _, has_e, has_w = has_sides()
    clear_pads(east_ref, south_ref)
    taps = read_taps(taps)
    sides = side_lanes(has_e, has_w)

    tiles = obs.shape[0] - 1

    def work(at, start, total):
        fields = begin(obs, cond, at, taps, sides)
        flags = [jnp.where(at + by >= start, 1.0, 0.0) for by in range(0, STRIP, EDGE)]
        total = total + product_sum(fields[3], fields[4], tiles, flags)
        return list(zip((east_ref, south_ref, inv_ref, res_ref, u_ref), fields)), total

    nothing = jnp.zeros((EDGE, LANES), jnp.float32)
    dot_ref[...] = sweep(3 * EDGE, obs.shape[1] - 3 * EDGE, work, nothing)


def inner(taps, obs, cond):
    field = obs.shape
    pixels = field[0] * field[1] * field[2]
    return pl.pallas_call(
        inner_kernel,
        in_specs=[SMEM] + [VMEM] * 2,
        out_specs=[VMEM] * 6,
        out_shape=floats(field, field, field, field, field, (EDGE, LANES)),
        compiler_params=params(),
        cost_estimate=pl.CostEstimate(
            flops=45 * pixels, bytes_accessed=24 * pixels, transcendentals=0
        ),
        name="inner_strips",
    )(taps, obs, cond)


def first_kernel(
    tiles,
    down,
    taps,
    obs_in,
    cond_in,
    res_in,
    east_in,
    south_in,
    inv_in,
    u_in,
    got_b,
    got_a,
    coarse_in,
    dot_in,
    obs,
    cond,
    res_ref,
    east_ref,
    south_ref,
    inv_ref,
    u_ref,
    p_ref,
    q_ref,
    table_ref,
    own_ref,
    chunk_ref,
    dots_ref,
    image,
    spread,
    work,
):
    height = down * COARSE
    window = down + 2 * EDGE
    at_col, at_row, n_cols, n_rows = place()
    has_n, has_s, has_e, has_w = has_sides()
    clear_pads(obs, cond, p_ref, image)
    clear_work(work)
    from_s, from_n = in_pair_order(
        at_row, lambda index: got_b[index], lambda index: got_a[index]
    )

    for which, field in enumerate((obs, cond)):
        for t in range(tiles):
            field[t, EDGE : 2 * EDGE, :] = from_n(which * tiles + t)
            field[t, 2 * EDGE + height : 3 * EDGE + height, :] = from_s(which * tiles + t)
    sides_n, sides_s = [split_sides(strip(2 * tiles + 4), 6) for strip in (from_n, from_s)]
    for which, field in enumerate((obs, cond)):
        field[tiles, EDGE : 2 * EDGE, :] = sides_n[4 + which]
        field[tiles, 2 * EDGE + height : 3 * EDGE + height, :] = sides_s[4 + which]

    edge_row = iota((EDGE, 2 * LANES), 0)

    def joined(index):
        def over(strip, row):
            line = [
                jnp.broadcast_to(
                    strip((2 * tiles + 5, pl.ds(2 * index + half, 1))), (EDGE, LANES)
                )
                for half in range(2)
            ]
            return jnp.where(edge_row == row, jnp.concatenate(line, axis=1), 0.0)

        def rows(strip, beyond):
            return jnp.concatenate([strip(2 * tiles + index), beyond[index]], axis=1)

        parts = [coarse_in[index, at : at + EDGE, :] for at in range(0, window, EDGE)]
        parts[0] = parts[0] + rows(from_n, sides_n)
        parts[1] = parts[1] + over(from_n, 0)
        parts[-2] = parts[-2] + over(from_s, EDGE - 1)
        parts[-1] = parts[-1] + rows(from_s, sides_s)
        return jnp.concatenate(parts, axis=0)

    source, east, south, around = [joined(index) for index in range(4)]
    row = iota(source.shape, 0)
    lane = iota(source.shape, 1)
    inside = jnp.where(row < EDGE, has_n, jnp.where(row < window - EDGE, 1.0, has_s))
    inside = inside * jnp.where(
        lane < LANES, 1.0, jnp.where(lane < LANES + HALF, has_e, has_w)
    )
    taps = read_taps(taps)
    taps_sum = tap_total(taps, 1)
    factor = inside * OMEGA / (COARSE * COARSE * taps_sum * taps_sum + around)
    weights = (east, roll(east, 1, 1), south, roll(south, 1, 0))
    table = [factor] + [factor * weight for weight in weights]
    for index, part in enumerate(table):
        table_ref[index] = part
    sides = side_lanes(has_e, has_w)
    half = iota((STRIP, LANES), 0) // EDGE
    pending = []
    total = dot_in[...]
    for index, known in ((0, has_n), (1, has_s)):
        at = EDGE + index * height
        fields = begin(obs, cond, at, taps, sides)
        own = jnp.where(half == index, 0.0, 1.0)
        total = total + fold(own * product_sum_rows(fields[3], fields[4], tiles))
        flag = jnp.where(half == index, known, 1.0)
        inverse, start = [[part * flag for part in fields[index]] for index in (2, 4)]
        fields = (*fields[:2], inverse, fields[3], start)
        pending += [
            (ref, at, strip)
            for ref, strip in zip((east_ref, south_ref, inv_ref, res_ref, u_ref), fields)
        ]
    cells = jacobi(source, table, work)
    spread_cells(cells, spread)
    inner_cells = slice(EDGE, EDGE + down)
    total = total + fold(source[inner_cells, :LANES] * cells[inner_cells, :LANES])
    dots_ref[0] = total
    for ref, at, strip in pending:
        store(ref, at, strip)

    def flags(at, start):
        rows = [at + by for by in range(0, STRIP, EDGE)]
        first_row = jnp.maximum(start, 2 * EDGE)
        return [
            jnp.where((row >= first_row) & (row < 2 * EDGE + height), 1.0, 0.0) for row in rows
        ]

    def begin_p(at, _, carry):
        start, cells = load(u_ref, at), cells_at(spread, at)
        return [(p_ref, [start[t] + cells[t] for t in range(tiles + 1)])], carry

    def blur(at, _, carry):
        strip = conv(p_ref, at, taps, False)
        strip[tiles] = strip[tiles] * sides
        return [(image, strip)], carry

    def finish(at, start, total):
        here, product = operate(p_ref, image, east_ref, south_ref, at, taps)
        return [(q_ref, product)], total + product_sum(here, product, tiles, flags(at, start))

    nothing = jnp.zeros((EDGE, LANES), jnp.float32)
    span = (EDGE, 3 * EDGE + height)
    sweep(*span, begin_p, 0)
    sweep(*span, blur, 0)
    mask_rows(image, has_n, has_s)
    dots_ref[1] = sweep(*span, finish, nothing)

    own = cell_sums(q_ref, tiles, down)
    own_ref[...] = own
    spare = jnp.zeros((LANES - down, LANES), jnp.float32)
    turned = jnp.transpose(jnp.concatenate([own, spare], axis=0))
    chunk_ref[...] = jnp.zeros_like(chunk_ref)
    for down_by in (-1, 0, 1):
        for right_by in (-1, 0, 1):
            if down_by == 0 and right_by == 0:
                continue
            if down_by == 0:
                piece = turned[:EDGE] if right_by < 0 else turned[LANES - EDGE :]
            else:
                piece = own[:EDGE] if down_by < 0 else own[down - EDGE :]
            to_row, to_col = at_row + down_by, at_col + right_by

            @pl.when((to_row >= 0) & (to_row < n_rows) & (to_col >= 0) & (to_col < n_cols))
            def _(piece=piece, to_row=to_row, to_col=to_col):
                chunk_ref[to_col * n_rows + to_row] = piece


def first(taps, fields, got_a, got_b, coarse, dot):
    field = fields[0].shape
    tiles, height = field[0] - 1, field[1] - 4 * EDGE
    down = height // COARSE
    window = down + 2 * EDGE
    count = lax.axis_size("cols") * lax.axis_size("rows")
    shapes = [field] * 9 + [
        (5, window, 2 * LANES),
        (down, LANES),
        (count, EDGE, LANES),
        (2, EDGE, LANES),
    ]
    return pl.pallas_call(
        functools.partial(first_kernel, tiles, down),
        in_specs=[SMEM] + [VMEM] * 11,
        out_specs=[VMEM] * len(shapes),
        out_shape=floats(*shapes),
        input_output_aliases={index + 1: index for index in range(7)},
        scratch_shapes=[
            pltpu.VMEM(field, jnp.float32),
            pltpu.VMEM((tiles + 1, window, LANES), jnp.float32),
            pltpu.VMEM((2, 2, window + 2 * EDGE, LANES), jnp.float32),
        ],
        compiler_params=params(),
        name="first_direction",
    )(taps, *fields, got_b, got_a, coarse, dot)[2:]


def second_kernel(
    tiles,
    down,
    taps,
    got_ref,
    own_ref,
    table_ref,
    q_ref,
    east_ref,
    south_ref,
    inv_ref,
    dots_in,
    w_ref,
    v_ref,
    out_ref,
    image,
    spread,
    work,
):
    height = down * COARSE
    has_n, has_s, has_e, has_w = has_sides()
    at_col, at_row, n_cols, n_rows = place()
    me = at_col * n_rows + at_row

    def got(down_by, right_by):
        to_row, to_col = at_row + down_by, at_col + right_by
        there = (to_row >= 0) & (to_row < n_rows) & (to_col >= 0) & (to_col < n_cols)
        return got_ref[jnp.where(there, to_col * n_rows + to_row, me)]

    low = iota((EDGE, LANES), 1) < HALF
    gap = jnp.zeros((LANES - 2 * EDGE, LANES), jnp.float32)
    beside = jnp.transpose(jnp.concatenate([got(0, 1), gap, got(0, -1)], axis=0))[:down]
    source = jnp.concatenate(
        [
            jnp.concatenate([got(-1, 0), jnp.where(low, got(-1, 1), got(-1, -1))], axis=1),
            jnp.concatenate([own_ref[...], beside], axis=1),
            jnp.concatenate([got(1, 0), jnp.where(low, got(1, 1), got(1, -1))], axis=1),
        ],
        axis=0,
    )
    clear_work(work)
    spread_cells(jacobi(source, table_ref, work), spread)
    clear_pads(w_ref, image)
    sides = side_lanes(has_e, has_w)
    taps = read_taps(taps)

    def begin_w(at, start, total):
        field, inverse, cells = load(q_ref, at), load(inv_ref, at), cells_at(spread, at)
        strip = [field[t] * inverse[t] + cells[t] for t in range(tiles + 1)]
        first_row = jnp.maximum(start, 2 * EDGE)
        flags = [
            jnp.where((row >= first_row) & (row < 2 * EDGE + height), 1.0, 0.0)
            for row in [at + by for by in range(0, STRIP, EDGE)]
        ]
        return [(w_ref, strip)], total + product_sum(field, strip, tiles, flags)

    def blur(at, _, carry):
        strip = conv(w_ref, at, taps, False)
        strip[tiles] = strip[tiles] * sides
        return [(image, strip)], carry

    def finish(at, _, total):
        here, product = operate(w_ref, image, east_ref, south_ref, at, taps)
        return [(v_ref, product[:tiles])], total + product_sum(here, product, tiles)

    nothing = jnp.zeros((EDGE, LANES), jnp.float32)
    span = (EDGE, 3 * EDGE + height)
    dot_qw = sweep(*span, begin_w, nothing)
    sweep(*span, blur, 0)
    mask_rows(image, has_n, has_s)
    dot_wv = sweep(2 * EDGE, 2 * EDGE + height, finish, nothing)
    line = jnp.zeros((1, LANES), jnp.float32)
    block = iota((1, LANES), 1) // (LANES // 4)
    for index, part in enumerate((dots_in[0], dots_in[1], dot_qw, dot_wv)):
        part = jnp.sum(part, axis=0, keepdims=True)
        part = part + roll(part, LANES // 2, 1)
        part = part + roll(part, LANES // 4, 1)
        line = jnp.where(block == index, part, line)
    for index in range(out_ref.shape[0]):
        out_ref[index] = line


def second(taps, got, own, table, q, east, south, inv, dots):
    tiles, height = q.shape[0] - 1, q.shape[1] - 4 * EDGE
    down = height // COARSE
    window = down + 2 * EDGE
    count = lax.axis_size("cols") * lax.axis_size("rows")
    return pl.pallas_call(
        functools.partial(second_kernel, tiles, down),
        in_specs=[SMEM] + [VMEM] * 8,
        out_specs=[VMEM] * 3,
        out_shape=floats(q.shape, q.shape, (count, 1, LANES)),
        scratch_shapes=[
            pltpu.VMEM(q.shape, jnp.float32),
            pltpu.VMEM((tiles + 1, window, LANES), jnp.float32),
            pltpu.VMEM((2, 2, window + 2 * EDGE, LANES), jnp.float32),
        ],
        compiler_params=params(),
        name="second_direction",
    )(taps, got, own, table, q, east, south, inv, dots)


def combine_kernel(
    tiles, height, sums_ref, p_ref, w_ref, r_ref, q_ref, v_ref, sol_out, res_out, sol, res, sem
):
    line = sums_ref[0]
    for index in range(1, sums_ref.shape[0]):
        line = line + sums_ref[index]
    block = iota((1, LANES), 1) // (LANES // 4)
    pick = lambda index: jnp.sum(jnp.where(block == index, line, 0.0), axis=1, keepdims=True)
    rp, pq, qw, wv = [pick(index) for index in range(4)]
    step = rp / pq
    rp_next = step * step * qw - rp
    ratio = rp_next / rp
    lead = 1.0 + ratio
    curvature = lead * lead * pq - 2.0 * lead * step * qw + step * step * wv
    step_next = rp_next / curvature
    on_p = jnp.broadcast_to(step + step_next * lead, (CHUNK, LANES))
    on_w = jnp.broadcast_to(step_next * step, (CHUNK, LANES))

    def copies(index):
        rows = pl.ds(pl.multiple_of(index * CHUNK, CHUNK), CHUNK)
        return (
            pltpu.make_async_copy(sol.at[rows, :], sol_out.at[rows, :], sem.at[0, index]),
            pltpu.make_async_copy(res.at[rows, :], res_out.at[rows, :], sem.at[1, index]),
        )

    def work(index, _):
        at = pl.multiple_of(index * CHUNK, CHUNK)
        p, w, r, q, v = [
            load(ref, at + 2 * EDGE, CHUNK) for ref in (p_ref, w_ref, r_ref, q_ref, v_ref)
        ]
        one = [on_p * p[t] - on_w * w[t] for t in range(tiles)]
        two = [r[t] - on_p * q[t] + on_w * v[t] for t in range(tiles)]
        for t in range(tiles):
            sol[pl.ds(at, CHUNK), t * LANES : (t + 1) * LANES] = one[t]
            res[pl.ds(at, CHUNK), t * LANES : (t + 1) * LANES] = two[t]
        for copy in copies(index):
            copy.start()
        return 0

    def settle(index, _):
        for copy in copies(index):
            copy.wait()
        return 0

    lax.fori_loop(0, height // CHUNK, work, 0)
    lax.fori_loop(0, height // CHUNK, settle, 0)


def combine(sums, p, w, r, q, v):
    tiles, height = q.shape[0] - 1, q.shape[1] - 4 * EDGE
    shape = (height, tiles * LANES)
    return pl.pallas_call(
        functools.partial(combine_kernel, tiles, height),
        in_specs=[VMEM] * 6,
        out_specs=[HBM] * 2,
        out_shape=floats(shape, shape),
        scratch_shapes=[
            pltpu.VMEM(shape, jnp.float32),
            pltpu.VMEM(shape, jnp.float32),
            pltpu.SemaphoreType.DMA((2, height // CHUNK)),
        ],
        compiler_params=params(),
        name="combine",
    )(sums, p, w, r, q, v)


def exchange(send_a, send_b, axis):
    count = lax.axis_size(axis)

    def pairs(begin):
        return [
            pair for i in range(begin, count - 1, 2) for pair in ((i, i + 1), (i + 1, i))
        ]

    got_b = lax.ppermute(send_b, axis, pairs(1))
    got_a = lax.ppermute(send_a, axis, pairs(0))
    return got_a, got_b


def body(observed, class_map, class_weights, blur_kernel):
    arguments = (observed, class_map, class_weights, blur_kernel)
    send_a, send_b = edge(*arguments)
    got_a, got_b = exchange(send_a, send_b, "cols")
    obs, cond, coarse = pack(*arguments, send_a)
    obs, cond, coarse, send_a, send_b = middle(got_a, got_b, coarse, obs, cond)
    got_a, got_b = exchange(send_a, send_b, "rows")
    r, east, south, inv, u, dot = inner(blur_kernel, obs, cond)
    fields = (obs, cond, r, east, south, inv, u)
    r, east, south, inv, _, p, q, table, own, chunk, dots = first(
        blur_kernel, fields, got_a, got_b, coarse, dot
    )
    got = lax.all_to_all(chunk, AXES, 0, 0, tiled=True)
    w, v, line = second(blur_kernel, got, own, table, q, east, south, inv, dots)
    sums = lax.all_to_all(line, AXES, 0, 0, tiled=True)
    return tuple(combine(sums, p, w, r, q, v))


def solution(mesh):
    return jax.shard_map(
        body,
        mesh=mesh,
        in_specs=(P("rows", "cols"), P("rows", "cols"), P(), P()),
        out_specs=(P("rows", "cols"), P("rows", "cols")),
        check_vma=False,
    )
```

```python
import functools

import jax
import jax.numpy as jnp
from jax import lax
from jax.experimental import pallas as pl
from jax.experimental.pallas import tpu as pltpu
from jax.sharding import PartitionSpec as P

COARSE = 8
SWEEPS = 8
CLASSES = 4
OMEGA = 0.8

LANES = 128
HALF = LANES // 2
EDGE = 8
STRIP = 2 * EDGE
GROUP = 2
CHUNK = 32
AXES = ("cols", "rows")
LIMIT = 40 * 1024 * 1024


VMEM = pl.BlockSpec(memory_space=pltpu.VMEM)
SMEM = pl.BlockSpec(memory_space=pltpu.SMEM)
HBM = pl.BlockSpec(memory_space=pltpu.HBM)


def params():
    return pltpu.CompilerParams(vmem_limit_bytes=LIMIT)


def in_hbm(array):
    return pltpu.with_memory_space_constraint(array, pltpu.HBM)


def floats(*shapes):
    return [jax.ShapeDtypeStruct(shape, jnp.float32) for shape in shapes]


def place():
    at_col, at_row = lax.axis_index("cols"), lax.axis_index("rows")
    n_cols, n_rows = lax.axis_size("cols"), lax.axis_size("rows")
    return at_col, at_row, n_cols, n_rows


def has_sides():
    at_col, at_row, n_cols, n_rows = place()
    flag = lambda test: jnp.where(test, 1.0, 0.0).astype(jnp.float32)
    return (
        flag(at_row > 0),
        flag(at_row < n_rows - 1),
        flag(at_col < n_cols - 1),
        flag(at_col > 0),
    )


def iota(shape, dim):
    return lax.broadcasted_iota(jnp.int32, shape, dim)


def cell_of(pixel, tiles):
    turn = (tiles + 1) * LANES
    return jnp.where(pixel < turn - HALF, pixel >> 3, ((pixel - turn) >> 3) & (2 * LANES - 1))


def gather_matrix(tiles):
    shape = ((tiles + 1) * LANES, 2 * LANES)
    hit = cell_of(iota(shape, 0), tiles) == iota(shape, 1)
    return jnp.where(hit, 1.0, 0.0).astype(jnp.bfloat16)


def split_dot(field, matrix):
    rows = field.shape[0]
    high = field.astype(jnp.bfloat16)
    low = (field - high.astype(jnp.float32)).astype(jnp.bfloat16)
    both = jnp.dot(
        jnp.concatenate([high, low], axis=0), matrix, preferred_element_type=jnp.float32
    )
    return both[:rows] + both[rows:]


def roll(field, by, axis):
    return pltpu.roll(field, by % field.shape[axis], axis)


def load(ref, at, rows=STRIP):
    return [ref[t, pl.ds(at, rows), :] for t in range(ref.shape[0])]


def store(ref, at, strip):
    for t, part in enumerate(strip):
        ref[t, pl.ds(at, part.shape[0]), :] = part


def wide(ref, at, rows):
    return jnp.concatenate(load(ref, at, rows), axis=1)


def read_taps(taps):
    return [[taps[a, b] for b in range(3)] for a in range(3)]


def tap_total(taps, power):
    return sum(tap * tap if power == 2 else tap for line in taps for tap in line)


def from_west(strip):
    lane = iota(strip[0].shape, 1)
    turned = [roll(part, 1, 1) for part in strip]
    return [jnp.where(lane == 0, turned[t - 1], turned[t]) for t in range(len(strip))]


def from_east(strip):
    lane = iota(strip[0].shape, 1)
    turned = [roll(part, -1, 1) for part in strip]
    count = len(strip)
    return [
        jnp.where(lane == LANES - 1, turned[(t + 1) % count], turned[t]) for t in range(count)
    ]


def tap_sums(ref, at, taps, flip):
    if flip:
        taps = [line[::-1] for line in taps[::-1]]
    above, here, below = load(ref, at - 1), load(ref, at), load(ref, at + 1)
    sums = [[], [], []]
    for t in range(len(here)):
        for b in range(3):
            sums[b].append(
                taps[0][b] * above[t] + taps[1][b] * here[t] + taps[2][b] * below[t]
            )
    return sums


def conv(ref, at, taps, flip):
    sums = tap_sums(ref, at, taps, flip)
    west, east = from_west(sums[0]), from_east(sums[2])
    return [sums[1][t] + west[t] + east[t] for t in range(len(west))]


def operate(ref, image, east_ref, south_ref, at, taps):
    above, here, below = load(ref, at - 1), load(ref, at), load(ref, at + 1)
    east, south, north = load(east_ref, at), load(south_ref, at), load(south_ref, at - 1)
    sums = tap_sums(image, at, taps, True)
    span = range(len(here))
    beside = from_east(here)
    flux = [east[t] * (here[t] - beside[t]) for t in span]
    from_left = from_west([sums[0][t] - flux[t] for t in span])
    from_right = from_east(sums[2])
    return here, [
        sums[1][t]
        + flux[t]
        + from_left[t]
        + from_right[t]
        + south[t] * (here[t] - below[t])
        - north[t] * (above[t] - here[t])
        for t in span
    ]


def begin(obs, cond, at, taps, sides):
    above, here, below = load(cond, at - 1), load(cond, at), load(cond, at + 1)
    span = range(len(here))
    right = from_east(here)
    east = [here[t] + right[t] for t in span]
    west = from_west(east)
    south = [here[t] + below[t] for t in span]
    squares = tap_total(taps, 2)
    diag = [squares + east[t] + west[t] + south[t] + (here[t] + above[t]) for t in span]
    inverse = [pl.reciprocal(part, approx=True) for part in diag]
    inverse = [inverse[t] * (2.0 - diag[t] * inverse[t]) for t in span]
    inverse[-1] = inverse[-1] * sides
    residual = conv(obs, at, taps, True)
    return east, south, inverse, residual, [residual[t] * inverse[t] for t in span]


def pick_lanes(field, lanes):
    return jnp.take_along_axis(field, lanes, axis=1, mode="promise_in_bounds")


def spread_cells(cells, spread):
    tiles = spread.shape[0] - 1
    lane = iota((cells.shape[0], LANES), 1)
    for t in range(tiles):
        spread[t] = pick_lanes(cells[:, :LANES], (lane >> 3) + t * (LANES // COARSE))
    turn = jnp.where(lane < HALF, 0, LANES - LANES // COARSE)
    spread[tiles] = pick_lanes(cells[:, LANES:], (lane >> 3) + turn)


def cells_at(spread, at):
    first = at // EDGE + EDGE - 2
    rows = [load(spread, first + index, 1) for index in range(STRIP // EDGE)]
    return [
        jnp.concatenate([jnp.broadcast_to(row, (EDGE, LANES)) for row in parts], axis=0)
        for parts in zip(*rows)
    ]


def cell_sums(ref, tiles, down):
    lane = iota((down, LANES), 1)

    def some(step, total):
        for t in (2 * step, 2 * step + 1):
            picked = [
                ref[t, pl.ds(2 * EDGE + k, down, stride=COARSE), :] for k in range(COARSE)
            ]
            part = sum(picked[1:], picked[0])
            for by in (1, 2, 4):
                part = part + roll(part, -by, 1)
            part = pick_lanes(part, (lane & (LANES // COARSE - 1)) * COARSE)
            total = jnp.where(lane // (LANES // COARSE) == t, part, total)
        return total

    return lax.fori_loop(0, tiles // 2, some, jnp.zeros((down, LANES), jnp.float32))


def side_lanes(has_e, has_w):
    return jnp.where(iota((STRIP, LANES), 1) < HALF, has_e, has_w)


def mask_rows(ref, has_n, has_s):
    last = ref.shape[1] - 2 * EDGE
    for at, flag in ((EDGE, has_n), (last, has_s)):
        ref[:, at : at + EDGE, :] = ref[:, at : at + EDGE, :] * flag


def clear_pads(*refs):
    empty = jnp.zeros((refs[0].shape[0], EDGE, LANES), jnp.float32)
    for ref in refs:
        ref[:, :EDGE, :] = empty
        ref[:, ref.shape[1] - EDGE :, :] = empty


def product_sum_rows(one, two, count):
    total = one[0] * two[0]
    for t in range(1, count):
        total = total + one[t] * two[t]
    return total


def product_sum(one, two, count, flags=None):
    return fold(product_sum_rows(one, two, count), flags)


def fold(total, flags=None):
    parts = [total[at : at + EDGE] for at in range(0, total.shape[0], EDGE)]
    if flags is not None:
        parts = [part * flag for part, flag in zip(parts, flags)]
    return sum(parts[1:], parts[0])


def sweep(first, last, body, carry):
    width = GROUP * STRIP
    steps = -(-(last - first) // width)

    def work(index, carry):
        start = first + index * width
        at = pl.multiple_of(jnp.minimum(start, last - width), EDGE)
        pending = []
        for by in range(0, width, STRIP):
            stores, carry = body(at + by, start, carry)
            pending += [(ref, at + by, strip) for ref, strip in stores]
        for ref, row, strip in pending:
            store(ref, row, strip)
        return carry

    return lax.fori_loop(0, steps, work, carry)


def jacobi(source, table, work):
    window = source.shape[0]
    source = table[0] * source

    def once(index, iterate):
        rows_ref = work.at[index % 2]
        for half in range(2):
            rows_ref[half, EDGE : EDGE + window, :] = iterate[
                :, half * LANES : (half + 1) * LANES
            ]
        above, below = [
            jnp.concatenate(
                [rows_ref[half, EDGE + by : EDGE + by + window, :] for half in range(2)], axis=1
            )
            for by in (-1, 1)
        ]
        across = table[1] * roll(iterate, -1, 1) + table[2] * roll(iterate, 1, 1)
        along = table[3] * below + table[4] * above
        return ((1.0 - OMEGA) * iterate + source) + (across + along)

    return lax.fori_loop(0, SWEEPS - 1, once, source)


def clear_work(work):
    for buffer in range(2):
        clear_pads(work.at[buffer])


def in_pair_order(at, for_before, for_after):
    even = at % 2 == 0
    if callable(for_before):
        return (
            lambda index: jnp.where(even, for_after(index), for_before(index)),
            lambda index: jnp.where(even, for_before(index), for_after(index)),
        )
    return jnp.where(even, for_after, for_before), jnp.where(even, for_before, for_after)


def reader(tiles_here, refs, scratch, obs, cond, down):
    obs_in, class_in, weight_in, taps_in = refs
    classes, weights, taps, sums, obs_sem, class_sem, small_sem = scratch
    own = pl.ds(2 * EDGE, down * COARSE)
    small = [
        pltpu.make_async_copy(weight_in, weights, small_sem.at[0]),
        pltpu.make_async_copy(taps_in, taps, small_sem.at[1]),
    ]
    moves = []
    for slot, t in enumerate(tiles_here):
        lanes = pl.ds(t * LANES, LANES)
        moves.append(
            (
                pltpu.make_async_copy(class_in.at[:, lanes], classes.at[slot], class_sem.at[slot]),
                pltpu.make_async_copy(
                    obs_in.at[:, lanes], obs.at[slot, own, :], obs_sem.at[slot]
                ),
            )
        )
    for copy in small:
        copy.start()
    for pair in moves:
        for copy in pair:
            copy.start()
    sums[...] = jnp.zeros_like(sums)

    def settle(slot):
        if slot == 0:
            for copy in small:
                copy.wait()
        for copy in moves[slot]:
            copy.wait()
        values = [0.5 * weights[class_id] for class_id in range(CLASSES)]
        kind = classes[slot]
        cond[slot, own, :] = jnp.where(
            kind < 2,
            jnp.where(kind == 0, values[0], values[1]),
            jnp.where(kind == 2, values[2], values[3]),
        )
        for which, ref in enumerate((obs, cond)):
            picked = [
                ref[slot, pl.ds(2 * EDGE + k, down, stride=COARSE), :] for k in range(COARSE)
            ]
            cells = slice(2 * EDGE, 2 * EDGE + down)
            sums[3 * which, slot, cells, :] = sum(picked[1:], picked[0])
            sums[3 * which + 1, slot, cells, :] = picked[0]
            sums[3 * which + 2, slot, cells, :] = picked[-1]

    return settle


def reader_scratch(tiles, height, window, class_weights, taps):
    return [
        pltpu.VMEM((tiles, height, LANES), jnp.int32),
        pltpu.SMEM(class_weights.shape, jnp.float32),
        pltpu.SMEM(taps.shape, jnp.float32),
        pltpu.VMEM((6, tiles + 1, window + 2 * EDGE, LANES), jnp.float32),
        pltpu.SemaphoreType.DMA((tiles,)),
        pltpu.SemaphoreType.DMA((tiles,)),
        pltpu.SemaphoreType.DMA((2,)),
    ]


def coarse_parts(sums, taps, matrix):
    window = sums.shape[2] - 2 * EDGE
    whole = lambda index, by=0: wide(sums.at[index], EDGE + by, window)
    full = whole(0)
    by_tap = [full - whole(1) + whole(1, 1), full, full - whole(2) + whole(2, -1)]
    across = [sum(taps[a][b] * by_tap[a] for a in range(3)) for b in range(3)]
    source = across[1] + roll(across[0], -1, 1) + roll(across[2], 1, 1)
    full = whole(3)
    last = (iota(full.shape, 1) & (COARSE - 1)) == COARSE - 1
    east = jnp.where(last, full + roll(full, -1, 1), 0.0)
    south = whole(5) + whole(4, 1)
    cells = split_dot(jnp.concatenate([source, east, south], axis=0), matrix)
    source, east, south = cells[:window], cells[window : 2 * window], cells[2 * window :]
    around = east + roll(east, 1, 1) + south + roll(south, 1, 0)
    return [source, east, south, around]


def edge_kernel(tiles, down, *refs):
    arguments, (send_a, send_b), (obs, cond, message, *scratch) = refs[:4], refs[4:6], refs[6:]
    height = down * COARSE
    halves = height // LANES
    window = down + 2 * EDGE
    settle = reader((0, tiles - 1), arguments, scratch, obs, cond, down)
    matrix = gather_matrix(2)
    for slot, begin_row in ((0, 0), (1, LANES - EDGE)):
        settle(slot)
        for which, ref in enumerate((obs, cond)):
            turned = jnp.transpose(ref[slot, 2 * EDGE : 2 * EDGE + height, :])
            turned = turned[begin_row : begin_row + EDGE]
            for half in range(halves):
                at = (which * halves + half) * EDGE
                message[slot, at : at + EDGE, :] = turned[:, half * LANES : (half + 1) * LANES]
    parts = coarse_parts(scratch[3], read_taps(scratch[2]), matrix)
    spare = jnp.zeros((2 * LANES - 4 * window, 2 * LANES), jnp.float32)
    stack = jnp.concatenate(parts + [spare], axis=0)
    left = jnp.transpose(stack[:, :LANES])
    right = jnp.transpose(stack[:, LANES:])
    base = 2 * halves * EDGE
    past = 2 * LANES // COARSE
    for slot, pieces in (
        (0, (left[:EDGE], right[LANES - EDGE :])),
        (1, (left[past - EDGE : past], left[past : past + EDGE])),
    ):
        for index, piece in enumerate(pieces):
            for half in range(2):
                at = base + (2 * index + half) * EDGE
                message[slot, at : at + EDGE, :] = piece[:, half * LANES : (half + 1) * LANES]
    send_a[...], send_b[...] = in_pair_order(place()[0], message[0], message[1])


def edge(observed, class_map, class_weights, taps):
    height, breadth = observed.shape
    tiles, down = breadth // LANES, height // COARSE
    window = down + 2 * EDGE
    field = (3, height + 4 * EDGE, LANES)
    strip = ((2 * (height // LANES) + 4) * EDGE, LANES)
    return pl.pallas_call(
        functools.partial(edge_kernel, tiles, down),
        in_specs=[HBM] * 4,
        out_specs=[VMEM] * 2,
        out_shape=floats(strip, strip),
        scratch_shapes=[
            pltpu.VMEM(field, jnp.float32),
            pltpu.VMEM(field, jnp.float32),
            pltpu.VMEM((2,) + strip, jnp.float32),
        ]
        + reader_scratch(2, height, window, class_weights, taps),
        compiler_params=params(),
        name="pack_east_west",
    )(*[in_hbm(array) for array in (observed, class_map, class_weights, taps)])


def pack_kernel(tiles, down, *refs):
    arguments, (obs, cond, coarse_ref), scratch = refs[:4], refs[5:8], refs[8:]
    settle = reader(range(tiles), arguments, scratch, obs, cond, down)
    matrix = gather_matrix(tiles)
    for t in range(tiles):
        settle(t)
    for index, part in enumerate(coarse_parts(scratch[3], read_taps(scratch[2]), matrix)):
        coarse_ref[index] = part


def pack(observed, class_map, class_weights, taps, after):
    height, breadth = observed.shape
    tiles, down = breadth // LANES, height // COARSE
    window = down + 2 * EDGE
    field = (tiles + 1, height + 4 * EDGE, LANES)
    pixels = height * breadth
    return pl.pallas_call(
        functools.partial(pack_kernel, tiles, down),
        in_specs=[HBM] * 4 + [VMEM],
        out_specs=[VMEM] * 3,
        out_shape=floats(field, field, (4, window, 2 * LANES)),
        scratch_shapes=reader_scratch(tiles, height, window, class_weights, taps),
        compiler_params=params(),
        cost_estimate=pl.CostEstimate(
            flops=20 * pixels, bytes_accessed=16 * pixels, transcendentals=0
        ),
        name="pack_all",
    )(*[in_hbm(array) for array in (observed, class_map, class_weights, taps)], after)


def merge_sides(parts):
    block = iota((EDGE, LANES), 1) // (2 * EDGE)
    merged = jnp.zeros((EDGE, LANES), jnp.float32)
    for index, part in enumerate(parts):
        merged = jnp.where(block == index, roll(part, (2 * index + 1) * EDGE, 1), merged)
    return merged


def split_sides(merged, count):
    lane = iota((EDGE, LANES), 1)
    outer = (lane < EDGE) | (lane >= LANES - EDGE)
    return [
        jnp.where(outer, roll(merged, -(2 * index + 1) * EDGE, 1), 0.0) for index in range(count)
    ]


def middle_kernel(
    tiles,
    down,
    got_b,
    got_a,
    coarse_in,
    obs_in,
    cond_in,
    obs,
    cond,
    coarse_ref,
    send_a,
    send_b,
    message,
):
    height = down * COARSE
    halves = height // LANES
    at_col, at_row, _, _ = place()
    from_e, from_w = in_pair_order(at_col, got_b[...], got_a[...])
    gap = jnp.zeros((LANES - 2 * EDGE, LANES), jnp.float32)

    def turned(low, high):
        return jnp.transpose(jnp.concatenate([low, gap, high], axis=0))

    for which, field in enumerate((obs, cond)):
        for half in range(halves):
            at = (which * halves + half) * EDGE
            begin_row = 2 * EDGE + half * LANES
            field[tiles, begin_row : begin_row + LANES, :] = turned(
                from_e[at : at + EDGE], from_w[at : at + EDGE]
            )
    base = 2 * halves * EDGE

    def piece(strip, index, half):
        at = base + (2 * index + half) * EDGE
        return strip[at : at + EDGE]

    left = [turned(piece(from_w, 1, half), piece(from_e, 1, half)) for half in range(2)]
    right = [turned(piece(from_e, 0, half), piece(from_w, 0, half)) for half in range(2)]
    left = jnp.concatenate(left, axis=0)
    right = jnp.concatenate(right, axis=0)
    window = down + 2 * EDGE
    for index in range(4):
        rows = slice(index * window, (index + 1) * window)
        coarse_ref[index, :, :LANES] = coarse_in[index, :, :LANES] + left[rows]
        coarse_ref[index, :, LANES:] = coarse_in[index, :, LANES:] + right[rows]
    fields = (obs, cond)
    for slot, begin_row, first_row, over_row in (
        (0, 2 * EDGE, EDGE, EDGE - 1),
        (1, EDGE + height, window - 2 * EDGE, window - EDGE),
    ):
        pieces = [field[t, begin_row : begin_row + EDGE, :] for field in fields for t in range(tiles)]
        rows = slice(first_row, first_row + EDGE)
        pieces += [coarse_ref[index, rows, :LANES] for index in range(4)]
        beyond = [coarse_ref[index, rows, LANES:] for index in range(4)]
        beyond += [field[tiles, begin_row : begin_row + EDGE, :] for field in fields]
        pieces.append(merge_sides(beyond))
        pieces.append(
            jnp.concatenate(
                [
                    coarse_ref[index, over_row : over_row + 1, half * LANES : (half + 1) * LANES]
                    for index in range(4)
                    for half in range(2)
                ],
                axis=0,
            )
        )
        for index, piece in enumerate(pieces):
            message[slot, index] = piece
    send_a[...], send_b[...] = in_pair_order(at_row, message[0], message[1])


def middle(got_a, got_b, coarse, obs, cond):
    tiles, height = obs.shape[0] - 1, obs.shape[1] - 4 * EDGE
    down = height // COARSE
    long = (2 * tiles + 6, EDGE, LANES)
    return pl.pallas_call(
        functools.partial(middle_kernel, tiles, down),
        in_specs=[VMEM] * 5,
        out_specs=[VMEM] * 5,
        out_shape=floats(obs.shape, cond.shape, coarse.shape, long, long),
        input_output_aliases={3: 0, 4: 1},
        scratch_shapes=[pltpu.VMEM((2,) + long, jnp.float32)],
        compiler_params=params(),
        name="pack_north_south",
    )(got_b, got_a, coarse, obs, cond)


def inner_kernel(taps, obs, cond, res_ref, east_ref, south_ref, inv_ref, u_ref, dot_ref):
    _, _, has_e, has_w = has_sides()
    clear_pads(east_ref, south_ref)
    taps = read_taps(taps)
    sides = side_lanes(has_e, has_w)

    tiles = obs.shape[0] - 1

    def work(at, start, total):
        fields = begin(obs, cond, at, taps, sides)
        flags = [jnp.where(at + by >= start, 1.0, 0.0) for by in range(0, STRIP, EDGE)]
        total = total + product_sum(fields[3], fields[4], tiles, flags)
        return list(zip((east_ref, south_ref, inv_ref, res_ref, u_ref), fields)), total

    nothing = jnp.zeros((EDGE, LANES), jnp.float32)
    dot_ref[...] = sweep(3 * EDGE, obs.shape[1] - 3 * EDGE, work, nothing)


def inner(taps, obs, cond):
    field = obs.shape
    pixels = field[0] * field[1] * field[2]
    return pl.pallas_call(
        inner_kernel,
        in_specs=[SMEM] + [VMEM] * 2,
        out_specs=[VMEM] * 6,
        out_shape=floats(field, field, field, field, field, (EDGE, LANES)),
        compiler_params=params(),
        cost_estimate=pl.CostEstimate(
            flops=45 * pixels, bytes_accessed=24 * pixels, transcendentals=0
        ),
        name="inner_strips",
    )(taps, obs, cond)


def first_kernel(
    tiles,
    down,
    taps,
    obs_in,
    cond_in,
    res_in,
    east_in,
    south_in,
    inv_in,
    u_in,
    got_b,
    got_a,
    coarse_in,
    dot_in,
    obs,
    cond,
    res_ref,
    east_ref,
    south_ref,
    inv_ref,
    u_ref,
    p_ref,
    q_ref,
    table_ref,
    own_ref,
    chunk_ref,
    dots_ref,
    image,
    spread,
    work,
):
    height = down * COARSE
    window = down + 2 * EDGE
    at_col, at_row, n_cols, n_rows = place()
    has_n, has_s, has_e, has_w = has_sides()
    clear_pads(obs, cond, p_ref, image)
    clear_work(work)
    from_s, from_n = in_pair_order(
        at_row, lambda index: got_b[index], lambda index: got_a[index]
    )

    for which, field in enumerate((obs, cond)):
        for t in range(tiles):
            field[t, EDGE : 2 * EDGE, :] = from_n(which * tiles + t)
            field[t, 2 * EDGE + height : 3 * EDGE + height, :] = from_s(which * tiles + t)
    sides_n, sides_s = [split_sides(strip(2 * tiles + 4), 6) for strip in (from_n, from_s)]
    for which, field in enumerate((obs, cond)):
        field[tiles, EDGE : 2 * EDGE, :] = sides_n[4 + which]
        field[tiles, 2 * EDGE + height : 3 * EDGE + height, :] = sides_s[4 + which]

    edge_row = iota((EDGE, 2 * LANES), 0)

    def joined(index):
        def over(strip, row):
            line = [
                jnp.broadcast_to(
                    strip((2 * tiles + 5, pl.ds(2 * index + half, 1))), (EDGE, LANES)
                )
                for half in range(2)
            ]
            return jnp.where(edge_row == row, jnp.concatenate(line, axis=1), 0.0)

        def rows(strip, beyond):
            return jnp.concatenate([strip(2 * tiles + index), beyond[index]], axis=1)

        parts = [coarse_in[index, at : at + EDGE, :] for at in range(0, window, EDGE)]
        parts[0] = parts[0] + rows(from_n, sides_n)
        parts[1] = parts[1] + over(from_n, 0)
        parts[-2] = parts[-2] + over(from_s, EDGE - 1)
        parts[-1] = parts[-1] + rows(from_s, sides_s)
        return jnp.concatenate(parts, axis=0)

    source, east, south, around = [joined(index) for index in range(4)]
    row = iota(source.shape, 0)
    lane = iota(source.shape, 1)
    inside = jnp.where(row < EDGE, has_n, jnp.where(row < window - EDGE, 1.0, has_s))
    inside = inside * jnp.where(
        lane < LANES, 1.0, jnp.where(lane < LANES + HALF, has_e, has_w)
    )
    taps = read_taps(taps)
    taps_sum = tap_total(taps, 1)
    factor = inside * OMEGA / (COARSE * COARSE * taps_sum * taps_sum + around)
    weights = (east, roll(east, 1, 1), south, roll(south, 1, 0))
    table = [factor] + [factor * weight for weight in weights]
    for index, part in enumerate(table):
        table_ref[index] = part
    sides = side_lanes(has_e, has_w)
    half = iota((STRIP, LANES), 0) // EDGE

    def ends(index, total):
        at = pl.multiple_of(EDGE + index * height, EDGE)
        fields = begin(obs, cond, at, taps, sides)
        own = jnp.where(half == index, 0.0, 1.0)
        total = total + fold(own * product_sum_rows(fields[3], fields[4], tiles))
        flag = jnp.where(half == index, jnp.where(index == 0, has_n, has_s), 1.0)
        inverse, start = [[part * flag for part in fields[which]] for which in (2, 4)]
        fields = (*fields[:2], inverse, fields[3], start)
        for ref, strip in zip((east_ref, south_ref, inv_ref, res_ref, u_ref), fields):
            store(ref, at, strip)
        return total

    total = lax.fori_loop(0, 2, ends, dot_in[...])
    cells = jacobi(source, table_ref, work)
    spread_cells(cells, spread)
    inner_cells = slice(EDGE, EDGE + down)
    total = total + fold(source[inner_cells, :LANES] * cells[inner_cells, :LANES])
    dots_ref[0] = total

    def flags(at, start):
        rows = [at + by for by in range(0, STRIP, EDGE)]
        first_row = jnp.maximum(start, 2 * EDGE)
        return [
            jnp.where((row >= first_row) & (row < 2 * EDGE + height), 1.0, 0.0) for row in rows
        ]

    def begin_p(at, _, carry):
        start, cells = load(u_ref, at), cells_at(spread, at)
        return [(p_ref, [start[t] + cells[t] for t in range(tiles + 1)])], carry

    def blur(at, _, carry):
        strip = conv(p_ref, at, taps, False)
        strip[tiles] = strip[tiles] * sides
        return [(image, strip)], carry

    def finish(at, start, total):
        here, product = operate(p_ref, image, east_ref, south_ref, at, taps)
        return [(q_ref, product)], total + product_sum(here, product, tiles, flags(at, start))

    nothing = jnp.zeros((EDGE, LANES), jnp.float32)
    span = (EDGE, 3 * EDGE + height)
    sweep(*span, begin_p, 0)
    sweep(*span, blur, 0)
    mask_rows(image, has_n, has_s)
    dots_ref[1] = sweep(*span, finish, nothing)

    own = cell_sums(q_ref, tiles, down)
    own_ref[...] = own
    spare = jnp.zeros((LANES - down, LANES), jnp.float32)
    turned = jnp.transpose(jnp.concatenate([own, spare], axis=0))
    chunk_ref[...] = jnp.zeros_like(chunk_ref)
    for down_by in (-1, 0, 1):
        for right_by in (-1, 0, 1):
            if down_by == 0 and right_by == 0:
                continue
            if down_by == 0:
                piece = turned[:EDGE] if right_by < 0 else turned[LANES - EDGE :]
            else:
                piece = own[:EDGE] if down_by < 0 else own[down - EDGE :]
            to_row, to_col = at_row + down_by, at_col + right_by
            there = (to_row >= 0) & (to_row < n_rows) & (to_col >= 0) & (to_col < n_cols)
            slot = jnp.where(there, to_col * n_rows + to_row, at_col * n_rows + at_row)
            chunk_ref[slot] = piece * jnp.where(there, 1.0, 0.0)


def first(taps, fields, got_a, got_b, coarse, dot):
    field = fields[0].shape
    tiles, height = field[0] - 1, field[1] - 4 * EDGE
    down = height // COARSE
    window = down + 2 * EDGE
    count = lax.axis_size("cols") * lax.axis_size("rows")
    shapes = [field] * 9 + [
        (5, window, 2 * LANES),
        (down, LANES),
        (count, EDGE, LANES),
        (2, EDGE, LANES),
    ]
    return pl.pallas_call(
        functools.partial(first_kernel, tiles, down),
        in_specs=[SMEM] + [VMEM] * 11,
        out_specs=[VMEM] * len(shapes),
        out_shape=floats(*shapes),
        input_output_aliases={index + 1: index for index in range(7)},
        scratch_shapes=[
            pltpu.VMEM(field, jnp.float32),
            pltpu.VMEM((tiles + 1, window, LANES), jnp.float32),
            pltpu.VMEM((2, 2, window + 2 * EDGE, LANES), jnp.float32),
        ],
        compiler_params=params(),
        name="first_direction",
    )(taps, *fields, got_b, got_a, coarse, dot)[2:]


def second_kernel(
    tiles,
    down,
    taps,
    got_ref,
    own_ref,
    table_ref,
    q_ref,
    east_ref,
    south_ref,
    inv_ref,
    dots_in,
    w_ref,
    v_ref,
    out_ref,
    image,
    spread,
    work,
):
    height = down * COARSE
    has_n, has_s, has_e, has_w = has_sides()
    at_col, at_row, n_cols, n_rows = place()
    me = at_col * n_rows + at_row

    def got(down_by, right_by):
        to_row, to_col = at_row + down_by, at_col + right_by
        there = (to_row >= 0) & (to_row < n_rows) & (to_col >= 0) & (to_col < n_cols)
        return got_ref[jnp.where(there, to_col * n_rows + to_row, me)]

    low = iota((EDGE, LANES), 1) < HALF
    gap = jnp.zeros((LANES - 2 * EDGE, LANES), jnp.float32)
    beside = jnp.transpose(jnp.concatenate([got(0, 1), gap, got(0, -1)], axis=0))[:down]
    source = jnp.concatenate(
        [
            jnp.concatenate([got(-1, 0), jnp.where(low, got(-1, 1), got(-1, -1))], axis=1),
            jnp.concatenate([own_ref[...], beside], axis=1),
            jnp.concatenate([got(1, 0), jnp.where(low, got(1, 1), got(1, -1))], axis=1),
        ],
        axis=0,
    )
    clear_work(work)
    spread_cells(jacobi(source, table_ref, work), spread)
    clear_pads(w_ref, image)
    sides = side_lanes(has_e, has_w)
    taps = read_taps(taps)

    def begin_w(at, start, total):
        field, inverse, cells = load(q_ref, at), load(inv_ref, at), cells_at(spread, at)
        strip = [field[t] * inverse[t] + cells[t] for t in range(tiles + 1)]
        first_row = jnp.maximum(start, 2 * EDGE)
        flags = [
            jnp.where((row >= first_row) & (row < 2 * EDGE + height), 1.0, 0.0)
            for row in [at + by for by in range(0, STRIP, EDGE)]
        ]
        return [(w_ref, strip)], total + product_sum(field, strip, tiles, flags)

    def blur(at, _, carry):
        strip = conv(w_ref, at, taps, False)
        strip[tiles] = strip[tiles] * sides
        return [(image, strip)], carry

    def finish(at, _, total):
        here, product = operate(w_ref, image, east_ref, south_ref, at, taps)
        return [(v_ref, product[:tiles])], total + product_sum(here, product, tiles)

    nothing = jnp.zeros((EDGE, LANES), jnp.float32)
    span = (EDGE, 3 * EDGE + height)
    dot_qw = sweep(*span, begin_w, nothing)
    sweep(*span, blur, 0)
    mask_rows(image, has_n, has_s)
    dot_wv = sweep(2 * EDGE, 2 * EDGE + height, finish, nothing)
    line = jnp.zeros((1, LANES), jnp.float32)
    block = iota((1, LANES), 1) // (LANES // 4)
    for index, part in enumerate((dots_in[0], dots_in[1], dot_qw, dot_wv)):
        part = jnp.sum(part, axis=0, keepdims=True)
        part = part + roll(part, LANES // 2, 1)
        part = part + roll(part, LANES // 4, 1)
        line = jnp.where(block == index, part, line)
    for index in range(out_ref.shape[0]):
        out_ref[index] = line


def second(taps, got, own, table, q, east, south, inv, dots):
    tiles, height = q.shape[0] - 1, q.shape[1] - 4 * EDGE
    down = height // COARSE
    window = down + 2 * EDGE
    count = lax.axis_size("cols") * lax.axis_size("rows")
    return pl.pallas_call(
        functools.partial(second_kernel, tiles, down),
        in_specs=[SMEM] + [VMEM] * 8,
        out_specs=[VMEM] * 3,
        out_shape=floats(q.shape, q.shape, (count, 1, LANES)),
        scratch_shapes=[
            pltpu.VMEM(q.shape, jnp.float32),
            pltpu.VMEM((tiles + 1, window, LANES), jnp.float32),
            pltpu.VMEM((2, 2, window + 2 * EDGE, LANES), jnp.float32),
        ],
        compiler_params=params(),
        name="second_direction",
    )(taps, got, own, table, q, east, south, inv, dots)


def combine_kernel(
    tiles, height, sums_ref, p_ref, w_ref, r_ref, q_ref, v_ref, sol_out, res_out, sol, res, sem
):
    line = sums_ref[0]
    for index in range(1, sums_ref.shape[0]):
        line = line + sums_ref[index]
    block = iota((1, LANES), 1) // (LANES // 4)
    pick = lambda index: jnp.sum(jnp.where(block == index, line, 0.0), axis=1, keepdims=True)
    rp, pq, qw, wv = [pick(index) for index in range(4)]
    step = rp / pq
    rp_next = step * step * qw - rp
    ratio = rp_next / rp
    lead = 1.0 + ratio
    curvature = lead * lead * pq - 2.0 * lead * step * qw + step * step * wv
    step_next = rp_next / curvature
    on_p = jnp.broadcast_to(step + step_next * lead, (CHUNK, LANES))
    on_w = jnp.broadcast_to(step_next * step, (CHUNK, LANES))

    def copies(index):
        rows = pl.ds(pl.multiple_of(index * CHUNK, CHUNK), CHUNK)
        return (
            pltpu.make_async_copy(sol.at[rows, :], sol_out.at[rows, :], sem.at[0, index]),
            pltpu.make_async_copy(res.at[rows, :], res_out.at[rows, :], sem.at[1, index]),
        )

    def work(index, _):
        at = pl.multiple_of(index * CHUNK, CHUNK)
        p, w, r, q, v = [
            load(ref, at + 2 * EDGE, CHUNK) for ref in (p_ref, w_ref, r_ref, q_ref, v_ref)
        ]
        one = [on_p * p[t] - on_w * w[t] for t in range(tiles)]
        two = [r[t] - on_p * q[t] + on_w * v[t] for t in range(tiles)]
        for t in range(tiles):
            sol[pl.ds(at, CHUNK), t * LANES : (t + 1) * LANES] = one[t]
            res[pl.ds(at, CHUNK), t * LANES : (t + 1) * LANES] = two[t]
        for copy in copies(index):
            copy.start()
        return 0

    def settle(index, _):
        for copy in copies(index):
            copy.wait()
        return 0

    lax.fori_loop(0, height // CHUNK, work, 0)
    lax.fori_loop(0, height // CHUNK, settle, 0)


def combine(sums, p, w, r, q, v):
    tiles, height = q.shape[0] - 1, q.shape[1] - 4 * EDGE
    shape = (height, tiles * LANES)
    return pl.pallas_call(
        functools.partial(combine_kernel, tiles, height),
        in_specs=[VMEM] * 6,
        out_specs=[HBM] * 2,
        out_shape=floats(shape, shape),
        scratch_shapes=[
            pltpu.VMEM(shape, jnp.float32),
            pltpu.VMEM(shape, jnp.float32),
            pltpu.SemaphoreType.DMA((2, height // CHUNK)),
        ],
        compiler_params=params(),
        name="combine",
    )(sums, p, w, r, q, v)


def exchange(send_a, send_b, axis):
    count = lax.axis_size(axis)

    def pairs(begin):
        return [
            pair for i in range(begin, count - 1, 2) for pair in ((i, i + 1), (i + 1, i))
        ]

    got_b = lax.ppermute(send_b, axis, pairs(1))
    got_a = lax.ppermute(send_a, axis, pairs(0))
    return got_a, got_b


def body(observed, class_map, class_weights, blur_kernel):
    arguments = (observed, class_map, class_weights, blur_kernel)
    send_a, send_b = edge(*arguments)
    got_a, got_b = exchange(send_a, send_b, "cols")
    obs, cond, coarse = pack(*arguments, send_a)
    obs, cond, coarse, send_a, send_b = middle(got_a, got_b, coarse, obs, cond)
    got_a, got_b = exchange(send_a, send_b, "rows")
    r, east, south, inv, u, dot = inner(blur_kernel, obs, cond)
    fields = (obs, cond, r, east, south, inv, u)
    r, east, south, inv, _, p, q, table, own, chunk, dots = first(
        blur_kernel, fields, got_a, got_b, coarse, dot
    )
    got = lax.all_to_all(chunk, AXES, 0, 0, tiled=True)
    w, v, line = second(blur_kernel, got, own, table, q, east, south, inv, dots)
    sums = lax.all_to_all(line, AXES, 0, 0, tiled=True)
    return tuple(combine(sums, p, w, r, q, v))


def solution(mesh):
    return jax.shard_map(
        body,
        mesh=mesh,
        in_specs=(P("rows", "cols"), P("rows", "cols"), P(), P()),
        out_specs=(P("rows", "cols"), P("rows", "cols")),
        check_vma=False,
    )
```

```python
import functools

import jax
import jax.numpy as jnp
from jax import lax
from jax.experimental import pallas as pl
from jax.experimental.pallas import tpu as pltpu
from jax.sharding import PartitionSpec as P

COARSE = 8
SWEEPS = 8
CLASSES = 4
OMEGA = 0.8

LANES = 128
HALF = LANES // 2
EDGE = 8
STRIP = 2 * EDGE
CHUNK = 32
AXES = ("cols", "rows")
LIMIT = 40 * 1024 * 1024


VMEM = pl.BlockSpec(memory_space=pltpu.VMEM)
SMEM = pl.BlockSpec(memory_space=pltpu.SMEM)
HBM = pl.BlockSpec(memory_space=pltpu.HBM)


def params():
    return pltpu.CompilerParams(vmem_limit_bytes=LIMIT)


def in_hbm(array):
    return pltpu.with_memory_space_constraint(array, pltpu.HBM)


def floats(*shapes):
    return [jax.ShapeDtypeStruct(shape, jnp.float32) for shape in shapes]


def place():
    at_col, at_row = lax.axis_index("cols"), lax.axis_index("rows")
    n_cols, n_rows = lax.axis_size("cols"), lax.axis_size("rows")
    return at_col, at_row, n_cols, n_rows


def has_sides():
    at_col, at_row, n_cols, n_rows = place()
    flag = lambda test: jnp.where(test, 1.0, 0.0).astype(jnp.float32)
    return (
        flag(at_row > 0),
        flag(at_row < n_rows - 1),
        flag(at_col < n_cols - 1),
        flag(at_col > 0),
    )


def iota(shape, dim):
    return lax.broadcasted_iota(jnp.int32, shape, dim)


def cell_of(pixel, tiles):
    turn = (tiles + 1) * LANES
    return jnp.where(pixel < turn - HALF, pixel >> 3, ((pixel - turn) >> 3) & (2 * LANES - 1))


def gather_matrix(tiles):
    shape = ((tiles + 1) * LANES, 2 * LANES)
    hit = cell_of(iota(shape, 0), tiles) == iota(shape, 1)
    return jnp.where(hit, 1.0, 0.0).astype(jnp.bfloat16)


def split_dot(field, matrix):
    rows = field.shape[0]
    high = field.astype(jnp.bfloat16)
    low = (field - high.astype(jnp.float32)).astype(jnp.bfloat16)
    both = jnp.dot(
        jnp.concatenate([high, low], axis=0), matrix, preferred_element_type=jnp.float32
    )
    return both[:rows] + both[rows:]


def roll(field, by, axis):
    return pltpu.roll(field, by % field.shape[axis], axis)


def load(ref, at, rows=STRIP):
    return [ref[t, pl.ds(at, rows), :] for t in range(ref.shape[0])]


def store(ref, at, strip):
    for t, part in enumerate(strip):
        ref[t, pl.ds(at, part.shape[0]), :] = part


def wide(ref, at, rows):
    return jnp.concatenate(load(ref, at, rows), axis=1)


def read_taps(taps):
    return [[taps[a, b] for b in range(3)] for a in range(3)]


def tap_total(taps, power):
    return sum(tap * tap if power == 2 else tap for line in taps for tap in line)


def from_west(strip):
    lane = iota(strip[0].shape, 1)
    turned = [roll(part, 1, 1) for part in strip]
    return [jnp.where(lane == 0, turned[t - 1], turned[t]) for t in range(len(strip))]


def from_east(strip):
    lane = iota(strip[0].shape, 1)
    turned = [roll(part, -1, 1) for part in strip]
    count = len(strip)
    return [
        jnp.where(lane == LANES - 1, turned[(t + 1) % count], turned[t]) for t in range(count)
    ]


def tap_sums(ref, at, taps, flip):
    if flip:
        taps = [line[::-1] for line in taps[::-1]]
    above, here, below = load(ref, at - 1), load(ref, at), load(ref, at + 1)
    sums = [[], [], []]
    for t in range(len(here)):
        for b in range(3):
            sums[b].append(
                taps[0][b] * above[t] + taps[1][b] * here[t] + taps[2][b] * below[t]
            )
    return sums


def conv(ref, at, taps, flip):
    sums = tap_sums(ref, at, taps, flip)
    west, east = from_west(sums[0]), from_east(sums[2])
    return [sums[1][t] + west[t] + east[t] for t in range(len(west))]


def operate(ref, image, east_ref, south_ref, at, taps):
    above, here, below = load(ref, at - 1), load(ref, at), load(ref, at + 1)
    east, south, north = load(east_ref, at), load(south_ref, at), load(south_ref, at - 1)
    sums = tap_sums(image, at, taps, True)
    span = range(len(here))
    beside = from_east(here)
    flux = [east[t] * (here[t] - beside[t]) for t in span]
    from_left = from_west([sums[0][t] - flux[t] for t in span])
    from_right = from_east(sums[2])
    return here, [
        sums[1][t]
        + flux[t]
        + from_left[t]
        + from_right[t]
        + south[t] * (here[t] - below[t])
        - north[t] * (above[t] - here[t])
        for t in span
    ]


def begin(obs, cond, at, taps, sides):
    above, here, below = load(cond, at - 1), load(cond, at), load(cond, at + 1)
    span = range(len(here))
    right = from_east(here)
    east = [here[t] + right[t] for t in span]
    west = from_west(east)
    south = [here[t] + below[t] for t in span]
    squares = tap_total(taps, 2)
    diag = [squares + east[t] + west[t] + south[t] + (here[t] + above[t]) for t in span]
    inverse = [pl.reciprocal(part, approx=True) for part in diag]
    inverse = [inverse[t] * (2.0 - diag[t] * inverse[t]) for t in span]
    inverse[-1] = inverse[-1] * sides
    residual = conv(obs, at, taps, True)
    return east, south, inverse, residual, [residual[t] * inverse[t] for t in span]


def pick_lanes(field, lanes):
    return jnp.take_along_axis(field, lanes, axis=1, mode="promise_in_bounds")


def spread_cells(cells, spread):
    tiles = spread.shape[0] - 1
    lane = iota((cells.shape[0], LANES), 1)
    for t in range(tiles):
        spread[t] = pick_lanes(cells[:, :LANES], (lane >> 3) + t * (LANES // COARSE))
    turn = jnp.where(lane < HALF, 0, LANES - LANES // COARSE)
    spread[tiles] = pick_lanes(cells[:, LANES:], (lane >> 3) + turn)


def cells_at(spread, at):
    first = at // EDGE + EDGE - 2
    rows = [load(spread, first + index, 1) for index in range(STRIP // EDGE)]
    return [
        jnp.concatenate([jnp.broadcast_to(row, (EDGE, LANES)) for row in parts], axis=0)
        for parts in zip(*rows)
    ]


def cell_sums(ref, tiles, down):
    lane = iota((down, LANES), 1)
    total = jnp.zeros((down, LANES), jnp.float32)
    for t in range(tiles):
        picked = [
            ref[t, pl.ds(2 * EDGE + k, down, stride=COARSE), :] for k in range(COARSE)
        ]
        part = sum(picked[1:], picked[0])
        for by in (1, 2, 4):
            part = part + roll(part, -by, 1)
        part = pick_lanes(part, (lane & (LANES // COARSE - 1)) * COARSE)
        total = jnp.where(lane // (LANES // COARSE) == t, part, total)
    return total


def side_lanes(has_e, has_w):
    return jnp.where(iota((STRIP, LANES), 1) < HALF, has_e, has_w)


def mask_rows(ref, has_n, has_s):
    last = ref.shape[1] - 2 * EDGE
    for at, flag in ((EDGE, has_n), (last, has_s)):
        ref[:, at : at + EDGE, :] = ref[:, at : at + EDGE, :] * flag


def clear_pads(*refs):
    empty = jnp.zeros((refs[0].shape[0], EDGE, LANES), jnp.float32)
    for ref in refs:
        ref[:, :EDGE, :] = empty
        ref[:, ref.shape[1] - EDGE :, :] = empty


def product_sum_rows(one, two, count):
    total = one[0] * two[0]
    for t in range(1, count):
        total = total + one[t] * two[t]
    return total


def product_sum(one, two, count, flags=None):
    return fold(product_sum_rows(one, two, count), flags)


def fold(total, flags=None):
    parts = [total[at : at + EDGE] for at in range(0, total.shape[0], EDGE)]
    if flags is not None:
        parts = [part * flag for part, flag in zip(parts, flags)]
    return sum(parts[1:], parts[0])


def sweep(group, first, last, body, carry):
    width = group * STRIP
    steps = -(-(last - first) // width)

    def work(index, carry):
        start = first + index * width
        at = pl.multiple_of(jnp.minimum(start, last - width), EDGE)
        pending = []
        for by in range(0, width, STRIP):
            stores, carry = body(at + by, start, carry)
            pending += [(ref, at + by, strip) for ref, strip in stores]
        for ref, row, strip in pending:
            store(ref, row, strip)
        return carry

    return lax.fori_loop(0, steps, work, carry)


def jacobi(source, table, work):
    factor, east, west, south, north = [table[index] for index in range(5)]
    window = source.shape[0]
    source = factor * source
    iterate = source
    for sweep_index in range(SWEEPS - 1):
        place_ref = work.at[sweep_index % 2]
        for half in range(2):
            place_ref[half, EDGE : EDGE + window, :] = iterate[
                :, half * LANES : (half + 1) * LANES
            ]
        above, below = [
            jnp.concatenate(
                [place_ref[half, EDGE + by : EDGE + by + window, :] for half in range(2)], axis=1
            )
            for by in (-1, 1)
        ]
        across = east * roll(iterate, -1, 1) + west * roll(iterate, 1, 1)
        along = south * below + north * above
        iterate = ((1.0 - OMEGA) * iterate + source) + (across + along)
    return iterate


def clear_work(work):
    for buffer in range(2):
        clear_pads(work.at[buffer])


def in_pair_order(at, for_before, for_after):
    even = at % 2 == 0
    if callable(for_before):
        return (
            lambda index: jnp.where(even, for_after(index), for_before(index)),
            lambda index: jnp.where(even, for_before(index), for_after(index)),
        )
    return jnp.where(even, for_after, for_before), jnp.where(even, for_before, for_after)


def reader(tiles_here, refs, scratch, obs, cond, down):
    obs_in, class_in, weight_in, taps_in = refs
    classes, weights, taps, sums, obs_sem, class_sem, small_sem = scratch
    own = pl.ds(2 * EDGE, down * COARSE)
    small = [
        pltpu.make_async_copy(weight_in, weights, small_sem.at[0]),
        pltpu.make_async_copy(taps_in, taps, small_sem.at[1]),
    ]
    moves = []
    for slot, t in enumerate(tiles_here):
        lanes = pl.ds(t * LANES, LANES)
        moves.append(
            (
                pltpu.make_async_copy(class_in.at[:, lanes], classes.at[slot], class_sem.at[slot]),
                pltpu.make_async_copy(
                    obs_in.at[:, lanes], obs.at[slot, own, :], obs_sem.at[slot]
                ),
            )
        )
    for copy in small:
        copy.start()
    for pair in moves:
        for copy in pair:
            copy.start()
    sums[...] = jnp.zeros_like(sums)

    def settle(slot):
        if slot == 0:
            for copy in small:
                copy.wait()
        for copy in moves[slot]:
            copy.wait()
        values = [0.5 * weights[class_id] for class_id in range(CLASSES)]
        kind = classes[slot]
        cond[slot, own, :] = jnp.where(
            kind < 2,
            jnp.where(kind == 0, values[0], values[1]),
            jnp.where(kind == 2, values[2], values[3]),
        )
        for which, ref in enumerate((obs, cond)):
            picked = [
                ref[slot, pl.ds(2 * EDGE + k, down, stride=COARSE), :] for k in range(COARSE)
            ]
            cells = slice(2 * EDGE, 2 * EDGE + down)
            sums[3 * which, slot, cells, :] = sum(picked[1:], picked[0])
            sums[3 * which + 1, slot, cells, :] = picked[0]
            sums[3 * which + 2, slot, cells, :] = picked[-1]

    return settle


def reader_scratch(tiles, height, window, class_weights, taps):
    return [
        pltpu.VMEM((tiles, height, LANES), jnp.int32),
        pltpu.SMEM(class_weights.shape, jnp.float32),
        pltpu.SMEM(taps.shape, jnp.float32),
        pltpu.VMEM((6, tiles + 1, window + 2 * EDGE, LANES), jnp.float32),
        pltpu.SemaphoreType.DMA((tiles,)),
        pltpu.SemaphoreType.DMA((tiles,)),
        pltpu.SemaphoreType.DMA((2,)),
    ]


def coarse_parts(sums, taps, matrix):
    window = sums.shape[2] - 2 * EDGE
    whole = lambda index, by=0: wide(sums.at[index], EDGE + by, window)
    full = whole(0)
    by_tap = [full - whole(1) + whole(1, 1), full, full - whole(2) + whole(2, -1)]
    across = [sum(taps[a][b] * by_tap[a] for a in range(3)) for b in range(3)]
    source = across[1] + roll(across[0], -1, 1) + roll(across[2], 1, 1)
    full = whole(3)
    last = (iota(full.shape, 1) & (COARSE - 1)) == COARSE - 1
    east = jnp.where(last, full + roll(full, -1, 1), 0.0)
    south = whole(5) + whole(4, 1)
    cells = split_dot(jnp.concatenate([source, east, south], axis=0), matrix)
    source, east, south = cells[:window], cells[window : 2 * window], cells[2 * window :]
    around = east + roll(east, 1, 1) + south + roll(south, 1, 0)
    return [source, east, south, around]


def edge_kernel(tiles, down, *refs):
    arguments, (send_a, send_b), (obs, cond, message, *scratch) = refs[:4], refs[4:6], refs[6:]
    height = down * COARSE
    halves = height // LANES
    window = down + 2 * EDGE
    settle = reader((0, tiles - 1), arguments, scratch, obs, cond, down)
    matrix = gather_matrix(2)
    for slot, begin_row in ((0, 0), (1, LANES - EDGE)):
        settle(slot)
        for which, ref in enumerate((obs, cond)):
            turned = jnp.transpose(ref[slot, 2 * EDGE : 2 * EDGE + height, :])
            turned = turned[begin_row : begin_row + EDGE]
            for half in range(halves):
                at = (which * halves + half) * EDGE
                message[slot, at : at + EDGE, :] = turned[:, half * LANES : (half + 1) * LANES]
    parts = coarse_parts(scratch[3], read_taps(scratch[2]), matrix)
    spare = jnp.zeros((2 * LANES - 4 * window, 2 * LANES), jnp.float32)
    stack = jnp.concatenate(parts + [spare], axis=0)
    left = jnp.transpose(stack[:, :LANES])
    right = jnp.transpose(stack[:, LANES:])
    base = 2 * halves * EDGE
    past = 2 * LANES // COARSE
    for slot, pieces in (
        (0, (left[:EDGE], right[LANES - EDGE :])),
        (1, (left[past - EDGE : past], left[past : past + EDGE])),
    ):
        for index, piece in enumerate(pieces):
            for half in range(2):
                at = base + (2 * index + half) * EDGE
                message[slot, at : at + EDGE, :] = piece[:, half * LANES : (half + 1) * LANES]
    send_a[...], send_b[...] = in_pair_order(place()[0], message[0], message[1])


def edge(observed, class_map, class_weights, taps):
    height, breadth = observed.shape
    tiles, down = breadth // LANES, height // COARSE
    window = down + 2 * EDGE
    field = (3, height + 4 * EDGE, LANES)
    strip = ((2 * (height // LANES) + 4) * EDGE, LANES)
    return pl.pallas_call(
        functools.partial(edge_kernel, tiles, down),
        in_specs=[HBM] * 4,
        out_specs=[VMEM] * 2,
        out_shape=floats(strip, strip),
        scratch_shapes=[
            pltpu.VMEM(field, jnp.float32),
            pltpu.VMEM(field, jnp.float32),
            pltpu.VMEM((2,) + strip, jnp.float32),
        ]
        + reader_scratch(2, height, window, class_weights, taps),
        compiler_params=params(),
        name="pack_east_west",
    )(*[in_hbm(array) for array in (observed, class_map, class_weights, taps)])


def pack_kernel(tiles, down, *refs):
    arguments, (obs, cond, coarse_ref), scratch = refs[:4], refs[5:8], refs[8:]
    settle = reader(range(tiles), arguments, scratch, obs, cond, down)
    matrix = gather_matrix(tiles)
    for t in range(tiles):
        settle(t)
    for index, part in enumerate(coarse_parts(scratch[3], read_taps(scratch[2]), matrix)):
        coarse_ref[index] = part


def pack(observed, class_map, class_weights, taps, after):
    height, breadth = observed.shape
    tiles, down = breadth // LANES, height // COARSE
    window = down + 2 * EDGE
    field = (tiles + 1, height + 4 * EDGE, LANES)
    pixels = height * breadth
    return pl.pallas_call(
        functools.partial(pack_kernel, tiles, down),
        in_specs=[HBM] * 4 + [VMEM],
        out_specs=[VMEM] * 3,
        out_shape=floats(field, field, (4, window, 2 * LANES)),
        scratch_shapes=reader_scratch(tiles, height, window, class_weights, taps),
        compiler_params=params(),
        cost_estimate=pl.CostEstimate(
            flops=20 * pixels, bytes_accessed=16 * pixels, transcendentals=0
        ),
        name="pack_all",
    )(*[in_hbm(array) for array in (observed, class_map, class_weights, taps)], after)


def merge_sides(parts):
    block = iota((EDGE, LANES), 1) // (2 * EDGE)
    merged = jnp.zeros((EDGE, LANES), jnp.float32)
    for index, part in enumerate(parts):
        merged = jnp.where(block == index, roll(part, (2 * index + 1) * EDGE, 1), merged)
    return merged


def split_sides(merged, count):
    lane = iota((EDGE, LANES), 1)
    outer = (lane < EDGE) | (lane >= LANES - EDGE)
    return [
        jnp.where(outer, roll(merged, -(2 * index + 1) * EDGE, 1), 0.0) for index in range(count)
    ]


def middle_kernel(
    tiles,
    down,
    got_b,
    got_a,
    coarse_in,
    obs_in,
    cond_in,
    obs,
    cond,
    coarse_ref,
    send_a,
    send_b,
    message,
):
    height = down * COARSE
    halves = height // LANES
    at_col, at_row, _, _ = place()
    from_e, from_w = in_pair_order(at_col, got_b[...], got_a[...])
    gap = jnp.zeros((LANES - 2 * EDGE, LANES), jnp.float32)

    def turned(low, high):
        return jnp.transpose(jnp.concatenate([low, gap, high], axis=0))

    for which, field in enumerate((obs, cond)):
        for half in range(halves):
            at = (which * halves + half) * EDGE
            begin_row = 2 * EDGE + half * LANES
            field[tiles, begin_row : begin_row + LANES, :] = turned(
                from_e[at : at + EDGE], from_w[at : at + EDGE]
            )
    base = 2 * halves * EDGE

    def piece(strip, index, half):
        at = base + (2 * index + half) * EDGE
        return strip[at : at + EDGE]

    left = [turned(piece(from_w, 1, half), piece(from_e, 1, half)) for half in range(2)]
    right = [turned(piece(from_e, 0, half), piece(from_w, 0, half)) for half in range(2)]
    left = jnp.concatenate(left, axis=0)
    right = jnp.concatenate(right, axis=0)
    window = down + 2 * EDGE
    for index in range(4):
        rows = slice(index * window, (index + 1) * window)
        coarse_ref[index, :, :LANES] = coarse_in[index, :, :LANES] + left[rows]
        coarse_ref[index, :, LANES:] = coarse_in[index, :, LANES:] + right[rows]
    fields = (obs, cond)
    for slot, begin_row, first_row, over_row in (
        (0, 2 * EDGE, EDGE, EDGE - 1),
        (1, EDGE + height, window - 2 * EDGE, window - EDGE),
    ):
        pieces = [field[t, begin_row : begin_row + EDGE, :] for field in fields for t in range(tiles)]
        rows = slice(first_row, first_row + EDGE)
        pieces += [coarse_ref[index, rows, :LANES] for index in range(4)]
        beyond = [coarse_ref[index, rows, LANES:] for index in range(4)]
        beyond += [field[tiles, begin_row : begin_row + EDGE, :] for field in fields]
        pieces.append(merge_sides(beyond))
        pieces.append(
            jnp.concatenate(
                [
                    coarse_ref[index, over_row : over_row + 1, half * LANES : (half + 1) * LANES]
                    for index in range(4)
                    for half in range(2)
                ],
                axis=0,
            )
        )
        for index, piece in enumerate(pieces):
            message[slot, index] = piece
    send_a[...], send_b[...] = in_pair_order(at_row, message[0], message[1])


def middle(got_a, got_b, coarse, obs, cond):
    tiles, height = obs.shape[0] - 1, obs.shape[1] - 4 * EDGE
    down = height // COARSE
    long = (2 * tiles + 6, EDGE, LANES)
    return pl.pallas_call(
        functools.partial(middle_kernel, tiles, down),
        in_specs=[VMEM] * 5,
        out_specs=[VMEM] * 5,
        out_shape=floats(obs.shape, cond.shape, coarse.shape, long, long),
        input_output_aliases={3: 0, 4: 1},
        scratch_shapes=[pltpu.VMEM((2,) + long, jnp.float32)],
        compiler_params=params(),
        name="pack_north_south",
    )(got_b, got_a, coarse, obs, cond)


def inner_kernel(taps, obs, cond, res_ref, east_ref, south_ref, inv_ref, u_ref, dot_ref):
    _, _, has_e, has_w = has_sides()
    clear_pads(east_ref, south_ref)
    taps = read_taps(taps)
    sides = side_lanes(has_e, has_w)

    tiles = obs.shape[0] - 1

    def work(at, start, total):
        fields = begin(obs, cond, at, taps, sides)
        flags = [jnp.where(at + by >= start, 1.0, 0.0) for by in range(0, STRIP, EDGE)]
        total = total + product_sum(fields[3], fields[4], tiles, flags)
        return list(zip((east_ref, south_ref, inv_ref, res_ref, u_ref), fields)), total

    nothing = jnp.zeros((EDGE, LANES), jnp.float32)
    dot_ref[...] = sweep(5, 3 * EDGE, obs.shape[1] - 3 * EDGE, work, nothing)


def inner(taps, obs, cond):
    field = obs.shape
    pixels = field[0] * field[1] * field[2]
    return pl.pallas_call(
        inner_kernel,
        in_specs=[SMEM] + [VMEM] * 2,
        out_specs=[VMEM] * 6,
        out_shape=floats(field, field, field, field, field, (EDGE, LANES)),
        compiler_params=params(),
        cost_estimate=pl.CostEstimate(
            flops=45 * pixels, bytes_accessed=24 * pixels, transcendentals=0
        ),
        name="inner_strips",
    )(taps, obs, cond)


def first_kernel(
    tiles,
    down,
    taps,
    obs_in,
    cond_in,
    res_in,
    east_in,
    south_in,
    inv_in,
    u_in,
    got_b,
    got_a,
    coarse_in,
    dot_in,
    obs,
    cond,
    res_ref,
    east_ref,
    south_ref,
    inv_ref,
    u_ref,
    p_ref,
    q_ref,
    table_ref,
    own_ref,
    chunk_ref,
    dots_ref,
    image,
    spread,
    work,
):
    height = down * COARSE
    window = down + 2 * EDGE
    at_col, at_row, n_cols, n_rows = place()
    has_n, has_s, has_e, has_w = has_sides()
    clear_pads(obs, cond, p_ref, image)
    clear_work(work)
    from_s, from_n = in_pair_order(
        at_row, lambda index: got_b[index], lambda index: got_a[index]
    )

    for which, field in enumerate((obs, cond)):
        for t in range(tiles):
            field[t, EDGE : 2 * EDGE, :] = from_n(which * tiles + t)
            field[t, 2 * EDGE + height : 3 * EDGE + height, :] = from_s(which * tiles + t)
    sides_n, sides_s = [split_sides(strip(2 * tiles + 4), 6) for strip in (from_n, from_s)]
    for which, field in enumerate((obs, cond)):
        field[tiles, EDGE : 2 * EDGE, :] = sides_n[4 + which]
        field[tiles, 2 * EDGE + height : 3 * EDGE + height, :] = sides_s[4 + which]

    edge_row = iota((EDGE, 2 * LANES), 0)

    def joined(index):
        def over(strip, row):
            line = [
                jnp.broadcast_to(
                    strip((2 * tiles + 5, pl.ds(2 * index + half, 1))), (EDGE, LANES)
                )
                for half in range(2)
            ]
            return jnp.where(edge_row == row, jnp.concatenate(line, axis=1), 0.0)

        def rows(strip, beyond):
            return jnp.concatenate([strip(2 * tiles + index), beyond[index]], axis=1)

        parts = [coarse_in[index, at : at + EDGE, :] for at in range(0, window, EDGE)]
        parts[0] = parts[0] + rows(from_n, sides_n)
        parts[1] = parts[1] + over(from_n, 0)
        parts[-2] = parts[-2] + over(from_s, EDGE - 1)
        parts[-1] = parts[-1] + rows(from_s, sides_s)
        return jnp.concatenate(parts, axis=0)

    source, east, south, around = [joined(index) for index in range(4)]
    row = iota(source.shape, 0)
    lane = iota(source.shape, 1)
    inside = jnp.where(row < EDGE, has_n, jnp.where(row < window - EDGE, 1.0, has_s))
    inside = inside * jnp.where(
        lane < LANES, 1.0, jnp.where(lane < LANES + HALF, has_e, has_w)
    )
    taps = read_taps(taps)
    taps_sum = tap_total(taps, 1)
    factor = inside * OMEGA / (COARSE * COARSE * taps_sum * taps_sum + around)
    weights = (east, roll(east, 1, 1), south, roll(south, 1, 0))
    table = [factor] + [factor * weight for weight in weights]
    for index, part in enumerate(table):
        table_ref[index] = part
    sides = side_lanes(has_e, has_w)
    half = iota((STRIP, LANES), 0) // EDGE
    pending = []
    total = dot_in[...]
    for index, known in ((0, has_n), (1, has_s)):
        at = EDGE + index * height
        fields = begin(obs, cond, at, taps, sides)
        own = jnp.where(half == index, 0.0, 1.0)
        total = total + fold(own * product_sum_rows(fields[3], fields[4], tiles))
        flag = jnp.where(half == index, known, 1.0)
        inverse, start = [[part * flag for part in fields[index]] for index in (2, 4)]
        fields = (*fields[:2], inverse, fields[3], start)
        pending += [
            (ref, at, strip)
            for ref, strip in zip((east_ref, south_ref, inv_ref, res_ref, u_ref), fields)
        ]
    cells = jacobi(source, table, work)
    spread_cells(cells, spread)
    inner_cells = slice(EDGE, EDGE + down)
    total = total + fold(source[inner_cells, :LANES] * cells[inner_cells, :LANES])
    dots_ref[0] = total
    for ref, at, strip in pending:
        store(ref, at, strip)

    def flags(at, start):
        rows = [at + by for by in range(0, STRIP, EDGE)]
        first_row = jnp.maximum(start, 2 * EDGE)
        return [
            jnp.where((row >= first_row) & (row < 2 * EDGE + height), 1.0, 0.0) for row in rows
        ]

    def begin_p(at, _, carry):
        start, cells = load(u_ref, at), cells_at(spread, at)
        return [(p_ref, [start[t] + cells[t] for t in range(tiles + 1)])], carry

    def blur(at, _, carry):
        strip = conv(p_ref, at, taps, False)
        strip[tiles] = strip[tiles] * sides
        return [(image, strip)], carry

    def finish(at, start, total):
        here, product = operate(p_ref, image, east_ref, south_ref, at, taps)
        return [(q_ref, product)], total + product_sum(here, product, tiles, flags(at, start))

    nothing = jnp.zeros((EDGE, LANES), jnp.float32)
    span = (EDGE, 3 * EDGE + height)
    sweep(6, *span, begin_p, 0)
    sweep(6, *span, blur, 0)
    mask_rows(image, has_n, has_s)
    dots_ref[1] = sweep(6, *span, finish, nothing)

    own = cell_sums(q_ref, tiles, down)
    own_ref[...] = own
    spare = jnp.zeros((LANES - down, LANES), jnp.float32)
    turned = jnp.transpose(jnp.concatenate([own, spare], axis=0))
    chunk_ref[...] = jnp.zeros_like(chunk_ref)
    for down_by in (-1, 0, 1):
        for right_by in (-1, 0, 1):
            if down_by == 0 and right_by == 0:
                continue
            if down_by == 0:
                piece = turned[:EDGE] if right_by < 0 else turned[LANES - EDGE :]
            else:
                piece = own[:EDGE] if down_by < 0 else own[down - EDGE :]
            to_row, to_col = at_row + down_by, at_col + right_by
            there = (to_row >= 0) & (to_row < n_rows) & (to_col >= 0) & (to_col < n_cols)
            slot = jnp.where(there, to_col * n_rows + to_row, at_col * n_rows + at_row)
            chunk_ref[slot] = piece * jnp.where(there, 1.0, 0.0)


def first(taps, fields, got_a, got_b, coarse, dot):
    field = fields[0].shape
    tiles, height = field[0] - 1, field[1] - 4 * EDGE
    down = height // COARSE
    window = down + 2 * EDGE
    count = lax.axis_size("cols") * lax.axis_size("rows")
    shapes = [field] * 9 + [
        (5, window, 2 * LANES),
        (down, LANES),
        (count, EDGE, LANES),
        (2, EDGE, LANES),
    ]
    return pl.pallas_call(
        functools.partial(first_kernel, tiles, down),
        in_specs=[SMEM] + [VMEM] * 11,
        out_specs=[VMEM] * len(shapes),
        out_shape=floats(*shapes),
        input_output_aliases={index + 1: index for index in range(7)},
        scratch_shapes=[
            pltpu.VMEM(field, jnp.float32),
            pltpu.VMEM((tiles + 1, window, LANES), jnp.float32),
            pltpu.VMEM((2, 2, window + 2 * EDGE, LANES), jnp.float32),
        ],
        compiler_params=params(),
        name="first_direction",
    )(taps, *fields, got_b, got_a, coarse, dot)[2:]


def second_kernel(
    tiles,
    down,
    taps,
    got_ref,
    own_ref,
    table_ref,
    q_ref,
    east_ref,
    south_ref,
    inv_ref,
    dots_in,
    w_ref,
    v_ref,
    out_ref,
    image,
    spread,
    work,
):
    height = down * COARSE
    has_n, has_s, has_e, has_w = has_sides()
    at_col, at_row, n_cols, n_rows = place()
    me = at_col * n_rows + at_row

    def got(down_by, right_by):
        to_row, to_col = at_row + down_by, at_col + right_by
        there = (to_row >= 0) & (to_row < n_rows) & (to_col >= 0) & (to_col < n_cols)
        return got_ref[jnp.where(there, to_col * n_rows + to_row, me)]

    low = iota((EDGE, LANES), 1) < HALF
    gap = jnp.zeros((LANES - 2 * EDGE, LANES), jnp.float32)
    beside = jnp.transpose(jnp.concatenate([got(0, 1), gap, got(0, -1)], axis=0))[:down]
    source = jnp.concatenate(
        [
            jnp.concatenate([got(-1, 0), jnp.where(low, got(-1, 1), got(-1, -1))], axis=1),
            jnp.concatenate([own_ref[...], beside], axis=1),
            jnp.concatenate([got(1, 0), jnp.where(low, got(1, 1), got(1, -1))], axis=1),
        ],
        axis=0,
    )
    clear_work(work)
    spread_cells(jacobi(source, table_ref, work), spread)
    clear_pads(w_ref, image)
    sides = side_lanes(has_e, has_w)
    taps = read_taps(taps)

    def begin_w(at, start, total):
        field, inverse, cells = load(q_ref, at), load(inv_ref, at), cells_at(spread, at)
        strip = [field[t] * inverse[t] + cells[t] for t in range(tiles + 1)]
        first_row = jnp.maximum(start, 2 * EDGE)
        flags = [
            jnp.where((row >= first_row) & (row < 2 * EDGE + height), 1.0, 0.0)
            for row in [at + by for by in range(0, STRIP, EDGE)]
        ]
        return [(w_ref, strip)], total + product_sum(field, strip, tiles, flags)

    def blur(at, _, carry):
        strip = conv(w_ref, at, taps, False)
        strip[tiles] = strip[tiles] * sides
        return [(image, strip)], carry

    def finish(at, _, total):
        here, product = operate(w_ref, image, east_ref, south_ref, at, taps)
        return [(v_ref, product[:tiles])], total + product_sum(here, product, tiles)

    nothing = jnp.zeros((EDGE, LANES), jnp.float32)
    span = (EDGE, 3 * EDGE + height)
    dot_qw = sweep(3, *span, begin_w, nothing)
    sweep(3, *span, blur, 0)
    mask_rows(image, has_n, has_s)
    dot_wv = sweep(4, 2 * EDGE, 2 * EDGE + height, finish, nothing)
    line = jnp.zeros((1, LANES), jnp.float32)
    block = iota((1, LANES), 1) // (LANES // 4)
    for index, part in enumerate((dots_in[0], dots_in[1], dot_qw, dot_wv)):
        part = jnp.sum(part, axis=0, keepdims=True)
        part = part + roll(part, LANES // 2, 1)
        part = part + roll(part, LANES // 4, 1)
        line = jnp.where(block == index, part, line)
    for index in range(out_ref.shape[0]):
        out_ref[index] = line


def second(taps, got, own, table, q, east, south, inv, dots):
    tiles, height = q.shape[0] - 1, q.shape[1] - 4 * EDGE
    down = height // COARSE
    window = down + 2 * EDGE
    count = lax.axis_size("cols") * lax.axis_size("rows")
    return pl.pallas_call(
        functools.partial(second_kernel, tiles, down),
        in_specs=[SMEM] + [VMEM] * 8,
        out_specs=[VMEM] * 3,
        out_shape=floats(q.shape, q.shape, (count, 1, LANES)),
        scratch_shapes=[
            pltpu.VMEM(q.shape, jnp.float32),
            pltpu.VMEM((tiles + 1, window, LANES), jnp.float32),
            pltpu.VMEM((2, 2, window + 2 * EDGE, LANES), jnp.float32),
        ],
        compiler_params=params(),
        name="second_direction",
    )(taps, got, own, table, q, east, south, inv, dots)


def combine_kernel(
    tiles, height, sums_ref, p_ref, w_ref, r_ref, q_ref, v_ref, sol_out, res_out, sol, res, sem
):
    line = sums_ref[0]
    for index in range(1, sums_ref.shape[0]):
        line = line + sums_ref[index]
    block = iota((1, LANES), 1) // (LANES // 4)
    pick = lambda index: jnp.sum(jnp.where(block == index, line, 0.0), axis=1, keepdims=True)
    rp, pq, qw, wv = [pick(index) for index in range(4)]
    step = rp / pq
    rp_next = step * step * qw - rp
    ratio = rp_next / rp
    lead = 1.0 + ratio
    curvature = lead * lead * pq - 2.0 * lead * step * qw + step * step * wv
    step_next = rp_next / curvature
    on_p = jnp.broadcast_to(step + step_next * lead, (CHUNK, LANES))
    on_w = jnp.broadcast_to(step_next * step, (CHUNK, LANES))

    def copies(index):
        rows = pl.ds(pl.multiple_of(index * CHUNK, CHUNK), CHUNK)
        return (
            pltpu.make_async_copy(sol.at[rows, :], sol_out.at[rows, :], sem.at[0, index]),
            pltpu.make_async_copy(res.at[rows, :], res_out.at[rows, :], sem.at[1, index]),
        )

    def work(index, _):
        at = pl.multiple_of(index * CHUNK, CHUNK)
        p, w, r, q, v = [
            load(ref, at + 2 * EDGE, CHUNK) for ref in (p_ref, w_ref, r_ref, q_ref, v_ref)
        ]
        one = [on_p * p[t] - on_w * w[t] for t in range(tiles)]
        two = [r[t] - on_p * q[t] + on_w * v[t] for t in range(tiles)]
        for t in range(tiles):
            sol[pl.ds(at, CHUNK), t * LANES : (t + 1) * LANES] = one[t]
            res[pl.ds(at, CHUNK), t * LANES : (t + 1) * LANES] = two[t]
        for copy in copies(index):
            copy.start()
        return 0

    def settle(index, _):
        for copy in copies(index):
            copy.wait()
        return 0

    lax.fori_loop(0, height // CHUNK, work, 0)
    lax.fori_loop(0, height // CHUNK, settle, 0)


def combine(sums, p, w, r, q, v):
    tiles, height = q.shape[0] - 1, q.shape[1] - 4 * EDGE
    shape = (height, tiles * LANES)
    return pl.pallas_call(
        functools.partial(combine_kernel, tiles, height),
        in_specs=[VMEM] * 6,
        out_specs=[HBM] * 2,
        out_shape=floats(shape, shape),
        scratch_shapes=[
            pltpu.VMEM(shape, jnp.float32),
            pltpu.VMEM(shape, jnp.float32),
            pltpu.SemaphoreType.DMA((2, height // CHUNK)),
        ],
        compiler_params=params(),
        name="combine",
    )(sums, p, w, r, q, v)


def exchange(send_a, send_b, axis):
    count = lax.axis_size(axis)

    def pairs(begin):
        return [
            pair for i in range(begin, count - 1, 2) for pair in ((i, i + 1), (i + 1, i))
        ]

    got_b = lax.ppermute(send_b, axis, pairs(1))
    got_a = lax.ppermute(send_a, axis, pairs(0))
    return got_a, got_b


def body(observed, class_map, class_weights, blur_kernel):
    arguments = (observed, class_map, class_weights, blur_kernel)
    send_a, send_b = edge(*arguments)
    got_a, got_b = exchange(send_a, send_b, "cols")
    obs, cond, coarse = pack(*arguments, send_a)
    obs, cond, coarse, send_a, send_b = middle(got_a, got_b, coarse, obs, cond)
    got_a, got_b = exchange(send_a, send_b, "rows")
    r, east, south, inv, u, dot = inner(blur_kernel, obs, cond)
    fields = (obs, cond, r, east, south, inv, u)
    r, east, south, inv, _, p, q, table, own, chunk, dots = first(
        blur_kernel, fields, got_a, got_b, coarse, dot
    )
    got = lax.all_to_all(chunk, AXES, 0, 0, tiled=True)
    w, v, line = second(blur_kernel, got, own, table, q, east, south, inv, dots)
    sums = lax.all_to_all(line, AXES, 0, 0, tiled=True)
    return tuple(combine(sums, p, w, r, q, v))


def solution(mesh):
    return jax.shard_map(
        body,
        mesh=mesh,
        in_specs=(P("rows", "cols"), P("rows", "cols"), P(), P()),
        out_specs=(P("rows", "cols"), P("rows", "cols")),
        check_vma=False,
    )
```

```python
import functools

import jax
import jax.numpy as jnp
from jax import lax
from jax.experimental import pallas as pl
from jax.experimental.pallas import tpu as pltpu
from jax.sharding import PartitionSpec as P

COARSE = 8
SWEEPS = 8
CLASSES = 4
OMEGA = 0.8

LANES = 128
HALF = LANES // 2
EDGE = 8
STRIP = 2 * EDGE
CHUNK = 64
AXES = ("cols", "rows")
LIMIT = 40 * 1024 * 1024


VMEM = pl.BlockSpec(memory_space=pltpu.VMEM)
SMEM = pl.BlockSpec(memory_space=pltpu.SMEM)
HBM = pl.BlockSpec(memory_space=pltpu.HBM)


def params():
    return pltpu.CompilerParams(vmem_limit_bytes=LIMIT)


def in_hbm(array):
    return pltpu.with_memory_space_constraint(array, pltpu.HBM)


def floats(*shapes):
    return [jax.ShapeDtypeStruct(shape, jnp.float32) for shape in shapes]


def place():
    at_col, at_row = lax.axis_index("cols"), lax.axis_index("rows")
    n_cols, n_rows = lax.axis_size("cols"), lax.axis_size("rows")
    return at_col, at_row, n_cols, n_rows


def has_sides():
    at_col, at_row, n_cols, n_rows = place()
    flag = lambda test: jnp.where(test, 1.0, 0.0).astype(jnp.float32)
    return (
        flag(at_row > 0),
        flag(at_row < n_rows - 1),
        flag(at_col < n_cols - 1),
        flag(at_col > 0),
    )


def iota(shape, dim):
    return lax.broadcasted_iota(jnp.int32, shape, dim)


def cell_of(pixel, tiles):
    turn = (tiles + 1) * LANES
    return jnp.where(pixel < turn - HALF, pixel >> 3, ((pixel - turn) >> 3) & (2 * LANES - 1))


def gather_matrix(tiles):
    shape = ((tiles + 1) * LANES, 2 * LANES)
    hit = cell_of(iota(shape, 0), tiles) == iota(shape, 1)
    return jnp.where(hit, 1.0, 0.0).astype(jnp.bfloat16)


def split_dot(field, matrix):
    rows = field.shape[0]
    high = field.astype(jnp.bfloat16)
    low = (field - high.astype(jnp.float32)).astype(jnp.bfloat16)
    both = jnp.dot(
        jnp.concatenate([high, low], axis=0), matrix, preferred_element_type=jnp.float32
    )
    return both[:rows] + both[rows:]


def roll(field, by, axis):
    return pltpu.roll(field, by % field.shape[axis], axis)


def load(ref, at, rows=STRIP):
    return [ref[t, pl.ds(at, rows), :] for t in range(ref.shape[0])]


def store(ref, at, strip):
    for t, part in enumerate(strip):
        ref[t, pl.ds(at, part.shape[0]), :] = part


def wide(ref, at, rows):
    return jnp.concatenate(load(ref, at, rows), axis=1)


def read_taps(taps):
    return [[taps[a, b] for b in range(3)] for a in range(3)]


def tap_total(taps, power):
    return sum(tap * tap if power == 2 else tap for line in taps for tap in line)


def from_west(strip):
    lane = iota(strip[0].shape, 1)
    turned = [roll(part, 1, 1) for part in strip]
    return [jnp.where(lane == 0, turned[t - 1], turned[t]) for t in range(len(strip))]


def from_east(strip):
    lane = iota(strip[0].shape, 1)
    turned = [roll(part, -1, 1) for part in strip]
    count = len(strip)
    return [
        jnp.where(lane == LANES - 1, turned[(t + 1) % count], turned[t]) for t in range(count)
    ]


def tap_sums(ref, at, taps, flip):
    if flip:
        taps = [line[::-1] for line in taps[::-1]]
    above, here, below = load(ref, at - 1), load(ref, at), load(ref, at + 1)
    sums = [[], [], []]
    for t in range(len(here)):
        for b in range(3):
            sums[b].append(
                taps[0][b] * above[t] + taps[1][b] * here[t] + taps[2][b] * below[t]
            )
    return sums


def conv(ref, at, taps, flip):
    sums = tap_sums(ref, at, taps, flip)
    west, east = from_west(sums[0]), from_east(sums[2])
    return [sums[1][t] + west[t] + east[t] for t in range(len(west))]


def operate(ref, image, east_ref, south_ref, at, taps):
    above, here, below = load(ref, at - 1), load(ref, at), load(ref, at + 1)
    east, south, north = load(east_ref, at), load(south_ref, at), load(south_ref, at - 1)
    sums = tap_sums(image, at, taps, True)
    span = range(len(here))
    beside = from_east(here)
    flux = [east[t] * (here[t] - beside[t]) for t in span]
    from_left = from_west([sums[0][t] - flux[t] for t in span])
    from_right = from_east(sums[2])
    return here, [
        sums[1][t]
        + flux[t]
        + from_left[t]
        + from_right[t]
        + south[t] * (here[t] - below[t])
        - north[t] * (above[t] - here[t])
        for t in span
    ]


def begin(obs, cond, at, taps, sides):
    above, here, below = load(cond, at - 1), load(cond, at), load(cond, at + 1)
    span = range(len(here))
    right = from_east(here)
    east = [here[t] + right[t] for t in span]
    west = from_west(east)
    south = [here[t] + below[t] for t in span]
    squares = tap_total(taps, 2)
    diag = [squares + east[t] + west[t] + south[t] + (here[t] + above[t]) for t in span]
    inverse = [pl.reciprocal(part, approx=True) for part in diag]
    inverse = [inverse[t] * (2.0 - diag[t] * inverse[t]) for t in span]
    inverse[-1] = inverse[-1] * sides
    residual = conv(obs, at, taps, True)
    return east, south, inverse, residual, [residual[t] * inverse[t] for t in span]


def pick_lanes(field, lanes):
    return jnp.take_along_axis(field, lanes, axis=1, mode="promise_in_bounds")


def spread_cells(cells, spread):
    tiles = spread.shape[0] - 1
    lane = iota((cells.shape[0], LANES), 1)
    for t in range(tiles):
        spread[t] = pick_lanes(cells[:, :LANES], (lane >> 3) + t * (LANES // COARSE))
    turn = jnp.where(lane < HALF, 0, LANES - LANES // COARSE)
    spread[tiles] = pick_lanes(cells[:, LANES:], (lane >> 3) + turn)


def cells_at(spread, at):
    first = at // EDGE + EDGE - 2
    rows = [load(spread, first + index, 1) for index in range(STRIP // EDGE)]
    return [
        jnp.concatenate([jnp.broadcast_to(row, (EDGE, LANES)) for row in parts], axis=0)
        for parts in zip(*rows)
    ]


def cell_sums(ref, tiles, down):
    lane = iota((down, LANES), 1)
    total = jnp.zeros((down, LANES), jnp.float32)
    for t in range(tiles):
        picked = [
            ref[t, pl.ds(2 * EDGE + k, down, stride=COARSE), :] for k in range(COARSE)
        ]
        part = sum(picked[1:], picked[0])
        for by in (1, 2, 4):
            part = part + roll(part, -by, 1)
        part = pick_lanes(part, (lane & (LANES // COARSE - 1)) * COARSE)
        total = jnp.where(lane // (LANES // COARSE) == t, part, total)
    return total


def side_lanes(has_e, has_w):
    return jnp.where(iota((STRIP, LANES), 1) < HALF, has_e, has_w)


def mask_rows(ref, has_n, has_s):
    last = ref.shape[1] - 2 * EDGE
    for at, flag in ((EDGE, has_n), (last, has_s)):
        ref[:, at : at + EDGE, :] = ref[:, at : at + EDGE, :] * flag


def clear_pads(*refs):
    empty = jnp.zeros((refs[0].shape[0], EDGE, LANES), jnp.float32)
    for ref in refs:
        ref[:, :EDGE, :] = empty
        ref[:, ref.shape[1] - EDGE :, :] = empty


def product_sum_rows(one, two, count):
    total = one[0] * two[0]
    for t in range(1, count):
        total = total + one[t] * two[t]
    return total


def product_sum(one, two, count, flags=None):
    return fold(product_sum_rows(one, two, count), flags)


def fold(total, flags=None):
    parts = [total[at : at + EDGE] for at in range(0, total.shape[0], EDGE)]
    if flags is not None:
        parts = [part * flag for part, flag in zip(parts, flags)]
    return sum(parts[1:], parts[0])


def sweep(group, first, last, body, carry):
    width = group * STRIP
    steps = -(-(last - first) // width)

    def work(index, carry):
        start = first + index * width
        at = pl.multiple_of(jnp.minimum(start, last - width), EDGE)
        pending = []
        for by in range(0, width, STRIP):
            stores, carry = body(at + by, start, carry)
            pending += [(ref, at + by, strip) for ref, strip in stores]
        for ref, row, strip in pending:
            store(ref, row, strip)
        return carry

    return lax.fori_loop(0, steps, work, carry)


def jacobi(source, table, work):
    factor, east, west, south, north = [table[index] for index in range(5)]
    window = source.shape[0]
    source = factor * source
    iterate = source
    for sweep_index in range(SWEEPS - 1):
        place_ref = work.at[sweep_index % 2]
        for half in range(2):
            place_ref[half, EDGE : EDGE + window, :] = iterate[
                :, half * LANES : (half + 1) * LANES
            ]
        above, below = [
            jnp.concatenate(
                [place_ref[half, EDGE + by : EDGE + by + window, :] for half in range(2)], axis=1
            )
            for by in (-1, 1)
        ]
        across = east * roll(iterate, -1, 1) + west * roll(iterate, 1, 1)
        along = south * below + north * above
        iterate = ((1.0 - OMEGA) * iterate + source) + (across + along)
    return iterate


def clear_work(work):
    for buffer in range(2):
        clear_pads(work.at[buffer])


def in_pair_order(at, for_before, for_after):
    even = at % 2 == 0
    if callable(for_before):
        return (
            lambda index: jnp.where(even, for_after(index), for_before(index)),
            lambda index: jnp.where(even, for_before(index), for_after(index)),
        )
    return jnp.where(even, for_after, for_before), jnp.where(even, for_before, for_after)


def reader(tiles_here, refs, scratch, obs, cond, down):
    obs_in, class_in, weight_in, taps_in = refs
    classes, weights, taps, sums, obs_sem, class_sem, small_sem = scratch
    own = pl.ds(2 * EDGE, down * COARSE)
    small = [
        pltpu.make_async_copy(weight_in, weights, small_sem.at[0]),
        pltpu.make_async_copy(taps_in, taps, small_sem.at[1]),
    ]
    moves = []
    for slot, t in enumerate(tiles_here):
        lanes = pl.ds(t * LANES, LANES)
        moves.append(
            (
                pltpu.make_async_copy(class_in.at[:, lanes], classes.at[slot], class_sem.at[slot]),
                pltpu.make_async_copy(
                    obs_in.at[:, lanes], obs.at[slot, own, :], obs_sem.at[slot]
                ),
            )
        )
    for copy in small:
        copy.start()
    for pair in moves:
        for copy in pair:
            copy.start()
    sums[...] = jnp.zeros_like(sums)

    def settle(slot):
        if slot == 0:
            for copy in small:
                copy.wait()
        for copy in moves[slot]:
            copy.wait()
        values = [0.5 * weights[class_id] for class_id in range(CLASSES)]
        kind = classes[slot]
        cond[slot, own, :] = jnp.where(
            kind < 2,
            jnp.where(kind == 0, values[0], values[1]),
            jnp.where(kind == 2, values[2], values[3]),
        )
        for which, ref in enumerate((obs, cond)):
            picked = [
                ref[slot, pl.ds(2 * EDGE + k, down, stride=COARSE), :] for k in range(COARSE)
            ]
            cells = slice(2 * EDGE, 2 * EDGE + down)
            sums[3 * which, slot, cells, :] = sum(picked[1:], picked[0])
            sums[3 * which + 1, slot, cells, :] = picked[0]
            sums[3 * which + 2, slot, cells, :] = picked[-1]

    return settle


def reader_scratch(tiles, height, window, class_weights, taps):
    return [
        pltpu.VMEM((tiles, height, LANES), jnp.int32),
        pltpu.SMEM(class_weights.shape, jnp.float32),
        pltpu.SMEM(taps.shape, jnp.float32),
        pltpu.VMEM((6, tiles + 1, window + 2 * EDGE, LANES), jnp.float32),
        pltpu.SemaphoreType.DMA((tiles,)),
        pltpu.SemaphoreType.DMA((tiles,)),
        pltpu.SemaphoreType.DMA((2,)),
    ]


def coarse_parts(sums, taps, matrix):
    window = sums.shape[2] - 2 * EDGE
    whole = lambda index, by=0: wide(sums.at[index], EDGE + by, window)
    full = whole(0)
    by_tap = [full - whole(1) + whole(1, 1), full, full - whole(2) + whole(2, -1)]
    across = [sum(taps[a][b] * by_tap[a] for a in range(3)) for b in range(3)]
    source = across[1] + roll(across[0], -1, 1) + roll(across[2], 1, 1)
    full = whole(3)
    last = (iota(full.shape, 1) & (COARSE - 1)) == COARSE - 1
    east = jnp.where(last, full + roll(full, -1, 1), 0.0)
    south = whole(5) + whole(4, 1)
    cells = split_dot(jnp.concatenate([source, east, south], axis=0), matrix)
    source, east, south = cells[:window], cells[window : 2 * window], cells[2 * window :]
    around = east + roll(east, 1, 1) + south + roll(south, 1, 0)
    return [source, east, south, around]


def edge_kernel(tiles, down, *refs):
    arguments, (send_a, send_b), (obs, cond, message, *scratch) = refs[:4], refs[4:6], refs[6:]
    height = down * COARSE
    halves = height // LANES
    window = down + 2 * EDGE
    settle = reader((0, tiles - 1), arguments, scratch, obs, cond, down)
    matrix = gather_matrix(2)
    for slot, begin_row in ((0, 0), (1, LANES - EDGE)):
        settle(slot)
        for which, ref in enumerate((obs, cond)):
            turned = jnp.transpose(ref[slot, 2 * EDGE : 2 * EDGE + height, :])
            turned = turned[begin_row : begin_row + EDGE]
            for half in range(halves):
                at = (which * halves + half) * EDGE
                message[slot, at : at + EDGE, :] = turned[:, half * LANES : (half + 1) * LANES]
    parts = coarse_parts(scratch[3], read_taps(scratch[2]), matrix)
    spare = jnp.zeros((2 * LANES - 4 * window, 2 * LANES), jnp.float32)
    stack = jnp.concatenate(parts + [spare], axis=0)
    left = jnp.transpose(stack[:, :LANES])
    right = jnp.transpose(stack[:, LANES:])
    base = 2 * halves * EDGE
    past = 2 * LANES // COARSE
    for slot, pieces in (
        (0, (left[:EDGE], right[LANES - EDGE :])),
        (1, (left[past - EDGE : past], left[past : past + EDGE])),
    ):
        for index, piece in enumerate(pieces):
            for half in range(2):
                at = base + (2 * index + half) * EDGE
                message[slot, at : at + EDGE, :] = piece[:, half * LANES : (half + 1) * LANES]
    send_a[...], send_b[...] = in_pair_order(place()[0], message[0], message[1])


def edge(observed, class_map, class_weights, taps):
    height, breadth = observed.shape
    tiles, down = breadth // LANES, height // COARSE
    window = down + 2 * EDGE
    field = (3, height + 4 * EDGE, LANES)
    strip = ((2 * (height // LANES) + 4) * EDGE, LANES)
    return pl.pallas_call(
        functools.partial(edge_kernel, tiles, down),
        in_specs=[HBM] * 4,
        out_specs=[VMEM] * 2,
        out_shape=floats(strip, strip),
        scratch_shapes=[
            pltpu.VMEM(field, jnp.float32),
            pltpu.VMEM(field, jnp.float32),
            pltpu.VMEM((2,) + strip, jnp.float32),
        ]
        + reader_scratch(2, height, window, class_weights, taps),
        compiler_params=params(),
        name="pack_east_west",
    )(*[in_hbm(array) for array in (observed, class_map, class_weights, taps)])


def pack_kernel(tiles, down, *refs):
    arguments, (obs, cond, coarse_ref), scratch = refs[:4], refs[5:8], refs[8:]
    settle = reader(range(tiles), arguments, scratch, obs, cond, down)
    matrix = gather_matrix(tiles)
    for t in range(tiles):
        settle(t)
    for index, part in enumerate(coarse_parts(scratch[3], read_taps(scratch[2]), matrix)):
        coarse_ref[index] = part


def pack(observed, class_map, class_weights, taps, after):
    height, breadth = observed.shape
    tiles, down = breadth // LANES, height // COARSE
    window = down + 2 * EDGE
    field = (tiles + 1, height + 4 * EDGE, LANES)
    pixels = height * breadth
    return pl.pallas_call(
        functools.partial(pack_kernel, tiles, down),
        in_specs=[HBM] * 4 + [VMEM],
        out_specs=[VMEM] * 3,
        out_shape=floats(field, field, (4, window, 2 * LANES)),
        scratch_shapes=reader_scratch(tiles, height, window, class_weights, taps),
        compiler_params=params(),
        cost_estimate=pl.CostEstimate(
            flops=20 * pixels, bytes_accessed=16 * pixels, transcendentals=0
        ),
        name="pack_all",
    )(*[in_hbm(array) for array in (observed, class_map, class_weights, taps)], after)


def merge_sides(parts):
    block = iota((EDGE, LANES), 1) // (2 * EDGE)
    merged = jnp.zeros((EDGE, LANES), jnp.float32)
    for index, part in enumerate(parts):
        merged = jnp.where(block == index, roll(part, (2 * index + 1) * EDGE, 1), merged)
    return merged


def split_sides(merged, count):
    lane = iota((EDGE, LANES), 1)
    outer = (lane < EDGE) | (lane >= LANES - EDGE)
    return [
        jnp.where(outer, roll(merged, -(2 * index + 1) * EDGE, 1), 0.0) for index in range(count)
    ]


def middle_kernel(
    tiles,
    down,
    got_b,
    got_a,
    coarse_in,
    obs_in,
    cond_in,
    obs,
    cond,
    coarse_ref,
    send_a,
    send_b,
    message,
):
    height = down * COARSE
    halves = height // LANES
    at_col, at_row, _, _ = place()
    from_e, from_w = in_pair_order(at_col, got_b[...], got_a[...])
    gap = jnp.zeros((LANES - 2 * EDGE, LANES), jnp.float32)

    def turned(low, high):
        return jnp.transpose(jnp.concatenate([low, gap, high], axis=0))

    for which, field in enumerate((obs, cond)):
        for half in range(halves):
            at = (which * halves + half) * EDGE
            begin_row = 2 * EDGE + half * LANES
            field[tiles, begin_row : begin_row + LANES, :] = turned(
                from_e[at : at + EDGE], from_w[at : at + EDGE]
            )
    base = 2 * halves * EDGE

    def piece(strip, index, half):
        at = base + (2 * index + half) * EDGE
        return strip[at : at + EDGE]

    left = [turned(piece(from_w, 1, half), piece(from_e, 1, half)) for half in range(2)]
    right = [turned(piece(from_e, 0, half), piece(from_w, 0, half)) for half in range(2)]
    left = jnp.concatenate(left, axis=0)
    right = jnp.concatenate(right, axis=0)
    window = down + 2 * EDGE
    for index in range(4):
        rows = slice(index * window, (index + 1) * window)
        coarse_ref[index, :, :LANES] = coarse_in[index, :, :LANES] + left[rows]
        coarse_ref[index, :, LANES:] = coarse_in[index, :, LANES:] + right[rows]
    fields = (obs, cond)
    for slot, begin_row, first_row, over_row in (
        (0, 2 * EDGE, EDGE, EDGE - 1),
        (1, EDGE + height, window - 2 * EDGE, window - EDGE),
    ):
        pieces = [field[t, begin_row : begin_row + EDGE, :] for field in fields for t in range(tiles)]
        rows = slice(first_row, first_row + EDGE)
        pieces += [coarse_ref[index, rows, :LANES] for index in range(4)]
        beyond = [coarse_ref[index, rows, LANES:] for index in range(4)]
        beyond += [field[tiles, begin_row : begin_row + EDGE, :] for field in fields]
        pieces.append(merge_sides(beyond))
        pieces.append(
            jnp.concatenate(
                [
                    coarse_ref[index, over_row : over_row + 1, half * LANES : (half + 1) * LANES]
                    for index in range(4)
                    for half in range(2)
                ],
                axis=0,
            )
        )
        for index, piece in enumerate(pieces):
            message[slot, index] = piece
    send_a[...], send_b[...] = in_pair_order(at_row, message[0], message[1])


def middle(got_a, got_b, coarse, obs, cond):
    tiles, height = obs.shape[0] - 1, obs.shape[1] - 4 * EDGE
    down = height // COARSE
    long = (2 * tiles + 6, EDGE, LANES)
    return pl.pallas_call(
        functools.partial(middle_kernel, tiles, down),
        in_specs=[VMEM] * 5,
        out_specs=[VMEM] * 5,
        out_shape=floats(obs.shape, cond.shape, coarse.shape, long, long),
        input_output_aliases={3: 0, 4: 1},
        scratch_shapes=[pltpu.VMEM((2,) + long, jnp.float32)],
        compiler_params=params(),
        name="pack_north_south",
    )(got_b, got_a, coarse, obs, cond)


def inner_kernel(taps, obs, cond, res_ref, east_ref, south_ref, inv_ref, u_ref, dot_ref):
    _, _, has_e, has_w = has_sides()
    clear_pads(east_ref, south_ref)
    taps = read_taps(taps)
    sides = side_lanes(has_e, has_w)

    tiles = obs.shape[0] - 1

    def work(at, start, total):
        fields = begin(obs, cond, at, taps, sides)
        flags = [jnp.where(at + by >= start, 1.0, 0.0) for by in range(0, STRIP, EDGE)]
        total = total + product_sum(fields[3], fields[4], tiles, flags)
        return list(zip((east_ref, south_ref, inv_ref, res_ref, u_ref), fields)), total

    nothing = jnp.zeros((EDGE, LANES), jnp.float32)
    dot_ref[...] = sweep(5, 3 * EDGE, obs.shape[1] - 3 * EDGE, work, nothing)


def inner(taps, obs, cond):
    field = obs.shape
    pixels = field[0] * field[1] * field[2]
    return pl.pallas_call(
        inner_kernel,
        in_specs=[SMEM] + [VMEM] * 2,
        out_specs=[VMEM] * 6,
        out_shape=floats(field, field, field, field, field, (EDGE, LANES)),
        compiler_params=params(),
        cost_estimate=pl.CostEstimate(
            flops=45 * pixels, bytes_accessed=24 * pixels, transcendentals=0
        ),
        name="inner_strips",
    )(taps, obs, cond)


def first_kernel(
    tiles,
    down,
    taps,
    obs_in,
    cond_in,
    res_in,
    east_in,
    south_in,
    inv_in,
    u_in,
    got_b,
    got_a,
    coarse_in,
    dot_in,
    obs,
    cond,
    res_ref,
    east_ref,
    south_ref,
    inv_ref,
    u_ref,
    p_ref,
    q_ref,
    table_ref,
    own_ref,
    chunk_ref,
    dots_ref,
    image,
    spread,
    work,
):
    height = down * COARSE
    window = down + 2 * EDGE
    at_col, at_row, n_cols, n_rows = place()
    has_n, has_s, has_e, has_w = has_sides()
    clear_pads(obs, cond, p_ref, image)
    clear_work(work)
    from_s, from_n = in_pair_order(
        at_row, lambda index: got_b[index], lambda index: got_a[index]
    )

    for which, field in enumerate((obs, cond)):
        for t in range(tiles):
            field[t, EDGE : 2 * EDGE, :] = from_n(which * tiles + t)
            field[t, 2 * EDGE + height : 3 * EDGE + height, :] = from_s(which * tiles + t)
    sides_n, sides_s = [split_sides(strip(2 * tiles + 4), 6) for strip in (from_n, from_s)]
    for which, field in enumerate((obs, cond)):
        field[tiles, EDGE : 2 * EDGE, :] = sides_n[4 + which]
        field[tiles, 2 * EDGE + height : 3 * EDGE + height, :] = sides_s[4 + which]

    edge_row = iota((EDGE, 2 * LANES), 0)

    def joined(index):
        def over(strip, row):
            line = [
                jnp.broadcast_to(
                    strip((2 * tiles + 5, pl.ds(2 * index + half, 1))), (EDGE, LANES)
                )
                for half in range(2)
            ]
            return jnp.where(edge_row == row, jnp.concatenate(line, axis=1), 0.0)

        def rows(strip, beyond):
            return jnp.concatenate([strip(2 * tiles + index), beyond[index]], axis=1)

        parts = [coarse_in[index, at : at + EDGE, :] for at in range(0, window, EDGE)]
        parts[0] = parts[0] + rows(from_n, sides_n)
        parts[1] = parts[1] + over(from_n, 0)
        parts[-2] = parts[-2] + over(from_s, EDGE - 1)
        parts[-1] = parts[-1] + rows(from_s, sides_s)
        return jnp.concatenate(parts, axis=0)

    source, east, south, around = [joined(index) for index in range(4)]
    row = iota(source.shape, 0)
    lane = iota(source.shape, 1)
    inside = jnp.where(row < EDGE, has_n, jnp.where(row < window - EDGE, 1.0, has_s))
    inside = inside * jnp.where(
        lane < LANES, 1.0, jnp.where(lane < LANES + HALF, has_e, has_w)
    )
    taps = read_taps(taps)
    taps_sum = tap_total(taps, 1)
    factor = inside * OMEGA / (COARSE * COARSE * taps_sum * taps_sum + around)
    weights = (east, roll(east, 1, 1), south, roll(south, 1, 0))
    table = [factor] + [factor * weight for weight in weights]
    for index, part in enumerate(table):
        table_ref[index] = part
    sides = side_lanes(has_e, has_w)
    half = iota((STRIP, LANES), 0) // EDGE
    pending = []
    total = dot_in[...]
    for index, known in ((0, has_n), (1, has_s)):
        at = EDGE + index * height
        fields = begin(obs, cond, at, taps, sides)
        own = jnp.where(half == index, 0.0, 1.0)
        total = total + fold(own * product_sum_rows(fields[3], fields[4], tiles))
        flag = jnp.where(half == index, known, 1.0)
        inverse, start = [[part * flag for part in fields[index]] for index in (2, 4)]
        fields = (*fields[:2], inverse, fields[3], start)
        pending += [
            (ref, at, strip)
            for ref, strip in zip((east_ref, south_ref, inv_ref, res_ref, u_ref), fields)
        ]
    cells = jacobi(source, table, work)
    spread_cells(cells, spread)
    inner_cells = slice(EDGE, EDGE + down)
    total = total + fold(source[inner_cells, :LANES] * cells[inner_cells, :LANES])
    dots_ref[0] = total
    for ref, at, strip in pending:
        store(ref, at, strip)

    def flags(at, start):
        rows = [at + by for by in range(0, STRIP, EDGE)]
        first_row = jnp.maximum(start, 2 * EDGE)
        return [
            jnp.where((row >= first_row) & (row < 2 * EDGE + height), 1.0, 0.0) for row in rows
        ]

    def begin_p(at, _, carry):
        start, cells = load(u_ref, at), cells_at(spread, at)
        return [(p_ref, [start[t] + cells[t] for t in range(tiles + 1)])], carry

    def blur(at, _, carry):
        strip = conv(p_ref, at, taps, False)
        strip[tiles] = strip[tiles] * sides
        return [(image, strip)], carry

    def finish(at, start, total):
        here, product = operate(p_ref, image, east_ref, south_ref, at, taps)
        return [(q_ref, product)], total + product_sum(here, product, tiles, flags(at, start))

    nothing = jnp.zeros((EDGE, LANES), jnp.float32)
    span = (EDGE, 3 * EDGE + height)
    sweep(3, *span, begin_p, 0)
    sweep(3, *span, blur, 0)
    mask_rows(image, has_n, has_s)
    dots_ref[1] = sweep(3, *span, finish, nothing)

    own = cell_sums(q_ref, tiles, down)
    own_ref[...] = own
    spare = jnp.zeros((LANES - down, LANES), jnp.float32)
    turned = jnp.transpose(jnp.concatenate([own, spare], axis=0))
    chunk_ref[...] = jnp.zeros_like(chunk_ref)
    for down_by in (-1, 0, 1):
        for right_by in (-1, 0, 1):
            if down_by == 0 and right_by == 0:
                continue
            if down_by == 0:
                piece = turned[:EDGE] if right_by < 0 else turned[LANES - EDGE :]
            else:
                piece = own[:EDGE] if down_by < 0 else own[down - EDGE :]
            to_row, to_col = at_row + down_by, at_col + right_by
            there = (to_row >= 0) & (to_row < n_rows) & (to_col >= 0) & (to_col < n_cols)
            slot = jnp.where(there, to_col * n_rows + to_row, at_col * n_rows + at_row)
            chunk_ref[slot] = piece * jnp.where(there, 1.0, 0.0)


def first(taps, fields, got_a, got_b, coarse, dot):
    field = fields[0].shape
    tiles, height = field[0] - 1, field[1] - 4 * EDGE
    down = height // COARSE
    window = down + 2 * EDGE
    count = lax.axis_size("cols") * lax.axis_size("rows")
    shapes = [field] * 9 + [
        (5, window, 2 * LANES),
        (down, LANES),
        (count, EDGE, LANES),
        (2, EDGE, LANES),
    ]
    return pl.pallas_call(
        functools.partial(first_kernel, tiles, down),
        in_specs=[SMEM] + [VMEM] * 11,
        out_specs=[VMEM] * len(shapes),
        out_shape=floats(*shapes),
        input_output_aliases={index + 1: index for index in range(7)},
        scratch_shapes=[
            pltpu.VMEM(field, jnp.float32),
            pltpu.VMEM((tiles + 1, window, LANES), jnp.float32),
            pltpu.VMEM((2, 2, window + 2 * EDGE, LANES), jnp.float32),
        ],
        compiler_params=params(),
        name="first_direction",
    )(taps, *fields, got_b, got_a, coarse, dot)[2:]


def second_kernel(
    tiles,
    down,
    taps,
    got_ref,
    own_ref,
    table_ref,
    q_ref,
    east_ref,
    south_ref,
    inv_ref,
    dots_in,
    w_ref,
    v_ref,
    out_ref,
    image,
    spread,
    work,
):
    height = down * COARSE
    has_n, has_s, has_e, has_w = has_sides()
    at_col, at_row, n_cols, n_rows = place()
    me = at_col * n_rows + at_row

    def got(down_by, right_by):
        to_row, to_col = at_row + down_by, at_col + right_by
        there = (to_row >= 0) & (to_row < n_rows) & (to_col >= 0) & (to_col < n_cols)
        return got_ref[jnp.where(there, to_col * n_rows + to_row, me)]

    low = iota((EDGE, LANES), 1) < HALF
    gap = jnp.zeros((LANES - 2 * EDGE, LANES), jnp.float32)
    beside = jnp.transpose(jnp.concatenate([got(0, 1), gap, got(0, -1)], axis=0))[:down]
    source = jnp.concatenate(
        [
            jnp.concatenate([got(-1, 0), jnp.where(low, got(-1, 1), got(-1, -1))], axis=1),
            jnp.concatenate([own_ref[...], beside], axis=1),
            jnp.concatenate([got(1, 0), jnp.where(low, got(1, 1), got(1, -1))], axis=1),
        ],
        axis=0,
    )
    clear_work(work)
    spread_cells(jacobi(source, table_ref, work), spread)
    clear_pads(w_ref, image)
    sides = side_lanes(has_e, has_w)
    taps = read_taps(taps)

    def begin_w(at, start, total):
        field, inverse, cells = load(q_ref, at), load(inv_ref, at), cells_at(spread, at)
        strip = [field[t] * inverse[t] + cells[t] for t in range(tiles + 1)]
        first_row = jnp.maximum(start, 2 * EDGE)
        flags = [
            jnp.where((row >= first_row) & (row < 2 * EDGE + height), 1.0, 0.0)
            for row in [at + by for by in range(0, STRIP, EDGE)]
        ]
        return [(w_ref, strip)], total + product_sum(field, strip, tiles, flags)

    def blur(at, _, carry):
        strip = conv(w_ref, at, taps, False)
        strip[tiles] = strip[tiles] * sides
        return [(image, strip)], carry

    def finish(at, _, total):
        here, product = operate(w_ref, image, east_ref, south_ref, at, taps)
        return [(v_ref, product[:tiles])], total + product_sum(here, product, tiles)

    nothing = jnp.zeros((EDGE, LANES), jnp.float32)
    span = (EDGE, 3 * EDGE + height)
    dot_qw = sweep(3, *span, begin_w, nothing)
    sweep(3, *span, blur, 0)
    mask_rows(image, has_n, has_s)
    dot_wv = sweep(4, 2 * EDGE, 2 * EDGE + height, finish, nothing)
    line = jnp.zeros((1, LANES), jnp.float32)
    block = iota((1, LANES), 1) // (LANES // 4)
    for index, part in enumerate((dots_in[0], dots_in[1], dot_qw, dot_wv)):
        part = jnp.sum(part, axis=0, keepdims=True)
        part = part + roll(part, LANES // 2, 1)
        part = part + roll(part, LANES // 4, 1)
        line = jnp.where(block == index, part, line)
    for index in range(out_ref.shape[0]):
        out_ref[index] = line


def second(taps, got, own, table, q, east, south, inv, dots):
    tiles, height = q.shape[0] - 1, q.shape[1] - 4 * EDGE
    down = height // COARSE
    window = down + 2 * EDGE
    count = lax.axis_size("cols") * lax.axis_size("rows")
    return pl.pallas_call(
        functools.partial(second_kernel, tiles, down),
        in_specs=[SMEM] + [VMEM] * 8,
        out_specs=[VMEM] * 3,
        out_shape=floats(q.shape, q.shape, (count, 1, LANES)),
        scratch_shapes=[
            pltpu.VMEM(q.shape, jnp.float32),
            pltpu.VMEM((tiles + 1, window, LANES), jnp.float32),
            pltpu.VMEM((2, 2, window + 2 * EDGE, LANES), jnp.float32),
        ],
        compiler_params=params(),
        name="second_direction",
    )(taps, got, own, table, q, east, south, inv, dots)


def combine_kernel(
    tiles, height, sums_ref, p_ref, w_ref, r_ref, q_ref, v_ref, sol_out, res_out, sol, res, sem
):
    line = sums_ref[0]
    for index in range(1, sums_ref.shape[0]):
        line = line + sums_ref[index]
    block = iota((1, LANES), 1) // (LANES // 4)
    pick = lambda index: jnp.sum(jnp.where(block == index, line, 0.0), axis=1, keepdims=True)
    rp, pq, qw, wv = [pick(index) for index in range(4)]
    step = rp / pq
    rp_next = step * step * qw - rp
    ratio = rp_next / rp
    lead = 1.0 + ratio
    curvature = lead * lead * pq - 2.0 * lead * step * qw + step * step * wv
    step_next = rp_next / curvature
    on_p = jnp.broadcast_to(step + step_next * lead, (CHUNK, LANES))
    on_w = jnp.broadcast_to(step_next * step, (CHUNK, LANES))

    def copies(index):
        rows = pl.ds(pl.multiple_of(index * CHUNK, CHUNK), CHUNK)
        return (
            pltpu.make_async_copy(sol.at[rows, :], sol_out.at[rows, :], sem.at[0, index]),
            pltpu.make_async_copy(res.at[rows, :], res_out.at[rows, :], sem.at[1, index]),
        )

    def work(index, _):
        at = pl.multiple_of(index * CHUNK, CHUNK)
        p, w, r, q, v = [
            load(ref, at + 2 * EDGE, CHUNK) for ref in (p_ref, w_ref, r_ref, q_ref, v_ref)
        ]
        one = [on_p * p[t] - on_w * w[t] for t in range(tiles)]
        two = [r[t] - on_p * q[t] + on_w * v[t] for t in range(tiles)]
        for t in range(tiles):
            sol[pl.ds(at, CHUNK), t * LANES : (t + 1) * LANES] = one[t]
            res[pl.ds(at, CHUNK), t * LANES : (t + 1) * LANES] = two[t]
        for copy in copies(index):
            copy.start()
        return 0

    def settle(index, _):
        for copy in copies(index):
            copy.wait()
        return 0

    lax.fori_loop(0, height // CHUNK, work, 0)
    lax.fori_loop(0, height // CHUNK, settle, 0)


def combine(sums, p, w, r, q, v):
    tiles, height = q.shape[0] - 1, q.shape[1] - 4 * EDGE
    shape = (height, tiles * LANES)
    return pl.pallas_call(
        functools.partial(combine_kernel, tiles, height),
        in_specs=[VMEM] * 6,
        out_specs=[HBM] * 2,
        out_shape=floats(shape, shape),
        scratch_shapes=[
            pltpu.VMEM(shape, jnp.float32),
            pltpu.VMEM(shape, jnp.float32),
            pltpu.SemaphoreType.DMA((2, height // CHUNK)),
        ],
        compiler_params=params(),
        name="combine",
    )(sums, p, w, r, q, v)


def exchange(send_a, send_b, axis):
    count = lax.axis_size(axis)

    def pairs(begin):
        return [
            pair for i in range(begin, count - 1, 2) for pair in ((i, i + 1), (i + 1, i))
        ]

    got_b = lax.ppermute(send_b, axis, pairs(1))
    got_a = lax.ppermute(send_a, axis, pairs(0))
    return got_a, got_b


def body(observed, class_map, class_weights, blur_kernel):
    arguments = (observed, class_map, class_weights, blur_kernel)
    send_a, send_b = edge(*arguments)
    got_a, got_b = exchange(send_a, send_b, "cols")
    obs, cond, coarse = pack(*arguments, send_a)
    obs, cond, coarse, send_a, send_b = middle(got_a, got_b, coarse, obs, cond)
    got_a, got_b = exchange(send_a, send_b, "rows")
    r, east, south, inv, u, dot = inner(blur_kernel, obs, cond)
    fields = (obs, cond, r, east, south, inv, u)
    r, east, south, inv, _, p, q, table, own, chunk, dots = first(
        blur_kernel, fields, got_a, got_b, coarse, dot
    )
    got = lax.all_to_all(chunk, AXES, 0, 0, tiled=True)
    w, v, line = second(blur_kernel, got, own, table, q, east, south, inv, dots)
    sums = lax.all_to_all(line, AXES[::-1], 0, 0, tiled=True)
    return tuple(combine(sums, p, w, r, q, v))


def solution(mesh):
    return jax.shard_map(
        body,
        mesh=mesh,
        in_specs=(P("rows", "cols"), P("rows", "cols"), P(), P()),
        out_specs=(P("rows", "cols"), P("rows", "cols")),
        check_vma=False,
    )
```

```python
import functools

import jax
import jax.numpy as jnp
from jax import lax
from jax.experimental import pallas as pl
from jax.experimental.pallas import tpu as pltpu
from jax.sharding import PartitionSpec as P

COARSE = 8
SWEEPS = 8
CLASSES = 4
OMEGA = 0.8

LANES = 128
HALF = LANES // 2
EDGE = 8
STRIP = 2 * EDGE
REACH = 5
CHUNK = 64
AXES = ("cols", "rows")
LIMIT = 40 * 1024 * 1024


VMEM = pl.BlockSpec(memory_space=pltpu.VMEM)
SMEM = pl.BlockSpec(memory_space=pltpu.SMEM)
HBM = pl.BlockSpec(memory_space=pltpu.HBM)


def params():
    return pltpu.CompilerParams(vmem_limit_bytes=LIMIT)


def in_hbm(array):
    return pltpu.with_memory_space_constraint(array, pltpu.HBM)


def floats(*shapes):
    return [jax.ShapeDtypeStruct(shape, jnp.float32) for shape in shapes]


def place():
    at_col, at_row = lax.axis_index("cols"), lax.axis_index("rows")
    n_cols, n_rows = lax.axis_size("cols"), lax.axis_size("rows")
    return at_col, at_row, n_cols, n_rows


def has_sides():
    at_col, at_row, n_cols, n_rows = place()
    flag = lambda test: jnp.where(test, 1.0, 0.0).astype(jnp.float32)
    return (
        flag(at_row > 0),
        flag(at_row < n_rows - 1),
        flag(at_col < n_cols - 1),
        flag(at_col > 0),
    )


def iota(shape, dim):
    return lax.broadcasted_iota(jnp.int32, shape, dim)


def cell_of(pixel, tiles):
    turn = (tiles + 1) * LANES
    return jnp.where(pixel < turn - HALF, pixel >> 3, ((pixel - turn) >> 3) & (2 * LANES - 1))


def gather_matrix(tiles):
    shape = ((tiles + 1) * LANES, 2 * LANES)
    hit = cell_of(iota(shape, 0), tiles) == iota(shape, 1)
    return jnp.where(hit, 1.0, 0.0).astype(jnp.bfloat16)


def split_dot(field, matrix):
    rows = field.shape[0]
    high = field.astype(jnp.bfloat16)
    low = (field - high.astype(jnp.float32)).astype(jnp.bfloat16)
    both = jnp.dot(
        jnp.concatenate([high, low], axis=0), matrix, preferred_element_type=jnp.float32
    )
    return both[:rows] + both[rows:]


def roll(field, by, axis):
    return pltpu.roll(field, by % field.shape[axis], axis)


def load(ref, at, rows=STRIP):
    return [ref[t, pl.ds(at, rows), :] for t in range(ref.shape[0])]


def store(ref, at, strip):
    for t, part in enumerate(strip):
        ref[t, pl.ds(at, part.shape[0]), :] = part


def wide(ref, at, rows):
    return jnp.concatenate(load(ref, at, rows), axis=1)


def read_taps(taps):
    return [[taps[a, b] for b in range(3)] for a in range(3)]


def tap_total(taps, power):
    return sum(tap * tap if power == 2 else tap for line in taps for tap in line)


def from_west(strip):
    lane = iota(strip[0].shape, 1)
    turned = [roll(part, 1, 1) for part in strip]
    return [jnp.where(lane == 0, turned[t - 1], turned[t]) for t in range(len(strip))]


def from_east(strip):
    lane = iota(strip[0].shape, 1)
    turned = [roll(part, -1, 1) for part in strip]
    count = len(strip)
    return [
        jnp.where(lane == LANES - 1, turned[(t + 1) % count], turned[t]) for t in range(count)
    ]


def tap_sums(ref, at, taps, flip):
    if flip:
        taps = [line[::-1] for line in taps[::-1]]
    above, here, below = load(ref, at - 1), load(ref, at), load(ref, at + 1)
    sums = [[], [], []]
    for t in range(len(here)):
        for b in range(3):
            sums[b].append(
                taps[0][b] * above[t] + taps[1][b] * here[t] + taps[2][b] * below[t]
            )
    return sums


def conv(ref, at, taps, flip):
    sums = tap_sums(ref, at, taps, flip)
    west, east = from_west(sums[0]), from_east(sums[2])
    return [sums[1][t] + west[t] + east[t] for t in range(len(west))]


def operate(ref, image, east_ref, south_ref, at, taps):
    above, here, below = load(ref, at - 1), load(ref, at), load(ref, at + 1)
    east, south, north = load(east_ref, at), load(south_ref, at), load(south_ref, at - 1)
    sums = tap_sums(image, at, taps, True)
    span = range(len(here))
    beside = from_east(here)
    flux = [east[t] * (here[t] - beside[t]) for t in span]
    from_left = from_west([sums[0][t] - flux[t] for t in span])
    from_right = from_east(sums[2])
    return here, [
        sums[1][t]
        + flux[t]
        + from_left[t]
        + from_right[t]
        + south[t] * (here[t] - below[t])
        - north[t] * (above[t] - here[t])
        for t in span
    ]


def begin(obs, cond, at, taps, sides):
    above, here, below = load(cond, at - 1), load(cond, at), load(cond, at + 1)
    span = range(len(here))
    right = from_east(here)
    east = [here[t] + right[t] for t in span]
    west = from_west(east)
    south = [here[t] + below[t] for t in span]
    squares = tap_total(taps, 2)
    diag = [squares + east[t] + west[t] + south[t] + (here[t] + above[t]) for t in span]
    inverse = [pl.reciprocal(part, approx=True) for part in diag]
    inverse = [inverse[t] * (2.0 - diag[t] * inverse[t]) for t in span]
    inverse[-1] = inverse[-1] * sides
    residual = conv(obs, at, taps, True)
    return east, south, inverse, residual, [residual[t] * inverse[t] for t in span]


def pick_lanes(field, lanes):
    return jnp.take_along_axis(field, lanes, axis=1, mode="promise_in_bounds")


def spread_cells(cells, spread):
    tiles = spread.shape[0] - 1
    lane = iota((cells.shape[0], LANES), 1)
    for t in range(tiles):
        spread[t] = pick_lanes(cells[:, :LANES], (lane >> 3) + t * (LANES // COARSE))
    turn = jnp.where(lane < HALF, 0, LANES - LANES // COARSE)
    spread[tiles] = pick_lanes(cells[:, LANES:], (lane >> 3) + turn)


def cells_at(spread, at):
    first = at // EDGE + EDGE - 2
    rows = [load(spread, first + index, 1) for index in range(STRIP // EDGE)]
    return [
        jnp.concatenate([jnp.broadcast_to(row, (EDGE, LANES)) for row in parts], axis=0)
        for parts in zip(*rows)
    ]


def cell_sums(ref, tiles, down):
    lane = iota((down, LANES), 1)
    total = jnp.zeros((down, LANES), jnp.float32)
    for t in range(tiles):
        picked = [
            ref[t, pl.ds(2 * EDGE + k, down, stride=COARSE), :] for k in range(COARSE)
        ]
        part = sum(picked[1:], picked[0])
        for by in (1, 2, 4):
            part = part + roll(part, -by, 1)
        part = pick_lanes(part, (lane & (LANES // COARSE - 1)) * COARSE)
        total = jnp.where(lane // (LANES // COARSE) == t, part, total)
    return total


def side_lanes(has_e, has_w):
    return jnp.where(iota((STRIP, LANES), 1) < HALF, has_e, has_w)


def mask_rows(ref, has_n, has_s):
    last = ref.shape[1] - 2 * EDGE
    for at, flag in ((EDGE, has_n), (last, has_s)):
        ref[:, at : at + EDGE, :] = ref[:, at : at + EDGE, :] * flag


def clear_pads(*refs):
    empty = jnp.zeros((refs[0].shape[0], EDGE, LANES), jnp.float32)
    for ref in refs:
        ref[:, :EDGE, :] = empty
        ref[:, ref.shape[1] - EDGE :, :] = empty


def product_sum_rows(one, two, count):
    total = one[0] * two[0]
    for t in range(1, count):
        total = total + one[t] * two[t]
    return total


def product_sum(one, two, count, flags=None):
    return fold(product_sum_rows(one, two, count), flags)


def fold(total, flags=None):
    parts = [total[at : at + EDGE] for at in range(0, total.shape[0], EDGE)]
    if flags is not None:
        parts = [part * flag for part, flag in zip(parts, flags)]
    return sum(parts[1:], parts[0])


def sweep(group, first, last, body, carry):
    width = group * STRIP
    steps = -(-(last - first) // width)

    def work(index, carry):
        start = first + index * width
        at = pl.multiple_of(jnp.minimum(start, last - width), EDGE)
        pending = []
        for by in range(0, width, STRIP):
            stores, carry = body(at + by, start, carry)
            pending += [(ref, at + by, strip) for ref, strip in stores]
        for ref, row, strip in pending:
            store(ref, row, strip)
        return carry

    return lax.fori_loop(0, steps, work, carry)


def jacobi(source, table, work):
    factor, east, west, south, north = [table[index] for index in range(5)]
    window = source.shape[0]
    source = factor * source
    iterate = source
    for sweep_index in range(SWEEPS - 1):
        place_ref = work.at[sweep_index % 2]
        for half in range(2):
            place_ref[half, EDGE : EDGE + window, :] = iterate[
                :, half * LANES : (half + 1) * LANES
            ]
        above, below = [
            jnp.concatenate(
                [place_ref[half, EDGE + by : EDGE + by + window, :] for half in range(2)], axis=1
            )
            for by in (-1, 1)
        ]
        across = east * roll(iterate, -1, 1) + west * roll(iterate, 1, 1)
        along = south * below + north * above
        iterate = ((1.0 - OMEGA) * iterate + source) + (across + along)
    return iterate


def clear_work(work):
    for buffer in range(2):
        clear_pads(work.at[buffer])


def in_pair_order(at, for_before, for_after):
    even = at % 2 == 0
    if callable(for_before):
        return (
            lambda *args: jnp.where(even, for_after(*args), for_before(*args)),
            lambda *args: jnp.where(even, for_before(*args), for_after(*args)),
        )
    return jnp.where(even, for_after, for_before), jnp.where(even, for_before, for_after)


def reader(tiles_here, refs, scratch, obs, cond, down):
    obs_in, class_in, weight_in, taps_in = refs
    classes, weights, taps, sums, obs_sem, class_sem, small_sem = scratch
    own = pl.ds(2 * EDGE, down * COARSE)
    small = [
        pltpu.make_async_copy(weight_in, weights, small_sem.at[0]),
        pltpu.make_async_copy(taps_in, taps, small_sem.at[1]),
    ]
    moves = []
    for slot, t in enumerate(tiles_here):
        lanes = pl.ds(t * LANES, LANES)
        moves.append(
            (
                pltpu.make_async_copy(class_in.at[:, lanes], classes.at[slot], class_sem.at[slot]),
                pltpu.make_async_copy(
                    obs_in.at[:, lanes], obs.at[slot, own, :], obs_sem.at[slot]
                ),
            )
        )
    for copy in small:
        copy.start()
    for pair in moves:
        for copy in pair:
            copy.start()
    sums[...] = jnp.zeros_like(sums)

    def settle(slot):
        if slot == 0:
            for copy in small:
                copy.wait()
        for copy in moves[slot]:
            copy.wait()
        values = [0.5 * weights[class_id] for class_id in range(CLASSES)]
        kind = classes[slot]
        cond[slot, own, :] = jnp.where(
            kind < 2,
            jnp.where(kind == 0, values[0], values[1]),
            jnp.where(kind == 2, values[2], values[3]),
        )
        for which, ref in enumerate((obs, cond)):
            picked = [
                ref[slot, pl.ds(2 * EDGE + k, down, stride=COARSE), :] for k in range(COARSE)
            ]
            cells = slice(2 * EDGE, 2 * EDGE + down)
            sums[3 * which, slot, cells, :] = sum(picked[1:], picked[0])
            sums[3 * which + 1, slot, cells, :] = picked[0]
            sums[3 * which + 2, slot, cells, :] = picked[-1]

    return settle


def reader_scratch(tiles, height, window, class_weights, taps):
    return [
        pltpu.VMEM((tiles, height, LANES), jnp.int32),
        pltpu.SMEM(class_weights.shape, jnp.float32),
        pltpu.SMEM(taps.shape, jnp.float32),
        pltpu.VMEM((6, tiles + 1, window + 2 * EDGE, LANES), jnp.float32),
        pltpu.SemaphoreType.DMA((tiles,)),
        pltpu.SemaphoreType.DMA((tiles,)),
        pltpu.SemaphoreType.DMA((2,)),
    ]


def coarse_parts(sums, taps, matrix):
    window = sums.shape[2] - 2 * EDGE
    whole = lambda index, by=0: wide(sums.at[index], EDGE + by, window)
    full = whole(0)
    by_tap = [full - whole(1) + whole(1, 1), full, full - whole(2) + whole(2, -1)]
    across = [sum(taps[a][b] * by_tap[a] for a in range(3)) for b in range(3)]
    source = across[1] + roll(across[0], -1, 1) + roll(across[2], 1, 1)
    full = whole(3)
    last = (iota(full.shape, 1) & (COARSE - 1)) == COARSE - 1
    east = jnp.where(last, full + roll(full, -1, 1), 0.0)
    south = whole(5) + whole(4, 1)
    cells = split_dot(jnp.concatenate([source, east, south], axis=0), matrix)
    source, east, south = cells[:window], cells[window : 2 * window], cells[2 * window :]
    around = east + roll(east, 1, 1) + south + roll(south, 1, 0)
    return [source, east, south, around]


def edge_kernel(tiles, down, *refs):
    arguments, (send_a, send_b), (obs, cond, message, *scratch) = refs[:4], refs[4:6], refs[6:]
    height = down * COARSE
    halves = height // LANES
    window = down + 2 * EDGE
    settle = reader((0, tiles - 1), arguments, scratch, obs, cond, down)
    matrix = gather_matrix(2)
    fine = [[], []]
    for slot, begin_row in ((0, 0), (1, LANES - REACH)):
        settle(slot)
        for ref in (obs, cond):
            turned = jnp.transpose(ref[slot, 2 * EDGE : 2 * EDGE + height, :])
            turned = turned[begin_row : begin_row + REACH]
            for half in range(halves):
                fine[slot].append(turned[:, half * LANES : (half + 1) * LANES])
    parts = coarse_parts(scratch[3], read_taps(scratch[2]), matrix)
    spare = jnp.zeros((2 * LANES - 4 * window, 2 * LANES), jnp.float32)
    stack = jnp.concatenate(parts + [spare], axis=0)
    left = jnp.transpose(stack[:, :LANES])
    right = jnp.transpose(stack[:, LANES:])
    past = 2 * LANES // COARSE
    split = lambda piece: [piece[:, half * LANES : (half + 1) * LANES] for half in range(2)]
    for slot, main, over in (
        (0, left[:EDGE], right[LANES - 1 :]),
        (1, left[past - EDGE : past], left[past : past + 1]),
    ):
        rows = split(main) + fine[slot] + split(over)
        filled = sum(piece.shape[0] for piece in rows)
        rows.append(jnp.zeros((message.shape[1] - filled, LANES), jnp.float32))
        message[slot] = jnp.concatenate(rows, axis=0)
    send_a[...], send_b[...] = in_pair_order(place()[0], message[0], message[1])


def edge(observed, class_map, class_weights, taps):
    height, breadth = observed.shape
    tiles, down = breadth // LANES, height // COARSE
    window = down + 2 * EDGE
    field = (3, height + 4 * EDGE, LANES)
    rows = 2 * EDGE + 2 * REACH * (height // LANES) + 2
    strip = (-(-rows // EDGE) * EDGE, LANES)
    return pl.pallas_call(
        functools.partial(edge_kernel, tiles, down),
        in_specs=[HBM] * 4,
        out_specs=[VMEM] * 2,
        out_shape=floats(strip, strip),
        scratch_shapes=[
            pltpu.VMEM(field, jnp.float32),
            pltpu.VMEM(field, jnp.float32),
            pltpu.VMEM((2,) + strip, jnp.float32),
        ]
        + reader_scratch(2, height, window, class_weights, taps),
        compiler_params=params(),
        name="pack_east_west",
    )(*[in_hbm(array) for array in (observed, class_map, class_weights, taps)])


def pack_kernel(tiles, down, *refs):
    arguments, (obs, cond, coarse_ref), scratch = refs[:4], refs[5:8], refs[8:]
    settle = reader(range(tiles), arguments, scratch, obs, cond, down)
    matrix = gather_matrix(tiles)
    for t in range(tiles):
        settle(t)
    for index, part in enumerate(coarse_parts(scratch[3], read_taps(scratch[2]), matrix)):
        coarse_ref[index] = part


def pack(observed, class_map, class_weights, taps, after):
    height, breadth = observed.shape
    tiles, down = breadth // LANES, height // COARSE
    window = down + 2 * EDGE
    field = (tiles + 1, height + 4 * EDGE, LANES)
    pixels = height * breadth
    return pl.pallas_call(
        functools.partial(pack_kernel, tiles, down),
        in_specs=[HBM] * 4 + [VMEM],
        out_specs=[VMEM] * 3,
        out_shape=floats(field, field, (4, window, 2 * LANES)),
        scratch_shapes=reader_scratch(tiles, height, window, class_weights, taps),
        compiler_params=params(),
        cost_estimate=pl.CostEstimate(
            flops=20 * pixels, bytes_accessed=16 * pixels, transcendentals=0
        ),
        name="pack_all",
    )(*[in_hbm(array) for array in (observed, class_map, class_weights, taps)], after)


def message_rows(tiles):
    rest = EDGE
    fine = rest + 2 * tiles
    sides = fine + tiles * EDGE
    return 0, rest, fine, sides, sides + EDGE


def merge_sides(parts):
    block = iota((EDGE, LANES), 1) // (2 * EDGE)
    merged = jnp.zeros((EDGE, LANES), jnp.float32)
    for index, part in enumerate(parts):
        merged = jnp.where(block == index, roll(part, (2 * index + 1) * EDGE, 1), merged)
    return merged


def split_sides(merged, count):
    lane = iota((EDGE, LANES), 1)
    outer = (lane < EDGE) | (lane >= LANES - EDGE)
    return [
        jnp.where(outer, roll(merged, -(2 * index + 1) * EDGE, 1), 0.0) for index in range(count)
    ]


def middle_kernel(
    tiles,
    down,
    got_b,
    got_a,
    coarse_in,
    obs_in,
    cond_in,
    obs,
    cond,
    coarse_ref,
    send_a,
    send_b,
    message,
):
    height = down * COARSE
    halves = height // LANES
    at_col, at_row, _, _ = place()
    from_e, from_w = in_pair_order(at_col, got_b[...], got_a[...])
    zeros = lambda rows: jnp.zeros((rows, LANES), jnp.float32)

    def turned(low, high):
        low = [low, zeros(EDGE - low.shape[0])] if low.shape[0] < EDGE else [low]
        high = [zeros(EDGE - high.shape[0]), high] if high.shape[0] < EDGE else [high]
        return jnp.transpose(jnp.concatenate([*low, zeros(LANES - 2 * EDGE), *high], axis=0))

    for which, field in enumerate((obs, cond)):
        for half in range(halves):
            at = 2 * EDGE + REACH * (which * halves + half)
            begin_row = 2 * EDGE + half * LANES
            field[tiles, begin_row : begin_row + LANES, :] = turned(
                from_e[at : at + REACH], from_w[at : at + REACH]
            )
    main = lambda strip, half: strip[half * EDGE : (half + 1) * EDGE]

    def over(strip, half):
        at = 2 * EDGE + 2 * REACH * halves + half
        return strip[at : at + 1]

    left = [turned(over(from_w, half), over(from_e, half)) for half in range(2)]
    right = [turned(main(from_e, half), main(from_w, half)) for half in range(2)]
    left = jnp.concatenate(left, axis=0)
    right = jnp.concatenate(right, axis=0)
    window = down + 2 * EDGE
    for index in range(4):
        rows = slice(index * window, (index + 1) * window)
        coarse_ref[index, :, :LANES] = coarse_in[index, :, :LANES] + left[rows]
        coarse_ref[index, :, LANES:] = coarse_in[index, :, LANES:] + right[rows]
    row = iota((EDGE, LANES), 0)
    over_at, rest_at, fine_at, sides_at, coarse_at = message_rows(tiles)
    for slot, begin_row, reach_row, first_row, over_row in (
        (0, 2 * EDGE, 2 * EDGE, EDGE, EDGE - 1),
        (1, EDGE + height, 2 * EDGE + height - REACH, window - 2 * EDGE, window - EDGE),
    ):
        for t in range(tiles):
            at = fine_at + t * EDGE
            message[slot, at : at + EDGE, :] = jnp.where(
                row < REACH,
                obs[t, reach_row : reach_row + EDGE, :],
                cond[t, reach_row - REACH : reach_row - REACH + EDGE, :],
            )
        for begin_tile in range(0, tiles, 4):
            rest = None
            for index in range(4):
                at = reach_row + EDGE - REACH - 2 * index
                piece = cond[begin_tile + index, at : at + EDGE, :]
                rest = piece if rest is None else jnp.where(row < 2 * index, rest, piece)
            at = rest_at + begin_tile * 2
            message[slot, at : at + EDGE, :] = rest
        rows = slice(first_row, first_row + EDGE)
        for index in range(4):
            at = coarse_at + index * EDGE
            message[slot, at : at + EDGE, :] = coarse_ref[index, rows, :LANES]
        beyond = [coarse_ref[index, rows, LANES:] for index in range(4)]
        beyond += [field[tiles, begin_row : begin_row + EDGE, :] for field in (obs, cond)]
        message[slot, sides_at : sides_at + EDGE, :] = merge_sides(beyond)
        message[slot, over_at : over_at + EDGE, :] = jnp.concatenate(
            [
                coarse_ref[index, over_row : over_row + 1, half * LANES : (half + 1) * LANES]
                for index in range(4)
                for half in range(2)
            ],
            axis=0,
        )
    send_a[...], send_b[...] = in_pair_order(at_row, message[0], message[1])


def middle(got_a, got_b, coarse, obs, cond):
    tiles, height = obs.shape[0] - 1, obs.shape[1] - 4 * EDGE
    down = height // COARSE
    long = (message_rows(tiles)[-1] + 4 * EDGE, LANES)
    return pl.pallas_call(
        functools.partial(middle_kernel, tiles, down),
        in_specs=[VMEM] * 5,
        out_specs=[VMEM] * 5,
        out_shape=floats(obs.shape, cond.shape, coarse.shape, long, long),
        input_output_aliases={3: 0, 4: 1},
        scratch_shapes=[pltpu.VMEM((2,) + long, jnp.float32)],
        compiler_params=params(),
        name="pack_north_south",
    )(got_b, got_a, coarse, obs, cond)


def inner_kernel(taps, obs, cond, res_ref, east_ref, south_ref, inv_ref, u_ref, dot_ref):
    _, _, has_e, has_w = has_sides()
    clear_pads(east_ref, south_ref)
    taps = read_taps(taps)
    sides = side_lanes(has_e, has_w)

    tiles = obs.shape[0] - 1

    def work(at, start, total):
        fields = begin(obs, cond, at, taps, sides)
        flags = [jnp.where(at + by >= start, 1.0, 0.0) for by in range(0, STRIP, EDGE)]
        total = total + product_sum(fields[3], fields[4], tiles, flags)
        return list(zip((east_ref, south_ref, inv_ref, res_ref, u_ref), fields)), total

    nothing = jnp.zeros((EDGE, LANES), jnp.float32)
    dot_ref[...] = sweep(5, 3 * EDGE, obs.shape[1] - 3 * EDGE, work, nothing)


def inner(taps, obs, cond):
    field = obs.shape
    pixels = field[0] * field[1] * field[2]
    return pl.pallas_call(
        inner_kernel,
        in_specs=[SMEM] + [VMEM] * 2,
        out_specs=[VMEM] * 6,
        out_shape=floats(field, field, field, field, field, (EDGE, LANES)),
        compiler_params=params(),
        cost_estimate=pl.CostEstimate(
            flops=45 * pixels, bytes_accessed=24 * pixels, transcendentals=0
        ),
        name="inner_strips",
    )(taps, obs, cond)


def first_kernel(
    tiles,
    down,
    taps,
    obs_in,
    cond_in,
    res_in,
    east_in,
    south_in,
    inv_in,
    u_in,
    got_b,
    got_a,
    coarse_in,
    dot_in,
    obs,
    cond,
    res_ref,
    east_ref,
    south_ref,
    inv_ref,
    u_ref,
    p_ref,
    q_ref,
    table_ref,
    own_ref,
    chunk_ref,
    dots_ref,
    image,
    spread,
    work,
):
    height = down * COARSE
    window = down + 2 * EDGE
    at_col, at_row, n_cols, n_rows = place()
    has_n, has_s, has_e, has_w = has_sides()
    clear_pads(obs, cond, p_ref, image)
    clear_work(work)
    from_s, from_n = in_pair_order(
        at_row,
        lambda at, rows=EDGE: got_b[at : at + rows, :],
        lambda at, rows=EDGE: got_a[at : at + rows, :],
    )
    over_at, rest_at, fine_at, sides_at, coarse_at = message_rows(tiles)
    row = iota((EDGE, LANES), 0)
    short = EDGE - REACH
    for t in range(tiles):
        at = fine_at + t * EDGE
        rest = rest_at + 2 * t
        begin_row = 2 * EDGE + height
        obs[t, EDGE : 2 * EDGE, :] = jnp.where(row >= short, from_n(at - short), 0.0)
        obs[t, begin_row : begin_row + EDGE, :] = jnp.where(row < REACH, from_s(at), 0.0)
        near, far = from_n(at + REACH - short), from_n(rest - 2 * short)
        near = jnp.where(row < short, 0.0, near)
        cond[t, EDGE : 2 * EDGE, :] = jnp.where(row < 2 * short, near, far)
        near, far = from_s(at + REACH), from_s(rest - short)
        far = jnp.where(row < REACH, far, 0.0)
        cond[t, begin_row : begin_row + EDGE, :] = jnp.where(row < short, near, far)
    sides_n, sides_s = [split_sides(strip(sides_at), 6) for strip in (from_n, from_s)]
    for which, field in enumerate((obs, cond)):
        field[tiles, EDGE : 2 * EDGE, :] = sides_n[4 + which]
        field[tiles, 2 * EDGE + height : 3 * EDGE + height, :] = sides_s[4 + which]

    edge_row = iota((EDGE, 2 * LANES), 0)

    def joined(index):
        def over(strip, row):
            line = [
                jnp.broadcast_to(
                    strip(over_at + 2 * index + half, 1), (EDGE, LANES)
                )
                for half in range(2)
            ]
            return jnp.where(edge_row == row, jnp.concatenate(line, axis=1), 0.0)

        def rows(strip, beyond):
            return jnp.concatenate([strip(coarse_at + index * EDGE), beyond[index]], axis=1)

        parts = [coarse_in[index, at : at + EDGE, :] for at in range(0, window, EDGE)]
        parts[0] = parts[0] + rows(from_n, sides_n)
        parts[1] = parts[1] + over(from_n, 0)
        parts[-2] = parts[-2] + over(from_s, EDGE - 1)
        parts[-1] = parts[-1] + rows(from_s, sides_s)
        return jnp.concatenate(parts, axis=0)

    source, east, south, around = [joined(index) for index in range(4)]
    row = iota(source.shape, 0)
    lane = iota(source.shape, 1)
    inside = jnp.where(row < EDGE, has_n, jnp.where(row < window - EDGE, 1.0, has_s))
    inside = inside * jnp.where(
        lane < LANES, 1.0, jnp.where(lane < LANES + HALF, has_e, has_w)
    )
    taps = read_taps(taps)
    taps_sum = tap_total(taps, 1)
    factor = inside * OMEGA / (COARSE * COARSE * taps_sum * taps_sum + around)
    weights = (east, roll(east, 1, 1), south, roll(south, 1, 0))
    table = [factor] + [factor * weight for weight in weights]
    for index, part in enumerate(table):
        table_ref[index] = part
    sides = side_lanes(has_e, has_w)
    half = iota((STRIP, LANES), 0) // EDGE
    pending = []
    total = dot_in[...]
    for index, known in ((0, has_n), (1, has_s)):
        at = EDGE + index * height
        fields = begin(obs, cond, at, taps, sides)
        own = jnp.where(half == index, 0.0, 1.0)
        total = total + fold(own * product_sum_rows(fields[3], fields[4], tiles))
        flag = jnp.where(half == index, known, 1.0)
        inverse, start = [[part * flag for part in fields[index]] for index in (2, 4)]
        fields = (*fields[:2], inverse, fields[3], start)
        pending += [
            (ref, at, strip)
            for ref, strip in zip((east_ref, south_ref, inv_ref, res_ref, u_ref), fields)
        ]
    cells = jacobi(source, table, work)
    spread_cells(cells, spread)
    inner_cells = slice(EDGE, EDGE + down)
    total = total + fold(source[inner_cells, :LANES] * cells[inner_cells, :LANES])
    dots_ref[0] = total
    for ref, at, strip in pending:
        store(ref, at, strip)

    def flags(at, start):
        rows = [at + by for by in range(0, STRIP, EDGE)]
        first_row = jnp.maximum(start, 2 * EDGE)
        return [
            jnp.where((row >= first_row) & (row < 2 * EDGE + height), 1.0, 0.0) for row in rows
        ]

    def begin_p(at, _, carry):
        start, cells = load(u_ref, at), cells_at(spread, at)
        return [(p_ref, [start[t] + cells[t] for t in range(tiles + 1)])], carry

    def blur(at, _, carry):
        strip = conv(p_ref, at, taps, False)
        strip[tiles] = strip[tiles] * sides
        return [(image, strip)], carry

    def finish(at, start, total):
        here, product = operate(p_ref, image, east_ref, south_ref, at, taps)
        return [(q_ref, product)], total + product_sum(here, product, tiles, flags(at, start))

    nothing = jnp.zeros((EDGE, LANES), jnp.float32)
    span = (EDGE, 3 * EDGE + height)
    sweep(3, *span, begin_p, 0)
    sweep(3, *span, blur, 0)
    mask_rows(image, has_n, has_s)
    dots_ref[1] = sweep(3, *span, finish, nothing)

    own = cell_sums(q_ref, tiles, down)
    own_ref[...] = own
    spare = jnp.zeros((LANES - down, LANES), jnp.float32)
    turned = jnp.transpose(jnp.concatenate([own, spare], axis=0))
    chunk_ref[...] = jnp.zeros_like(chunk_ref)
    for down_by in (-1, 0, 1):
        for right_by in (-1, 0, 1):
            if down_by == 0 and right_by == 0:
                continue
            if down_by == 0:
                piece = turned[:EDGE] if right_by < 0 else turned[LANES - EDGE :]
            else:
                piece = own[:EDGE] if down_by < 0 else own[down - EDGE :]
            to_row, to_col = at_row + down_by, at_col + right_by
            there = (to_row >= 0) & (to_row < n_rows) & (to_col >= 0) & (to_col < n_cols)
            slot = jnp.where(there, to_col * n_rows + to_row, at_col * n_rows + at_row)
            chunk_ref[slot] = piece * jnp.where(there, 1.0, 0.0)


def first(taps, fields, got_a, got_b, coarse, dot):
    field = fields[0].shape
    tiles, height = field[0] - 1, field[1] - 4 * EDGE
    down = height // COARSE
    window = down + 2 * EDGE
    count = lax.axis_size("cols") * lax.axis_size("rows")
    shapes = [field] * 9 + [
        (5, window, 2 * LANES),
        (down, LANES),
        (count, EDGE, LANES),
        (2, EDGE, LANES),
    ]
    return pl.pallas_call(
        functools.partial(first_kernel, tiles, down),
        in_specs=[SMEM] + [VMEM] * 11,
        out_specs=[VMEM] * len(shapes),
        out_shape=floats(*shapes),
        input_output_aliases={index + 1: index for index in range(7)},
        scratch_shapes=[
            pltpu.VMEM(field, jnp.float32),
            pltpu.VMEM((tiles + 1, window, LANES), jnp.float32),
            pltpu.VMEM((2, 2, window + 2 * EDGE, LANES), jnp.float32),
        ],
        compiler_params=params(),
        name="first_direction",
    )(taps, *fields, got_b, got_a, coarse, dot)[2:]


def second_kernel(
    tiles,
    down,
    taps,
    got_ref,
    own_ref,
    table_ref,
    q_ref,
    east_ref,
    south_ref,
    inv_ref,
    dots_in,
    w_ref,
    v_ref,
    out_ref,
    image,
    spread,
    work,
):
    height = down * COARSE
    has_n, has_s, has_e, has_w = has_sides()
    at_col, at_row, n_cols, n_rows = place()
    me = at_col * n_rows + at_row

    def got(down_by, right_by):
        to_row, to_col = at_row + down_by, at_col + right_by
        there = (to_row >= 0) & (to_row < n_rows) & (to_col >= 0) & (to_col < n_cols)
        return got_ref[jnp.where(there, to_col * n_rows + to_row, me)]

    low = iota((EDGE, LANES), 1) < HALF
    gap = jnp.zeros((LANES - 2 * EDGE, LANES), jnp.float32)
    beside = jnp.transpose(jnp.concatenate([got(0, 1), gap, got(0, -1)], axis=0))[:down]
    source = jnp.concatenate(
        [
            jnp.concatenate([got(-1, 0), jnp.where(low, got(-1, 1), got(-1, -1))], axis=1),
            jnp.concatenate([own_ref[...], beside], axis=1),
            jnp.concatenate([got(1, 0), jnp.where(low, got(1, 1), got(1, -1))], axis=1),
        ],
        axis=0,
    )
    clear_work(work)
    spread_cells(jacobi(source, table_ref, work), spread)
    clear_pads(w_ref, image)
    sides = side_lanes(has_e, has_w)
    taps = read_taps(taps)

    def begin_w(at, start, total):
        field, inverse, cells = load(q_ref, at), load(inv_ref, at), cells_at(spread, at)
        strip = [field[t] * inverse[t] + cells[t] for t in range(tiles + 1)]
        first_row = jnp.maximum(start, 2 * EDGE)
        flags = [
            jnp.where((row >= first_row) & (row < 2 * EDGE + height), 1.0, 0.0)
            for row in [at + by for by in range(0, STRIP, EDGE)]
        ]
        return [(w_ref, strip)], total + product_sum(field, strip, tiles, flags)

    def blur(at, _, carry):
        strip = conv(w_ref, at, taps, False)
        strip[tiles] = strip[tiles] * sides
        return [(image, strip)], carry

    def finish(at, _, total):
        here, product = operate(w_ref, image, east_ref, south_ref, at, taps)
        return [(v_ref, product[:tiles])], total + product_sum(here, product, tiles)

    nothing = jnp.zeros((EDGE, LANES), jnp.float32)
    span = (EDGE, 3 * EDGE + height)
    dot_qw = sweep(3, *span, begin_w, nothing)
    sweep(3, *span, blur, 0)
    mask_rows(image, has_n, has_s)
    dot_wv = sweep(4, 2 * EDGE, 2 * EDGE + height, finish, nothing)
    line = jnp.zeros((1, LANES), jnp.float32)
    block = iota((1, LANES), 1) // (LANES // 4)
    for index, part in enumerate((dots_in[0], dots_in[1], dot_qw, dot_wv)):
        part = jnp.sum(part, axis=0, keepdims=True)
        part = part + roll(part, LANES // 2, 1)
        part = part + roll(part, LANES // 4, 1)
        line = jnp.where(block == index, part, line)
    for index in range(out_ref.shape[0]):
        out_ref[index] = line


def second(taps, got, own, table, q, east, south, inv, dots):
    tiles, height = q.shape[0] - 1, q.shape[1] - 4 * EDGE
    down = height // COARSE
    window = down + 2 * EDGE
    count = lax.axis_size("cols") * lax.axis_size("rows")
    return pl.pallas_call(
        functools.partial(second_kernel, tiles, down),
        in_specs=[SMEM] + [VMEM] * 8,
        out_specs=[VMEM] * 3,
        out_shape=floats(q.shape, q.shape, (count, 1, LANES)),
        scratch_shapes=[
            pltpu.VMEM(q.shape, jnp.float32),
            pltpu.VMEM((tiles + 1, window, LANES), jnp.float32),
            pltpu.VMEM((2, 2, window + 2 * EDGE, LANES), jnp.float32),
        ],
        compiler_params=params(),
        name="second_direction",
    )(taps, got, own, table, q, east, south, inv, dots)


def combine_kernel(
    tiles, height, sums_ref, p_ref, w_ref, r_ref, q_ref, v_ref, sol_out, res_out, sol, res, sem
):
    line = sums_ref[0]
    for index in range(1, sums_ref.shape[0]):
        line = line + sums_ref[index]
    block = iota((1, LANES), 1) // (LANES // 4)
    pick = lambda index: jnp.sum(jnp.where(block == index, line, 0.0), axis=1, keepdims=True)
    rp, pq, qw, wv = [pick(index) for index in range(4)]
    step = rp / pq
    rp_next = step * step * qw - rp
    ratio = rp_next / rp
    lead = 1.0 + ratio
    curvature = lead * lead * pq - 2.0 * lead * step * qw + step * step * wv
    step_next = rp_next / curvature
    on_p = jnp.broadcast_to(step + step_next * lead, (CHUNK, LANES))
    on_w = jnp.broadcast_to(step_next * step, (CHUNK, LANES))

    def copies(index):
        rows = pl.ds(pl.multiple_of(index * CHUNK, CHUNK), CHUNK)
        return (
            pltpu.make_async_copy(sol.at[rows, :], sol_out.at[rows, :], sem.at[0, index]),
            pltpu.make_async_copy(res.at[rows, :], res_out.at[rows, :], sem.at[1, index]),
        )

    def work(index, _):
        at = pl.multiple_of(index * CHUNK, CHUNK)
        p, w, r, q, v = [
            load(ref, at + 2 * EDGE, CHUNK) for ref in (p_ref, w_ref, r_ref, q_ref, v_ref)
        ]
        one = [on_p * p[t] - on_w * w[t] for t in range(tiles)]
        two = [r[t] - on_p * q[t] + on_w * v[t] for t in range(tiles)]
        for t in range(tiles):
            sol[pl.ds(at, CHUNK), t * LANES : (t + 1) * LANES] = one[t]
            res[pl.ds(at, CHUNK), t * LANES : (t + 1) * LANES] = two[t]
        for copy in copies(index):
            copy.start()
        return 0

    def settle(index, _):
        for copy in copies(index):
            copy.wait()
        return 0

    lax.fori_loop(0, height // CHUNK, work, 0)
    lax.fori_loop(0, height // CHUNK, settle, 0)


def combine(sums, p, w, r, q, v):
    tiles, height = q.shape[0] - 1, q.shape[1] - 4 * EDGE
    shape = (height, tiles * LANES)
    return pl.pallas_call(
        functools.partial(combine_kernel, tiles, height),
        in_specs=[VMEM] * 6,
        out_specs=[HBM] * 2,
        out_shape=floats(shape, shape),
        scratch_shapes=[
            pltpu.VMEM(shape, jnp.float32),
            pltpu.VMEM(shape, jnp.float32),
            pltpu.SemaphoreType.DMA((2, height // CHUNK)),
        ],
        compiler_params=params(),
        name="combine",
    )(sums, p, w, r, q, v)


def exchange(send_a, send_b, axis):
    count = lax.axis_size(axis)

    def pairs(begin):
        return [
            pair for i in range(begin, count - 1, 2) for pair in ((i, i + 1), (i + 1, i))
        ]

    got_b = lax.ppermute(send_b, axis, pairs(1))
    got_a = lax.ppermute(send_a, axis, pairs(0))
    return got_a, got_b


def body(observed, class_map, class_weights, blur_kernel):
    arguments = (observed, class_map, class_weights, blur_kernel)
    send_a, send_b = edge(*arguments)
    got_a, got_b = exchange(send_a, send_b, "cols")
    obs, cond, coarse = pack(*arguments, send_a)
    obs, cond, coarse, send_a, send_b = middle(got_a, got_b, coarse, obs, cond)
    got_a, got_b = exchange(send_a, send_b, "rows")
    r, east, south, inv, u, dot = inner(blur_kernel, obs, cond)
    fields = (obs, cond, r, east, south, inv, u)
    r, east, south, inv, _, p, q, table, own, chunk, dots = first(
        blur_kernel, fields, got_a, got_b, coarse, dot
    )
    got = lax.all_to_all(chunk, AXES, 0, 0, tiled=True)
    w, v, line = second(blur_kernel, got, own, table, q, east, south, inv, dots)
    sums = lax.all_to_all(line, AXES[::-1], 0, 0, tiled=True)
    return tuple(combine(sums, p, w, r, q, v))


def solution(mesh):
    return jax.shard_map(
        body,
        mesh=mesh,
        in_specs=(P("rows", "cols"), P("rows", "cols"), P(), P()),
        out_specs=(P("rows", "cols"), P("rows", "cols")),
        check_vma=False,
    )
```

```python
import functools

import jax
import jax.numpy as jnp
from jax import lax
from jax.experimental import pallas as pl
from jax.experimental.pallas import tpu as pltpu
from jax.sharding import PartitionSpec as P

COARSE = 8
SWEEPS = 8
CLASSES = 4
OMEGA = 0.8

LANES = 128
HALF = LANES // 2
EDGE = 8
STRIP = 2 * EDGE
REACH = 5
PIECE = EDGE + 1
CHUNK = 64
AXES = ("cols", "rows")
LIMIT = 40 * 1024 * 1024


VMEM = pl.BlockSpec(memory_space=pltpu.VMEM)
SMEM = pl.BlockSpec(memory_space=pltpu.SMEM)
HBM = pl.BlockSpec(memory_space=pltpu.HBM)


def params():
    return pltpu.CompilerParams(vmem_limit_bytes=LIMIT)


def in_hbm(array):
    return pltpu.with_memory_space_constraint(array, pltpu.HBM)


def floats(*shapes):
    return [jax.ShapeDtypeStruct(shape, jnp.float32) for shape in shapes]


def place():
    at_col, at_row = lax.axis_index("cols"), lax.axis_index("rows")
    n_cols, n_rows = lax.axis_size("cols"), lax.axis_size("rows")
    return at_col, at_row, n_cols, n_rows


def has_sides():
    at_col, at_row, n_cols, n_rows = place()
    flag = lambda test: jnp.where(test, 1.0, 0.0).astype(jnp.float32)
    return (
        flag(at_row > 0),
        flag(at_row < n_rows - 1),
        flag(at_col < n_cols - 1),
        flag(at_col > 0),
    )


def iota(shape, dim):
    return lax.broadcasted_iota(jnp.int32, shape, dim)


def cell_of(pixel, tiles):
    turn = (tiles + 1) * LANES
    return jnp.where(pixel < turn - HALF, pixel >> 3, ((pixel - turn) >> 3) & (2 * LANES - 1))


def gather_matrix(tiles):
    shape = ((tiles + 1) * LANES, 2 * LANES)
    hit = cell_of(iota(shape, 0), tiles) == iota(shape, 1)
    return jnp.where(hit, 1.0, 0.0).astype(jnp.bfloat16)


def split_dot(field, matrix):
    rows = field.shape[0]
    parts, rest = [], field
    for _ in range(3):
        parts.append(rest.astype(jnp.bfloat16))
        rest = rest - parts[-1].astype(jnp.float32)
    product = jnp.dot(
        jnp.concatenate(parts, axis=0), matrix, preferred_element_type=jnp.float32
    )
    return product[:rows] + (product[rows : 2 * rows] + product[2 * rows :])


def roll(field, by, axis):
    return pltpu.roll(field, by % field.shape[axis], axis)


def load(ref, at, rows=STRIP):
    return [ref[t, pl.ds(at, rows), :] for t in range(ref.shape[0])]


def store(ref, at, strip):
    for t, part in enumerate(strip):
        ref[t, pl.ds(at, part.shape[0]), :] = part


def wide(ref, at, rows):
    return jnp.concatenate(load(ref, at, rows), axis=1)


def read_taps(taps):
    return [[taps[a, b] for b in range(3)] for a in range(3)]


def tap_total(taps, power):
    return sum(tap * tap if power == 2 else tap for line in taps for tap in line)


def from_west(strip):
    lane = iota(strip[0].shape, 1)
    turned = [roll(part, 1, 1) for part in strip]
    return [jnp.where(lane == 0, turned[t - 1], turned[t]) for t in range(len(strip))]


def from_east(strip):
    lane = iota(strip[0].shape, 1)
    turned = [roll(part, -1, 1) for part in strip]
    count = len(strip)
    return [
        jnp.where(lane == LANES - 1, turned[(t + 1) % count], turned[t]) for t in range(count)
    ]


def tap_sums(ref, at, taps, flip):
    if flip:
        taps = [line[::-1] for line in taps[::-1]]
    above, here, below = load(ref, at - 1), load(ref, at), load(ref, at + 1)
    sums = [[], [], []]
    for t in range(len(here)):
        for b in range(3):
            sums[b].append(
                taps[0][b] * above[t] + taps[1][b] * here[t] + taps[2][b] * below[t]
            )
    return sums


def conv(ref, at, taps, flip):
    sums = tap_sums(ref, at, taps, flip)
    west, east = from_west(sums[0]), from_east(sums[2])
    return [sums[1][t] + west[t] + east[t] for t in range(len(west))]


def operate(ref, image, east_ref, south_ref, at, taps):
    above, here, below = load(ref, at - 1), load(ref, at), load(ref, at + 1)
    east, south, north = load(east_ref, at), load(south_ref, at), load(south_ref, at - 1)
    sums = tap_sums(image, at, taps, True)
    span = range(len(here))
    beside = from_east(here)
    flux = [east[t] * (here[t] - beside[t]) for t in span]
    from_left = from_west([sums[0][t] - flux[t] for t in span])
    from_right = from_east(sums[2])
    return here, [
        sums[1][t]
        + flux[t]
        + from_left[t]
        + from_right[t]
        + south[t] * (here[t] - below[t])
        - north[t] * (above[t] - here[t])
        for t in span
    ]


def begin(obs, cond, at, taps, sides):
    above, here, below = load(cond, at - 1), load(cond, at), load(cond, at + 1)
    span = range(len(here))
    right = from_east(here)
    east = [here[t] + right[t] for t in span]
    west = from_west(east)
    south = [here[t] + below[t] for t in span]
    squares = tap_total(taps, 2)
    diag = [squares + east[t] + west[t] + south[t] + (here[t] + above[t]) for t in span]
    inverse = [pl.reciprocal(part, approx=True) for part in diag]
    inverse = [inverse[t] * (2.0 - diag[t] * inverse[t]) for t in span]
    inverse[-1] = inverse[-1] * sides
    residual = conv(obs, at, taps, True)
    return east, south, inverse, residual, [residual[t] * inverse[t] for t in span]


def pick_lanes(field, lanes):
    return jnp.take_along_axis(field, lanes, axis=1, mode="promise_in_bounds")


def spread_cells(cells, spread):
    tiles = spread.shape[0] - 1
    lane = iota((cells.shape[0], LANES), 1)
    for t in range(tiles):
        spread[t] = pick_lanes(cells[:, :LANES], (lane >> 3) + t * (LANES // COARSE))
    turn = jnp.where(lane < HALF, 0, LANES - LANES // COARSE)
    spread[tiles] = pick_lanes(cells[:, LANES:], (lane >> 3) + turn)


def cells_at(spread, at):
    first = at // EDGE + EDGE - 2
    rows = [load(spread, first + index, 1) for index in range(STRIP // EDGE)]
    return [
        jnp.concatenate([jnp.broadcast_to(row, (EDGE, LANES)) for row in parts], axis=0)
        for parts in zip(*rows)
    ]


def cell_sums(ref, tiles, down):
    lane = iota((down, LANES), 1)
    total = jnp.zeros((down, LANES), jnp.float32)
    for t in range(tiles):
        picked = [
            ref[t, pl.ds(2 * EDGE + k, down, stride=COARSE), :] for k in range(COARSE)
        ]
        part = sum(picked[1:], picked[0])
        for by in (1, 2, 4):
            part = part + roll(part, -by, 1)
        part = pick_lanes(part, (lane & (LANES // COARSE - 1)) * COARSE)
        total = jnp.where(lane // (LANES // COARSE) == t, part, total)
    return total


def side_lanes(has_e, has_w):
    return jnp.where(iota((STRIP, LANES), 1) < HALF, has_e, has_w)


def mask_rows(ref, has_n, has_s):
    last = ref.shape[1] - 2 * EDGE
    for at, flag in ((EDGE, has_n), (last, has_s)):
        ref[:, at : at + EDGE, :] = ref[:, at : at + EDGE, :] * flag


def clear_pads(*refs):
    empty = jnp.zeros((refs[0].shape[0], EDGE, LANES), jnp.float32)
    for ref in refs:
        ref[:, :EDGE, :] = empty
        ref[:, ref.shape[1] - EDGE :, :] = empty


def product_sum_rows(one, two, count):
    total = one[0] * two[0]
    for t in range(1, count):
        total = total + one[t] * two[t]
    return total


def product_sum(one, two, count, flags=None):
    return fold(product_sum_rows(one, two, count), flags)


def fold(total, flags=None):
    parts = [total[at : at + EDGE] for at in range(0, total.shape[0], EDGE)]
    if flags is not None:
        parts = [part * flag for part, flag in zip(parts, flags)]
    return sum(parts[1:], parts[0])


def sweep(group, first, last, body, carry):
    width = group * STRIP
    steps = -(-(last - first) // width)

    def work(index, carry):
        start = first + index * width
        at = pl.multiple_of(jnp.minimum(start, last - width), EDGE)
        pending = []
        for by in range(0, width, STRIP):
            stores, carry = body(at + by, start, carry)
            pending += [(ref, at + by, strip) for ref, strip in stores]
        for ref, row, strip in pending:
            store(ref, row, strip)
        return carry

    return lax.fori_loop(0, steps, work, carry)


def sum_line(parts):
    line = jnp.zeros((1, LANES), jnp.float32)
    block = iota((1, LANES), 1) // (LANES // 4)
    for index, part in enumerate(parts):
        part = jnp.sum(part, axis=0, keepdims=True)
        part = part + roll(part, LANES // 2, 1)
        part = part + roll(part, LANES // 4, 1)
        line = jnp.where(block == index, part, line)
    return line


def line_totals(lines, count):
    while len(lines) > 1:
        lines = [sum(lines[at + 1 : at + 2], lines[at]) for at in range(0, len(lines), 2)]
    block = iota((1, LANES), 1) // (LANES // 4)
    return [
        jnp.sum(jnp.where(block == index, lines[0], 0.0), axis=1, keepdims=True)
        for index in range(count)
    ]


def jacobi(source, table, work):
    factor, east, west, south, north = [table[index] for index in range(5)]
    window = source.shape[0]
    source = factor * source
    iterate = source
    for sweep_index in range(SWEEPS - 1):
        place_ref = work.at[sweep_index % 2]
        for half in range(2):
            place_ref[half, EDGE : EDGE + window, :] = iterate[
                :, half * LANES : (half + 1) * LANES
            ]
        above, below = [
            jnp.concatenate(
                [place_ref[half, EDGE + by : EDGE + by + window, :] for half in range(2)], axis=1
            )
            for by in (-1, 1)
        ]
        across = east * roll(iterate, -1, 1) + west * roll(iterate, 1, 1)
        along = south * below + north * above
        iterate = ((1.0 - OMEGA) * iterate + source) + (across + along)
    return iterate


def clear_work(work):
    for buffer in range(2):
        clear_pads(work.at[buffer])


def in_pair_order(at, for_before, for_after):
    even = at % 2 == 0
    if callable(for_before):
        return (
            lambda *args: jnp.where(even, for_after(*args), for_before(*args)),
            lambda *args: jnp.where(even, for_before(*args), for_after(*args)),
        )
    return jnp.where(even, for_after, for_before), jnp.where(even, for_before, for_after)


def reader(tiles_here, refs, scratch, obs, cond, down):
    obs_in, class_in, weight_in, taps_in = refs
    classes, weights, taps, sums, obs_sem, class_sem, small_sem = scratch
    own = pl.ds(2 * EDGE, down * COARSE)
    small = [
        pltpu.make_async_copy(weight_in, weights, small_sem.at[0]),
        pltpu.make_async_copy(taps_in, taps, small_sem.at[1]),
    ]
    moves = []
    for slot, t in enumerate(tiles_here):
        lanes = pl.ds(t * LANES, LANES)
        moves.append(
            (
                pltpu.make_async_copy(class_in.at[:, lanes], classes.at[slot], class_sem.at[slot]),
                pltpu.make_async_copy(
                    obs_in.at[:, lanes], obs.at[slot, own, :], obs_sem.at[slot]
                ),
            )
        )
    for copy in small:
        copy.start()
    for pair in moves:
        for copy in pair:
            copy.start()
    sums[...] = jnp.zeros_like(sums)

    def settle(slot):
        if slot == 0:
            for copy in small:
                copy.wait()
        for copy in moves[slot]:
            copy.wait()
        values = [0.5 * weights[class_id] for class_id in range(CLASSES)]
        kind = classes[slot]
        cond[slot, own, :] = jnp.where(
            kind < 2,
            jnp.where(kind == 0, values[0], values[1]),
            jnp.where(kind == 2, values[2], values[3]),
        )
        for which, ref in enumerate((obs, cond)):
            picked = [
                ref[slot, pl.ds(2 * EDGE + k, down, stride=COARSE), :] for k in range(COARSE)
            ]
            cells = slice(2 * EDGE, 2 * EDGE + down)
            sums[3 * which, slot, cells, :] = sum(picked[1:], picked[0])
            sums[3 * which + 1, slot, cells, :] = picked[0]
            sums[3 * which + 2, slot, cells, :] = picked[-1]

    return settle


def reader_scratch(tiles, height, window, class_weights, taps):
    return [
        pltpu.VMEM((tiles, height, LANES), jnp.int32),
        pltpu.SMEM(class_weights.shape, jnp.float32),
        pltpu.SMEM(taps.shape, jnp.float32),
        pltpu.VMEM((6, tiles + 1, window + 2 * EDGE, LANES), jnp.float32),
        pltpu.SemaphoreType.DMA((tiles,)),
        pltpu.SemaphoreType.DMA((tiles,)),
        pltpu.SemaphoreType.DMA((2,)),
    ]


def coarse_parts(sums, taps, matrix):
    window = sums.shape[2] - 2 * EDGE
    whole = lambda index, by=0: wide(sums.at[index], EDGE + by, window)
    full = whole(0)
    by_tap = [full - whole(1) + whole(1, 1), full, full - whole(2) + whole(2, -1)]
    across = [sum(taps[a][b] * by_tap[a] for a in range(3)) for b in range(3)]
    source = across[1] + roll(across[0], -1, 1) + roll(across[2], 1, 1)
    full = whole(3)
    last = (iota(full.shape, 1) & (COARSE - 1)) == COARSE - 1
    east = jnp.where(last, full + roll(full, -1, 1), 0.0)
    south = whole(5) + whole(4, 1)
    cells = split_dot(jnp.concatenate([source, east, south], axis=0), matrix)
    source, east, south = cells[:window], cells[window : 2 * window], cells[2 * window :]
    around = east + roll(east, 1, 1) + south + roll(south, 1, 0)
    return [source, east, south, around]


def edge_kernel(tiles, down, *refs):
    arguments, (send_a, send_b), (obs, cond, message, *scratch) = refs[:4], refs[4:6], refs[6:]
    height = down * COARSE
    halves = height // LANES
    window = down + 2 * EDGE
    settle = reader((0, tiles - 1), arguments, scratch, obs, cond, down)
    matrix = gather_matrix(2)
    fine = [[], []]
    for slot, begin_row in ((0, 0), (1, LANES - REACH)):
        settle(slot)
        for ref in (obs, cond):
            turned = jnp.transpose(ref[slot, 2 * EDGE : 2 * EDGE + height, :])
            turned = turned[begin_row : begin_row + REACH]
            for half in range(halves):
                fine[slot].append(turned[:, half * LANES : (half + 1) * LANES])
    parts = coarse_parts(scratch[3], read_taps(scratch[2]), matrix)
    spare = jnp.zeros((2 * LANES - 4 * window, 2 * LANES), jnp.float32)
    stack = jnp.concatenate(parts + [spare], axis=0)
    left = jnp.transpose(stack[:, :LANES])
    right = jnp.transpose(stack[:, LANES:])
    past = 2 * LANES // COARSE
    split = lambda piece: [piece[:, half * LANES : (half + 1) * LANES] for half in range(2)]
    for slot, main, over in (
        (0, left[:EDGE], right[LANES - 1 :]),
        (1, left[past - EDGE : past], left[past : past + 1]),
    ):
        rows = split(main) + fine[slot] + split(over)
        filled = sum(piece.shape[0] for piece in rows)
        rows.append(jnp.zeros((message.shape[1] - filled, LANES), jnp.float32))
        message[slot] = jnp.concatenate(rows, axis=0)
    send_a[...], send_b[...] = in_pair_order(place()[0], message[0], message[1])


def edge(observed, class_map, class_weights, taps):
    height, breadth = observed.shape
    tiles, down = breadth // LANES, height // COARSE
    window = down + 2 * EDGE
    field = (3, height + 4 * EDGE, LANES)
    rows = 2 * EDGE + 2 * REACH * (height // LANES) + 2
    strip = (-(-rows // EDGE) * EDGE, LANES)
    return pl.pallas_call(
        functools.partial(edge_kernel, tiles, down),
        in_specs=[HBM] * 4,
        out_specs=[VMEM] * 2,
        out_shape=floats(strip, strip),
        scratch_shapes=[
            pltpu.VMEM(field, jnp.float32),
            pltpu.VMEM(field, jnp.float32),
            pltpu.VMEM((2,) + strip, jnp.float32),
        ]
        + reader_scratch(2, height, window, class_weights, taps),
        compiler_params=params(),
        name="pack_east_west",
    )(*[in_hbm(array) for array in (observed, class_map, class_weights, taps)])


def pack_kernel(tiles, down, *refs):
    arguments, (obs, cond, coarse_ref), scratch = refs[:4], refs[5:8], refs[8:]
    settle = reader(range(tiles), arguments, scratch, obs, cond, down)
    matrix = gather_matrix(tiles)
    for t in range(tiles):
        settle(t)
    for index, part in enumerate(coarse_parts(scratch[3], read_taps(scratch[2]), matrix)):
        coarse_ref[index] = part


def pack(observed, class_map, class_weights, taps, after):
    height, breadth = observed.shape
    tiles, down = breadth // LANES, height // COARSE
    window = down + 2 * EDGE
    field = (tiles + 1, height + 4 * EDGE, LANES)
    pixels = height * breadth
    return pl.pallas_call(
        functools.partial(pack_kernel, tiles, down),
        in_specs=[HBM] * 4 + [VMEM],
        out_specs=[VMEM] * 3,
        out_shape=floats(field, field, (4, window, 2 * LANES)),
        scratch_shapes=reader_scratch(tiles, height, window, class_weights, taps),
        compiler_params=params(),
        cost_estimate=pl.CostEstimate(
            flops=20 * pixels, bytes_accessed=16 * pixels, transcendentals=0
        ),
        name="pack_all",
    )(*[in_hbm(array) for array in (observed, class_map, class_weights, taps)], after)


def message_rows(tiles):
    rest = EDGE
    fine = rest + 2 * tiles
    sides = fine + tiles * EDGE
    return 0, rest, fine, sides, sides + EDGE


def merge_sides(parts):
    block = iota((EDGE, LANES), 1) // (2 * EDGE)
    merged = jnp.zeros((EDGE, LANES), jnp.float32)
    for index, part in enumerate(parts):
        merged = jnp.where(block == index, roll(part, (2 * index + 1) * EDGE, 1), merged)
    return merged


def split_sides(merged, count):
    lane = iota((EDGE, LANES), 1)
    outer = (lane < EDGE) | (lane >= LANES - EDGE)
    return [
        jnp.where(outer, roll(merged, -(2 * index + 1) * EDGE, 1), 0.0) for index in range(count)
    ]


def middle_kernel(
    tiles,
    down,
    got_b,
    got_a,
    coarse_in,
    obs_in,
    cond_in,
    obs,
    cond,
    coarse_ref,
    send_a,
    send_b,
    message,
):
    height = down * COARSE
    halves = height // LANES
    at_col, at_row, _, _ = place()
    from_e, from_w = in_pair_order(at_col, got_b[...], got_a[...])
    zeros = lambda rows: jnp.zeros((rows, LANES), jnp.float32)

    def turned(low, high):
        low = [low, zeros(EDGE - low.shape[0])] if low.shape[0] < EDGE else [low]
        high = [zeros(EDGE - high.shape[0]), high] if high.shape[0] < EDGE else [high]
        return jnp.transpose(jnp.concatenate([*low, zeros(LANES - 2 * EDGE), *high], axis=0))

    for which, field in enumerate((obs, cond)):
        for half in range(halves):
            at = 2 * EDGE + REACH * (which * halves + half)
            begin_row = 2 * EDGE + half * LANES
            field[tiles, begin_row : begin_row + LANES, :] = turned(
                from_e[at : at + REACH], from_w[at : at + REACH]
            )
    main = lambda strip, half: strip[half * EDGE : (half + 1) * EDGE]

    def over(strip, half):
        at = 2 * EDGE + 2 * REACH * halves + half
        return strip[at : at + 1]

    left = [turned(over(from_w, half), over(from_e, half)) for half in range(2)]
    right = [turned(main(from_e, half), main(from_w, half)) for half in range(2)]
    left = jnp.concatenate(left, axis=0)
    right = jnp.concatenate(right, axis=0)
    window = down + 2 * EDGE
    for index in range(4):
        rows = slice(index * window, (index + 1) * window)
        coarse_ref[index, :, :LANES] = coarse_in[index, :, :LANES] + left[rows]
        coarse_ref[index, :, LANES:] = coarse_in[index, :, LANES:] + right[rows]
    row = iota((EDGE, LANES), 0)
    over_at, rest_at, fine_at, sides_at, coarse_at = message_rows(tiles)
    for slot, begin_row, reach_row, first_row, over_row in (
        (0, 2 * EDGE, 2 * EDGE, EDGE, EDGE - 1),
        (1, EDGE + height, 2 * EDGE + height - REACH, window - 2 * EDGE, window - EDGE),
    ):
        for t in range(tiles):
            at = fine_at + t * EDGE
            message[slot, at : at + EDGE, :] = jnp.where(
                row < REACH,
                obs[t, reach_row : reach_row + EDGE, :],
                cond[t, reach_row - REACH : reach_row - REACH + EDGE, :],
            )
        for begin_tile in range(0, tiles, 4):
            rest = None
            for index in range(4):
                at = reach_row + EDGE - REACH - 2 * index
                piece = cond[begin_tile + index, at : at + EDGE, :]
                rest = piece if rest is None else jnp.where(row < 2 * index, rest, piece)
            at = rest_at + begin_tile * 2
            message[slot, at : at + EDGE, :] = rest
        rows = slice(first_row, first_row + EDGE)
        for index in range(4):
            at = coarse_at + index * EDGE
            message[slot, at : at + EDGE, :] = coarse_ref[index, rows, :LANES]
        beyond = [coarse_ref[index, rows, LANES:] for index in range(4)]
        beyond += [field[tiles, begin_row : begin_row + EDGE, :] for field in (obs, cond)]
        message[slot, sides_at : sides_at + EDGE, :] = merge_sides(beyond)
        message[slot, over_at : over_at + EDGE, :] = jnp.concatenate(
            [
                coarse_ref[index, over_row : over_row + 1, half * LANES : (half + 1) * LANES]
                for index in range(4)
                for half in range(2)
            ],
            axis=0,
        )
    send_a[...], send_b[...] = in_pair_order(at_row, message[0], message[1])


def middle(got_a, got_b, coarse, obs, cond):
    tiles, height = obs.shape[0] - 1, obs.shape[1] - 4 * EDGE
    down = height // COARSE
    long = (message_rows(tiles)[-1] + 4 * EDGE, LANES)
    return pl.pallas_call(
        functools.partial(middle_kernel, tiles, down),
        in_specs=[VMEM] * 5,
        out_specs=[VMEM] * 5,
        out_shape=floats(obs.shape, cond.shape, coarse.shape, long, long),
        input_output_aliases={3: 0, 4: 1},
        scratch_shapes=[pltpu.VMEM((2,) + long, jnp.float32)],
        compiler_params=params(),
        name="pack_north_south",
    )(got_b, got_a, coarse, obs, cond)


def inner_kernel(taps, obs, cond, res_ref, east_ref, south_ref, inv_ref, u_ref, dot_ref):
    _, _, has_e, has_w = has_sides()
    clear_pads(east_ref, south_ref)
    taps = read_taps(taps)
    sides = side_lanes(has_e, has_w)

    tiles = obs.shape[0] - 1

    def work(at, start, total):
        fields = begin(obs, cond, at, taps, sides)
        flags = [jnp.where(at + by >= start, 1.0, 0.0) for by in range(0, STRIP, EDGE)]
        total = total + product_sum(fields[3], fields[4], tiles, flags)
        return list(zip((east_ref, south_ref, inv_ref, res_ref, u_ref), fields)), total

    nothing = jnp.zeros((EDGE, LANES), jnp.float32)
    dot_ref[...] = sweep(5, 3 * EDGE, obs.shape[1] - 3 * EDGE, work, nothing)


def inner(taps, obs, cond):
    field = obs.shape
    pixels = field[0] * field[1] * field[2]
    return pl.pallas_call(
        inner_kernel,
        in_specs=[SMEM] + [VMEM] * 2,
        out_specs=[VMEM] * 6,
        out_shape=floats(field, field, field, field, field, (EDGE, LANES)),
        compiler_params=params(),
        cost_estimate=pl.CostEstimate(
            flops=45 * pixels, bytes_accessed=24 * pixels, transcendentals=0
        ),
        name="inner_strips",
    )(taps, obs, cond)


def first_kernel(
    tiles,
    down,
    taps,
    obs_in,
    cond_in,
    res_in,
    east_in,
    south_in,
    inv_in,
    u_in,
    got_b,
    got_a,
    coarse_in,
    dot_in,
    obs,
    cond,
    res_ref,
    east_ref,
    south_ref,
    inv_ref,
    u_ref,
    p_ref,
    q_ref,
    table_ref,
    own_ref,
    chunk_ref,
    image,
    spread,
    work,
):
    height = down * COARSE
    window = down + 2 * EDGE
    at_col, at_row, n_cols, n_rows = place()
    has_n, has_s, has_e, has_w = has_sides()
    clear_pads(obs, cond, p_ref, image)
    clear_work(work)
    from_s, from_n = in_pair_order(
        at_row,
        lambda at, rows=EDGE: got_b[at : at + rows, :],
        lambda at, rows=EDGE: got_a[at : at + rows, :],
    )
    over_at, rest_at, fine_at, sides_at, coarse_at = message_rows(tiles)
    row = iota((EDGE, LANES), 0)
    short = EDGE - REACH
    for t in range(tiles):
        at = fine_at + t * EDGE
        rest = rest_at + 2 * t
        begin_row = 2 * EDGE + height
        obs[t, EDGE : 2 * EDGE, :] = jnp.where(row >= short, from_n(at - short), 0.0)
        obs[t, begin_row : begin_row + EDGE, :] = jnp.where(row < REACH, from_s(at), 0.0)
        near, far = from_n(at + REACH - short), from_n(rest - 2 * short)
        near = jnp.where(row < short, 0.0, near)
        cond[t, EDGE : 2 * EDGE, :] = jnp.where(row < 2 * short, near, far)
        near, far = from_s(at + REACH), from_s(rest - short)
        far = jnp.where(row < REACH, far, 0.0)
        cond[t, begin_row : begin_row + EDGE, :] = jnp.where(row < short, near, far)
    sides_n, sides_s = [split_sides(strip(sides_at), 6) for strip in (from_n, from_s)]
    for which, field in enumerate((obs, cond)):
        field[tiles, EDGE : 2 * EDGE, :] = sides_n[4 + which]
        field[tiles, 2 * EDGE + height : 3 * EDGE + height, :] = sides_s[4 + which]

    edge_row = iota((EDGE, 2 * LANES), 0)

    def joined(index):
        def over(strip, row):
            line = [
                jnp.broadcast_to(
                    strip(over_at + 2 * index + half, 1), (EDGE, LANES)
                )
                for half in range(2)
            ]
            return jnp.where(edge_row == row, jnp.concatenate(line, axis=1), 0.0)

        def rows(strip, beyond):
            return jnp.concatenate([strip(coarse_at + index * EDGE), beyond[index]], axis=1)

        parts = [coarse_in[index, at : at + EDGE, :] for at in range(0, window, EDGE)]
        parts[0] = parts[0] + rows(from_n, sides_n)
        parts[1] = parts[1] + over(from_n, 0)
        parts[-2] = parts[-2] + over(from_s, EDGE - 1)
        parts[-1] = parts[-1] + rows(from_s, sides_s)
        return jnp.concatenate(parts, axis=0)

    source, east, south, around = [joined(index) for index in range(4)]
    row = iota(source.shape, 0)
    lane = iota(source.shape, 1)
    inside = jnp.where(row < EDGE, has_n, jnp.where(row < window - EDGE, 1.0, has_s))
    inside = inside * jnp.where(
        lane < LANES, 1.0, jnp.where(lane < LANES + HALF, has_e, has_w)
    )
    taps = read_taps(taps)
    taps_sum = tap_total(taps, 1)
    factor = inside * OMEGA / (COARSE * COARSE * taps_sum * taps_sum + around)
    weights = (east, roll(east, 1, 1), south, roll(south, 1, 0))
    table = [factor] + [factor * weight for weight in weights]
    for index, part in enumerate([*table, source]):
        table_ref[index] = part
    sides = side_lanes(has_e, has_w)
    half = iota((STRIP, LANES), 0) // EDGE
    pending = []
    total = dot_in[...]
    for index, known in ((0, has_n), (1, has_s)):
        at = EDGE + index * height
        fields = begin(obs, cond, at, taps, sides)
        own = jnp.where(half == index, 0.0, 1.0)
        total = total + fold(own * product_sum_rows(fields[3], fields[4], tiles))
        flag = jnp.where(half == index, known, 1.0)
        inverse, start = [[part * flag for part in fields[index]] for index in (2, 4)]
        fields = (*fields[:2], inverse, fields[3], start)
        pending += [
            (ref, at, strip)
            for ref, strip in zip((east_ref, south_ref, inv_ref, res_ref, u_ref), fields)
        ]
    cells = jacobi(source, table, work)
    spread_cells(cells, spread)
    inner_cells = slice(EDGE, EDGE + down)
    total = total + fold(source[inner_cells, :LANES] * cells[inner_cells, :LANES])
    dot_rp = total
    for ref, at, strip in pending:
        store(ref, at, strip)

    def flags(at, start):
        rows = [at + by for by in range(0, STRIP, EDGE)]
        first_row = jnp.maximum(start, 2 * EDGE)
        return [
            jnp.where((row >= first_row) & (row < 2 * EDGE + height), 1.0, 0.0) for row in rows
        ]

    def begin_p(at, _, carry):
        start, cells = load(u_ref, at), cells_at(spread, at)
        return [(p_ref, [start[t] + cells[t] for t in range(tiles + 1)])], carry

    def blur(at, _, carry):
        strip = conv(p_ref, at, taps, False)
        strip[tiles] = strip[tiles] * sides
        return [(image, strip)], carry

    def finish(at, start, total):
        here, product = operate(p_ref, image, east_ref, south_ref, at, taps)
        return [(q_ref, product)], total + product_sum(here, product, tiles, flags(at, start))

    nothing = jnp.zeros((EDGE, LANES), jnp.float32)
    span = (EDGE, 3 * EDGE + height)
    sweep(3, *span, begin_p, 0)
    sweep(3, *span, blur, 0)
    mask_rows(image, has_n, has_s)
    dot_pq = sweep(3, *span, finish, nothing)

    own = cell_sums(q_ref, tiles, down)
    own_ref[...] = own
    spare = jnp.zeros((LANES - down, LANES), jnp.float32)
    turned = jnp.transpose(jnp.concatenate([own, spare], axis=0))
    chunk_ref[...] = jnp.zeros_like(chunk_ref)
    for down_by in (-1, 0, 1):
        for right_by in (-1, 0, 1):
            if down_by == 0 and right_by == 0:
                continue
            if down_by == 0:
                piece = turned[:EDGE] if right_by < 0 else turned[LANES - EDGE :]
            else:
                piece = own[:EDGE] if down_by < 0 else own[down - EDGE :]
            to_row, to_col = at_row + down_by, at_col + right_by
            there = (to_row >= 0) & (to_row < n_rows) & (to_col >= 0) & (to_col < n_cols)
            slot = jnp.where(there, to_col * n_rows + to_row, at_col * n_rows + at_row)
            chunk_ref[pl.ds(slot * PIECE, EDGE), 0, :] = piece * jnp.where(there, 1.0, 0.0)
    line = sum_line((dot_rp, dot_pq))
    for at in range(EDGE, chunk_ref.shape[0], PIECE):
        chunk_ref[at] = line


def first(taps, fields, got_a, got_b, coarse, dot):
    field = fields[0].shape
    tiles, height = field[0] - 1, field[1] - 4 * EDGE
    down = height // COARSE
    window = down + 2 * EDGE
    count = lax.axis_size("cols") * lax.axis_size("rows")
    shapes = [field] * 9 + [
        (6, window, 2 * LANES),
        (down, LANES),
        (count * PIECE, 1, LANES),
    ]
    return pl.pallas_call(
        functools.partial(first_kernel, tiles, down),
        in_specs=[SMEM] + [VMEM] * 11,
        out_specs=[VMEM] * len(shapes),
        out_shape=floats(*shapes),
        input_output_aliases={index + 1: index for index in range(7)},
        scratch_shapes=[
            pltpu.VMEM(field, jnp.float32),
            pltpu.VMEM((tiles + 1, window, LANES), jnp.float32),
            pltpu.VMEM((2, 2, window + 2 * EDGE, LANES), jnp.float32),
        ],
        compiler_params=params(),
        name="first_direction",
    )(taps, *fields, got_b, got_a, coarse, dot)[2:]


def second_kernel(
    tiles,
    down,
    taps,
    got_ref,
    own_ref,
    table_ref,
    res_ref,
    q_ref,
    east_ref,
    south_ref,
    inv_ref,
    w_ref,
    v_ref,
    out_ref,
    known_ref,
    image,
    spread,
    work,
):
    height = down * COARSE
    has_n, has_s, has_e, has_w = has_sides()
    at_col, at_row, n_cols, n_rows = place()
    me = at_col * n_rows + at_row

    def got(down_by, right_by):
        to_row, to_col = at_row + down_by, at_col + right_by
        there = (to_row >= 0) & (to_row < n_rows) & (to_col >= 0) & (to_col < n_cols)
        slot = jnp.where(there, to_col * n_rows + to_row, me)
        return got_ref[pl.ds(slot * PIECE, EDGE), 0, :]

    low = iota((EDGE, LANES), 1) < HALF
    gap = jnp.zeros((LANES - 2 * EDGE, LANES), jnp.float32)
    beside = jnp.transpose(jnp.concatenate([got(0, 1), gap, got(0, -1)], axis=0))[:down]
    source = jnp.concatenate(
        [
            jnp.concatenate([got(-1, 0), jnp.where(low, got(-1, 1), got(-1, -1))], axis=1),
            jnp.concatenate([own_ref[...], beside], axis=1),
            jnp.concatenate([got(1, 0), jnp.where(low, got(1, 1), got(1, -1))], axis=1),
        ],
        axis=0,
    )
    clear_work(work)
    rp, pq = line_totals(
        [got_ref[at] for at in range(EDGE, got_ref.shape[0], PIECE)], 2
    )
    step = rp / pq
    for index, value in enumerate((step, rp, pq)):
        known_ref[index] = jnp.broadcast_to(value, (EDGE, LANES))
    source = table_ref[5] - jnp.broadcast_to(step, source.shape) * source
    spread_cells(jacobi(source, table_ref, work), spread)
    step = jnp.broadcast_to(step, (STRIP, LANES))
    clear_pads(w_ref, image)
    sides = side_lanes(has_e, has_w)
    taps = read_taps(taps)

    def begin_w(at, start, totals):
        right, field, inverse = load(res_ref, at), load(q_ref, at), load(inv_ref, at)
        cells = cells_at(spread, at)
        span = range(tiles + 1)
        residual = [right[t] - step * field[t] for t in span]
        strip = [residual[t] * inverse[t] + cells[t] for t in span]
        first_row = jnp.maximum(start, 2 * EDGE)
        flags = [
            jnp.where((row >= first_row) & (row < 2 * EDGE + height), 1.0, 0.0)
            for row in [at + by for by in range(0, STRIP, EDGE)]
        ]
        return [(w_ref, strip)], (
            totals[0] + product_sum(residual, strip, tiles, flags),
            totals[1] + product_sum(strip, field, tiles, flags),
        )

    def blur(at, _, carry):
        strip = conv(w_ref, at, taps, False)
        strip[tiles] = strip[tiles] * sides
        return [(image, strip)], carry

    def finish(at, _, total):
        here, product = operate(w_ref, image, east_ref, south_ref, at, taps)
        return [(v_ref, product[:tiles])], total + product_sum(here, product, tiles)

    nothing = jnp.zeros((EDGE, LANES), jnp.float32)
    span = (EDGE, 3 * EDGE + height)
    dot_rz, dot_zq = sweep(3, *span, begin_w, (nothing, nothing))
    sweep(3, *span, blur, 0)
    mask_rows(image, has_n, has_s)
    dot_zz = sweep(4, 2 * EDGE, 2 * EDGE + height, finish, nothing)
    line = sum_line((dot_rz, dot_zq, dot_zz))
    for index in range(out_ref.shape[0]):
        out_ref[index] = line


def second(taps, got, own, table, r, q, east, south, inv):
    tiles, height = q.shape[0] - 1, q.shape[1] - 4 * EDGE
    down = height // COARSE
    window = down + 2 * EDGE
    count = lax.axis_size("cols") * lax.axis_size("rows")
    return pl.pallas_call(
        functools.partial(second_kernel, tiles, down),
        in_specs=[SMEM] + [VMEM] * 8,
        out_specs=[VMEM] * 4,
        out_shape=floats(q.shape, q.shape, (count, 1, LANES), (3, EDGE, LANES)),
        scratch_shapes=[
            pltpu.VMEM(q.shape, jnp.float32),
            pltpu.VMEM((tiles + 1, window, LANES), jnp.float32),
            pltpu.VMEM((2, 2, window + 2 * EDGE, LANES), jnp.float32),
        ],
        compiler_params=params(),
        name="second_direction",
    )(taps, got, own, table, r, q, east, south, inv)


def combine_kernel(
    tiles, height, sums_ref, known_ref, p_ref, w_ref, r_ref, q_ref, v_ref, sol_out, res_out, sol, res, sem
):
    rz, zq, zz = line_totals([sums_ref[index] for index in range(sums_ref.shape[0])], 3)
    step, rp, pq = [known_ref[index, :1, :] for index in range(3)]
    ratio = rz / rp
    step_next = rz / (zz + ratio * (2.0 * zq + ratio * pq))
    on_w = jnp.broadcast_to(step_next, (CHUNK, LANES))
    on_p = jnp.broadcast_to(step + step_next * ratio, (CHUNK, LANES))

    def copies(index):
        rows = pl.ds(pl.multiple_of(index * CHUNK, CHUNK), CHUNK)
        return (
            pltpu.make_async_copy(sol.at[rows, :], sol_out.at[rows, :], sem.at[0, index]),
            pltpu.make_async_copy(res.at[rows, :], res_out.at[rows, :], sem.at[1, index]),
        )

    def work(index, _):
        at = pl.multiple_of(index * CHUNK, CHUNK)
        p, w, r, q, v = [
            load(ref, at + 2 * EDGE, CHUNK) for ref in (p_ref, w_ref, r_ref, q_ref, v_ref)
        ]
        one = [on_p * p[t] + on_w * w[t] for t in range(tiles)]
        two = [r[t] - on_p * q[t] - on_w * v[t] for t in range(tiles)]
        for t in range(tiles):
            sol[pl.ds(at, CHUNK), t * LANES : (t + 1) * LANES] = one[t]
            res[pl.ds(at, CHUNK), t * LANES : (t + 1) * LANES] = two[t]
        for copy in copies(index):
            copy.start()
        return 0

    def settle(index, _):
        for copy in copies(index):
            copy.wait()
        return 0

    lax.fori_loop(0, height // CHUNK, work, 0)
    lax.fori_loop(0, height // CHUNK, settle, 0)


def combine(sums, known, p, w, r, q, v):
    tiles, height = q.shape[0] - 1, q.shape[1] - 4 * EDGE
    shape = (height, tiles * LANES)
    return pl.pallas_call(
        functools.partial(combine_kernel, tiles, height),
        in_specs=[VMEM] * 7,
        out_specs=[HBM] * 2,
        out_shape=floats(shape, shape),
        scratch_shapes=[
            pltpu.VMEM(shape, jnp.float32),
            pltpu.VMEM(shape, jnp.float32),
            pltpu.SemaphoreType.DMA((2, height // CHUNK)),
        ],
        compiler_params=params(),
        name="combine",
    )(sums, known, p, w, r, q, v)


def exchange(send_a, send_b, axis):
    count = lax.axis_size(axis)

    def pairs(begin):
        return [
            pair for i in range(begin, count - 1, 2) for pair in ((i, i + 1), (i + 1, i))
        ]

    got_b = lax.ppermute(send_b, axis, pairs(1))
    got_a = lax.ppermute(send_a, axis, pairs(0))
    return got_a, got_b


def body(observed, class_map, class_weights, blur_kernel):
    arguments = (observed, class_map, class_weights, blur_kernel)
    send_a, send_b = edge(*arguments)
    got_a, got_b = exchange(send_a, send_b, "cols")
    obs, cond, coarse = pack(*arguments, send_a)
    obs, cond, coarse, send_a, send_b = middle(got_a, got_b, coarse, obs, cond)
    got_a, got_b = exchange(send_a, send_b, "rows")
    r, east, south, inv, u, dot = inner(blur_kernel, obs, cond)
    fields = (obs, cond, r, east, south, inv, u)
    r, east, south, inv, _, p, q, table, own, chunk = first(
        blur_kernel, fields, got_a, got_b, coarse, dot
    )
    got = lax.all_to_all(chunk, AXES, 0, 0, tiled=True)
    w, v, line, known = second(blur_kernel, got, own, table, r, q, east, south, inv)
    sums = lax.all_to_all(line, AXES[::-1], 0, 0, tiled=True)
    return tuple(combine(sums, known, p, w, r, q, v))


def solution(mesh):
    return jax.shard_map(
        body,
        mesh=mesh,
        in_specs=(P("rows", "cols"), P("rows", "cols"), P(), P()),
        out_specs=(P("rows", "cols"), P("rows", "cols")),
        check_vma=False,
    )
```

```python
import functools

import jax
import jax.numpy as jnp
from jax import lax
from jax.experimental import pallas as pl
from jax.experimental.pallas import tpu as pltpu
from jax.sharding import PartitionSpec as P

COARSE = 8
SWEEPS = 8
CLASSES = 4
OMEGA = 0.8

LANES = 128
HALF = LANES // 2
EDGE = 8
STRIP = 2 * EDGE
REACH = 5
PIECE = EDGE + 1
CHUNK = 64
AXES = ("cols", "rows")
LIMIT = 40 * 1024 * 1024


VMEM = pl.BlockSpec(memory_space=pltpu.VMEM)
SMEM = pl.BlockSpec(memory_space=pltpu.SMEM)
HBM = pl.BlockSpec(memory_space=pltpu.HBM)


def params():
    return pltpu.CompilerParams(vmem_limit_bytes=LIMIT)


def in_hbm(array):
    return pltpu.with_memory_space_constraint(array, pltpu.HBM)


def floats(*shapes):
    return [jax.ShapeDtypeStruct(shape, jnp.float32) for shape in shapes]


def place():
    at_col, at_row = lax.axis_index("cols"), lax.axis_index("rows")
    n_cols, n_rows = lax.axis_size("cols"), lax.axis_size("rows")
    return at_col, at_row, n_cols, n_rows


def has_sides():
    at_col, at_row, n_cols, n_rows = place()
    flag = lambda test: jnp.where(test, 1.0, 0.0).astype(jnp.float32)
    return (
        flag(at_row > 0),
        flag(at_row < n_rows - 1),
        flag(at_col < n_cols - 1),
        flag(at_col > 0),
    )


def iota(shape, dim):
    return lax.broadcasted_iota(jnp.int32, shape, dim)


def cell_of(pixel, tiles):
    turn = (tiles + 1) * LANES
    return jnp.where(pixel < turn - HALF, pixel >> 3, ((pixel - turn) >> 3) & (2 * LANES - 1))


def gather_matrix(tiles):
    shape = ((tiles + 1) * LANES, 2 * LANES)
    hit = cell_of(iota(shape, 0), tiles) == iota(shape, 1)
    return jnp.where(hit, 1.0, 0.0).astype(jnp.bfloat16)


def split_dot(field, matrix):
    rows = field.shape[0]
    parts, rest = [], field
    for _ in range(3):
        parts.append(rest.astype(jnp.bfloat16))
        rest = rest - parts[-1].astype(jnp.float32)
    product = jnp.dot(
        jnp.concatenate(parts, axis=0), matrix, preferred_element_type=jnp.float32
    )
    return product[:rows] + (product[rows : 2 * rows] + product[2 * rows :])


def roll(field, by, axis):
    return pltpu.roll(field, by % field.shape[axis], axis)


def load(ref, at, rows=STRIP):
    return [ref[t, pl.ds(at, rows), :] for t in range(ref.shape[0])]


def store(ref, at, strip):
    for t, part in enumerate(strip):
        ref[t, pl.ds(at, part.shape[0]), :] = part


def wide(ref, at, rows):
    return jnp.concatenate(load(ref, at, rows), axis=1)


def read_taps(taps):
    return [[taps[a, b] for b in range(3)] for a in range(3)]


def tap_total(taps, power):
    return sum(tap * tap if power == 2 else tap for line in taps for tap in line)


def from_west(strip):
    lane = iota(strip[0].shape, 1)
    turned = [roll(part, 1, 1) for part in strip]
    return [jnp.where(lane == 0, turned[t - 1], turned[t]) for t in range(len(strip))]


def from_east(strip):
    lane = iota(strip[0].shape, 1)
    turned = [roll(part, -1, 1) for part in strip]
    count = len(strip)
    return [
        jnp.where(lane == LANES - 1, turned[(t + 1) % count], turned[t]) for t in range(count)
    ]


def tap_sums(ref, at, taps, flip):
    if flip:
        taps = [line[::-1] for line in taps[::-1]]
    above, here, below = load(ref, at - 1), load(ref, at), load(ref, at + 1)
    sums = [[], [], []]
    for t in range(len(here)):
        for b in range(3):
            sums[b].append(
                taps[0][b] * above[t] + taps[1][b] * here[t] + taps[2][b] * below[t]
            )
    return sums


def conv(ref, at, taps, flip):
    sums = tap_sums(ref, at, taps, flip)
    west, east = from_west(sums[0]), from_east(sums[2])
    return [sums[1][t] + west[t] + east[t] for t in range(len(west))]


def operate(ref, image, east_ref, south_ref, at, taps):
    above, here, below = load(ref, at - 1), load(ref, at), load(ref, at + 1)
    east, south, north = load(east_ref, at), load(south_ref, at), load(south_ref, at - 1)
    sums = tap_sums(image, at, taps, True)
    span = range(len(here))
    beside = from_east(here)
    flux = [east[t] * (here[t] - beside[t]) for t in span]
    from_left = from_west([sums[0][t] - flux[t] for t in span])
    from_right = from_east(sums[2])
    return here, [
        sums[1][t]
        + flux[t]
        + from_left[t]
        + from_right[t]
        + south[t] * (here[t] - below[t])
        - north[t] * (above[t] - here[t])
        for t in span
    ]


def begin(obs, cond, at, taps, sides):
    above, here, below = load(cond, at - 1), load(cond, at), load(cond, at + 1)
    span = range(len(here))
    right = from_east(here)
    east = [here[t] + right[t] for t in span]
    west = from_west(east)
    south = [here[t] + below[t] for t in span]
    squares = tap_total(taps, 2)
    diag = [squares + east[t] + west[t] + south[t] + (here[t] + above[t]) for t in span]
    inverse = [pl.reciprocal(part, approx=True) for part in diag]
    inverse = [inverse[t] * (2.0 - diag[t] * inverse[t]) for t in span]
    inverse[-1] = inverse[-1] * sides
    residual = conv(obs, at, taps, True)
    return east, south, inverse, residual, [residual[t] * inverse[t] for t in span]


def pick_lanes(field, lanes):
    return jnp.take_along_axis(field, lanes, axis=1, mode="promise_in_bounds")


def spread_cells(cells, spread):
    tiles = spread.shape[0] - 1
    lane = iota((cells.shape[0], LANES), 1)
    for t in range(tiles):
        spread[t] = pick_lanes(cells[:, :LANES], (lane >> 3) + t * (LANES // COARSE))
    turn = jnp.where(lane < HALF, 0, LANES - LANES // COARSE)
    spread[tiles] = pick_lanes(cells[:, LANES:], (lane >> 3) + turn)


def cells_at(spread, at):
    first = at // EDGE + EDGE - 2
    rows = [load(spread, first + index, 1) for index in range(STRIP // EDGE)]
    return [
        jnp.concatenate([jnp.broadcast_to(row, (EDGE, LANES)) for row in parts], axis=0)
        for parts in zip(*rows)
    ]


def cell_sums(ref, tiles, down):
    lane = iota((down, LANES), 1)
    total = jnp.zeros((down, LANES), jnp.float32)
    for t in range(tiles):
        picked = [
            ref[t, pl.ds(2 * EDGE + k, down, stride=COARSE), :] for k in range(COARSE)
        ]
        part = sum(picked[1:], picked[0])
        for by in (1, 2, 4):
            part = part + roll(part, -by, 1)
        part = pick_lanes(part, (lane & (LANES // COARSE - 1)) * COARSE)
        total = jnp.where(lane // (LANES // COARSE) == t, part, total)
    return total


def side_lanes(has_e, has_w):
    return jnp.where(iota((STRIP, LANES), 1) < HALF, has_e, has_w)


def mask_rows(ref, has_n, has_s):
    last = ref.shape[1] - 2 * EDGE
    for at, flag in ((EDGE, has_n), (last, has_s)):
        ref[:, at : at + EDGE, :] = ref[:, at : at + EDGE, :] * flag


def clear_pads(*refs):
    empty = jnp.zeros((refs[0].shape[0], EDGE, LANES), jnp.float32)
    for ref in refs:
        ref[:, :EDGE, :] = empty
        ref[:, ref.shape[1] - EDGE :, :] = empty


def product_sum_rows(one, two, count):
    total = one[0] * two[0]
    for t in range(1, count):
        total = total + one[t] * two[t]
    return total


def product_sum(one, two, count, flags=None):
    return fold(product_sum_rows(one, two, count), flags)


def fold(total, flags=None):
    parts = [total[at : at + EDGE] for at in range(0, total.shape[0], EDGE)]
    if flags is not None:
        parts = [part * flag for part, flag in zip(parts, flags)]
    return sum(parts[1:], parts[0])


def sweep(group, first, last, body, carry):
    width = group * STRIP
    steps = -(-(last - first) // width)

    def work(index, carry):
        start = first + index * width
        at = pl.multiple_of(jnp.minimum(start, last - width), EDGE)
        pending = []
        for by in range(0, width, STRIP):
            stores, carry = body(at + by, start, carry)
            pending += [(ref, at + by, strip) for ref, strip in stores]
        for ref, row, strip in pending:
            store(ref, row, strip)
        return carry

    return lax.fori_loop(0, steps, work, carry)


def sum_line(parts):
    line = jnp.zeros((1, LANES), jnp.float32)
    block = iota((1, LANES), 1) // (LANES // 4)
    for index, part in enumerate(parts):
        part = jnp.sum(part, axis=0, keepdims=True)
        part = part + roll(part, LANES // 2, 1)
        part = part + roll(part, LANES // 4, 1)
        line = jnp.where(block == index, part, line)
    return line


def line_totals(lines, count):
    while len(lines) > 1:
        lines = [sum(lines[at + 1 : at + 2], lines[at]) for at in range(0, len(lines), 2)]
    block = iota((1, LANES), 1) // (LANES // 4)
    return [
        jnp.sum(jnp.where(block == index, lines[0], 0.0), axis=1, keepdims=True)
        for index in range(count)
    ]


def jacobi(source, table, work):
    factor, east, west, south, north = [table[index] for index in range(5)]
    window = source.shape[0]
    source = factor * source
    iterate = source
    for sweep_index in range(SWEEPS - 1):
        place_ref = work.at[sweep_index % 2]
        for half in range(2):
            place_ref[half, EDGE : EDGE + window, :] = iterate[
                :, half * LANES : (half + 1) * LANES
            ]
        above, below = [
            jnp.concatenate(
                [place_ref[half, EDGE + by : EDGE + by + window, :] for half in range(2)], axis=1
            )
            for by in (-1, 1)
        ]
        across = east * roll(iterate, -1, 1) + west * roll(iterate, 1, 1)
        along = south * below + north * above
        iterate = ((1.0 - OMEGA) * iterate + source) + (across + along)
    return iterate


def clear_work(work):
    for buffer in range(2):
        clear_pads(work.at[buffer])


def in_pair_order(at, for_before, for_after):
    even = at % 2 == 0
    if callable(for_before):
        return (
            lambda *args: jnp.where(even, for_after(*args), for_before(*args)),
            lambda *args: jnp.where(even, for_before(*args), for_after(*args)),
        )
    return jnp.where(even, for_after, for_before), jnp.where(even, for_before, for_after)


def reader(tiles_here, refs, scratch, obs, cond, down):
    obs_in, class_in, weight_in, taps_in = refs
    classes, weights, taps, sums, obs_sem, class_sem, small_sem = scratch
    own = pl.ds(2 * EDGE, down * COARSE)
    small = [
        pltpu.make_async_copy(weight_in, weights, small_sem.at[0]),
        pltpu.make_async_copy(taps_in, taps, small_sem.at[1]),
    ]
    moves = []
    for slot, t in enumerate(tiles_here):
        lanes = pl.ds(t * LANES, LANES)
        moves.append(
            (
                pltpu.make_async_copy(class_in.at[:, lanes], classes.at[slot], class_sem.at[slot]),
                pltpu.make_async_copy(
                    obs_in.at[:, lanes], obs.at[slot, own, :], obs_sem.at[slot]
                ),
            )
        )
    for copy in small:
        copy.start()
    for pair in moves:
        for copy in pair:
            copy.start()
    sums[...] = jnp.zeros_like(sums)

    def settle(slot):
        if slot == 0:
            for copy in small:
                copy.wait()
        for copy in moves[slot]:
            copy.wait()
        values = [0.5 * weights[class_id] for class_id in range(CLASSES)]
        kind = classes[slot]
        cond[slot, own, :] = jnp.where(
            kind < 2,
            jnp.where(kind == 0, values[0], values[1]),
            jnp.where(kind == 2, values[2], values[3]),
        )
        for which, ref in enumerate((obs, cond)):
            picked = [
                ref[slot, pl.ds(2 * EDGE + k, down, stride=COARSE), :] for k in range(COARSE)
            ]
            cells = slice(2 * EDGE, 2 * EDGE + down)
            sums[3 * which, slot, cells, :] = sum(picked[1:], picked[0])
            sums[3 * which + 1, slot, cells, :] = picked[0]
            sums[3 * which + 2, slot, cells, :] = picked[-1]

    return settle


def reader_scratch(tiles, height, window, class_weights, taps):
    return [
        pltpu.VMEM((tiles, height, LANES), jnp.int32),
        pltpu.SMEM(class_weights.shape, jnp.float32),
        pltpu.SMEM(taps.shape, jnp.float32),
        pltpu.VMEM((6, tiles + 1, window + 2 * EDGE, LANES), jnp.float32),
        pltpu.SemaphoreType.DMA((tiles,)),
        pltpu.SemaphoreType.DMA((tiles,)),
        pltpu.SemaphoreType.DMA((2,)),
    ]


def coarse_parts(sums, taps, matrix):
    window = sums.shape[2] - 2 * EDGE
    whole = lambda index, by=0: wide(sums.at[index], EDGE + by, window)
    full = whole(0)
    by_tap = [full - whole(1) + whole(1, 1), full, full - whole(2) + whole(2, -1)]
    across = [sum(taps[a][b] * by_tap[a] for a in range(3)) for b in range(3)]
    source = across[1] + roll(across[0], -1, 1) + roll(across[2], 1, 1)
    full = whole(3)
    last = (iota(full.shape, 1) & (COARSE - 1)) == COARSE - 1
    east = jnp.where(last, full + roll(full, -1, 1), 0.0)
    south = whole(5) + whole(4, 1)
    cells = split_dot(jnp.concatenate([source, east, south], axis=0), matrix)
    source, east, south = cells[:window], cells[window : 2 * window], cells[2 * window :]
    around = east + roll(east, 1, 1) + south + roll(south, 1, 0)
    return [source, east, south, around]


def edge_kernel(tiles, down, *refs):
    arguments, (send_a, send_b), (obs, cond, message, *scratch) = refs[:4], refs[4:6], refs[6:]
    height = down * COARSE
    halves = height // LANES
    window = down + 2 * EDGE
    settle = reader((0, tiles - 1), arguments, scratch, obs, cond, down)
    matrix = gather_matrix(2)
    fine = [[], []]
    for slot, begin_row in ((0, 0), (1, LANES - REACH)):
        settle(slot)
        for ref in (obs, cond):
            turned = jnp.transpose(ref[slot, 2 * EDGE : 2 * EDGE + height, :])
            turned = turned[begin_row : begin_row + REACH]
            for half in range(halves):
                fine[slot].append(turned[:, half * LANES : (half + 1) * LANES])
    parts = coarse_parts(scratch[3], read_taps(scratch[2]), matrix)
    spare = jnp.zeros((2 * LANES - 4 * window, 2 * LANES), jnp.float32)
    stack = jnp.concatenate(parts + [spare], axis=0)
    left = jnp.transpose(stack[:, :LANES])
    right = jnp.transpose(stack[:, LANES:])
    past = 2 * LANES // COARSE
    split = lambda piece: [piece[:, half * LANES : (half + 1) * LANES] for half in range(2)]
    for slot, main, over in (
        (0, left[:EDGE], right[LANES - 1 :]),
        (1, left[past - EDGE : past], left[past : past + 1]),
    ):
        rows = split(main) + fine[slot] + split(over)
        filled = sum(piece.shape[0] for piece in rows)
        rows.append(jnp.zeros((message.shape[1] - filled, LANES), jnp.float32))
        message[slot] = jnp.concatenate(rows, axis=0)
    send_a[...], send_b[...] = in_pair_order(place()[0], message[0], message[1])


def edge(observed, class_map, class_weights, taps):
    height, breadth = observed.shape
    tiles, down = breadth // LANES, height // COARSE
    window = down + 2 * EDGE
    field = (3, height + 4 * EDGE, LANES)
    rows = 2 * EDGE + 2 * REACH * (height // LANES) + 2
    strip = (-(-rows // EDGE) * EDGE, LANES)
    return pl.pallas_call(
        functools.partial(edge_kernel, tiles, down),
        in_specs=[HBM] * 4,
        out_specs=[VMEM] * 2,
        out_shape=floats(strip, strip),
        scratch_shapes=[
            pltpu.VMEM(field, jnp.float32),
            pltpu.VMEM(field, jnp.float32),
            pltpu.VMEM((2,) + strip, jnp.float32),
        ]
        + reader_scratch(2, height, window, class_weights, taps),
        compiler_params=params(),
        name="pack_east_west",
    )(*[in_hbm(array) for array in (observed, class_map, class_weights, taps)])


def pack_kernel(tiles, down, *refs):
    arguments, (obs, cond, coarse_ref), scratch = refs[:4], refs[5:8], refs[8:]
    settle = reader(range(tiles), arguments, scratch, obs, cond, down)
    matrix = gather_matrix(tiles)
    for t in range(tiles):
        settle(t)
    for index, part in enumerate(coarse_parts(scratch[3], read_taps(scratch[2]), matrix)):
        coarse_ref[index] = part


def pack(observed, class_map, class_weights, taps, after):
    height, breadth = observed.shape
    tiles, down = breadth // LANES, height // COARSE
    window = down + 2 * EDGE
    field = (tiles + 1, height + 4 * EDGE, LANES)
    pixels = height * breadth
    return pl.pallas_call(
        functools.partial(pack_kernel, tiles, down),
        in_specs=[HBM] * 4 + [VMEM],
        out_specs=[VMEM] * 3,
        out_shape=floats(field, field, (4, window, 2 * LANES)),
        scratch_shapes=reader_scratch(tiles, height, window, class_weights, taps),
        compiler_params=params(),
        cost_estimate=pl.CostEstimate(
            flops=20 * pixels, bytes_accessed=16 * pixels, transcendentals=0
        ),
        name="pack_all",
    )(*[in_hbm(array) for array in (observed, class_map, class_weights, taps)], after)


def message_rows(tiles):
    rest = EDGE
    fine = rest + 2 * tiles
    sides = fine + tiles * EDGE
    return 0, rest, fine, sides, sides + EDGE


def merge_sides(parts):
    block = iota((EDGE, LANES), 1) // (2 * EDGE)
    merged = jnp.zeros((EDGE, LANES), jnp.float32)
    for index, part in enumerate(parts):
        merged = jnp.where(block == index, roll(part, (2 * index + 1) * EDGE, 1), merged)
    return merged


def split_sides(merged, count):
    lane = iota((EDGE, LANES), 1)
    outer = (lane < EDGE) | (lane >= LANES - EDGE)
    return [
        jnp.where(outer, roll(merged, -(2 * index + 1) * EDGE, 1), 0.0) for index in range(count)
    ]


def middle_kernel(
    tiles,
    down,
    got_b,
    got_a,
    coarse_in,
    obs_in,
    cond_in,
    obs,
    cond,
    coarse_ref,
    send_a,
    send_b,
    message,
):
    height = down * COARSE
    halves = height // LANES
    at_col, at_row, _, _ = place()
    from_e, from_w = in_pair_order(at_col, got_b[...], got_a[...])
    zeros = lambda rows: jnp.zeros((rows, LANES), jnp.float32)

    def turned(low, high):
        low = [low, zeros(EDGE - low.shape[0])] if low.shape[0] < EDGE else [low]
        high = [zeros(EDGE - high.shape[0]), high] if high.shape[0] < EDGE else [high]
        return jnp.transpose(jnp.concatenate([*low, zeros(LANES - 2 * EDGE), *high], axis=0))

    for which, field in enumerate((obs, cond)):
        for half in range(halves):
            at = 2 * EDGE + REACH * (which * halves + half)
            begin_row = 2 * EDGE + half * LANES
            field[tiles, begin_row : begin_row + LANES, :] = turned(
                from_e[at : at + REACH], from_w[at : at + REACH]
            )
    main = lambda strip, half: strip[half * EDGE : (half + 1) * EDGE]

    def over(strip, half):
        at = 2 * EDGE + 2 * REACH * halves + half
        return strip[at : at + 1]

    left = [turned(over(from_w, half), over(from_e, half)) for half in range(2)]
    right = [turned(main(from_e, half), main(from_w, half)) for half in range(2)]
    left = jnp.concatenate(left, axis=0)
    right = jnp.concatenate(right, axis=0)
    window = down + 2 * EDGE
    for index in range(4):
        rows = slice(index * window, (index + 1) * window)
        coarse_ref[index, :, :LANES] = coarse_in[index, :, :LANES] + left[rows]
        coarse_ref[index, :, LANES:] = coarse_in[index, :, LANES:] + right[rows]
    row = iota((EDGE, LANES), 0)
    over_at, rest_at, fine_at, sides_at, coarse_at = message_rows(tiles)
    for slot, begin_row, reach_row, first_row, over_row in (
        (0, 2 * EDGE, 2 * EDGE, EDGE, EDGE - 1),
        (1, EDGE + height, 2 * EDGE + height - REACH, window - 2 * EDGE, window - EDGE),
    ):
        for t in range(tiles):
            at = fine_at + t * EDGE
            message[slot, at : at + EDGE, :] = jnp.where(
                row < REACH,
                obs[t, reach_row : reach_row + EDGE, :],
                cond[t, reach_row - REACH : reach_row - REACH + EDGE, :],
            )
        for begin_tile in range(0, tiles, 4):
            rest = None
            for index in range(4):
                at = reach_row + EDGE - REACH - 2 * index
                piece = cond[begin_tile + index, at : at + EDGE, :]
                rest = piece if rest is None else jnp.where(row < 2 * index, rest, piece)
            at = rest_at + begin_tile * 2
            message[slot, at : at + EDGE, :] = rest
        rows = slice(first_row, first_row + EDGE)
        for index in range(4):
            at = coarse_at + index * EDGE
            message[slot, at : at + EDGE, :] = coarse_ref[index, rows, :LANES]
        beyond = [coarse_ref[index, rows, LANES:] for index in range(4)]
        beyond += [field[tiles, begin_row : begin_row + EDGE, :] for field in (obs, cond)]
        message[slot, sides_at : sides_at + EDGE, :] = merge_sides(beyond)
        message[slot, over_at : over_at + EDGE, :] = jnp.concatenate(
            [
                coarse_ref[index, over_row : over_row + 1, half * LANES : (half + 1) * LANES]
                for index in range(4)
                for half in range(2)
            ],
            axis=0,
        )
    send_a[...], send_b[...] = in_pair_order(at_row, message[0], message[1])


def middle(got_a, got_b, coarse, obs, cond):
    tiles, height = obs.shape[0] - 1, obs.shape[1] - 4 * EDGE
    down = height // COARSE
    long = (message_rows(tiles)[-1] + 4 * EDGE, LANES)
    return pl.pallas_call(
        functools.partial(middle_kernel, tiles, down),
        in_specs=[VMEM] * 5,
        out_specs=[VMEM] * 5,
        out_shape=floats(obs.shape, cond.shape, coarse.shape, long, long),
        input_output_aliases={3: 0, 4: 1},
        scratch_shapes=[pltpu.VMEM((2,) + long, jnp.float32)],
        compiler_params=params(),
        name="pack_north_south",
    )(got_b, got_a, coarse, obs, cond)


def inner_kernel(taps, obs, cond, res_ref, east_ref, south_ref, inv_ref, u_ref, dot_ref):
    _, _, has_e, has_w = has_sides()
    clear_pads(east_ref, south_ref)
    taps = read_taps(taps)
    sides = side_lanes(has_e, has_w)

    tiles = obs.shape[0] - 1

    def work(at, start, total):
        fields = begin(obs, cond, at, taps, sides)
        flags = [jnp.where(at + by >= start, 1.0, 0.0) for by in range(0, STRIP, EDGE)]
        total = total + product_sum(fields[3], fields[4], tiles, flags)
        return list(zip((east_ref, south_ref, inv_ref, res_ref, u_ref), fields)), total

    nothing = jnp.zeros((EDGE, LANES), jnp.float32)
    dot_ref[...] = sweep(5, 3 * EDGE, obs.shape[1] - 3 * EDGE, work, nothing)


def inner(taps, obs, cond):
    field = obs.shape
    pixels = field[0] * field[1] * field[2]
    return pl.pallas_call(
        inner_kernel,
        in_specs=[SMEM] + [VMEM] * 2,
        out_specs=[VMEM] * 6,
        out_shape=floats(field, field, field, field, field, (EDGE, LANES)),
        compiler_params=params(),
        cost_estimate=pl.CostEstimate(
            flops=45 * pixels, bytes_accessed=24 * pixels, transcendentals=0
        ),
        name="inner_strips",
    )(taps, obs, cond)


def first_kernel(
    tiles,
    down,
    taps,
    obs_in,
    cond_in,
    res_in,
    east_in,
    south_in,
    inv_in,
    u_in,
    got_b,
    got_a,
    coarse_in,
    dot_in,
    obs,
    cond,
    res_ref,
    east_ref,
    south_ref,
    inv_ref,
    u_ref,
    p_ref,
    q_ref,
    table_ref,
    own_ref,
    chunk_ref,
    image,
    spread,
    work,
):
    height = down * COARSE
    window = down + 2 * EDGE
    at_col, at_row, n_cols, n_rows = place()
    has_n, has_s, has_e, has_w = has_sides()
    clear_pads(obs, cond, p_ref, image)
    clear_work(work)
    from_s, from_n = in_pair_order(
        at_row,
        lambda at, rows=EDGE: got_b[at : at + rows, :],
        lambda at, rows=EDGE: got_a[at : at + rows, :],
    )
    over_at, rest_at, fine_at, sides_at, coarse_at = message_rows(tiles)
    row = iota((EDGE, LANES), 0)
    short = EDGE - REACH
    for t in range(tiles):
        at = fine_at + t * EDGE
        rest = rest_at + 2 * t
        begin_row = 2 * EDGE + height
        obs[t, EDGE : 2 * EDGE, :] = jnp.where(row >= short, from_n(at - short), 0.0)
        obs[t, begin_row : begin_row + EDGE, :] = jnp.where(row < REACH, from_s(at), 0.0)
        near, far = from_n(at + REACH - short), from_n(rest - 2 * short)
        near = jnp.where(row < short, 0.0, near)
        cond[t, EDGE : 2 * EDGE, :] = jnp.where(row < 2 * short, near, far)
        near, far = from_s(at + REACH), from_s(rest - short)
        far = jnp.where(row < REACH, far, 0.0)
        cond[t, begin_row : begin_row + EDGE, :] = jnp.where(row < short, near, far)
    sides_n, sides_s = [split_sides(strip(sides_at), 6) for strip in (from_n, from_s)]
    for which, field in enumerate((obs, cond)):
        field[tiles, EDGE : 2 * EDGE, :] = sides_n[4 + which]
        field[tiles, 2 * EDGE + height : 3 * EDGE + height, :] = sides_s[4 + which]

    edge_row = iota((EDGE, 2 * LANES), 0)

    def joined(index):
        def over(strip, row):
            line = [
                jnp.broadcast_to(
                    strip(over_at + 2 * index + half, 1), (EDGE, LANES)
                )
                for half in range(2)
            ]
            return jnp.where(edge_row == row, jnp.concatenate(line, axis=1), 0.0)

        def rows(strip, beyond):
            return jnp.concatenate([strip(coarse_at + index * EDGE), beyond[index]], axis=1)

        parts = [coarse_in[index, at : at + EDGE, :] for at in range(0, window, EDGE)]
        parts[0] = parts[0] + rows(from_n, sides_n)
        parts[1] = parts[1] + over(from_n, 0)
        parts[-2] = parts[-2] + over(from_s, EDGE - 1)
        parts[-1] = parts[-1] + rows(from_s, sides_s)
        return jnp.concatenate(parts, axis=0)

    source, east, south, around = [joined(index) for index in range(4)]
    row = iota(source.shape, 0)
    lane = iota(source.shape, 1)
    inside = jnp.where(row < EDGE, has_n, jnp.where(row < window - EDGE, 1.0, has_s))
    inside = inside * jnp.where(
        lane < LANES, 1.0, jnp.where(lane < LANES + HALF, has_e, has_w)
    )
    taps = read_taps(taps)
    taps_sum = tap_total(taps, 1)
    factor = inside * OMEGA / (COARSE * COARSE * taps_sum * taps_sum + around)
    weights = (east, roll(east, 1, 1), south, roll(south, 1, 0))
    table = [factor] + [factor * weight for weight in weights]
    for index, part in enumerate([*table, source]):
        table_ref[index] = part
    sides = side_lanes(has_e, has_w)
    half = iota((STRIP, LANES), 0) // EDGE
    pending = []
    total = dot_in[...]
    for index, known in ((0, has_n), (1, has_s)):
        at = EDGE + index * height
        fields = begin(obs, cond, at, taps, sides)
        own = jnp.where(half == index, 0.0, 1.0)
        total = total + fold(own * product_sum_rows(fields[3], fields[4], tiles))
        flag = jnp.where(half == index, known, 1.0)
        inverse, start = [[part * flag for part in fields[index]] for index in (2, 4)]
        fields = (*fields[:2], inverse, fields[3], start)
        pending += [
            (ref, at, strip)
            for ref, strip in zip((east_ref, south_ref, inv_ref, res_ref, u_ref), fields)
        ]
    cells = jacobi(source, table, work)
    spread_cells(cells, spread)
    inner_cells = slice(EDGE, EDGE + down)
    total = total + fold(source[inner_cells, :LANES] * cells[inner_cells, :LANES])
    dot_rp = total
    for ref, at, strip in pending:
        store(ref, at, strip)

    def flags(at, start):
        rows = [at + by for by in range(0, STRIP, EDGE)]
        first_row = jnp.maximum(start, 2 * EDGE)
        return [
            jnp.where((row >= first_row) & (row < 2 * EDGE + height), 1.0, 0.0) for row in rows
        ]

    def begin_p(at, _, carry):
        start, cells = load(u_ref, at), cells_at(spread, at)
        return [(p_ref, [start[t] + cells[t] for t in range(tiles + 1)])], carry

    def blur(at, _, carry):
        strip = conv(p_ref, at, taps, False)
        strip[tiles] = strip[tiles] * sides
        return [(image, strip)], carry

    def finish(at, start, total):
        here, product = operate(p_ref, image, east_ref, south_ref, at, taps)
        return [(q_ref, product)], total + product_sum(here, product, tiles, flags(at, start))

    nothing = jnp.zeros((EDGE, LANES), jnp.float32)
    span = (EDGE, 3 * EDGE + height)
    sweep(3, *span, begin_p, 0)
    sweep(3, *span, blur, 0)
    mask_rows(image, has_n, has_s)
    dot_pq = sweep(3, *span, finish, nothing)

    own = cell_sums(q_ref, tiles, down)
    own_ref[...] = own
    spare = jnp.zeros((LANES - down, LANES), jnp.float32)
    turned = jnp.transpose(jnp.concatenate([own, spare], axis=0))
    me = at_col * n_rows + at_row
    chunk_ref[pl.ds(me * PIECE, EDGE), 0, :] = jnp.zeros((EDGE, LANES), jnp.float32)
    for down_by in (-1, 0, 1):
        for right_by in (-1, 0, 1):
            if down_by == 0 and right_by == 0:
                continue
            if down_by == 0:
                piece = turned[:EDGE] if right_by < 0 else turned[LANES - EDGE :]
            else:
                piece = own[:EDGE] if down_by < 0 else own[down - EDGE :]
            to_row, to_col = at_row + down_by, at_col + right_by
            there = (to_row >= 0) & (to_row < n_rows) & (to_col >= 0) & (to_col < n_cols)
            slot = jnp.where(there, to_col * n_rows + to_row, me)
            chunk_ref[pl.ds(slot * PIECE, EDGE), 0, :] = piece * jnp.where(there, 1.0, 0.0)
    line = sum_line((dot_rp, dot_pq))
    for at in range(EDGE, chunk_ref.shape[0], PIECE):
        chunk_ref[at] = line


def first(taps, fields, got_a, got_b, coarse, dot):
    field = fields[0].shape
    tiles, height = field[0] - 1, field[1] - 4 * EDGE
    down = height // COARSE
    window = down + 2 * EDGE
    count = lax.axis_size("cols") * lax.axis_size("rows")
    shapes = [field] * 9 + [
        (6, window, 2 * LANES),
        (down, LANES),
        (count * PIECE, 1, LANES),
    ]
    return pl.pallas_call(
        functools.partial(first_kernel, tiles, down),
        in_specs=[SMEM] + [VMEM] * 11,
        out_specs=[VMEM] * len(shapes),
        out_shape=floats(*shapes),
        input_output_aliases={index + 1: index for index in range(7)},
        scratch_shapes=[
            pltpu.VMEM(field, jnp.float32),
            pltpu.VMEM((tiles + 1, window, LANES), jnp.float32),
            pltpu.VMEM((2, 2, window + 2 * EDGE, LANES), jnp.float32),
        ],
        compiler_params=params(),
        name="first_direction",
    )(taps, *fields, got_b, got_a, coarse, dot)[2:]


def second_kernel(
    tiles,
    down,
    taps,
    got_ref,
    own_ref,
    table_ref,
    res_ref,
    q_ref,
    east_ref,
    south_ref,
    inv_ref,
    w_ref,
    v_ref,
    out_ref,
    known_ref,
    image,
    spread,
    work,
):
    height = down * COARSE
    has_n, has_s, has_e, has_w = has_sides()
    at_col, at_row, n_cols, n_rows = place()
    me = at_col * n_rows + at_row

    def got(down_by, right_by):
        to_row, to_col = at_row + down_by, at_col + right_by
        there = (to_row >= 0) & (to_row < n_rows) & (to_col >= 0) & (to_col < n_cols)
        slot = jnp.where(there, to_col * n_rows + to_row, me)
        return got_ref[pl.ds(slot * PIECE, EDGE), 0, :]

    low = iota((EDGE, LANES), 1) < HALF
    gap = jnp.zeros((LANES - 2 * EDGE, LANES), jnp.float32)
    beside = jnp.transpose(jnp.concatenate([got(0, 1), gap, got(0, -1)], axis=0))[:down]
    source = jnp.concatenate(
        [
            jnp.concatenate([got(-1, 0), jnp.where(low, got(-1, 1), got(-1, -1))], axis=1),
            jnp.concatenate([own_ref[...], beside], axis=1),
            jnp.concatenate([got(1, 0), jnp.where(low, got(1, 1), got(1, -1))], axis=1),
        ],
        axis=0,
    )
    clear_work(work)
    rp, pq = line_totals(
        [got_ref[at] for at in range(EDGE, got_ref.shape[0], PIECE)], 2
    )
    step = rp / pq
    for index, value in enumerate((step, rp)):
        known_ref[index] = jnp.broadcast_to(value, (EDGE, LANES))
    source = table_ref[5] - jnp.broadcast_to(step, source.shape) * source
    spread_cells(jacobi(source, table_ref, work), spread)
    step = jnp.broadcast_to(step, (STRIP, LANES))
    clear_pads(w_ref, image)
    sides = side_lanes(has_e, has_w)
    taps = read_taps(taps)

    def begin_w(at, start, total):
        right, field, inverse = load(res_ref, at), load(q_ref, at), load(inv_ref, at)
        cells = cells_at(spread, at)
        span = range(tiles + 1)
        residual = [right[t] - step * field[t] for t in span]
        strip = [residual[t] * inverse[t] + cells[t] for t in span]
        first_row = jnp.maximum(start, 2 * EDGE)
        flags = [
            jnp.where((row >= first_row) & (row < 2 * EDGE + height), 1.0, 0.0)
            for row in [at + by for by in range(0, STRIP, EDGE)]
        ]
        return [(w_ref, strip)], total + product_sum(residual, strip, tiles, flags)

    def blur(at, _, carry):
        strip = conv(w_ref, at, taps, False)
        strip[tiles] = strip[tiles] * sides
        return [(image, strip)], carry

    def finish(at, _, total):
        here, product = operate(w_ref, image, east_ref, south_ref, at, taps)
        return [(v_ref, product[:tiles])], total + product_sum(here, product, tiles)

    nothing = jnp.zeros((EDGE, LANES), jnp.float32)
    span = (EDGE, 3 * EDGE + height)
    dot_rz = sweep(3, *span, begin_w, nothing)
    sweep(3, *span, blur, 0)
    mask_rows(image, has_n, has_s)
    dot_zz = sweep(4, 2 * EDGE, 2 * EDGE + height, finish, nothing)
    line = sum_line((dot_rz, dot_zz))
    for index in range(out_ref.shape[0]):
        out_ref[index] = line


def second(taps, got, own, table, r, q, east, south, inv):
    tiles, height = q.shape[0] - 1, q.shape[1] - 4 * EDGE
    down = height // COARSE
    window = down + 2 * EDGE
    count = lax.axis_size("cols") * lax.axis_size("rows")
    return pl.pallas_call(
        functools.partial(second_kernel, tiles, down),
        in_specs=[SMEM] + [VMEM] * 8,
        out_specs=[VMEM] * 4,
        out_shape=floats(q.shape, q.shape, (count, 1, LANES), (2, EDGE, LANES)),
        scratch_shapes=[
            pltpu.VMEM(q.shape, jnp.float32),
            pltpu.VMEM((tiles + 1, window, LANES), jnp.float32),
            pltpu.VMEM((2, 2, window + 2 * EDGE, LANES), jnp.float32),
        ],
        compiler_params=params(),
        name="second_direction",
    )(taps, got, own, table, r, q, east, south, inv)


def combine_kernel(
    tiles, height, sums_ref, known_ref, p_ref, w_ref, r_ref, q_ref, v_ref, sol_out, res_out, sol, res, sem
):
    rz, zz = line_totals([sums_ref[index] for index in range(sums_ref.shape[0])], 2)
    step, rp = [known_ref[index, :1, :] for index in range(2)]
    ratio = rz / rp
    step_next = rz / (zz - ratio * (rz / step))
    on_w = jnp.broadcast_to(step_next, (CHUNK, LANES))
    on_p = jnp.broadcast_to(step + step_next * ratio, (CHUNK, LANES))

    def copies(index):
        rows = pl.ds(pl.multiple_of(index * CHUNK, CHUNK), CHUNK)
        return (
            pltpu.make_async_copy(sol.at[rows, :], sol_out.at[rows, :], sem.at[0, index]),
            pltpu.make_async_copy(res.at[rows, :], res_out.at[rows, :], sem.at[1, index]),
        )

    def work(index, _):
        at = pl.multiple_of(index * CHUNK, CHUNK)
        p, w, r, q, v = [
            load(ref, at + 2 * EDGE, CHUNK) for ref in (p_ref, w_ref, r_ref, q_ref, v_ref)
        ]
        one = [on_p * p[t] + on_w * w[t] for t in range(tiles)]
        two = [r[t] - on_p * q[t] - on_w * v[t] for t in range(tiles)]
        for t in range(tiles):
            sol[pl.ds(at, CHUNK), t * LANES : (t + 1) * LANES] = one[t]
            res[pl.ds(at, CHUNK), t * LANES : (t + 1) * LANES] = two[t]
        for copy in copies(index):
            copy.start()
        return 0

    def settle(index, _):
        for copy in copies(index):
            copy.wait()
        return 0

    lax.fori_loop(0, height // CHUNK, work, 0)
    lax.fori_loop(0, height // CHUNK, settle, 0)


def combine(sums, known, p, w, r, q, v):
    tiles, height = q.shape[0] - 1, q.shape[1] - 4 * EDGE
    shape = (height, tiles * LANES)
    return pl.pallas_call(
        functools.partial(combine_kernel, tiles, height),
        in_specs=[VMEM] * 7,
        out_specs=[HBM] * 2,
        out_shape=floats(shape, shape),
        scratch_shapes=[
            pltpu.VMEM(shape, jnp.float32),
            pltpu.VMEM(shape, jnp.float32),
            pltpu.SemaphoreType.DMA((2, height // CHUNK)),
        ],
        compiler_params=params(),
        name="combine",
    )(sums, known, p, w, r, q, v)


def exchange(send_a, send_b, axis):
    count = lax.axis_size(axis)

    def pairs(begin):
        return [
            pair for i in range(begin, count - 1, 2) for pair in ((i, i + 1), (i + 1, i))
        ]

    got_b = lax.ppermute(send_b, axis, pairs(1))
    got_a = lax.ppermute(send_a, axis, pairs(0))
    return got_a, got_b


def body(observed, class_map, class_weights, blur_kernel):
    arguments = (observed, class_map, class_weights, blur_kernel)
    send_a, send_b = edge(*arguments)
    got_a, got_b = exchange(send_a, send_b, "cols")
    obs, cond, coarse = pack(*arguments, send_a)
    obs, cond, coarse, send_a, send_b = middle(got_a, got_b, coarse, obs, cond)
    got_a, got_b = exchange(send_a, send_b, "rows")
    r, east, south, inv, u, dot = inner(blur_kernel, obs, cond)
    fields = (obs, cond, r, east, south, inv, u)
    r, east, south, inv, _, p, q, table, own, chunk = first(
        blur_kernel, fields, got_a, got_b, coarse, dot
    )
    got = lax.all_to_all(chunk, AXES, 0, 0, tiled=True)
    w, v, line, known = second(blur_kernel, got, own, table, r, q, east, south, inv)
    sums = lax.all_to_all(line, AXES[::-1], 0, 0, tiled=True)
    return tuple(combine(sums, known, p, w, r, q, v))


def solution(mesh):
    return jax.shard_map(
        body,
        mesh=mesh,
        in_specs=(P("rows", "cols"), P("rows", "cols"), P(), P()),
        out_specs=(P("rows", "cols"), P("rows", "cols")),
        check_vma=False,
    )
```

```python
import functools

import jax
import jax.numpy as jnp
from jax import lax
from jax.experimental import pallas as pl
from jax.experimental.pallas import tpu as pltpu
from jax.sharding import PartitionSpec as P

COARSE = 8
SWEEPS = 8
CLASSES = 4
OMEGA = 0.8

LANES = 128
HALF = LANES // 2
EDGE = 8
STRIP = 2 * EDGE
REACH = 5
PIECE = EDGE + 1
CHUNK = 128
AXES = ("cols", "rows")
LIMIT = 40 * 1024 * 1024


VMEM = pl.BlockSpec(memory_space=pltpu.VMEM)
SMEM = pl.BlockSpec(memory_space=pltpu.SMEM)
HBM = pl.BlockSpec(memory_space=pltpu.HBM)


def params():
    return pltpu.CompilerParams(vmem_limit_bytes=LIMIT)


def in_hbm(array):
    return pltpu.with_memory_space_constraint(array, pltpu.HBM)


def floats(*shapes):
    return [jax.ShapeDtypeStruct(shape, jnp.float32) for shape in shapes]


def place():
    at_col, at_row = lax.axis_index("cols"), lax.axis_index("rows")
    n_cols, n_rows = lax.axis_size("cols"), lax.axis_size("rows")
    return at_col, at_row, n_cols, n_rows


def has_sides():
    at_col, at_row, n_cols, n_rows = place()
    flag = lambda test: jnp.where(test, 1.0, 0.0).astype(jnp.float32)
    return (
        flag(at_row > 0),
        flag(at_row < n_rows - 1),
        flag(at_col < n_cols - 1),
        flag(at_col > 0),
    )


def iota(shape, dim):
    return lax.broadcasted_iota(jnp.int32, shape, dim)


def cell_of(pixel, tiles):
    turn = (tiles + 1) * LANES
    return jnp.where(pixel < turn - HALF, pixel >> 3, ((pixel - turn) >> 3) & (2 * LANES - 1))


def gather_matrix(tiles):
    shape = ((tiles + 1) * LANES, 2 * LANES)
    hit = cell_of(iota(shape, 0), tiles) == iota(shape, 1)
    return jnp.where(hit, 1.0, 0.0).astype(jnp.bfloat16)


def split_dot(field, matrix):
    rows = field.shape[0]
    parts, rest = [], field
    for _ in range(3):
        parts.append(rest.astype(jnp.bfloat16))
        rest = rest - parts[-1].astype(jnp.float32)
    product = jnp.dot(
        jnp.concatenate(parts, axis=0), matrix, preferred_element_type=jnp.float32
    )
    return product[:rows] + (product[rows : 2 * rows] + product[2 * rows :])


def roll(field, by, axis):
    return pltpu.roll(field, by % field.shape[axis], axis)


def load(ref, at, rows=STRIP):
    return [ref[t, pl.ds(at, rows), :] for t in range(ref.shape[0])]


def store(ref, at, strip):
    for t, part in enumerate(strip):
        ref[t, pl.ds(at, part.shape[0]), :] = part


def wide(ref, at, rows):
    return jnp.concatenate(load(ref, at, rows), axis=1)


def read_taps(taps):
    return [[taps[a, b] for b in range(3)] for a in range(3)]


def tap_total(taps, power):
    return sum(tap * tap if power == 2 else tap for line in taps for tap in line)


def from_west(strip):
    lane = iota(strip[0].shape, 1)
    turned = [roll(part, 1, 1) for part in strip]
    return [jnp.where(lane == 0, turned[t - 1], turned[t]) for t in range(len(strip))]


def from_east(strip):
    lane = iota(strip[0].shape, 1)
    turned = [roll(part, -1, 1) for part in strip]
    count = len(strip)
    return [
        jnp.where(lane == LANES - 1, turned[(t + 1) % count], turned[t]) for t in range(count)
    ]


def tap_sums(ref, at, taps, flip):
    if flip:
        taps = [line[::-1] for line in taps[::-1]]
    above, here, below = load(ref, at - 1), load(ref, at), load(ref, at + 1)
    sums = [[], [], []]
    for t in range(len(here)):
        for b in range(3):
            sums[b].append(
                taps[0][b] * above[t] + taps[1][b] * here[t] + taps[2][b] * below[t]
            )
    return sums


def conv(ref, at, taps, flip):
    sums = tap_sums(ref, at, taps, flip)
    west, east = from_west(sums[0]), from_east(sums[2])
    return [sums[1][t] + west[t] + east[t] for t in range(len(west))]


def operate(ref, image, east_ref, south_ref, at, taps):
    above, here, below = load(ref, at - 1), load(ref, at), load(ref, at + 1)
    east, south, north = load(east_ref, at), load(south_ref, at), load(south_ref, at - 1)
    sums = tap_sums(image, at, taps, True)
    span = range(len(here))
    beside = from_east(here)
    flux = [east[t] * (here[t] - beside[t]) for t in span]
    from_left = from_west([sums[0][t] - flux[t] for t in span])
    from_right = from_east(sums[2])
    return here, [
        sums[1][t]
        + flux[t]
        + from_left[t]
        + from_right[t]
        + south[t] * (here[t] - below[t])
        - north[t] * (above[t] - here[t])
        for t in span
    ]


def begin(obs, cond, at, taps, sides):
    above, here, below = load(cond, at - 1), load(cond, at), load(cond, at + 1)
    span = range(len(here))
    right = from_east(here)
    east = [here[t] + right[t] for t in span]
    west = from_west(east)
    south = [here[t] + below[t] for t in span]
    squares = tap_total(taps, 2)
    diag = [squares + east[t] + west[t] + south[t] + (here[t] + above[t]) for t in span]
    inverse = [pl.reciprocal(part, approx=True) for part in diag]
    inverse = [inverse[t] * (2.0 - diag[t] * inverse[t]) for t in span]
    inverse[-1] = inverse[-1] * sides
    residual = conv(obs, at, taps, True)
    return east, south, inverse, residual, [residual[t] * inverse[t] for t in span]


def pick_lanes(field, lanes):
    return jnp.take_along_axis(field, lanes, axis=1, mode="promise_in_bounds")


def spread_cells(cells, spread):
    tiles = spread.shape[0] - 1
    lane = iota((cells.shape[0], LANES), 1)
    for t in range(tiles):
        spread[t] = pick_lanes(cells[:, :LANES], (lane >> 3) + t * (LANES // COARSE))
    turn = jnp.where(lane < HALF, 0, LANES - LANES // COARSE)
    spread[tiles] = pick_lanes(cells[:, LANES:], (lane >> 3) + turn)


def cells_at(spread, at):
    first = at // EDGE + EDGE - 2
    rows = [load(spread, first + index, 1) for index in range(STRIP // EDGE)]
    return [
        jnp.concatenate([jnp.broadcast_to(row, (EDGE, LANES)) for row in parts], axis=0)
        for parts in zip(*rows)
    ]


def cell_sums(ref, tiles, down):
    lane = iota((down, LANES), 1)
    total = jnp.zeros((down, LANES), jnp.float32)
    for t in range(tiles):
        picked = [
            ref[t, pl.ds(2 * EDGE + k, down, stride=COARSE), :] for k in range(COARSE)
        ]
        part = sum(picked[1:], picked[0])
        for by in (1, 2, 4):
            part = part + roll(part, -by, 1)
        part = pick_lanes(part, (lane & (LANES // COARSE - 1)) * COARSE)
        total = jnp.where(lane // (LANES // COARSE) == t, part, total)
    return total


def side_lanes(has_e, has_w):
    return jnp.where(iota((STRIP, LANES), 1) < HALF, has_e, has_w)


def mask_rows(ref, has_n, has_s):
    last = ref.shape[1] - 2 * EDGE
    for at, flag in ((EDGE, has_n), (last, has_s)):
        ref[:, at : at + EDGE, :] = ref[:, at : at + EDGE, :] * flag


def clear_pads(*refs):
    empty = jnp.zeros((refs[0].shape[0], EDGE, LANES), jnp.float32)
    for ref in refs:
        ref[:, :EDGE, :] = empty
        ref[:, ref.shape[1] - EDGE :, :] = empty


def product_sum_rows(one, two, count):
    total = one[0] * two[0]
    for t in range(1, count):
        total = total + one[t] * two[t]
    return total


def product_sum(one, two, count, flags=None):
    return fold(product_sum_rows(one, two, count), flags)


def fold(total, flags=None):
    parts = [total[at : at + EDGE] for at in range(0, total.shape[0], EDGE)]
    if flags is not None:
        parts = [part * flag for part, flag in zip(parts, flags)]
    return sum(parts[1:], parts[0])


def sweep(group, first, last, body, carry):
    width = group * STRIP
    steps = -(-(last - first) // width)

    def work(index, carry):
        start = first + index * width
        at = pl.multiple_of(jnp.minimum(start, last - width), EDGE)
        pending = []
        for by in range(0, width, STRIP):
            stores, carry = body(at + by, start, carry)
            pending += [(ref, at + by, strip) for ref, strip in stores]
        for ref, row, strip in pending:
            store(ref, row, strip)
        return carry

    return lax.fori_loop(0, steps, work, carry)


def sum_line(parts):
    line = jnp.zeros((1, LANES), jnp.float32)
    block = iota((1, LANES), 1) // (LANES // 4)
    for index, part in enumerate(parts):
        part = jnp.sum(part, axis=0, keepdims=True)
        part = part + roll(part, LANES // 2, 1)
        part = part + roll(part, LANES // 4, 1)
        line = jnp.where(block == index, part, line)
    return line


def line_totals(lines, count):
    while len(lines) > 1:
        lines = [sum(lines[at + 1 : at + 2], lines[at]) for at in range(0, len(lines), 2)]
    block = iota((1, LANES), 1) // (LANES // 4)
    return [
        jnp.sum(jnp.where(block == index, lines[0], 0.0), axis=1, keepdims=True)
        for index in range(count)
    ]


def jacobi(source, table, work):
    factor, east, west, south, north = [table[index] for index in range(5)]
    window = source.shape[0]
    source = factor * source
    iterate = source
    for sweep_index in range(SWEEPS - 1):
        place_ref = work.at[sweep_index % 2]
        for half in range(2):
            place_ref[half, EDGE : EDGE + window, :] = iterate[
                :, half * LANES : (half + 1) * LANES
            ]
        above, below = [
            jnp.concatenate(
                [place_ref[half, EDGE + by : EDGE + by + window, :] for half in range(2)], axis=1
            )
            for by in (-1, 1)
        ]
        across = east * roll(iterate, -1, 1) + west * roll(iterate, 1, 1)
        along = south * below + north * above
        iterate = ((1.0 - OMEGA) * iterate + source) + (across + along)
    return iterate


def clear_work(work):
    for buffer in range(2):
        clear_pads(work.at[buffer])


def in_pair_order(at, for_before, for_after):
    even = at % 2 == 0
    if callable(for_before):
        return (
            lambda *args: jnp.where(even, for_after(*args), for_before(*args)),
            lambda *args: jnp.where(even, for_before(*args), for_after(*args)),
        )
    return jnp.where(even, for_after, for_before), jnp.where(even, for_before, for_after)


def reader(tiles_here, refs, scratch, obs, cond, down):
    obs_in, class_in, weight_in, taps_in = refs
    classes, weights, taps, sums, obs_sem, class_sem, small_sem = scratch
    own = pl.ds(2 * EDGE, down * COARSE)
    small = [
        pltpu.make_async_copy(weight_in, weights, small_sem.at[0]),
        pltpu.make_async_copy(taps_in, taps, small_sem.at[1]),
    ]
    moves = []
    for slot, t in enumerate(tiles_here):
        lanes = pl.ds(t * LANES, LANES)
        moves.append(
            (
                pltpu.make_async_copy(class_in.at[:, lanes], classes.at[slot], class_sem.at[slot]),
                pltpu.make_async_copy(
                    obs_in.at[:, lanes], obs.at[slot, own, :], obs_sem.at[slot]
                ),
            )
        )
    for copy in small:
        copy.start()
    for pair in moves:
        for copy in pair:
            copy.start()
    sums[...] = jnp.zeros_like(sums)

    def settle(slot):
        if slot == 0:
            for copy in small:
                copy.wait()
        for copy in moves[slot]:
            copy.wait()
        values = [0.5 * weights[class_id] for class_id in range(CLASSES)]
        kind = classes[slot]
        cond[slot, own, :] = jnp.where(
            kind < 2,
            jnp.where(kind == 0, values[0], values[1]),
            jnp.where(kind == 2, values[2], values[3]),
        )
        for which, ref in enumerate((obs, cond)):
            picked = [
                ref[slot, pl.ds(2 * EDGE + k, down, stride=COARSE), :] for k in range(COARSE)
            ]
            cells = slice(2 * EDGE, 2 * EDGE + down)
            sums[3 * which, slot, cells, :] = sum(picked[1:], picked[0])
            sums[3 * which + 1, slot, cells, :] = picked[0]
            sums[3 * which + 2, slot, cells, :] = picked[-1]

    return settle


def reader_scratch(tiles, height, window, class_weights, taps):
    return [
        pltpu.VMEM((tiles, height, LANES), jnp.int32),
        pltpu.SMEM(class_weights.shape, jnp.float32),
        pltpu.SMEM(taps.shape, jnp.float32),
        pltpu.VMEM((6, tiles + 1, window + 2 * EDGE, LANES), jnp.float32),
        pltpu.SemaphoreType.DMA((tiles,)),
        pltpu.SemaphoreType.DMA((tiles,)),
        pltpu.SemaphoreType.DMA((2,)),
    ]


def coarse_parts(sums, taps, matrix):
    window = sums.shape[2] - 2 * EDGE
    whole = lambda index, by=0: wide(sums.at[index], EDGE + by, window)
    full = whole(0)
    by_tap = [full - whole(1) + whole(1, 1), full, full - whole(2) + whole(2, -1)]
    across = [sum(taps[a][b] * by_tap[a] for a in range(3)) for b in range(3)]
    source = across[1] + roll(across[0], -1, 1) + roll(across[2], 1, 1)
    full = whole(3)
    last = (iota(full.shape, 1) & (COARSE - 1)) == COARSE - 1
    east = jnp.where(last, full + roll(full, -1, 1), 0.0)
    south = whole(5) + whole(4, 1)
    cells = split_dot(jnp.concatenate([source, east, south], axis=0), matrix)
    source, east, south = cells[:window], cells[window : 2 * window], cells[2 * window :]
    around = east + roll(east, 1, 1) + south + roll(south, 1, 0)
    return [source, east, south, around]


def edge_kernel(tiles, down, *refs):
    arguments, (send_a, send_b), (obs, cond, message, *scratch) = refs[:4], refs[4:6], refs[6:]
    height = down * COARSE
    halves = height // LANES
    window = down + 2 * EDGE
    settle = reader((0, tiles - 1), arguments, scratch, obs, cond, down)
    matrix = gather_matrix(2)
    fine = [[], []]
    for slot, begin_row in ((0, 0), (1, LANES - REACH)):
        settle(slot)
        for ref in (obs, cond):
            turned = jnp.transpose(ref[slot, 2 * EDGE : 2 * EDGE + height, :])
            turned = turned[begin_row : begin_row + REACH]
            for half in range(halves):
                fine[slot].append(turned[:, half * LANES : (half + 1) * LANES])
    parts = coarse_parts(scratch[3], read_taps(scratch[2]), matrix)
    spare = jnp.zeros((2 * LANES - 4 * window, 2 * LANES), jnp.float32)
    stack = jnp.concatenate(parts + [spare], axis=0)
    left = jnp.transpose(stack[:, :LANES])
    right = jnp.transpose(stack[:, LANES:])
    past = 2 * LANES // COARSE
    split = lambda piece: [piece[:, half * LANES : (half + 1) * LANES] for half in range(2)]
    for slot, main, over in (
        (0, left[:EDGE], right[LANES - 1 :]),
        (1, left[past - EDGE : past], left[past : past + 1]),
    ):
        rows = split(main) + fine[slot] + split(over)
        filled = sum(piece.shape[0] for piece in rows)
        rows.append(jnp.zeros((message.shape[1] - filled, LANES), jnp.float32))
        message[slot] = jnp.concatenate(rows, axis=0)
    send_a[...], send_b[...] = in_pair_order(place()[0], message[0], message[1])


def edge(observed, class_map, class_weights, taps):
    height, breadth = observed.shape
    tiles, down = breadth // LANES, height // COARSE
    window = down + 2 * EDGE
    field = (3, height + 4 * EDGE, LANES)
    rows = 2 * EDGE + 2 * REACH * (height // LANES) + 2
    strip = (-(-rows // EDGE) * EDGE, LANES)
    return pl.pallas_call(
        functools.partial(edge_kernel, tiles, down),
        in_specs=[HBM] * 4,
        out_specs=[VMEM] * 2,
        out_shape=floats(strip, strip),
        scratch_shapes=[
            pltpu.VMEM(field, jnp.float32),
            pltpu.VMEM(field, jnp.float32),
            pltpu.VMEM((2,) + strip, jnp.float32),
        ]
        + reader_scratch(2, height, window, class_weights, taps),
        compiler_params=params(),
        name="pack_east_west",
    )(*[in_hbm(array) for array in (observed, class_map, class_weights, taps)])


def pack_kernel(tiles, down, *refs):
    arguments, (obs, cond, coarse_ref), scratch = refs[:4], refs[5:8], refs[8:]
    settle = reader(range(tiles), arguments, scratch, obs, cond, down)
    matrix = gather_matrix(tiles)
    for t in range(tiles):
        settle(t)
    for index, part in enumerate(coarse_parts(scratch[3], read_taps(scratch[2]), matrix)):
        coarse_ref[index] = part


def pack(observed, class_map, class_weights, taps, after):
    height, breadth = observed.shape
    tiles, down = breadth // LANES, height // COARSE
    window = down + 2 * EDGE
    field = (tiles + 1, height + 4 * EDGE, LANES)
    pixels = height * breadth
    return pl.pallas_call(
        functools.partial(pack_kernel, tiles, down),
        in_specs=[HBM] * 4 + [VMEM],
        out_specs=[VMEM] * 3,
        out_shape=floats(field, field, (4, window, 2 * LANES)),
        scratch_shapes=reader_scratch(tiles, height, window, class_weights, taps),
        compiler_params=params(),
        cost_estimate=pl.CostEstimate(
            flops=20 * pixels, bytes_accessed=16 * pixels, transcendentals=0
        ),
        name="pack_all",
    )(*[in_hbm(array) for array in (observed, class_map, class_weights, taps)], after)


def message_rows(tiles):
    rest = EDGE
    fine = rest + 2 * tiles
    sides = fine + tiles * EDGE
    return 0, rest, fine, sides, sides + EDGE


def merge_sides(parts):
    block = iota((EDGE, LANES), 1) // (2 * EDGE)
    merged = jnp.zeros((EDGE, LANES), jnp.float32)
    for index, part in enumerate(parts):
        merged = jnp.where(block == index, roll(part, (2 * index + 1) * EDGE, 1), merged)
    return merged


def split_sides(merged, count):
    lane = iota((EDGE, LANES), 1)
    outer = (lane < EDGE) | (lane >= LANES - EDGE)
    return [
        jnp.where(outer, roll(merged, -(2 * index + 1) * EDGE, 1), 0.0) for index in range(count)
    ]


def middle_kernel(
    tiles,
    down,
    got_b,
    got_a,
    coarse_in,
    obs_in,
    cond_in,
    obs,
    cond,
    coarse_ref,
    send_a,
    send_b,
    message,
):
    height = down * COARSE
    halves = height // LANES
    at_col, at_row, _, _ = place()
    from_e, from_w = in_pair_order(at_col, got_b[...], got_a[...])
    zeros = lambda rows: jnp.zeros((rows, LANES), jnp.float32)

    def turned(low, high):
        low = [low, zeros(EDGE - low.shape[0])] if low.shape[0] < EDGE else [low]
        high = [zeros(EDGE - high.shape[0]), high] if high.shape[0] < EDGE else [high]
        return jnp.transpose(jnp.concatenate([*low, zeros(LANES - 2 * EDGE), *high], axis=0))

    for which, field in enumerate((obs, cond)):
        for half in range(halves):
            at = 2 * EDGE + REACH * (which * halves + half)
            begin_row = 2 * EDGE + half * LANES
            field[tiles, begin_row : begin_row + LANES, :] = turned(
                from_e[at : at + REACH], from_w[at : at + REACH]
            )
    main = lambda strip, half: strip[half * EDGE : (half + 1) * EDGE]

    def over(strip, half):
        at = 2 * EDGE + 2 * REACH * halves + half
        return strip[at : at + 1]

    left = [turned(over(from_w, half), over(from_e, half)) for half in range(2)]
    right = [turned(main(from_e, half), main(from_w, half)) for half in range(2)]
    left = jnp.concatenate(left, axis=0)
    right = jnp.concatenate(right, axis=0)
    window = down + 2 * EDGE
    for index in range(4):
        rows = slice(index * window, (index + 1) * window)
        coarse_ref[index, :, :LANES] = coarse_in[index, :, :LANES] + left[rows]
        coarse_ref[index, :, LANES:] = coarse_in[index, :, LANES:] + right[rows]
    row = iota((EDGE, LANES), 0)
    over_at, rest_at, fine_at, sides_at, coarse_at = message_rows(tiles)
    for slot, begin_row, reach_row, first_row, over_row in (
        (0, 2 * EDGE, 2 * EDGE, EDGE, EDGE - 1),
        (1, EDGE + height, 2 * EDGE + height - REACH, window - 2 * EDGE, window - EDGE),
    ):
        for t in range(tiles):
            at = fine_at + t * EDGE
            message[slot, at : at + EDGE, :] = jnp.where(
                row < REACH,
                obs[t, reach_row : reach_row + EDGE, :],
                cond[t, reach_row - REACH : reach_row - REACH + EDGE, :],
            )
        for begin_tile in range(0, tiles, 4):
            rest = None
            for index in range(4):
                at = reach_row + EDGE - REACH - 2 * index
                piece = cond[begin_tile + index, at : at + EDGE, :]
                rest = piece if rest is None else jnp.where(row < 2 * index, rest, piece)
            at = rest_at + begin_tile * 2
            message[slot, at : at + EDGE, :] = rest
        rows = slice(first_row, first_row + EDGE)
        for index in range(4):
            at = coarse_at + index * EDGE
            message[slot, at : at + EDGE, :] = coarse_ref[index, rows, :LANES]
        beyond = [coarse_ref[index, rows, LANES:] for index in range(4)]
        beyond += [field[tiles, begin_row : begin_row + EDGE, :] for field in (obs, cond)]
        message[slot, sides_at : sides_at + EDGE, :] = merge_sides(beyond)
        message[slot, over_at : over_at + EDGE, :] = jnp.concatenate(
            [
                coarse_ref[index, over_row : over_row + 1, half * LANES : (half + 1) * LANES]
                for index in range(4)
                for half in range(2)
            ],
            axis=0,
        )
    send_a[...], send_b[...] = in_pair_order(at_row, message[0], message[1])


def middle(got_a, got_b, coarse, obs, cond):
    tiles, height = obs.shape[0] - 1, obs.shape[1] - 4 * EDGE
    down = height // COARSE
    long = (message_rows(tiles)[-1] + 4 * EDGE, LANES)
    return pl.pallas_call(
        functools.partial(middle_kernel, tiles, down),
        in_specs=[VMEM] * 5,
        out_specs=[VMEM] * 5,
        out_shape=floats(obs.shape, cond.shape, coarse.shape, long, long),
        input_output_aliases={3: 0, 4: 1},
        scratch_shapes=[pltpu.VMEM((2,) + long, jnp.float32)],
        compiler_params=params(),
        name="pack_north_south",
    )(got_b, got_a, coarse, obs, cond)


def inner_kernel(taps, obs, cond, res_ref, east_ref, south_ref, inv_ref, u_ref, dot_ref):
    _, _, has_e, has_w = has_sides()
    clear_pads(east_ref, south_ref)
    taps = read_taps(taps)
    sides = side_lanes(has_e, has_w)

    tiles = obs.shape[0] - 1

    def work(at, start, total):
        fields = begin(obs, cond, at, taps, sides)
        flags = [jnp.where(at + by >= start, 1.0, 0.0) for by in range(0, STRIP, EDGE)]
        total = total + product_sum(fields[3], fields[4], tiles, flags)
        return list(zip((east_ref, south_ref, inv_ref, res_ref, u_ref), fields)), total

    nothing = jnp.zeros((EDGE, LANES), jnp.float32)
    dot_ref[...] = sweep(5, 3 * EDGE, obs.shape[1] - 3 * EDGE, work, nothing)


def inner(taps, obs, cond):
    field = obs.shape
    pixels = field[0] * field[1] * field[2]
    return pl.pallas_call(
        inner_kernel,
        in_specs=[SMEM] + [VMEM] * 2,
        out_specs=[VMEM] * 6,
        out_shape=floats(field, field, field, field, field, (EDGE, LANES)),
        compiler_params=params(),
        cost_estimate=pl.CostEstimate(
            flops=45 * pixels, bytes_accessed=24 * pixels, transcendentals=0
        ),
        name="inner_strips",
    )(taps, obs, cond)


def first_kernel(
    tiles,
    down,
    taps,
    obs_in,
    cond_in,
    res_in,
    east_in,
    south_in,
    inv_in,
    u_in,
    got_b,
    got_a,
    coarse_in,
    dot_in,
    obs,
    cond,
    res_ref,
    east_ref,
    south_ref,
    inv_ref,
    u_ref,
    p_ref,
    q_ref,
    table_ref,
    own_ref,
    chunk_ref,
    image,
    spread,
    work,
):
    height = down * COARSE
    window = down + 2 * EDGE
    at_col, at_row, n_cols, n_rows = place()
    has_n, has_s, has_e, has_w = has_sides()
    clear_pads(obs, cond, p_ref, image)
    clear_work(work)
    from_s, from_n = in_pair_order(
        at_row,
        lambda at, rows=EDGE: got_b[at : at + rows, :],
        lambda at, rows=EDGE: got_a[at : at + rows, :],
    )
    over_at, rest_at, fine_at, sides_at, coarse_at = message_rows(tiles)
    row = iota((EDGE, LANES), 0)
    short = EDGE - REACH
    for t in range(tiles):
        at = fine_at + t * EDGE
        rest = rest_at + 2 * t
        begin_row = 2 * EDGE + height
        obs[t, EDGE : 2 * EDGE, :] = jnp.where(row >= short, from_n(at - short), 0.0)
        obs[t, begin_row : begin_row + EDGE, :] = jnp.where(row < REACH, from_s(at), 0.0)
        near, far = from_n(at + REACH - short), from_n(rest - 2 * short)
        near = jnp.where(row < short, 0.0, near)
        cond[t, EDGE : 2 * EDGE, :] = jnp.where(row < 2 * short, near, far)
        near, far = from_s(at + REACH), from_s(rest - short)
        far = jnp.where(row < REACH, far, 0.0)
        cond[t, begin_row : begin_row + EDGE, :] = jnp.where(row < short, near, far)
    sides_n, sides_s = [split_sides(strip(sides_at), 6) for strip in (from_n, from_s)]
    for which, field in enumerate((obs, cond)):
        field[tiles, EDGE : 2 * EDGE, :] = sides_n[4 + which]
        field[tiles, 2 * EDGE + height : 3 * EDGE + height, :] = sides_s[4 + which]

    edge_row = iota((EDGE, 2 * LANES), 0)

    def joined(index):
        def over(strip, row):
            line = [
                jnp.broadcast_to(
                    strip(over_at + 2 * index + half, 1), (EDGE, LANES)
                )
                for half in range(2)
            ]
            return jnp.where(edge_row == row, jnp.concatenate(line, axis=1), 0.0)

        def rows(strip, beyond):
            return jnp.concatenate([strip(coarse_at + index * EDGE), beyond[index]], axis=1)

        parts = [coarse_in[index, at : at + EDGE, :] for at in range(0, window, EDGE)]
        parts[0] = parts[0] + rows(from_n, sides_n)
        parts[1] = parts[1] + over(from_n, 0)
        parts[-2] = parts[-2] + over(from_s, EDGE - 1)
        parts[-1] = parts[-1] + rows(from_s, sides_s)
        return jnp.concatenate(parts, axis=0)

    source, east, south, around = [joined(index) for index in range(4)]
    row = iota(source.shape, 0)
    lane = iota(source.shape, 1)
    inside = jnp.where(row < EDGE, has_n, jnp.where(row < window - EDGE, 1.0, has_s))
    inside = inside * jnp.where(
        lane < LANES, 1.0, jnp.where(lane < LANES + HALF, has_e, has_w)
    )
    taps = read_taps(taps)
    taps_sum = tap_total(taps, 1)
    factor = inside * OMEGA / (COARSE * COARSE * taps_sum * taps_sum + around)
    weights = (east, roll(east, 1, 1), south, roll(south, 1, 0))
    table = [factor] + [factor * weight for weight in weights]
    for index, part in enumerate([*table, source]):
        table_ref[index] = part
    sides = side_lanes(has_e, has_w)
    half = iota((STRIP, LANES), 0) // EDGE
    pending = []
    total = dot_in[...]
    for index, known in ((0, has_n), (1, has_s)):
        at = EDGE + index * height
        fields = begin(obs, cond, at, taps, sides)
        own = jnp.where(half == index, 0.0, 1.0)
        total = total + fold(own * product_sum_rows(fields[3], fields[4], tiles))
        flag = jnp.where(half == index, known, 1.0)
        inverse, start = [[part * flag for part in fields[index]] for index in (2, 4)]
        fields = (*fields[:2], inverse, fields[3], start)
        pending += [
            (ref, at, strip)
            for ref, strip in zip((east_ref, south_ref, inv_ref, res_ref, u_ref), fields)
        ]
    cells = jacobi(source, table, work)
    spread_cells(cells, spread)
    inner_cells = slice(EDGE, EDGE + down)
    total = total + fold(source[inner_cells, :LANES] * cells[inner_cells, :LANES])
    dot_rp = total
    for ref, at, strip in pending:
        store(ref, at, strip)

    def flags(at, start):
        rows = [at + by for by in range(0, STRIP, EDGE)]
        first_row = jnp.maximum(start, 2 * EDGE)
        return [
            jnp.where((row >= first_row) & (row < 2 * EDGE + height), 1.0, 0.0) for row in rows
        ]

    def begin_p(at, _, carry):
        start, cells = load(u_ref, at), cells_at(spread, at)
        return [(p_ref, [start[t] + cells[t] for t in range(tiles + 1)])], carry

    def blur(at, _, carry):
        strip = conv(p_ref, at, taps, False)
        strip[tiles] = strip[tiles] * sides
        return [(image, strip)], carry

    def finish(at, start, total):
        here, product = operate(p_ref, image, east_ref, south_ref, at, taps)
        return [(q_ref, product)], total + product_sum(here, product, tiles, flags(at, start))

    nothing = jnp.zeros((EDGE, LANES), jnp.float32)
    span = (EDGE, 3 * EDGE + height)
    sweep(6, *span, begin_p, 0)
    sweep(3, *span, blur, 0)
    mask_rows(image, has_n, has_s)
    dot_pq = sweep(3, *span, finish, nothing)

    own = cell_sums(q_ref, tiles, down)
    own_ref[...] = own
    spare = jnp.zeros((LANES - down, LANES), jnp.float32)
    turned = jnp.transpose(jnp.concatenate([own, spare], axis=0))
    me = at_col * n_rows + at_row
    chunk_ref[pl.ds(me * PIECE, EDGE), 0, :] = jnp.zeros((EDGE, LANES), jnp.float32)
    for down_by in (-1, 0, 1):
        for right_by in (-1, 0, 1):
            if down_by == 0 and right_by == 0:
                continue
            if down_by == 0:
                piece = turned[:EDGE] if right_by < 0 else turned[LANES - EDGE :]
            else:
                piece = own[:EDGE] if down_by < 0 else own[down - EDGE :]
            to_row, to_col = at_row + down_by, at_col + right_by
            there = (to_row >= 0) & (to_row < n_rows) & (to_col >= 0) & (to_col < n_cols)
            slot = jnp.where(there, to_col * n_rows + to_row, me)
            chunk_ref[pl.ds(slot * PIECE, EDGE), 0, :] = piece * jnp.where(there, 1.0, 0.0)
    line = sum_line((dot_rp, dot_pq))
    for at in range(EDGE, chunk_ref.shape[0], PIECE):
        chunk_ref[at] = line


def first(taps, fields, got_a, got_b, coarse, dot):
    field = fields[0].shape
    tiles, height = field[0] - 1, field[1] - 4 * EDGE
    down = height // COARSE
    window = down + 2 * EDGE
    count = lax.axis_size("cols") * lax.axis_size("rows")
    shapes = [field] * 9 + [
        (6, window, 2 * LANES),
        (down, LANES),
        (count * PIECE, 1, LANES),
    ]
    return pl.pallas_call(
        functools.partial(first_kernel, tiles, down),
        in_specs=[SMEM] + [VMEM] * 11,
        out_specs=[VMEM] * len(shapes),
        out_shape=floats(*shapes),
        input_output_aliases={index + 1: index for index in range(7)},
        scratch_shapes=[
            pltpu.VMEM(field, jnp.float32),
            pltpu.VMEM((tiles + 1, window, LANES), jnp.float32),
            pltpu.VMEM((2, 2, window + 2 * EDGE, LANES), jnp.float32),
        ],
        compiler_params=params(),
        name="first_direction",
    )(taps, *fields, got_b, got_a, coarse, dot)[2:]


def second_kernel(
    tiles,
    down,
    taps,
    got_ref,
    own_ref,
    table_ref,
    res_ref,
    q_ref,
    east_ref,
    south_ref,
    inv_ref,
    w_ref,
    v_ref,
    out_ref,
    known_ref,
    image,
    spread,
    work,
):
    height = down * COARSE
    has_n, has_s, has_e, has_w = has_sides()
    at_col, at_row, n_cols, n_rows = place()
    me = at_col * n_rows + at_row

    def got(down_by, right_by):
        to_row, to_col = at_row + down_by, at_col + right_by
        there = (to_row >= 0) & (to_row < n_rows) & (to_col >= 0) & (to_col < n_cols)
        slot = jnp.where(there, to_col * n_rows + to_row, me)
        return got_ref[pl.ds(slot * PIECE, EDGE), 0, :]

    low = iota((EDGE, LANES), 1) < HALF
    gap = jnp.zeros((LANES - 2 * EDGE, LANES), jnp.float32)
    beside = jnp.transpose(jnp.concatenate([got(0, 1), gap, got(0, -1)], axis=0))[:down]
    source = jnp.concatenate(
        [
            jnp.concatenate([got(-1, 0), jnp.where(low, got(-1, 1), got(-1, -1))], axis=1),
            jnp.concatenate([own_ref[...], beside], axis=1),
            jnp.concatenate([got(1, 0), jnp.where(low, got(1, 1), got(1, -1))], axis=1),
        ],
        axis=0,
    )
    clear_work(work)
    rp, pq = line_totals(
        [got_ref[at] for at in range(EDGE, got_ref.shape[0], PIECE)], 2
    )
    step = rp / pq
    for index, value in enumerate((step, rp)):
        known_ref[index] = jnp.broadcast_to(value, (EDGE, LANES))
    source = table_ref[5] - jnp.broadcast_to(step, source.shape) * source
    spread_cells(jacobi(source, table_ref, work), spread)
    step = jnp.broadcast_to(step, (STRIP, LANES))
    clear_pads(w_ref, image)
    sides = side_lanes(has_e, has_w)
    taps = read_taps(taps)

    def begin_w(at, start, total):
        right, field, inverse = load(res_ref, at), load(q_ref, at), load(inv_ref, at)
        cells = cells_at(spread, at)
        span = range(tiles + 1)
        residual = [right[t] - step * field[t] for t in span]
        strip = [residual[t] * inverse[t] + cells[t] for t in span]
        first_row = jnp.maximum(start, 2 * EDGE)
        flags = [
            jnp.where((row >= first_row) & (row < 2 * EDGE + height), 1.0, 0.0)
            for row in [at + by for by in range(0, STRIP, EDGE)]
        ]
        return [(w_ref, strip)], total + product_sum(residual, strip, tiles, flags)

    def blur(at, _, carry):
        strip = conv(w_ref, at, taps, False)
        strip[tiles] = strip[tiles] * sides
        return [(image, strip)], carry

    def finish(at, _, total):
        here, product = operate(w_ref, image, east_ref, south_ref, at, taps)
        return [(v_ref, product[:tiles])], total + product_sum(here, product, tiles)

    nothing = jnp.zeros((EDGE, LANES), jnp.float32)
    span = (EDGE, 3 * EDGE + height)
    dot_rz = sweep(6, *span, begin_w, nothing)
    sweep(3, *span, blur, 0)
    mask_rows(image, has_n, has_s)
    dot_zz = sweep(4, 2 * EDGE, 2 * EDGE + height, finish, nothing)
    line = sum_line((dot_rz, dot_zz))
    for index in range(out_ref.shape[0]):
        out_ref[index] = line


def second(taps, got, own, table, r, q, east, south, inv):
    tiles, height = q.shape[0] - 1, q.shape[1] - 4 * EDGE
    down = height // COARSE
    window = down + 2 * EDGE
    count = lax.axis_size("cols") * lax.axis_size("rows")
    return pl.pallas_call(
        functools.partial(second_kernel, tiles, down),
        in_specs=[SMEM] + [VMEM] * 8,
        out_specs=[VMEM] * 4,
        out_shape=floats(q.shape, q.shape, (count, 1, LANES), (2, EDGE, LANES)),
        scratch_shapes=[
            pltpu.VMEM(q.shape, jnp.float32),
            pltpu.VMEM((tiles + 1, window, LANES), jnp.float32),
            pltpu.VMEM((2, 2, window + 2 * EDGE, LANES), jnp.float32),
        ],
        compiler_params=params(),
        name="second_direction",
    )(taps, got, own, table, r, q, east, south, inv)


def combine_kernel(
    tiles, height, sums_ref, known_ref, p_ref, w_ref, r_ref, q_ref, v_ref, sol_out, res_out, sol, res, sem
):
    rz, zz = line_totals([sums_ref[index] for index in range(sums_ref.shape[0])], 2)
    step, rp = [known_ref[index, :1, :] for index in range(2)]
    ratio = rz / rp
    step_next = rz / (zz - ratio * (rz / step))
    on_w = jnp.broadcast_to(step_next, (CHUNK, LANES))
    on_p = jnp.broadcast_to(step + step_next * ratio, (CHUNK, LANES))

    def copies(index):
        rows = pl.ds(pl.multiple_of(index * CHUNK, CHUNK), CHUNK)
        return (
            pltpu.make_async_copy(sol.at[rows, :], sol_out.at[rows, :], sem.at[0, index]),
            pltpu.make_async_copy(res.at[rows, :], res_out.at[rows, :], sem.at[1, index]),
        )

    def work(index, _):
        at = pl.multiple_of(index * CHUNK, CHUNK)
        p, w, r, q, v = [
            load(ref, at + 2 * EDGE, CHUNK) for ref in (p_ref, w_ref, r_ref, q_ref, v_ref)
        ]
        one = [on_p * p[t] + on_w * w[t] for t in range(tiles)]
        two = [r[t] - on_p * q[t] - on_w * v[t] for t in range(tiles)]
        for t in range(tiles):
            sol[pl.ds(at, CHUNK), t * LANES : (t + 1) * LANES] = one[t]
            res[pl.ds(at, CHUNK), t * LANES : (t + 1) * LANES] = two[t]
        for copy in copies(index):
            copy.start()
        return 0

    def settle(index, _):
        for copy in copies(index):
            copy.wait()
        return 0

    lax.fori_loop(0, height // CHUNK, work, 0)
    lax.fori_loop(0, height // CHUNK, settle, 0)


def combine(sums, known, p, w, r, q, v):
    tiles, height = q.shape[0] - 1, q.shape[1] - 4 * EDGE
    shape = (height, tiles * LANES)
    return pl.pallas_call(
        functools.partial(combine_kernel, tiles, height),
        in_specs=[VMEM] * 7,
        out_specs=[HBM] * 2,
        out_shape=floats(shape, shape),
        scratch_shapes=[
            pltpu.VMEM(shape, jnp.float32),
            pltpu.VMEM(shape, jnp.float32),
            pltpu.SemaphoreType.DMA((2, height // CHUNK)),
        ],
        compiler_params=params(),
        name="combine",
    )(sums, known, p, w, r, q, v)


def exchange(send_a, send_b, axis):
    count = lax.axis_size(axis)

    def pairs(begin):
        return [
            pair for i in range(begin, count - 1, 2) for pair in ((i, i + 1), (i + 1, i))
        ]

    got_b = lax.ppermute(send_b, axis, pairs(1))
    got_a = lax.ppermute(send_a, axis, pairs(0))
    return got_a, got_b


def body(observed, class_map, class_weights, blur_kernel):
    arguments = (observed, class_map, class_weights, blur_kernel)
    send_a, send_b = edge(*arguments)
    got_a, got_b = exchange(send_a, send_b, "cols")
    obs, cond, coarse = pack(*arguments, send_a)
    obs, cond, coarse, send_a, send_b = middle(got_a, got_b, coarse, obs, cond)
    got_a, got_b = exchange(send_a, send_b, "rows")
    r, east, south, inv, u, dot = inner(blur_kernel, obs, cond)
    fields = (obs, cond, r, east, south, inv, u)
    r, east, south, inv, _, p, q, table, own, chunk = first(
        blur_kernel, fields, got_a, got_b, coarse, dot
    )
    got = lax.all_to_all(chunk, AXES, 0, 0, tiled=True)
    w, v, line, known = second(blur_kernel, got, own, table, r, q, east, south, inv)
    sums = lax.all_to_all(line, AXES[::-1], 0, 0, tiled=True)
    return tuple(combine(sums, known, p, w, r, q, v))


def solution(mesh):
    return jax.shard_map(
        body,
        mesh=mesh,
        in_specs=(P("rows", "cols"), P("rows", "cols"), P(), P()),
        out_specs=(P("rows", "cols"), P("rows", "cols")),
        check_vma=False,
    )
```

```python
import functools

import jax
import jax.numpy as jnp
from jax import lax
from jax.experimental import pallas as pl
from jax.experimental.pallas import tpu as pltpu
from jax.sharding import PartitionSpec as P

COARSE = 8
SWEEPS = 8
CLASSES = 4
OMEGA = 0.8

LANES = 128
HALF = LANES // 2
EDGE = 8
STRIP = 2 * EDGE
REACH = 5
PIECE = EDGE + 1
CHUNK = 64
AXES = ("cols", "rows")
LIMIT = 40 * 1024 * 1024


VMEM = pl.BlockSpec(memory_space=pltpu.VMEM)
SMEM = pl.BlockSpec(memory_space=pltpu.SMEM)
HBM = pl.BlockSpec(memory_space=pltpu.HBM)


def params():
    return pltpu.CompilerParams(vmem_limit_bytes=LIMIT)


def in_hbm(array):
    return pltpu.with_memory_space_constraint(array, pltpu.HBM)


def floats(*shapes):
    return [jax.ShapeDtypeStruct(shape, jnp.float32) for shape in shapes]


def place():
    at_col, at_row = lax.axis_index("cols"), lax.axis_index("rows")
    n_cols, n_rows = lax.axis_size("cols"), lax.axis_size("rows")
    return at_col, at_row, n_cols, n_rows


def has_sides():
    at_col, at_row, n_cols, n_rows = place()
    flag = lambda test: jnp.where(test, 1.0, 0.0).astype(jnp.float32)
    return (
        flag(at_row > 0),
        flag(at_row < n_rows - 1),
        flag(at_col < n_cols - 1),
        flag(at_col > 0),
    )


def iota(shape, dim):
    return lax.broadcasted_iota(jnp.int32, shape, dim)


def cell_of(pixel, tiles):
    turn = (tiles + 1) * LANES
    return jnp.where(pixel < turn - HALF, pixel >> 3, ((pixel - turn) >> 3) & (2 * LANES - 1))


def gather_matrix(tiles):
    shape = ((tiles + 1) * LANES, 2 * LANES)
    hit = cell_of(iota(shape, 0), tiles) == iota(shape, 1)
    return jnp.where(hit, 1.0, 0.0).astype(jnp.bfloat16)


def split_dot(field, matrix):
    rows = field.shape[0]
    parts, rest = [], field
    for _ in range(3):
        parts.append(rest.astype(jnp.bfloat16))
        rest = rest - parts[-1].astype(jnp.float32)
    product = jnp.dot(
        jnp.concatenate(parts, axis=0), matrix, preferred_element_type=jnp.float32
    )
    return product[:rows] + (product[rows : 2 * rows] + product[2 * rows :])


def roll(field, by, axis):
    return pltpu.roll(field, by % field.shape[axis], axis)


def load(ref, at, rows=STRIP):
    return [ref[t, pl.ds(at, rows), :] for t in range(ref.shape[0])]


def store(ref, at, strip):
    for t, part in enumerate(strip):
        ref[t, pl.ds(at, part.shape[0]), :] = part


def wide(ref, at, rows):
    return jnp.concatenate(load(ref, at, rows), axis=1)


def read_taps(taps):
    return [[taps[a, b] for b in range(3)] for a in range(3)]


def tap_total(taps, power):
    return sum(tap * tap if power == 2 else tap for line in taps for tap in line)


def from_west(strip):
    lane = iota(strip[0].shape, 1)
    turned = [roll(part, 1, 1) for part in strip]
    return [jnp.where(lane == 0, turned[t - 1], turned[t]) for t in range(len(strip))]


def from_east(strip):
    lane = iota(strip[0].shape, 1)
    turned = [roll(part, -1, 1) for part in strip]
    count = len(strip)
    return [
        jnp.where(lane == LANES - 1, turned[(t + 1) % count], turned[t]) for t in range(count)
    ]


def tap_sums(ref, at, taps, flip):
    if flip:
        taps = [line[::-1] for line in taps[::-1]]
    above, here, below = load(ref, at - 1), load(ref, at), load(ref, at + 1)
    sums = [[], [], []]
    for t in range(len(here)):
        for b in range(3):
            sums[b].append(
                taps[0][b] * above[t] + taps[1][b] * here[t] + taps[2][b] * below[t]
            )
    return sums


def conv(ref, at, taps, flip):
    sums = tap_sums(ref, at, taps, flip)
    west, east = from_west(sums[0]), from_east(sums[2])
    return [sums[1][t] + west[t] + east[t] for t in range(len(west))]


def operate(ref, image, east_ref, south_ref, at, taps):
    above, here, below = load(ref, at - 1), load(ref, at), load(ref, at + 1)
    east, south, north = load(east_ref, at), load(south_ref, at), load(south_ref, at - 1)
    sums = tap_sums(image, at, taps, True)
    span = range(len(here))
    beside = from_east(here)
    flux = [east[t] * (here[t] - beside[t]) for t in span]
    from_left = from_west([sums[0][t] - flux[t] for t in span])
    from_right = from_east(sums[2])
    return here, [
        sums[1][t]
        + flux[t]
        + from_left[t]
        + from_right[t]
        + south[t] * (here[t] - below[t])
        - north[t] * (above[t] - here[t])
        for t in span
    ]


def begin(obs, cond, at, taps, sides):
    above, here, below = load(cond, at - 1), load(cond, at), load(cond, at + 1)
    span = range(len(here))
    right = from_east(here)
    east = [here[t] + right[t] for t in span]
    west = from_west(east)
    south = [here[t] + below[t] for t in span]
    squares = tap_total(taps, 2)
    diag = [squares + east[t] + west[t] + south[t] + (here[t] + above[t]) for t in span]
    inverse = [pl.reciprocal(part, approx=True) for part in diag]
    inverse = [inverse[t] * (2.0 - diag[t] * inverse[t]) for t in span]
    inverse[-1] = inverse[-1] * sides
    residual = conv(obs, at, taps, True)
    return east, south, inverse, residual, [residual[t] * inverse[t] for t in span]


def pick_lanes(field, lanes):
    return jnp.take_along_axis(field, lanes, axis=1, mode="promise_in_bounds")


def spread_cells(cells, spread):
    tiles = spread.shape[0] - 1
    lane = iota((cells.shape[0], LANES), 1)
    for t in range(tiles):
        spread[t] = pick_lanes(cells[:, :LANES], (lane >> 3) + t * (LANES // COARSE))
    turn = jnp.where(lane < HALF, 0, LANES - LANES // COARSE)
    spread[tiles] = pick_lanes(cells[:, LANES:], (lane >> 3) + turn)


def cells_at(spread, at):
    first = at // EDGE + EDGE - 2
    rows = [load(spread, first + index, 1) for index in range(STRIP // EDGE)]
    return [
        jnp.concatenate([jnp.broadcast_to(row, (EDGE, LANES)) for row in parts], axis=0)
        for parts in zip(*rows)
    ]


def cell_sums(ref, tiles, down, matrix):
    rows = []
    for t in range(tiles):
        picked = [
            ref[t, pl.ds(2 * EDGE + k, down, stride=COARSE), :] for k in range(COARSE)
        ]
        rows.append(sum(picked[1:], picked[0]))
    return split_dot(jnp.concatenate(rows, axis=1), matrix)


def cell_matrix(tiles):
    shape = (tiles * LANES, LANES)
    hit = iota(shape, 0) // COARSE == iota(shape, 1)
    return jnp.where(hit, 1.0, 0.0).astype(jnp.bfloat16)


def side_lanes(has_e, has_w):
    return jnp.where(iota((STRIP, LANES), 1) < HALF, has_e, has_w)


def mask_rows(ref, has_n, has_s):
    last = ref.shape[1] - 2 * EDGE
    for at, flag in ((EDGE, has_n), (last, has_s)):
        ref[:, at : at + EDGE, :] = ref[:, at : at + EDGE, :] * flag


def clear_pads(*refs):
    empty = jnp.zeros((refs[0].shape[0], EDGE, LANES), jnp.float32)
    for ref in refs:
        ref[:, :EDGE, :] = empty
        ref[:, ref.shape[1] - EDGE :, :] = empty


def product_sum_rows(one, two, count):
    total = one[0] * two[0]
    for t in range(1, count):
        total = total + one[t] * two[t]
    return total


def product_sum(one, two, count, flags=None):
    return fold(product_sum_rows(one, two, count), flags)


def fold(total, flags=None):
    parts = [total[at : at + EDGE] for at in range(0, total.shape[0], EDGE)]
    if flags is not None:
        parts = [part * flag for part, flag in zip(parts, flags)]
    return sum(parts[1:], parts[0])


def sweep(group, first, last, body, carry):
    width = group * STRIP
    steps = -(-(last - first) // width)

    def work(index, carry):
        start = first + index * width
        at = pl.multiple_of(jnp.minimum(start, last - width), EDGE)
        pending = []
        for by in range(0, width, STRIP):
            stores, carry = body(at + by, start, carry)
            pending += [(ref, at + by, strip) for ref, strip in stores]
        for ref, row, strip in pending:
            store(ref, row, strip)
        return carry

    return lax.fori_loop(0, steps, work, carry)


def sum_line(parts):
    line = jnp.zeros((1, LANES), jnp.float32)
    block = iota((1, LANES), 1) // (LANES // 4)
    for index, part in enumerate(parts):
        part = jnp.sum(part, axis=0, keepdims=True)
        part = part + roll(part, LANES // 2, 1)
        part = part + roll(part, LANES // 4, 1)
        line = jnp.where(block == index, part, line)
    return line


def line_totals(lines, count):
    while len(lines) > 1:
        lines = [sum(lines[at + 1 : at + 2], lines[at]) for at in range(0, len(lines), 2)]
    block = iota((1, LANES), 1) // (LANES // 4)
    return [
        jnp.sum(jnp.where(block == index, lines[0], 0.0), axis=1, keepdims=True)
        for index in range(count)
    ]


def jacobi(source, table, work):
    factor, east, west, south, north = [table[index] for index in range(5)]
    window = source.shape[0]
    source = factor * source
    iterate = source
    for sweep_index in range(SWEEPS - 1):
        place_ref = work.at[sweep_index % 2]
        for half in range(2):
            place_ref[half, EDGE : EDGE + window, :] = iterate[
                :, half * LANES : (half + 1) * LANES
            ]
        above, below = [
            jnp.concatenate(
                [place_ref[half, EDGE + by : EDGE + by + window, :] for half in range(2)], axis=1
            )
            for by in (-1, 1)
        ]
        across = east * roll(iterate, -1, 1) + west * roll(iterate, 1, 1)
        along = south * below + north * above
        iterate = ((1.0 - OMEGA) * iterate + source) + (across + along)
    return iterate


def clear_work(work):
    for buffer in range(2):
        clear_pads(work.at[buffer])


def in_pair_order(at, for_before, for_after):
    even = at % 2 == 0
    if callable(for_before):
        return (
            lambda *args: jnp.where(even, for_after(*args), for_before(*args)),
            lambda *args: jnp.where(even, for_before(*args), for_after(*args)),
        )
    return jnp.where(even, for_after, for_before), jnp.where(even, for_before, for_after)


def reader(tiles_here, refs, scratch, obs, cond, down):
    obs_in, class_in, weight_in, taps_in = refs
    classes, weights, taps, sums, obs_sem, class_sem, small_sem = scratch
    own = pl.ds(2 * EDGE, down * COARSE)
    small = [
        pltpu.make_async_copy(weight_in, weights, small_sem.at[0]),
        pltpu.make_async_copy(taps_in, taps, small_sem.at[1]),
    ]
    moves = []
    for slot, t in enumerate(tiles_here):
        lanes = pl.ds(t * LANES, LANES)
        moves.append(
            (
                pltpu.make_async_copy(class_in.at[:, lanes], classes.at[slot], class_sem.at[slot]),
                pltpu.make_async_copy(
                    obs_in.at[:, lanes], obs.at[slot, own, :], obs_sem.at[slot]
                ),
            )
        )
    for copy in small:
        copy.start()
    for pair in moves:
        for copy in pair:
            copy.start()
    sums[...] = jnp.zeros_like(sums)

    def settle(slot):
        if slot == 0:
            for copy in small:
                copy.wait()
        for copy in moves[slot]:
            copy.wait()
        values = [0.5 * weights[class_id] for class_id in range(CLASSES)]
        kind = classes[slot]
        cond[slot, own, :] = jnp.where(
            kind < 2,
            jnp.where(kind == 0, values[0], values[1]),
            jnp.where(kind == 2, values[2], values[3]),
        )
        for which, ref in enumerate((obs, cond)):
            picked = [
                ref[slot, pl.ds(2 * EDGE + k, down, stride=COARSE), :] for k in range(COARSE)
            ]
            cells = slice(2 * EDGE, 2 * EDGE + down)
            sums[3 * which, slot, cells, :] = sum(picked[1:], picked[0])
            sums[3 * which + 1, slot, cells, :] = picked[0]
            sums[3 * which + 2, slot, cells, :] = picked[-1]

    return settle


def reader_scratch(tiles, height, window, class_weights, taps):
    return [
        pltpu.VMEM((tiles, height, LANES), jnp.int32),
        pltpu.SMEM(class_weights.shape, jnp.float32),
        pltpu.SMEM(taps.shape, jnp.float32),
        pltpu.VMEM((6, tiles + 1, window + 2 * EDGE, LANES), jnp.float32),
        pltpu.SemaphoreType.DMA((tiles,)),
        pltpu.SemaphoreType.DMA((tiles,)),
        pltpu.SemaphoreType.DMA((2,)),
    ]


def coarse_parts(sums, taps, matrix):
    window = sums.shape[2] - 2 * EDGE
    whole = lambda index, by=0: wide(sums.at[index], EDGE + by, window)
    full = whole(0)
    by_tap = [full - whole(1) + whole(1, 1), full, full - whole(2) + whole(2, -1)]
    across = [sum(taps[a][b] * by_tap[a] for a in range(3)) for b in range(3)]
    source = across[1] + roll(across[0], -1, 1) + roll(across[2], 1, 1)
    full = whole(3)
    last = (iota(full.shape, 1) & (COARSE - 1)) == COARSE - 1
    east = jnp.where(last, full + roll(full, -1, 1), 0.0)
    south = whole(5) + whole(4, 1)
    cells = split_dot(jnp.concatenate([source, east, south], axis=0), matrix)
    source, east, south = cells[:window], cells[window : 2 * window], cells[2 * window :]
    around = east + roll(east, 1, 1) + south + roll(south, 1, 0)
    return [source, east, south, around]


def edge_kernel(tiles, down, *refs):
    arguments, (send_a, send_b), (obs, cond, message, *scratch) = refs[:4], refs[4:6], refs[6:]
    height = down * COARSE
    halves = height // LANES
    window = down + 2 * EDGE
    settle = reader((0, tiles - 1), arguments, scratch, obs, cond, down)
    matrix = gather_matrix(2)
    fine = [[], []]
    for slot, begin_row in ((0, 0), (1, LANES - REACH)):
        settle(slot)
        for ref in (obs, cond):
            turned = jnp.transpose(ref[slot, 2 * EDGE : 2 * EDGE + height, :])
            turned = turned[begin_row : begin_row + REACH]
            for half in range(halves):
                fine[slot].append(turned[:, half * LANES : (half + 1) * LANES])
    parts = coarse_parts(scratch[3], read_taps(scratch[2]), matrix)
    spare = jnp.zeros((2 * LANES - 4 * window, 2 * LANES), jnp.float32)
    stack = jnp.concatenate(parts + [spare], axis=0)
    left = jnp.transpose(stack[:, :LANES])
    right = jnp.transpose(stack[:, LANES:])
    past = 2 * LANES // COARSE
    split = lambda piece: [piece[:, half * LANES : (half + 1) * LANES] for half in range(2)]
    for slot, main, over in (
        (0, left[:EDGE], right[LANES - 1 :]),
        (1, left[past - EDGE : past], left[past : past + 1]),
    ):
        rows = split(main) + fine[slot] + split(over)
        filled = sum(piece.shape[0] for piece in rows)
        rows.append(jnp.zeros((message.shape[1] - filled, LANES), jnp.float32))
        message[slot] = jnp.concatenate(rows, axis=0)
    send_a[...], send_b[...] = in_pair_order(place()[0], message[0], message[1])


def edge(observed, class_map, class_weights, taps):
    height, breadth = observed.shape
    tiles, down = breadth // LANES, height // COARSE
    window = down + 2 * EDGE
    field = (3, height + 4 * EDGE, LANES)
    rows = 2 * EDGE + 2 * REACH * (height // LANES) + 2
    strip = (-(-rows // EDGE) * EDGE, LANES)
    return pl.pallas_call(
        functools.partial(edge_kernel, tiles, down),
        in_specs=[HBM] * 4,
        out_specs=[VMEM] * 2,
        out_shape=floats(strip, strip),
        scratch_shapes=[
            pltpu.VMEM(field, jnp.float32),
            pltpu.VMEM(field, jnp.float32),
            pltpu.VMEM((2,) + strip, jnp.float32),
        ]
        + reader_scratch(2, height, window, class_weights, taps),
        compiler_params=params(),
        name="pack_east_west",
    )(*[in_hbm(array) for array in (observed, class_map, class_weights, taps)])


def pack_kernel(tiles, down, *refs):
    arguments, (obs, cond, coarse_ref), scratch = refs[:4], refs[5:8], refs[8:]
    settle = reader(range(tiles), arguments, scratch, obs, cond, down)
    matrix = gather_matrix(tiles)
    for t in range(tiles):
        settle(t)
    for index, part in enumerate(coarse_parts(scratch[3], read_taps(scratch[2]), matrix)):
        coarse_ref[index] = part


def pack(observed, class_map, class_weights, taps, after):
    height, breadth = observed.shape
    tiles, down = breadth // LANES, height // COARSE
    window = down + 2 * EDGE
    field = (tiles + 1, height + 4 * EDGE, LANES)
    pixels = height * breadth
    return pl.pallas_call(
        functools.partial(pack_kernel, tiles, down),
        in_specs=[HBM] * 4 + [VMEM],
        out_specs=[VMEM] * 3,
        out_shape=floats(field, field, (4, window, 2 * LANES)),
        scratch_shapes=reader_scratch(tiles, height, window, class_weights, taps),
        compiler_params=params(),
        cost_estimate=pl.CostEstimate(
            flops=20 * pixels, bytes_accessed=16 * pixels, transcendentals=0
        ),
        name="pack_all",
    )(*[in_hbm(array) for array in (observed, class_map, class_weights, taps)], after)


def message_rows(tiles):
    rest = EDGE
    fine = rest + 2 * tiles
    sides = fine + tiles * EDGE
    return 0, rest, fine, sides, sides + EDGE


def merge_sides(parts):
    block = iota((EDGE, LANES), 1) // (2 * EDGE)
    merged = jnp.zeros((EDGE, LANES), jnp.float32)
    for index, part in enumerate(parts):
        merged = jnp.where(block == index, roll(part, (2 * index + 1) * EDGE, 1), merged)
    return merged


def split_sides(merged, count):
    lane = iota((EDGE, LANES), 1)
    outer = (lane < EDGE) | (lane >= LANES - EDGE)
    return [
        jnp.where(outer, roll(merged, -(2 * index + 1) * EDGE, 1), 0.0) for index in range(count)
    ]


def middle_kernel(
    tiles,
    down,
    got_b,
    got_a,
    coarse_in,
    obs_in,
    cond_in,
    obs,
    cond,
    coarse_ref,
    send_a,
    send_b,
    message,
):
    height = down * COARSE
    halves = height // LANES
    at_col, at_row, _, _ = place()
    from_e, from_w = in_pair_order(at_col, got_b[...], got_a[...])
    zeros = lambda rows: jnp.zeros((rows, LANES), jnp.float32)

    def turned(low, high):
        low = [low, zeros(EDGE - low.shape[0])] if low.shape[0] < EDGE else [low]
        high = [zeros(EDGE - high.shape[0]), high] if high.shape[0] < EDGE else [high]
        return jnp.transpose(jnp.concatenate([*low, zeros(LANES - 2 * EDGE), *high], axis=0))

    for which, field in enumerate((obs, cond)):
        for half in range(halves):
            at = 2 * EDGE + REACH * (which * halves + half)
            begin_row = 2 * EDGE + half * LANES
            field[tiles, begin_row : begin_row + LANES, :] = turned(
                from_e[at : at + REACH], from_w[at : at + REACH]
            )
    main = lambda strip, half: strip[half * EDGE : (half + 1) * EDGE]

    def over(strip, half):
        at = 2 * EDGE + 2 * REACH * halves + half
        return strip[at : at + 1]

    left = [turned(over(from_w, half), over(from_e, half)) for half in range(2)]
    right = [turned(main(from_e, half), main(from_w, half)) for half in range(2)]
    left = jnp.concatenate(left, axis=0)
    right = jnp.concatenate(right, axis=0)
    window = down + 2 * EDGE
    for index in range(4):
        rows = slice(index * window, (index + 1) * window)
        coarse_ref[index, :, :LANES] = coarse_in[index, :, :LANES] + left[rows]
        coarse_ref[index, :, LANES:] = coarse_in[index, :, LANES:] + right[rows]
    row = iota((EDGE, LANES), 0)
    over_at, rest_at, fine_at, sides_at, coarse_at = message_rows(tiles)
    for slot, begin_row, reach_row, first_row, over_row in (
        (0, 2 * EDGE, 2 * EDGE, EDGE, EDGE - 1),
        (1, EDGE + height, 2 * EDGE + height - REACH, window - 2 * EDGE, window - EDGE),
    ):
        for t in range(tiles):
            at = fine_at + t * EDGE
            message[slot, at : at + EDGE, :] = jnp.where(
                row < REACH,
                obs[t, reach_row : reach_row + EDGE, :],
                cond[t, reach_row - REACH : reach_row - REACH + EDGE, :],
            )
        for begin_tile in range(0, tiles, 4):
            rest = None
            for index in range(4):
                at = reach_row + EDGE - REACH - 2 * index
                piece = cond[begin_tile + index, at : at + EDGE, :]
                rest = piece if rest is None else jnp.where(row < 2 * index, rest, piece)
            at = rest_at + begin_tile * 2
            message[slot, at : at + EDGE, :] = rest
        rows = slice(first_row, first_row + EDGE)
        for index in range(4):
            at = coarse_at + index * EDGE
            message[slot, at : at + EDGE, :] = coarse_ref[index, rows, :LANES]
        beyond = [coarse_ref[index, rows, LANES:] for index in range(4)]
        beyond += [field[tiles, begin_row : begin_row + EDGE, :] for field in (obs, cond)]
        message[slot, sides_at : sides_at + EDGE, :] = merge_sides(beyond)
        message[slot, over_at : over_at + EDGE, :] = jnp.concatenate(
            [
                coarse_ref[index, over_row : over_row + 1, half * LANES : (half + 1) * LANES]
                for index in range(4)
                for half in range(2)
            ],
            axis=0,
        )
    send_a[...], send_b[...] = in_pair_order(at_row, message[0], message[1])


def middle(got_a, got_b, coarse, obs, cond):
    tiles, height = obs.shape[0] - 1, obs.shape[1] - 4 * EDGE
    down = height // COARSE
    long = (message_rows(tiles)[-1] + 4 * EDGE, LANES)
    return pl.pallas_call(
        functools.partial(middle_kernel, tiles, down),
        in_specs=[VMEM] * 5,
        out_specs=[VMEM] * 5,
        out_shape=floats(obs.shape, cond.shape, coarse.shape, long, long),
        input_output_aliases={3: 0, 4: 1},
        scratch_shapes=[pltpu.VMEM((2,) + long, jnp.float32)],
        compiler_params=params(),
        name="pack_north_south",
    )(got_b, got_a, coarse, obs, cond)


def inner_kernel(taps, obs, cond, res_ref, east_ref, south_ref, inv_ref, u_ref, dot_ref, cells_ref):
    _, _, has_e, has_w = has_sides()
    clear_pads(east_ref, south_ref)
    taps = read_taps(taps)
    sides = side_lanes(has_e, has_w)

    tiles = obs.shape[0] - 1
    cells_ref[...] = cell_matrix(tiles)

    def work(at, start, total):
        fields = begin(obs, cond, at, taps, sides)
        flags = [jnp.where(at + by >= start, 1.0, 0.0) for by in range(0, STRIP, EDGE)]
        total = total + product_sum(fields[3], fields[4], tiles, flags)
        return list(zip((east_ref, south_ref, inv_ref, res_ref, u_ref), fields)), total

    nothing = jnp.zeros((EDGE, LANES), jnp.float32)
    dot_ref[...] = sweep(5, 3 * EDGE, obs.shape[1] - 3 * EDGE, work, nothing)


def inner(taps, obs, cond):
    field = obs.shape
    pixels = field[0] * field[1] * field[2]
    return pl.pallas_call(
        inner_kernel,
        in_specs=[SMEM] + [VMEM] * 2,
        out_specs=[VMEM] * 7,
        out_shape=floats(field, field, field, field, field, (EDGE, LANES))
        + [jax.ShapeDtypeStruct(((field[0] - 1) * LANES, LANES), jnp.bfloat16)],
        compiler_params=params(),
        cost_estimate=pl.CostEstimate(
            flops=45 * pixels, bytes_accessed=24 * pixels, transcendentals=0
        ),
        name="inner_strips",
    )(taps, obs, cond)


def first_kernel(
    tiles,
    down,
    taps,
    obs_in,
    cond_in,
    res_in,
    east_in,
    south_in,
    inv_in,
    u_in,
    got_b,
    got_a,
    coarse_in,
    dot_in,
    cells_in,
    obs,
    cond,
    res_ref,
    east_ref,
    south_ref,
    inv_ref,
    u_ref,
    p_ref,
    q_ref,
    table_ref,
    own_ref,
    chunk_ref,
    image,
    spread,
    work,
):
    height = down * COARSE
    window = down + 2 * EDGE
    at_col, at_row, n_cols, n_rows = place()
    has_n, has_s, has_e, has_w = has_sides()
    clear_pads(obs, cond, p_ref, image)
    clear_work(work)
    from_s, from_n = in_pair_order(
        at_row,
        lambda at, rows=EDGE: got_b[at : at + rows, :],
        lambda at, rows=EDGE: got_a[at : at + rows, :],
    )
    over_at, rest_at, fine_at, sides_at, coarse_at = message_rows(tiles)
    row = iota((EDGE, LANES), 0)
    short = EDGE - REACH
    for t in range(tiles):
        at = fine_at + t * EDGE
        rest = rest_at + 2 * t
        begin_row = 2 * EDGE + height
        obs[t, EDGE : 2 * EDGE, :] = jnp.where(row >= short, from_n(at - short), 0.0)
        obs[t, begin_row : begin_row + EDGE, :] = jnp.where(row < REACH, from_s(at), 0.0)
        near, far = from_n(at + REACH - short), from_n(rest - 2 * short)
        near = jnp.where(row < short, 0.0, near)
        cond[t, EDGE : 2 * EDGE, :] = jnp.where(row < 2 * short, near, far)
        near, far = from_s(at + REACH), from_s(rest - short)
        far = jnp.where(row < REACH, far, 0.0)
        cond[t, begin_row : begin_row + EDGE, :] = jnp.where(row < short, near, far)
    sides_n, sides_s = [split_sides(strip(sides_at), 6) for strip in (from_n, from_s)]
    for which, field in enumerate((obs, cond)):
        field[tiles, EDGE : 2 * EDGE, :] = sides_n[4 + which]
        field[tiles, 2 * EDGE + height : 3 * EDGE + height, :] = sides_s[4 + which]

    edge_row = iota((EDGE, 2 * LANES), 0)

    def joined(index):
        def over(strip, row):
            line = [
                jnp.broadcast_to(
                    strip(over_at + 2 * index + half, 1), (EDGE, LANES)
                )
                for half in range(2)
            ]
            return jnp.where(edge_row == row, jnp.concatenate(line, axis=1), 0.0)

        def rows(strip, beyond):
            return jnp.concatenate([strip(coarse_at + index * EDGE), beyond[index]], axis=1)

        parts = [coarse_in[index, at : at + EDGE, :] for at in range(0, window, EDGE)]
        parts[0] = parts[0] + rows(from_n, sides_n)
        parts[1] = parts[1] + over(from_n, 0)
        parts[-2] = parts[-2] + over(from_s, EDGE - 1)
        parts[-1] = parts[-1] + rows(from_s, sides_s)
        return jnp.concatenate(parts, axis=0)

    source, east, south, around = [joined(index) for index in range(4)]
    row = iota(source.shape, 0)
    lane = iota(source.shape, 1)
    inside = jnp.where(row < EDGE, has_n, jnp.where(row < window - EDGE, 1.0, has_s))
    inside = inside * jnp.where(
        lane < LANES, 1.0, jnp.where(lane < LANES + HALF, has_e, has_w)
    )
    taps = read_taps(taps)
    taps_sum = tap_total(taps, 1)
    factor = inside * OMEGA / (COARSE * COARSE * taps_sum * taps_sum + around)
    weights = (east, roll(east, 1, 1), south, roll(south, 1, 0))
    table = [factor] + [factor * weight for weight in weights]
    for index, part in enumerate([*table, source]):
        table_ref[index] = part
    sides = side_lanes(has_e, has_w)
    half = iota((STRIP, LANES), 0) // EDGE
    pending = []
    total = dot_in[...]
    for index, known in ((0, has_n), (1, has_s)):
        at = EDGE + index * height
        fields = begin(obs, cond, at, taps, sides)
        own = jnp.where(half == index, 0.0, 1.0)
        total = total + fold(own * product_sum_rows(fields[3], fields[4], tiles))
        flag = jnp.where(half == index, known, 1.0)
        inverse, start = [[part * flag for part in fields[index]] for index in (2, 4)]
        fields = (*fields[:2], inverse, fields[3], start)
        pending += [
            (ref, at, strip)
            for ref, strip in zip((east_ref, south_ref, inv_ref, res_ref, u_ref), fields)
        ]
    cells = jacobi(source, table, work)
    spread_cells(cells, spread)
    inner_cells = slice(EDGE, EDGE + down)
    total = total + fold(source[inner_cells, :LANES] * cells[inner_cells, :LANES])
    dot_rp = total
    for ref, at, strip in pending:
        store(ref, at, strip)

    def flags(at, start):
        rows = [at + by for by in range(0, STRIP, EDGE)]
        first_row = jnp.maximum(start, 2 * EDGE)
        return [
            jnp.where((row >= first_row) & (row < 2 * EDGE + height), 1.0, 0.0) for row in rows
        ]

    def begin_p(at, _, carry):
        start, cells = load(u_ref, at), cells_at(spread, at)
        return [(p_ref, [start[t] + cells[t] for t in range(tiles + 1)])], carry

    def blur(at, _, carry):
        strip = conv(p_ref, at, taps, False)
        strip[tiles] = strip[tiles] * sides
        return [(image, strip)], carry

    def finish(at, start, total):
        here, product = operate(p_ref, image, east_ref, south_ref, at, taps)
        return [(q_ref, product)], total + product_sum(here, product, tiles, flags(at, start))

    nothing = jnp.zeros((EDGE, LANES), jnp.float32)
    span = (EDGE, 3 * EDGE + height)
    sweep(3, *span, begin_p, 0)
    sweep(3, *span, blur, 0)
    mask_rows(image, has_n, has_s)
    dot_pq = sweep(3, *span, finish, nothing)

    own = cell_sums(q_ref, tiles, down, cells_in[...])
    own_ref[...] = own
    spare = jnp.zeros((LANES - down, LANES), jnp.float32)
    turned = jnp.transpose(jnp.concatenate([own, spare], axis=0))
    me = at_col * n_rows + at_row
    chunk_ref[pl.ds(me * PIECE, EDGE), 0, :] = jnp.zeros((EDGE, LANES), jnp.float32)
    for down_by in (-1, 0, 1):
        for right_by in (-1, 0, 1):
            if down_by == 0 and right_by == 0:
                continue
            if down_by == 0:
                piece = turned[:EDGE] if right_by < 0 else turned[LANES - EDGE :]
            else:
                piece = own[:EDGE] if down_by < 0 else own[down - EDGE :]
            to_row, to_col = at_row + down_by, at_col + right_by
            there = (to_row >= 0) & (to_row < n_rows) & (to_col >= 0) & (to_col < n_cols)
            slot = jnp.where(there, to_col * n_rows + to_row, me)
            chunk_ref[pl.ds(slot * PIECE, EDGE), 0, :] = piece * jnp.where(there, 1.0, 0.0)
    line = sum_line((dot_rp, dot_pq))
    for at in range(EDGE, chunk_ref.shape[0], PIECE):
        chunk_ref[at] = line


def first(taps, fields, got_a, got_b, coarse, dot, matrix):
    field = fields[0].shape
    tiles, height = field[0] - 1, field[1] - 4 * EDGE
    down = height // COARSE
    window = down + 2 * EDGE
    count = lax.axis_size("cols") * lax.axis_size("rows")
    shapes = [field] * 9 + [
        (6, window, 2 * LANES),
        (down, LANES),
        (count * PIECE, 1, LANES),
    ]
    return pl.pallas_call(
        functools.partial(first_kernel, tiles, down),
        in_specs=[SMEM] + [VMEM] * 12,
        out_specs=[VMEM] * len(shapes),
        out_shape=floats(*shapes),
        input_output_aliases={index + 1: index for index in range(7)},
        scratch_shapes=[
            pltpu.VMEM(field, jnp.float32),
            pltpu.VMEM((tiles + 1, window, LANES), jnp.float32),
            pltpu.VMEM((2, 2, window + 2 * EDGE, LANES), jnp.float32),
        ],
        compiler_params=params(),
        name="first_direction",
    )(taps, *fields, got_b, got_a, coarse, dot, matrix)[2:]


def second_kernel(
    tiles,
    down,
    taps,
    got_ref,
    own_ref,
    table_ref,
    res_ref,
    q_ref,
    east_ref,
    south_ref,
    inv_ref,
    w_ref,
    v_ref,
    out_ref,
    known_ref,
    image,
    spread,
    work,
):
    height = down * COARSE
    has_n, has_s, has_e, has_w = has_sides()
    at_col, at_row, n_cols, n_rows = place()
    me = at_col * n_rows + at_row

    def got(down_by, right_by):
        to_row, to_col = at_row + down_by, at_col + right_by
        there = (to_row >= 0) & (to_row < n_rows) & (to_col >= 0) & (to_col < n_cols)
        slot = jnp.where(there, to_col * n_rows + to_row, me)
        return got_ref[pl.ds(slot * PIECE, EDGE), 0, :]

    low = iota((EDGE, LANES), 1) < HALF
    gap = jnp.zeros((LANES - 2 * EDGE, LANES), jnp.float32)
    beside = jnp.transpose(jnp.concatenate([got(0, 1), gap, got(0, -1)], axis=0))[:down]
    source = jnp.concatenate(
        [
            jnp.concatenate([got(-1, 0), jnp.where(low, got(-1, 1), got(-1, -1))], axis=1),
            jnp.concatenate([own_ref[...], beside], axis=1),
            jnp.concatenate([got(1, 0), jnp.where(low, got(1, 1), got(1, -1))], axis=1),
        ],
        axis=0,
    )
    clear_work(work)
    rp, pq = line_totals(
        [got_ref[at] for at in range(EDGE, got_ref.shape[0], PIECE)], 2
    )
    step = rp / pq
    for index, value in enumerate((step, rp)):
        known_ref[index] = jnp.broadcast_to(value, (EDGE, LANES))
    source = table_ref[5] - jnp.broadcast_to(step, source.shape) * source
    spread_cells(jacobi(source, table_ref, work), spread)
    step = jnp.broadcast_to(step, (STRIP, LANES))
    clear_pads(w_ref, image)
    sides = side_lanes(has_e, has_w)
    taps = read_taps(taps)

    def begin_w(at, start, total):
        right, field, inverse = load(res_ref, at), load(q_ref, at), load(inv_ref, at)
        cells = cells_at(spread, at)
        span = range(tiles + 1)
        residual = [right[t] - step * field[t] for t in span]
        strip = [residual[t] * inverse[t] + cells[t] for t in span]
        first_row = jnp.maximum(start, 2 * EDGE)
        flags = [
            jnp.where((row >= first_row) & (row < 2 * EDGE + height), 1.0, 0.0)
            for row in [at + by for by in range(0, STRIP, EDGE)]
        ]
        return [(w_ref, strip)], total + product_sum(residual, strip, tiles, flags)

    def blur(at, _, carry):
        strip = conv(w_ref, at, taps, False)
        strip[tiles] = strip[tiles] * sides
        return [(image, strip)], carry

    def finish(at, _, total):
        here, product = operate(w_ref, image, east_ref, south_ref, at, taps)
        return [(v_ref, product[:tiles])], total + product_sum(here, product, tiles)

    nothing = jnp.zeros((EDGE, LANES), jnp.float32)
    span = (EDGE, 3 * EDGE + height)
    dot_rz = sweep(3, *span, begin_w, nothing)
    sweep(3, *span, blur, 0)
    mask_rows(image, has_n, has_s)
    dot_zz = sweep(4, 2 * EDGE, 2 * EDGE + height, finish, nothing)
    line = sum_line((dot_rz, dot_zz))
    for index in range(out_ref.shape[0]):
        out_ref[index] = line


def second(taps, got, own, table, r, q, east, south, inv):
    tiles, height = q.shape[0] - 1, q.shape[1] - 4 * EDGE
    down = height // COARSE
    window = down + 2 * EDGE
    count = lax.axis_size("cols") * lax.axis_size("rows")
    return pl.pallas_call(
        functools.partial(second_kernel, tiles, down),
        in_specs=[SMEM] + [VMEM] * 8,
        out_specs=[VMEM] * 4,
        out_shape=floats(q.shape, q.shape, (count, 1, LANES), (2, EDGE, LANES)),
        scratch_shapes=[
            pltpu.VMEM(q.shape, jnp.float32),
            pltpu.VMEM((tiles + 1, window, LANES), jnp.float32),
            pltpu.VMEM((2, 2, window + 2 * EDGE, LANES), jnp.float32),
        ],
        compiler_params=params(),
        name="second_direction",
    )(taps, got, own, table, r, q, east, south, inv)


def combine_kernel(
    tiles, height, sums_ref, known_ref, p_ref, w_ref, r_ref, q_ref, v_ref, sol_out, res_out, sol, res, sem
):
    rz, zz = line_totals([sums_ref[index] for index in range(sums_ref.shape[0])], 2)
    step, rp = [known_ref[index, :1, :] for index in range(2)]
    ratio = rz / rp
    step_next = rz / (zz - ratio * (rz / step))
    on_w = jnp.broadcast_to(step_next, (CHUNK, LANES))
    on_p = jnp.broadcast_to(step + step_next * ratio, (CHUNK, LANES))

    def copies(index):
        rows = pl.ds(pl.multiple_of(index * CHUNK, CHUNK), CHUNK)
        return (
            pltpu.make_async_copy(sol.at[rows, :], sol_out.at[rows, :], sem.at[0, index]),
            pltpu.make_async_copy(res.at[rows, :], res_out.at[rows, :], sem.at[1, index]),
        )

    def work(index, _):
        at = pl.multiple_of(index * CHUNK, CHUNK)
        p, w, r, q, v = [
            load(ref, at + 2 * EDGE, CHUNK) for ref in (p_ref, w_ref, r_ref, q_ref, v_ref)
        ]
        one = [on_p * p[t] + on_w * w[t] for t in range(tiles)]
        two = [r[t] - on_p * q[t] - on_w * v[t] for t in range(tiles)]
        for t in range(tiles):
            sol[pl.ds(at, CHUNK), t * LANES : (t + 1) * LANES] = one[t]
            res[pl.ds(at, CHUNK), t * LANES : (t + 1) * LANES] = two[t]
        for copy in copies(index):
            copy.start()
        return 0

    def settle(index, _):
        for copy in copies(index):
            copy.wait()
        return 0

    lax.fori_loop(0, height // CHUNK, work, 0)
    lax.fori_loop(0, height // CHUNK, settle, 0)


def combine(sums, known, p, w, r, q, v):
    tiles, height = q.shape[0] - 1, q.shape[1] - 4 * EDGE
    shape = (height, tiles * LANES)
    return pl.pallas_call(
        functools.partial(combine_kernel, tiles, height),
        in_specs=[VMEM] * 7,
        out_specs=[HBM] * 2,
        out_shape=floats(shape, shape),
        scratch_shapes=[
            pltpu.VMEM(shape, jnp.float32),
            pltpu.VMEM(shape, jnp.float32),
            pltpu.SemaphoreType.DMA((2, height // CHUNK)),
        ],
        compiler_params=params(),
        name="combine",
    )(sums, known, p, w, r, q, v)


def exchange(send_a, send_b, axis):
    count = lax.axis_size(axis)

    def pairs(begin):
        return [
            pair for i in range(begin, count - 1, 2) for pair in ((i, i + 1), (i + 1, i))
        ]

    got_b = lax.ppermute(send_b, axis, pairs(1))
    got_a = lax.ppermute(send_a, axis, pairs(0))
    return got_a, got_b


def body(observed, class_map, class_weights, blur_kernel):
    arguments = (observed, class_map, class_weights, blur_kernel)
    send_a, send_b = edge(*arguments)
    got_a, got_b = exchange(send_a, send_b, "cols")
    obs, cond, coarse = pack(*arguments, send_a)
    obs, cond, coarse, send_a, send_b = middle(got_a, got_b, coarse, obs, cond)
    got_a, got_b = exchange(send_a, send_b, "rows")
    r, east, south, inv, u, dot, matrix = inner(blur_kernel, obs, cond)
    fields = (obs, cond, r, east, south, inv, u)
    r, east, south, inv, _, p, q, table, own, chunk = first(
        blur_kernel, fields, got_a, got_b, coarse, dot, matrix
    )
    got = lax.all_to_all(chunk, AXES, 0, 0, tiled=True)
    w, v, line, known = second(blur_kernel, got, own, table, r, q, east, south, inv)
    sums = lax.all_to_all(line, AXES[::-1], 0, 0, tiled=True)
    return tuple(combine(sums, known, p, w, r, q, v))


def solution(mesh):
    return jax.shard_map(
        body,
        mesh=mesh,
        in_specs=(P("rows", "cols"), P("rows", "cols"), P(), P()),
        out_specs=(P("rows", "cols"), P("rows", "cols")),
        check_vma=False,
    )
```

```python
import functools

import jax
import jax.numpy as jnp
from jax import lax
from jax.experimental import pallas as pl
from jax.experimental.pallas import tpu as pltpu
from jax.sharding import PartitionSpec as P

COARSE = 8
SWEEPS = 8
CLASSES = 4
OMEGA = 0.8

LANES = 128
HALF = LANES // 2
EDGE = 8
STRIP = 2 * EDGE
REACH = 5
PIECE = EDGE + 1
CHUNK = 64
AXES = ("rows", "cols")
LIMIT = 40 * 1024 * 1024


VMEM = pl.BlockSpec(memory_space=pltpu.VMEM)
SMEM = pl.BlockSpec(memory_space=pltpu.SMEM)
HBM = pl.BlockSpec(memory_space=pltpu.HBM)


def params():
    return pltpu.CompilerParams(vmem_limit_bytes=LIMIT)


def in_hbm(array):
    return pltpu.with_memory_space_constraint(array, pltpu.HBM)


def floats(*shapes):
    return [jax.ShapeDtypeStruct(shape, jnp.float32) for shape in shapes]


def place():
    at_col, at_row = lax.axis_index("cols"), lax.axis_index("rows")
    n_cols, n_rows = lax.axis_size("cols"), lax.axis_size("rows")
    return at_col, at_row, n_cols, n_rows


def has_sides():
    at_col, at_row, n_cols, n_rows = place()
    flag = lambda test: jnp.where(test, 1.0, 0.0).astype(jnp.float32)
    return (
        flag(at_row > 0),
        flag(at_row < n_rows - 1),
        flag(at_col < n_cols - 1),
        flag(at_col > 0),
    )


def iota(shape, dim):
    return lax.broadcasted_iota(jnp.int32, shape, dim)


def cell_of(pixel, tiles):
    turn = (tiles + 1) * LANES
    return jnp.where(pixel < turn - HALF, pixel >> 3, ((pixel - turn) >> 3) & (2 * LANES - 1))


def gather_matrix(tiles):
    shape = ((tiles + 1) * LANES, 2 * LANES)
    hit = cell_of(iota(shape, 0), tiles) == iota(shape, 1)
    return jnp.where(hit, 1.0, 0.0).astype(jnp.bfloat16)


def split_dot(field, matrix):
    rows = field.shape[0]
    parts, rest = [], field
    for _ in range(3):
        parts.append(rest.astype(jnp.bfloat16))
        rest = rest - parts[-1].astype(jnp.float32)
    product = jnp.dot(
        jnp.concatenate(parts, axis=0), matrix, preferred_element_type=jnp.float32
    )
    return product[:rows] + (product[rows : 2 * rows] + product[2 * rows :])


def roll(field, by, axis):
    return pltpu.roll(field, by % field.shape[axis], axis)


def load(ref, at, rows=STRIP):
    return [ref[t, pl.ds(at, rows), :] for t in range(ref.shape[0])]


def store(ref, at, strip):
    for t, part in enumerate(strip):
        ref[t, pl.ds(at, part.shape[0]), :] = part


def wide(ref, at, rows):
    return jnp.concatenate(load(ref, at, rows), axis=1)


def read_taps(taps):
    return [[taps[a, b] for b in range(3)] for a in range(3)]


def tap_total(taps, power):
    return sum(tap * tap if power == 2 else tap for line in taps for tap in line)


def from_west(strip):
    lane = iota(strip[0].shape, 1)
    turned = [roll(part, 1, 1) for part in strip]
    return [jnp.where(lane == 0, turned[t - 1], turned[t]) for t in range(len(strip))]


def from_east(strip):
    lane = iota(strip[0].shape, 1)
    turned = [roll(part, -1, 1) for part in strip]
    count = len(strip)
    return [
        jnp.where(lane == LANES - 1, turned[(t + 1) % count], turned[t]) for t in range(count)
    ]


def tap_sums(ref, at, taps, flip):
    if flip:
        taps = [line[::-1] for line in taps[::-1]]
    above, here, below = load(ref, at - 1), load(ref, at), load(ref, at + 1)
    sums = [[], [], []]
    for t in range(len(here)):
        for b in range(3):
            sums[b].append(
                taps[0][b] * above[t] + taps[1][b] * here[t] + taps[2][b] * below[t]
            )
    return sums


def conv(ref, at, taps, flip):
    sums = tap_sums(ref, at, taps, flip)
    west, east = from_west(sums[0]), from_east(sums[2])
    return [sums[1][t] + west[t] + east[t] for t in range(len(west))]


def operate(ref, image, east_ref, south_ref, at, taps):
    above, here, below = load(ref, at - 1), load(ref, at), load(ref, at + 1)
    east, south, north = load(east_ref, at), load(south_ref, at), load(south_ref, at - 1)
    sums = tap_sums(image, at, taps, True)
    span = range(len(here))
    beside = from_east(here)
    flux = [east[t] * (here[t] - beside[t]) for t in span]
    from_left = from_west([sums[0][t] - flux[t] for t in span])
    from_right = from_east(sums[2])
    return here, [
        sums[1][t]
        + flux[t]
        + from_left[t]
        + from_right[t]
        + south[t] * (here[t] - below[t])
        - north[t] * (above[t] - here[t])
        for t in span
    ]


def begin(obs, cond, at, taps, sides):
    above, here, below = load(cond, at - 1), load(cond, at), load(cond, at + 1)
    span = range(len(here))
    right = from_east(here)
    east = [here[t] + right[t] for t in span]
    west = from_west(east)
    south = [here[t] + below[t] for t in span]
    squares = tap_total(taps, 2)
    diag = [squares + east[t] + west[t] + south[t] + (here[t] + above[t]) for t in span]
    inverse = [pl.reciprocal(part, approx=True) for part in diag]
    inverse = [inverse[t] * (2.0 - diag[t] * inverse[t]) for t in span]
    inverse[-1] = inverse[-1] * sides
    residual = conv(obs, at, taps, True)
    return east, south, inverse, residual, [residual[t] * inverse[t] for t in span]


def pick_lanes(field, lanes):
    return jnp.take_along_axis(field, lanes, axis=1, mode="promise_in_bounds")


def spread_cells(cells, spread):
    tiles = spread.shape[0] - 1
    lane = iota((cells.shape[0], LANES), 1)
    for t in range(tiles):
        spread[t] = pick_lanes(cells[:, :LANES], (lane >> 3) + t * (LANES // COARSE))
    turn = jnp.where(lane < HALF, 0, LANES - LANES // COARSE)
    spread[tiles] = pick_lanes(cells[:, LANES:], (lane >> 3) + turn)


def cells_at(spread, at):
    first = at // EDGE + EDGE - 2
    rows = [load(spread, first + index, 1) for index in range(STRIP // EDGE)]
    return [
        jnp.concatenate([jnp.broadcast_to(row, (EDGE, LANES)) for row in parts], axis=0)
        for parts in zip(*rows)
    ]


def cell_sums(ref, tiles, down, matrix):
    rows = []
    for t in range(tiles):
        picked = [
            ref[t, pl.ds(2 * EDGE + k, down, stride=COARSE), :] for k in range(COARSE)
        ]
        rows.append(sum(picked[1:], picked[0]))
    return split_dot(jnp.concatenate(rows, axis=1), matrix)


def cell_matrix(tiles):
    shape = (tiles * LANES, LANES)
    hit = iota(shape, 0) // COARSE == iota(shape, 1)
    return jnp.where(hit, 1.0, 0.0).astype(jnp.bfloat16)


def side_lanes(has_e, has_w):
    return jnp.where(iota((STRIP, LANES), 1) < HALF, has_e, has_w)


def mask_rows(ref, has_n, has_s):
    last = ref.shape[1] - 2 * EDGE
    for at, flag in ((EDGE, has_n), (last, has_s)):
        ref[:, at : at + EDGE, :] = ref[:, at : at + EDGE, :] * flag


def clear_pads(*refs):
    empty = jnp.zeros((refs[0].shape[0], EDGE, LANES), jnp.float32)
    for ref in refs:
        ref[:, :EDGE, :] = empty
        ref[:, ref.shape[1] - EDGE :, :] = empty


def product_sum_rows(one, two, count):
    total = one[0] * two[0]
    for t in range(1, count):
        total = total + one[t] * two[t]
    return total


def product_sum(one, two, count, flags=None):
    return fold(product_sum_rows(one, two, count), flags)


def fold(total, flags=None):
    parts = [total[at : at + EDGE] for at in range(0, total.shape[0], EDGE)]
    if flags is not None:
        parts = [part * flag for part, flag in zip(parts, flags)]
    return sum(parts[1:], parts[0])


def sweep(group, first, last, body, carry):
    width = group * STRIP
    steps = -(-(last - first) // width)

    def work(index, carry):
        start = first + index * width
        at = pl.multiple_of(jnp.minimum(start, last - width), EDGE)
        pending = []
        for by in range(0, width, STRIP):
            stores, carry = body(at + by, start, carry)
            pending += [(ref, at + by, strip) for ref, strip in stores]
        for ref, row, strip in pending:
            store(ref, row, strip)
        return carry

    return lax.fori_loop(0, steps, work, carry)


def sum_line(parts):
    line = jnp.zeros((1, LANES), jnp.float32)
    block = iota((1, LANES), 1) // (LANES // 4)
    for index, part in enumerate(parts):
        part = jnp.sum(part, axis=0, keepdims=True)
        part = part + roll(part, LANES // 2, 1)
        part = part + roll(part, LANES // 4, 1)
        line = jnp.where(block == index, part, line)
    return line


def line_totals(lines, count):
    while len(lines) > 1:
        lines = [sum(lines[at + 1 : at + 2], lines[at]) for at in range(0, len(lines), 2)]
    block = iota((1, LANES), 1) // (LANES // 4)
    return [
        jnp.sum(jnp.where(block == index, lines[0], 0.0), axis=1, keepdims=True)
        for index in range(count)
    ]


def jacobi(source, table, work):
    factor, east, west, south, north = [table[index] for index in range(5)]
    window = source.shape[0]
    source = factor * source
    iterate = source
    for sweep_index in range(SWEEPS - 1):
        place_ref = work.at[sweep_index % 2]
        for half in range(2):
            place_ref[half, EDGE : EDGE + window, :] = iterate[
                :, half * LANES : (half + 1) * LANES
            ]
        above, below = [
            jnp.concatenate(
                [place_ref[half, EDGE + by : EDGE + by + window, :] for half in range(2)], axis=1
            )
            for by in (-1, 1)
        ]
        across = east * roll(iterate, -1, 1) + west * roll(iterate, 1, 1)
        along = south * below + north * above
        iterate = ((1.0 - OMEGA) * iterate + source) + (across + along)
    return iterate


def clear_work(work):
    for buffer in range(2):
        clear_pads(work.at[buffer])


def in_pair_order(at, for_before, for_after):
    even = at % 2 == 0
    if callable(for_before):
        return (
            lambda *args: jnp.where(even, for_after(*args), for_before(*args)),
            lambda *args: jnp.where(even, for_before(*args), for_after(*args)),
        )
    return jnp.where(even, for_after, for_before), jnp.where(even, for_before, for_after)


def reader(tiles_here, refs, scratch, obs, cond, down):
    obs_in, class_in, weight_in, taps_in = refs
    classes, weights, taps, sums, obs_sem, class_sem, small_sem = scratch
    own = pl.ds(2 * EDGE, down * COARSE)
    small = [
        pltpu.make_async_copy(weight_in, weights, small_sem.at[0]),
        pltpu.make_async_copy(taps_in, taps, small_sem.at[1]),
    ]
    moves = []
    for slot, t in enumerate(tiles_here):
        lanes = pl.ds(t * LANES, LANES)
        moves.append(
            (
                pltpu.make_async_copy(class_in.at[:, lanes], classes.at[slot], class_sem.at[slot]),
                pltpu.make_async_copy(
                    obs_in.at[:, lanes], obs.at[slot, own, :], obs_sem.at[slot]
                ),
            )
        )
    for copy in small:
        copy.start()
    for pair in moves:
        for copy in pair:
            copy.start()
    sums[...] = jnp.zeros_like(sums)

    def settle(slot):
        if slot == 0:
            for copy in small:
                copy.wait()
        for copy in moves[slot]:
            copy.wait()
        values = [0.5 * weights[class_id] for class_id in range(CLASSES)]
        kind = classes[slot]
        cond[slot, own, :] = jnp.where(
            kind < 2,
            jnp.where(kind == 0, values[0], values[1]),
            jnp.where(kind == 2, values[2], values[3]),
        )
        for which, ref in enumerate((obs, cond)):
            picked = [
                ref[slot, pl.ds(2 * EDGE + k, down, stride=COARSE), :] for k in range(COARSE)
            ]
            cells = slice(2 * EDGE, 2 * EDGE + down)
            sums[3 * which, slot, cells, :] = sum(picked[1:], picked[0])
            sums[3 * which + 1, slot, cells, :] = picked[0]
            sums[3 * which + 2, slot, cells, :] = picked[-1]

    return settle


def reader_scratch(tiles, height, window, class_weights, taps):
    return [
        pltpu.VMEM((tiles, height, LANES), jnp.int32),
        pltpu.SMEM(class_weights.shape, jnp.float32),
        pltpu.SMEM(taps.shape, jnp.float32),
        pltpu.VMEM((6, tiles + 1, window + 2 * EDGE, LANES), jnp.float32),
        pltpu.SemaphoreType.DMA((tiles,)),
        pltpu.SemaphoreType.DMA((tiles,)),
        pltpu.SemaphoreType.DMA((2,)),
    ]


def coarse_parts(sums, taps, matrix):
    window = sums.shape[2] - 2 * EDGE
    whole = lambda index, by=0: wide(sums.at[index], EDGE + by, window)
    full = whole(0)
    by_tap = [full - whole(1) + whole(1, 1), full, full - whole(2) + whole(2, -1)]
    across = [sum(taps[a][b] * by_tap[a] for a in range(3)) for b in range(3)]
    source = across[1] + roll(across[0], -1, 1) + roll(across[2], 1, 1)
    full = whole(3)
    last = (iota(full.shape, 1) & (COARSE - 1)) == COARSE - 1
    east = jnp.where(last, full + roll(full, -1, 1), 0.0)
    south = whole(5) + whole(4, 1)
    cells = split_dot(jnp.concatenate([source, east, south], axis=0), matrix)
    source, east, south = cells[:window], cells[window : 2 * window], cells[2 * window :]
    around = east + roll(east, 1, 1) + south + roll(south, 1, 0)
    return [source, east, south, around]


def edge_kernel(tiles, down, *refs):
    arguments, (send_a, send_b), (obs, cond, message, *scratch) = refs[:4], refs[4:6], refs[6:]
    height = down * COARSE
    halves = height // LANES
    window = down + 2 * EDGE
    settle = reader((0, tiles - 1), arguments, scratch, obs, cond, down)
    matrix = gather_matrix(2)
    fine = [[], []]
    for slot, begin_row in ((0, 0), (1, LANES - REACH)):
        settle(slot)
        for ref in (obs, cond):
            turned = jnp.transpose(ref[slot, 2 * EDGE : 2 * EDGE + height, :])
            turned = turned[begin_row : begin_row + REACH]
            for half in range(halves):
                fine[slot].append(turned[:, half * LANES : (half + 1) * LANES])
    parts = coarse_parts(scratch[3], read_taps(scratch[2]), matrix)
    spare = jnp.zeros((2 * LANES - 4 * window, 2 * LANES), jnp.float32)
    stack = jnp.concatenate(parts + [spare], axis=0)
    left = jnp.transpose(stack[:, :LANES])
    right = jnp.transpose(stack[:, LANES:])
    past = 2 * LANES // COARSE
    split = lambda piece: [piece[:, half * LANES : (half + 1) * LANES] for half in range(2)]
    for slot, main, over in (
        (0, left[:EDGE], right[LANES - 1 :]),
        (1, left[past - EDGE : past], left[past : past + 1]),
    ):
        rows = split(main) + fine[slot] + split(over)
        filled = sum(piece.shape[0] for piece in rows)
        rows.append(jnp.zeros((message.shape[1] - filled, LANES), jnp.float32))
        message[slot] = jnp.concatenate(rows, axis=0)
    send_a[...], send_b[...] = in_pair_order(place()[0], message[0], message[1])


def edge(observed, class_map, class_weights, taps):
    height, breadth = observed.shape
    tiles, down = breadth // LANES, height // COARSE
    window = down + 2 * EDGE
    field = (3, height + 4 * EDGE, LANES)
    rows = 2 * EDGE + 2 * REACH * (height // LANES) + 2
    strip = (-(-rows // EDGE) * EDGE, LANES)
    return pl.pallas_call(
        functools.partial(edge_kernel, tiles, down),
        in_specs=[HBM] * 4,
        out_specs=[VMEM] * 2,
        out_shape=floats(strip, strip),
        scratch_shapes=[
            pltpu.VMEM(field, jnp.float32),
            pltpu.VMEM(field, jnp.float32),
            pltpu.VMEM((2,) + strip, jnp.float32),
        ]
        + reader_scratch(2, height, window, class_weights, taps),
        compiler_params=params(),
        name="pack_east_west",
    )(*[in_hbm(array) for array in (observed, class_map, class_weights, taps)])


def pack_kernel(tiles, down, *refs):
    arguments, (obs, cond, coarse_ref), scratch = refs[:4], refs[5:8], refs[8:]
    settle = reader(range(tiles), arguments, scratch, obs, cond, down)
    matrix = gather_matrix(tiles)
    for t in range(tiles):
        settle(t)
    for index, part in enumerate(coarse_parts(scratch[3], read_taps(scratch[2]), matrix)):
        coarse_ref[index] = part


def pack(observed, class_map, class_weights, taps, after):
    height, breadth = observed.shape
    tiles, down = breadth // LANES, height // COARSE
    window = down + 2 * EDGE
    field = (tiles + 1, height + 4 * EDGE, LANES)
    pixels = height * breadth
    return pl.pallas_call(
        functools.partial(pack_kernel, tiles, down),
        in_specs=[HBM] * 4 + [VMEM],
        out_specs=[VMEM] * 3,
        out_shape=floats(field, field, (4, window, 2 * LANES)),
        scratch_shapes=reader_scratch(tiles, height, window, class_weights, taps),
        compiler_params=params(),
        cost_estimate=pl.CostEstimate(
            flops=20 * pixels, bytes_accessed=16 * pixels, transcendentals=0
        ),
        name="pack_all",
    )(*[in_hbm(array) for array in (observed, class_map, class_weights, taps)], after)


def message_rows(tiles):
    rest = EDGE
    fine = rest + 2 * tiles
    sides = fine + tiles * EDGE
    return 0, rest, fine, sides, sides + EDGE


def merge_sides(parts):
    block = iota((EDGE, LANES), 1) // (2 * EDGE)
    merged = jnp.zeros((EDGE, LANES), jnp.float32)
    for index, part in enumerate(parts):
        merged = jnp.where(block == index, roll(part, (2 * index + 1) * EDGE, 1), merged)
    return merged


def split_sides(merged, count):
    lane = iota((EDGE, LANES), 1)
    outer = (lane < EDGE) | (lane >= LANES - EDGE)
    return [
        jnp.where(outer, roll(merged, -(2 * index + 1) * EDGE, 1), 0.0) for index in range(count)
    ]


def middle_kernel(
    tiles,
    down,
    got_b,
    got_a,
    coarse_in,
    obs_in,
    cond_in,
    obs,
    cond,
    coarse_ref,
    send_a,
    send_b,
    message,
):
    height = down * COARSE
    halves = height // LANES
    at_col, at_row, _, _ = place()
    from_e, from_w = in_pair_order(at_col, got_b[...], got_a[...])
    zeros = lambda rows: jnp.zeros((rows, LANES), jnp.float32)

    def turned(low, high):
        low = [low, zeros(EDGE - low.shape[0])] if low.shape[0] < EDGE else [low]
        high = [zeros(EDGE - high.shape[0]), high] if high.shape[0] < EDGE else [high]
        return jnp.transpose(jnp.concatenate([*low, zeros(LANES - 2 * EDGE), *high], axis=0))

    for which, field in enumerate((obs, cond)):
        for half in range(halves):
            at = 2 * EDGE + REACH * (which * halves + half)
            begin_row = 2 * EDGE + half * LANES
            field[tiles, begin_row : begin_row + LANES, :] = turned(
                from_e[at : at + REACH], from_w[at : at + REACH]
            )
    main = lambda strip, half: strip[half * EDGE : (half + 1) * EDGE]

    def over(strip, half):
        at = 2 * EDGE + 2 * REACH * halves + half
        return strip[at : at + 1]

    left = [turned(over(from_w, half), over(from_e, half)) for half in range(2)]
    right = [turned(main(from_e, half), main(from_w, half)) for half in range(2)]
    left = jnp.concatenate(left, axis=0)
    right = jnp.concatenate(right, axis=0)
    window = down + 2 * EDGE
    for index in range(4):
        rows = slice(index * window, (index + 1) * window)
        coarse_ref[index, :, :LANES] = coarse_in[index, :, :LANES] + left[rows]
        coarse_ref[index, :, LANES:] = coarse_in[index, :, LANES:] + right[rows]
    row = iota((EDGE, LANES), 0)
    over_at, rest_at, fine_at, sides_at, coarse_at = message_rows(tiles)
    for slot, begin_row, reach_row, first_row, over_row in (
        (0, 2 * EDGE, 2 * EDGE, EDGE, EDGE - 1),
        (1, EDGE + height, 2 * EDGE + height - REACH, window - 2 * EDGE, window - EDGE),
    ):
        for t in range(tiles):
            at = fine_at + t * EDGE
            message[slot, at : at + EDGE, :] = jnp.where(
                row < REACH,
                obs[t, reach_row : reach_row + EDGE, :],
                cond[t, reach_row - REACH : reach_row - REACH + EDGE, :],
            )
        for begin_tile in range(0, tiles, 4):
            rest = None
            for index in range(4):
                at = reach_row + EDGE - REACH - 2 * index
                piece = cond[begin_tile + index, at : at + EDGE, :]
                rest = piece if rest is None else jnp.where(row < 2 * index, rest, piece)
            at = rest_at + begin_tile * 2
            message[slot, at : at + EDGE, :] = rest
        rows = slice(first_row, first_row + EDGE)
        for index in range(4):
            at = coarse_at + index * EDGE
            message[slot, at : at + EDGE, :] = coarse_ref[index, rows, :LANES]
        beyond = [coarse_ref[index, rows, LANES:] for index in range(4)]
        beyond += [field[tiles, begin_row : begin_row + EDGE, :] for field in (obs, cond)]
        message[slot, sides_at : sides_at + EDGE, :] = merge_sides(beyond)
        message[slot, over_at : over_at + EDGE, :] = jnp.concatenate(
            [
                coarse_ref[index, over_row : over_row + 1, half * LANES : (half + 1) * LANES]
                for index in range(4)
                for half in range(2)
            ],
            axis=0,
        )
    send_a[...], send_b[...] = in_pair_order(at_row, message[0], message[1])


def middle(got_a, got_b, coarse, obs, cond):
    tiles, height = obs.shape[0] - 1, obs.shape[1] - 4 * EDGE
    down = height // COARSE
    long = (message_rows(tiles)[-1] + 4 * EDGE, LANES)
    return pl.pallas_call(
        functools.partial(middle_kernel, tiles, down),
        in_specs=[VMEM] * 5,
        out_specs=[VMEM] * 5,
        out_shape=floats(obs.shape, cond.shape, coarse.shape, long, long),
        input_output_aliases={3: 0, 4: 1},
        scratch_shapes=[pltpu.VMEM((2,) + long, jnp.float32)],
        compiler_params=params(),
        name="pack_north_south",
    )(got_b, got_a, coarse, obs, cond)


def inner_kernel(taps, obs, cond, res_ref, east_ref, south_ref, inv_ref, u_ref, dot_ref, cells_ref):
    _, _, has_e, has_w = has_sides()
    clear_pads(east_ref, south_ref)
    taps = read_taps(taps)
    sides = side_lanes(has_e, has_w)

    tiles = obs.shape[0] - 1
    cells_ref[...] = cell_matrix(tiles)

    def work(at, start, total):
        fields = begin(obs, cond, at, taps, sides)
        flags = [jnp.where(at + by >= start, 1.0, 0.0) for by in range(0, STRIP, EDGE)]
        total = total + product_sum(fields[3], fields[4], tiles, flags)
        return list(zip((east_ref, south_ref, inv_ref, res_ref, u_ref), fields)), total

    nothing = jnp.zeros((EDGE, LANES), jnp.float32)
    dot_ref[...] = sweep(5, 3 * EDGE, obs.shape[1] - 3 * EDGE, work, nothing)


def inner(taps, obs, cond):
    field = obs.shape
    pixels = field[0] * field[1] * field[2]
    return pl.pallas_call(
        inner_kernel,
        in_specs=[SMEM] + [VMEM] * 2,
        out_specs=[VMEM] * 7,
        out_shape=floats(field, field, field, field, field, (EDGE, LANES))
        + [jax.ShapeDtypeStruct(((field[0] - 1) * LANES, LANES), jnp.bfloat16)],
        compiler_params=params(),
        cost_estimate=pl.CostEstimate(
            flops=45 * pixels, bytes_accessed=24 * pixels, transcendentals=0
        ),
        name="inner_strips",
    )(taps, obs, cond)


def first_kernel(
    tiles,
    down,
    taps,
    obs_in,
    cond_in,
    res_in,
    east_in,
    south_in,
    inv_in,
    u_in,
    got_b,
    got_a,
    coarse_in,
    dot_in,
    cells_in,
    obs,
    cond,
    res_ref,
    east_ref,
    south_ref,
    inv_ref,
    u_ref,
    p_ref,
    q_ref,
    table_ref,
    own_ref,
    chunk_ref,
    image,
    spread,
    work,
):
    height = down * COARSE
    window = down + 2 * EDGE
    at_col, at_row, n_cols, n_rows = place()
    has_n, has_s, has_e, has_w = has_sides()
    clear_pads(obs, cond, p_ref, image)
    clear_work(work)
    from_s, from_n = in_pair_order(
        at_row,
        lambda at, rows=EDGE: got_b[at : at + rows, :],
        lambda at, rows=EDGE: got_a[at : at + rows, :],
    )
    over_at, rest_at, fine_at, sides_at, coarse_at = message_rows(tiles)
    row = iota((EDGE, LANES), 0)
    short = EDGE - REACH
    for t in range(tiles):
        at = fine_at + t * EDGE
        rest = rest_at + 2 * t
        begin_row = 2 * EDGE + height
        obs[t, EDGE : 2 * EDGE, :] = jnp.where(row >= short, from_n(at - short), 0.0)
        obs[t, begin_row : begin_row + EDGE, :] = jnp.where(row < REACH, from_s(at), 0.0)
        near, far = from_n(at + REACH - short), from_n(rest - 2 * short)
        near = jnp.where(row < short, 0.0, near)
        cond[t, EDGE : 2 * EDGE, :] = jnp.where(row < 2 * short, near, far)
        near, far = from_s(at + REACH), from_s(rest - short)
        far = jnp.where(row < REACH, far, 0.0)
        cond[t, begin_row : begin_row + EDGE, :] = jnp.where(row < short, near, far)
    sides_n, sides_s = [split_sides(strip(sides_at), 6) for strip in (from_n, from_s)]
    for which, field in enumerate((obs, cond)):
        field[tiles, EDGE : 2 * EDGE, :] = sides_n[4 + which]
        field[tiles, 2 * EDGE + height : 3 * EDGE + height, :] = sides_s[4 + which]

    edge_row = iota((EDGE, 2 * LANES), 0)

    def joined(index):
        def over(strip, row):
            line = [
                jnp.broadcast_to(
                    strip(over_at + 2 * index + half, 1), (EDGE, LANES)
                )
                for half in range(2)
            ]
            return jnp.where(edge_row == row, jnp.concatenate(line, axis=1), 0.0)

        def rows(strip, beyond):
            return jnp.concatenate([strip(coarse_at + index * EDGE), beyond[index]], axis=1)

        parts = [coarse_in[index, at : at + EDGE, :] for at in range(0, window, EDGE)]
        parts[0] = parts[0] + rows(from_n, sides_n)
        parts[1] = parts[1] + over(from_n, 0)
        parts[-2] = parts[-2] + over(from_s, EDGE - 1)
        parts[-1] = parts[-1] + rows(from_s, sides_s)
        return jnp.concatenate(parts, axis=0)

    source, east, south, around = [joined(index) for index in range(4)]
    row = iota(source.shape, 0)
    lane = iota(source.shape, 1)
    inside = jnp.where(row < EDGE, has_n, jnp.where(row < window - EDGE, 1.0, has_s))
    inside = inside * jnp.where(
        lane < LANES, 1.0, jnp.where(lane < LANES + HALF, has_e, has_w)
    )
    taps = read_taps(taps)
    taps_sum = tap_total(taps, 1)
    factor = inside * OMEGA / (COARSE * COARSE * taps_sum * taps_sum + around)
    weights = (east, roll(east, 1, 1), south, roll(south, 1, 0))
    table = [factor] + [factor * weight for weight in weights]
    for index, part in enumerate([*table, source]):
        table_ref[index] = part
    sides = side_lanes(has_e, has_w)
    half = iota((STRIP, LANES), 0) // EDGE
    pending = []
    total = dot_in[...]
    for index, known in ((0, has_n), (1, has_s)):
        at = EDGE + index * height
        fields = begin(obs, cond, at, taps, sides)
        own = jnp.where(half == index, 0.0, 1.0)
        total = total + fold(own * product_sum_rows(fields[3], fields[4], tiles))
        flag = jnp.where(half == index, known, 1.0)
        inverse, start = [[part * flag for part in fields[index]] for index in (2, 4)]
        fields = (*fields[:2], inverse, fields[3], start)
        pending += [
            (ref, at, strip)
            for ref, strip in zip((east_ref, south_ref, inv_ref, res_ref, u_ref), fields)
        ]
    cells = jacobi(source, table, work)
    spread_cells(cells, spread)
    inner_cells = slice(EDGE, EDGE + down)
    total = total + fold(source[inner_cells, :LANES] * cells[inner_cells, :LANES])
    dot_rp = total
    for ref, at, strip in pending:
        store(ref, at, strip)

    def flags(at, start):
        rows = [at + by for by in range(0, STRIP, EDGE)]
        first_row = jnp.maximum(start, 2 * EDGE)
        return [
            jnp.where((row >= first_row) & (row < 2 * EDGE + height), 1.0, 0.0) for row in rows
        ]

    def begin_p(at, _, carry):
        start, cells = load(u_ref, at), cells_at(spread, at)
        return [(p_ref, [start[t] + cells[t] for t in range(tiles + 1)])], carry

    def blur(at, _, carry):
        strip = conv(p_ref, at, taps, False)
        strip[tiles] = strip[tiles] * sides
        return [(image, strip)], carry

    def finish(at, start, total):
        here, product = operate(p_ref, image, east_ref, south_ref, at, taps)
        return [(q_ref, product)], total + product_sum(here, product, tiles, flags(at, start))

    nothing = jnp.zeros((EDGE, LANES), jnp.float32)
    span = (EDGE, 3 * EDGE + height)
    sweep(3, *span, begin_p, 0)
    sweep(3, *span, blur, 0)
    mask_rows(image, has_n, has_s)
    dot_pq = sweep(3, *span, finish, nothing)

    own = cell_sums(q_ref, tiles, down, cells_in[...])
    own_ref[...] = own
    spare = jnp.zeros((LANES - down, LANES), jnp.float32)
    turned = jnp.transpose(jnp.concatenate([own, spare], axis=0))
    me = at_row * n_cols + at_col
    chunk_ref[pl.ds(me * PIECE, EDGE), 0, :] = jnp.zeros((EDGE, LANES), jnp.float32)
    for down_by in (-1, 0, 1):
        for right_by in (-1, 0, 1):
            if down_by == 0 and right_by == 0:
                continue
            if down_by == 0:
                piece = turned[:EDGE] if right_by < 0 else turned[LANES - EDGE :]
            else:
                piece = own[:EDGE] if down_by < 0 else own[down - EDGE :]
            to_row, to_col = at_row + down_by, at_col + right_by
            there = (to_row >= 0) & (to_row < n_rows) & (to_col >= 0) & (to_col < n_cols)
            slot = jnp.where(there, to_row * n_cols + to_col, me)
            chunk_ref[pl.ds(slot * PIECE, EDGE), 0, :] = piece * jnp.where(there, 1.0, 0.0)
    line = sum_line((dot_rp, dot_pq))
    for at in range(EDGE, chunk_ref.shape[0], PIECE):
        chunk_ref[at] = line


def first(taps, fields, got_a, got_b, coarse, dot, matrix):
    field = fields[0].shape
    tiles, height = field[0] - 1, field[1] - 4 * EDGE
    down = height // COARSE
    window = down + 2 * EDGE
    count = lax.axis_size("cols") * lax.axis_size("rows")
    shapes = [field] * 9 + [
        (6, window, 2 * LANES),
        (down, LANES),
        (count * PIECE, 1, LANES),
    ]
    return pl.pallas_call(
        functools.partial(first_kernel, tiles, down),
        in_specs=[SMEM] + [VMEM] * 12,
        out_specs=[VMEM] * len(shapes),
        out_shape=floats(*shapes),
        input_output_aliases={index + 1: index for index in range(7)},
        scratch_shapes=[
            pltpu.VMEM(field, jnp.float32),
            pltpu.VMEM((tiles + 1, window, LANES), jnp.float32),
            pltpu.VMEM((2, 2, window + 2 * EDGE, LANES), jnp.float32),
        ],
        compiler_params=params(),
        name="first_direction",
    )(taps, *fields, got_b, got_a, coarse, dot, matrix)[2:]


def second_kernel(
    tiles,
    down,
    taps,
    got_ref,
    own_ref,
    table_ref,
    res_ref,
    q_ref,
    east_ref,
    south_ref,
    inv_ref,
    w_ref,
    v_ref,
    out_ref,
    known_ref,
    image,
    spread,
    work,
):
    height = down * COARSE
    has_n, has_s, has_e, has_w = has_sides()
    at_col, at_row, n_cols, n_rows = place()
    me = at_row * n_cols + at_col

    def got(down_by, right_by):
        to_row, to_col = at_row + down_by, at_col + right_by
        there = (to_row >= 0) & (to_row < n_rows) & (to_col >= 0) & (to_col < n_cols)
        slot = jnp.where(there, to_row * n_cols + to_col, me)
        return got_ref[pl.ds(slot * PIECE, EDGE), 0, :]

    low = iota((EDGE, LANES), 1) < HALF
    gap = jnp.zeros((LANES - 2 * EDGE, LANES), jnp.float32)
    beside = jnp.transpose(jnp.concatenate([got(0, 1), gap, got(0, -1)], axis=0))[:down]
    source = jnp.concatenate(
        [
            jnp.concatenate([got(-1, 0), jnp.where(low, got(-1, 1), got(-1, -1))], axis=1),
            jnp.concatenate([own_ref[...], beside], axis=1),
            jnp.concatenate([got(1, 0), jnp.where(low, got(1, 1), got(1, -1))], axis=1),
        ],
        axis=0,
    )
    clear_work(work)
    rp, pq = line_totals(
        [got_ref[at] for at in range(EDGE, got_ref.shape[0], PIECE)], 2
    )
    step = rp / pq
    for index, value in enumerate((step, rp)):
        known_ref[index] = jnp.broadcast_to(value, (EDGE, LANES))
    source = table_ref[5] - jnp.broadcast_to(step, source.shape) * source
    spread_cells(jacobi(source, table_ref, work), spread)
    step = jnp.broadcast_to(step, (STRIP, LANES))
    clear_pads(w_ref, image)
    sides = side_lanes(has_e, has_w)
    taps = read_taps(taps)

    def begin_w(at, start, total):
        right, field, inverse = load(res_ref, at), load(q_ref, at), load(inv_ref, at)
        cells = cells_at(spread, at)
        span = range(tiles + 1)
        residual = [right[t] - step * field[t] for t in span]
        strip = [residual[t] * inverse[t] + cells[t] for t in span]
        first_row = jnp.maximum(start, 2 * EDGE)
        flags = [
            jnp.where((row >= first_row) & (row < 2 * EDGE + height), 1.0, 0.0)
            for row in [at + by for by in range(0, STRIP, EDGE)]
        ]
        return [(w_ref, strip)], total + product_sum(residual, strip, tiles, flags)

    def blur(at, _, carry):
        strip = conv(w_ref, at, taps, False)
        strip[tiles] = strip[tiles] * sides
        return [(image, strip)], carry

    def finish(at, _, total):
        here, product = operate(w_ref, image, east_ref, south_ref, at, taps)
        return [(v_ref, product[:tiles])], total + product_sum(here, product, tiles)

    nothing = jnp.zeros((EDGE, LANES), jnp.float32)
    span = (EDGE, 3 * EDGE + height)
    dot_rz = sweep(3, *span, begin_w, nothing)
    sweep(3, *span, blur, 0)
    mask_rows(image, has_n, has_s)
    dot_zz = sweep(4, 2 * EDGE, 2 * EDGE + height, finish, nothing)
    line = sum_line((dot_rz, dot_zz))
    for index in range(out_ref.shape[0]):
        out_ref[index] = line


def second(taps, got, own, table, r, q, east, south, inv):
    tiles, height = q.shape[0] - 1, q.shape[1] - 4 * EDGE
    down = height // COARSE
    window = down + 2 * EDGE
    count = lax.axis_size("cols") * lax.axis_size("rows")
    return pl.pallas_call(
        functools.partial(second_kernel, tiles, down),
        in_specs=[SMEM] + [VMEM] * 8,
        out_specs=[VMEM] * 4,
        out_shape=floats(q.shape, q.shape, (count, 1, LANES), (2, EDGE, LANES)),
        scratch_shapes=[
            pltpu.VMEM(q.shape, jnp.float32),
            pltpu.VMEM((tiles + 1, window, LANES), jnp.float32),
            pltpu.VMEM((2, 2, window + 2 * EDGE, LANES), jnp.float32),
        ],
        compiler_params=params(),
        name="second_direction",
    )(taps, got, own, table, r, q, east, south, inv)


def combine_kernel(
    tiles, height, sums_ref, known_ref, p_ref, w_ref, r_ref, q_ref, v_ref, sol_out, res_out, sol, res, sem
):
    rz, zz = line_totals([sums_ref[index] for index in range(sums_ref.shape[0])], 2)
    step, rp = [known_ref[index, :1, :] for index in range(2)]
    ratio = rz / rp
    step_next = rz / (zz - ratio * (rz / step))
    on_w = jnp.broadcast_to(step_next, (CHUNK, LANES))
    on_p = jnp.broadcast_to(step + step_next * ratio, (CHUNK, LANES))

    def copies(index):
        rows = pl.ds(pl.multiple_of(index * CHUNK, CHUNK), CHUNK)
        return (
            pltpu.make_async_copy(sol.at[rows, :], sol_out.at[rows, :], sem.at[0, index]),
            pltpu.make_async_copy(res.at[rows, :], res_out.at[rows, :], sem.at[1, index]),
        )

    def work(index, _):
        at = pl.multiple_of(index * CHUNK, CHUNK)
        p, w, r, q, v = [
            load(ref, at + 2 * EDGE, CHUNK) for ref in (p_ref, w_ref, r_ref, q_ref, v_ref)
        ]
        one = [on_p * p[t] + on_w * w[t] for t in range(tiles)]
        two = [r[t] - on_p * q[t] - on_w * v[t] for t in range(tiles)]
        for t in range(tiles):
            sol[pl.ds(at, CHUNK), t * LANES : (t + 1) * LANES] = one[t]
            res[pl.ds(at, CHUNK), t * LANES : (t + 1) * LANES] = two[t]
        for copy in copies(index):
            copy.start()
        return 0

    def settle(index, _):
        for copy in copies(index):
            copy.wait()
        return 0

    lax.fori_loop(0, height // CHUNK, work, 0)
    lax.fori_loop(0, height // CHUNK, settle, 0)


def combine(sums, known, p, w, r, q, v):
    tiles, height = q.shape[0] - 1, q.shape[1] - 4 * EDGE
    shape = (height, tiles * LANES)
    return pl.pallas_call(
        functools.partial(combine_kernel, tiles, height),
        in_specs=[VMEM] * 7,
        out_specs=[HBM] * 2,
        out_shape=floats(shape, shape),
        scratch_shapes=[
            pltpu.VMEM(shape, jnp.float32),
            pltpu.VMEM(shape, jnp.float32),
            pltpu.SemaphoreType.DMA((2, height // CHUNK)),
        ],
        compiler_params=params(),
        name="combine",
    )(sums, known, p, w, r, q, v)


def exchange(send_a, send_b, axis):
    count = lax.axis_size(axis)

    def pairs(begin):
        return [
            pair for i in range(begin, count - 1, 2) for pair in ((i, i + 1), (i + 1, i))
        ]

    got_b = lax.ppermute(send_b, axis, pairs(1))
    got_a = lax.ppermute(send_a, axis, pairs(0))
    return got_a, got_b


def body(observed, class_map, class_weights, blur_kernel):
    arguments = (observed, class_map, class_weights, blur_kernel)
    send_a, send_b = edge(*arguments)
    got_a, got_b = exchange(send_a, send_b, "cols")
    obs, cond, coarse = pack(*arguments, send_a)
    obs, cond, coarse, send_a, send_b = middle(got_a, got_b, coarse, obs, cond)
    got_a, got_b = exchange(send_a, send_b, "rows")
    r, east, south, inv, u, dot, matrix = inner(blur_kernel, obs, cond)
    fields = (obs, cond, r, east, south, inv, u)
    r, east, south, inv, _, p, q, table, own, chunk = first(
        blur_kernel, fields, got_a, got_b, coarse, dot, matrix
    )
    got = lax.all_to_all(chunk, AXES, 0, 0, tiled=True)
    w, v, line, known = second(blur_kernel, got, own, table, r, q, east, south, inv)
    sums = lax.all_to_all(line, AXES, 0, 0, tiled=True)
    return tuple(combine(sums, known, p, w, r, q, v))


def solution(mesh):
    return jax.shard_map(
        body,
        mesh=mesh,
        in_specs=(P("rows", "cols"), P("rows", "cols"), P(), P()),
        out_specs=(P("rows", "cols"), P("rows", "cols")),
        check_vma=False,
    )
```

```python
import functools

import jax
import jax.numpy as jnp
from jax import lax
from jax.experimental import pallas as pl
from jax.experimental.pallas import tpu as pltpu
from jax.sharding import PartitionSpec as P

COARSE = 8
SWEEPS = 8
CLASSES = 4
OMEGA = 0.8

LANES = 128
HALF = LANES // 2
EDGE = 8
STRIP = 2 * EDGE
REACH = 5
PIECE = EDGE + 1
CHUNK = 64
AXES = ("cols", "rows")
LIMIT = 40 * 1024 * 1024


VMEM = pl.BlockSpec(memory_space=pltpu.VMEM)
SMEM = pl.BlockSpec(memory_space=pltpu.SMEM)
HBM = pl.BlockSpec(memory_space=pltpu.HBM)


def params():
    return pltpu.CompilerParams(vmem_limit_bytes=LIMIT)


def in_hbm(array):
    return pltpu.with_memory_space_constraint(array, pltpu.HBM)


def floats(*shapes):
    return [jax.ShapeDtypeStruct(shape, jnp.float32) for shape in shapes]


def place():
    at_col, at_row = lax.axis_index("cols"), lax.axis_index("rows")
    n_cols, n_rows = lax.axis_size("cols"), lax.axis_size("rows")
    return at_col, at_row, n_cols, n_rows


def has_sides():
    at_col, at_row, n_cols, n_rows = place()
    flag = lambda test: jnp.where(test, 1.0, 0.0).astype(jnp.float32)
    return (
        flag(at_row > 0),
        flag(at_row < n_rows - 1),
        flag(at_col < n_cols - 1),
        flag(at_col > 0),
    )


def iota(shape, dim):
    return lax.broadcasted_iota(jnp.int32, shape, dim)


def cell_of(pixel, tiles):
    turn = (tiles + 1) * LANES
    return jnp.where(pixel < turn - HALF, pixel >> 3, ((pixel - turn) >> 3) & (2 * LANES - 1))


def gather_matrix(tiles):
    shape = ((tiles + 1) * LANES, 2 * LANES)
    hit = cell_of(iota(shape, 0), tiles) == iota(shape, 1)
    return jnp.where(hit, 1.0, 0.0).astype(jnp.bfloat16)


def split_dot(field, matrix):
    rows = field.shape[0]
    parts, rest = [], field
    for _ in range(3):
        parts.append(rest.astype(jnp.bfloat16))
        rest = rest - parts[-1].astype(jnp.float32)
    product = jnp.dot(
        jnp.concatenate(parts, axis=0), matrix, preferred_element_type=jnp.float32
    )
    return product[:rows] + (product[rows : 2 * rows] + product[2 * rows :])


def roll(field, by, axis):
    return pltpu.roll(field, by % field.shape[axis], axis)


def load(ref, at, rows=STRIP):
    return [ref[t, pl.ds(at, rows), :] for t in range(ref.shape[0])]


def store(ref, at, strip):
    for t, part in enumerate(strip):
        ref[t, pl.ds(at, part.shape[0]), :] = part


def wide(ref, at, rows):
    return jnp.concatenate(load(ref, at, rows), axis=1)


def read_taps(taps):
    return [[taps[a, b] for b in range(3)] for a in range(3)]


def tap_total(taps, power):
    return sum(tap * tap if power == 2 else tap for line in taps for tap in line)


def from_west(strip):
    lane = iota(strip[0].shape, 1)
    turned = [roll(part, 1, 1) for part in strip]
    return [jnp.where(lane == 0, turned[t - 1], turned[t]) for t in range(len(strip))]


def from_east(strip):
    lane = iota(strip[0].shape, 1)
    turned = [roll(part, -1, 1) for part in strip]
    count = len(strip)
    return [
        jnp.where(lane == LANES - 1, turned[(t + 1) % count], turned[t]) for t in range(count)
    ]


def tap_sums(ref, at, taps, flip):
    if flip:
        taps = [line[::-1] for line in taps[::-1]]
    above, here, below = load(ref, at - 1), load(ref, at), load(ref, at + 1)
    sums = [[], [], []]
    for t in range(len(here)):
        for b in range(3):
            sums[b].append(
                taps[0][b] * above[t] + taps[1][b] * here[t] + taps[2][b] * below[t]
            )
    return sums


def conv(ref, at, taps, flip):
    sums = tap_sums(ref, at, taps, flip)
    west, east = from_west(sums[0]), from_east(sums[2])
    return [sums[1][t] + west[t] + east[t] for t in range(len(west))]


def operate(ref, image, east_ref, south_ref, at, taps):
    above, here, below = load(ref, at - 1), load(ref, at), load(ref, at + 1)
    east, south, north = load(east_ref, at), load(south_ref, at), load(south_ref, at - 1)
    sums = tap_sums(image, at, taps, True)
    span = range(len(here))
    beside = from_east(here)
    flux = [east[t] * (here[t] - beside[t]) for t in span]
    from_left = from_west([sums[0][t] - flux[t] for t in span])
    from_right = from_east(sums[2])
    return here, [
        sums[1][t]
        + flux[t]
        + from_left[t]
        + from_right[t]
        + south[t] * (here[t] - below[t])
        - north[t] * (above[t] - here[t])
        for t in span
    ]


def begin(obs, cond, at, taps, sides):
    above, here, below = load(cond, at - 1), load(cond, at), load(cond, at + 1)
    span = range(len(here))
    right = from_east(here)
    east = [here[t] + right[t] for t in span]
    west = from_west(east)
    south = [here[t] + below[t] for t in span]
    squares = tap_total(taps, 2)
    diag = [squares + east[t] + west[t] + south[t] + (here[t] + above[t]) for t in span]
    inverse = [pl.reciprocal(part, approx=True) for part in diag]
    inverse = [inverse[t] * (2.0 - diag[t] * inverse[t]) for t in span]
    inverse[-1] = inverse[-1] * sides
    residual = conv(obs, at, taps, True)
    return east, south, inverse, residual, [residual[t] * inverse[t] for t in span]


def pick_lanes(field, lanes):
    return jnp.take_along_axis(field, lanes, axis=1, mode="promise_in_bounds")


def spread_cells(cells, spread):
    tiles = spread.shape[0] - 1
    lane = iota((cells.shape[0], LANES), 1)
    for t in range(tiles):
        spread[t] = pick_lanes(cells[:, :LANES], (lane >> 3) + t * (LANES // COARSE))
    turn = jnp.where(lane < HALF, 0, LANES - LANES // COARSE)
    spread[tiles] = pick_lanes(cells[:, LANES:], (lane >> 3) + turn)


def cells_at(spread, at):
    first = at // EDGE + EDGE - 2
    rows = [load(spread, first + index, 1) for index in range(STRIP // EDGE)]
    return [
        jnp.concatenate([jnp.broadcast_to(row, (EDGE, LANES)) for row in parts], axis=0)
        for parts in zip(*rows)
    ]


def cell_sums(ref, tiles, down, matrix):
    rows = []
    for t in range(tiles):
        picked = [
            ref[t, pl.ds(2 * EDGE + k, down, stride=COARSE), :] for k in range(COARSE)
        ]
        rows.append(sum(picked[1:], picked[0]))
    return split_dot(jnp.concatenate(rows, axis=1), matrix)


def cell_matrix(tiles):
    shape = (tiles * LANES, LANES)
    hit = iota(shape, 0) // COARSE == iota(shape, 1)
    return jnp.where(hit, 1.0, 0.0).astype(jnp.bfloat16)


def side_lanes(has_e, has_w):
    return jnp.where(iota((STRIP, LANES), 1) < HALF, has_e, has_w)


def mask_rows(ref, has_n, has_s):
    last = ref.shape[1] - 2 * EDGE
    for at, flag in ((EDGE, has_n), (last, has_s)):
        ref[:, at : at + EDGE, :] = ref[:, at : at + EDGE, :] * flag


def clear_pads(*refs):
    empty = jnp.zeros((refs[0].shape[0], EDGE, LANES), jnp.float32)
    for ref in refs:
        ref[:, :EDGE, :] = empty
        ref[:, ref.shape[1] - EDGE :, :] = empty


def product_sum_rows(one, two, count):
    total = one[0] * two[0]
    for t in range(1, count):
        total = total + one[t] * two[t]
    return total


def product_sum(one, two, count, flags=None):
    return fold(product_sum_rows(one, two, count), flags)


def fold(total, flags=None):
    parts = [total[at : at + EDGE] for at in range(0, total.shape[0], EDGE)]
    if flags is not None:
        parts = [part * flag for part, flag in zip(parts, flags)]
    return sum(parts[1:], parts[0])


def sweep(group, first, last, body, carry):
    width = group * STRIP
    steps = -(-(last - first) // width)

    def work(index, carry):
        start = first + index * width
        at = pl.multiple_of(jnp.minimum(start, last - width), EDGE)
        pending = []
        for by in range(0, width, STRIP):
            stores, carry = body(at + by, start, carry)
            pending += [(ref, at + by, strip) for ref, strip in stores]
        for ref, row, strip in pending:
            store(ref, row, strip)
        return carry

    return lax.fori_loop(0, steps, work, carry)


def sum_line(parts):
    line = jnp.zeros((1, LANES), jnp.float32)
    block = iota((1, LANES), 1) // (LANES // 4)
    for index, part in enumerate(parts):
        part = jnp.sum(part, axis=0, keepdims=True)
        part = part + roll(part, LANES // 2, 1)
        part = part + roll(part, LANES // 4, 1)
        line = jnp.where(block == index, part, line)
    return line


def line_totals(lines, count):
    while len(lines) > 1:
        lines = [sum(lines[at + 1 : at + 2], lines[at]) for at in range(0, len(lines), 2)]
    block = iota((1, LANES), 1) // (LANES // 4)
    return [
        jnp.sum(jnp.where(block == index, lines[0], 0.0), axis=1, keepdims=True)
        for index in range(count)
    ]


def jacobi(source, table, work):
    factor, east, west, south, north = [table[index] for index in range(5)]
    window = source.shape[0]
    source = factor * source
    iterate = source
    for sweep_index in range(SWEEPS - 1):
        place_ref = work.at[sweep_index % 2]
        for half in range(2):
            place_ref[half, EDGE : EDGE + window, :] = iterate[
                :, half * LANES : (half + 1) * LANES
            ]
        above, below = [
            jnp.concatenate(
                [place_ref[half, EDGE + by : EDGE + by + window, :] for half in range(2)], axis=1
            )
            for by in (-1, 1)
        ]
        across = east * roll(iterate, -1, 1) + west * roll(iterate, 1, 1)
        along = south * below + north * above
        iterate = ((1.0 - OMEGA) * iterate + source) + (across + along)
    return iterate


def clear_work(work):
    for buffer in range(2):
        clear_pads(work.at[buffer])


def in_pair_order(at, for_before, for_after):
    even = at % 2 == 0
    if callable(for_before):
        return (
            lambda *args: jnp.where(even, for_after(*args), for_before(*args)),
            lambda *args: jnp.where(even, for_before(*args), for_after(*args)),
        )
    return jnp.where(even, for_after, for_before), jnp.where(even, for_before, for_after)


def reader(tiles_here, refs, scratch, obs, cond, down):
    obs_in, class_in, weight_in, taps_in = refs
    classes, weights, taps, sums, obs_sem, class_sem, small_sem = scratch
    own = pl.ds(2 * EDGE, down * COARSE)
    small = [
        pltpu.make_async_copy(weight_in, weights, small_sem.at[0]),
        pltpu.make_async_copy(taps_in, taps, small_sem.at[1]),
    ]
    moves = []
    for slot, t in enumerate(tiles_here):
        lanes = pl.ds(t * LANES, LANES)
        moves.append(
            (
                pltpu.make_async_copy(class_in.at[:, lanes], classes.at[slot], class_sem.at[slot]),
                pltpu.make_async_copy(
                    obs_in.at[:, lanes], obs.at[slot, own, :], obs_sem.at[slot]
                ),
            )
        )
    for copy in small:
        copy.start()
    for pair in moves:
        for copy in pair:
            copy.start()
    sums[...] = jnp.zeros_like(sums)

    def settle(slot):
        if slot == 0:
            for copy in small:
                copy.wait()
        for copy in moves[slot]:
            copy.wait()
        values = [0.5 * weights[class_id] for class_id in range(CLASSES)]
        kind = classes[slot]
        cond[slot, own, :] = jnp.where(
            kind < 2,
            jnp.where(kind == 0, values[0], values[1]),
            jnp.where(kind == 2, values[2], values[3]),
        )
        for which, ref in enumerate((obs, cond)):
            picked = [
                ref[slot, pl.ds(2 * EDGE + k, down, stride=COARSE), :] for k in range(COARSE)
            ]
            cells = slice(2 * EDGE, 2 * EDGE + down)
            sums[3 * which, slot, cells, :] = sum(picked[1:], picked[0])
            sums[3 * which + 1, slot, cells, :] = picked[0]
            sums[3 * which + 2, slot, cells, :] = picked[-1]

    return settle


def reader_scratch(tiles, height, window, class_weights, taps):
    return [
        pltpu.VMEM((tiles, height, LANES), jnp.int32),
        pltpu.SMEM(class_weights.shape, jnp.float32),
        pltpu.SMEM(taps.shape, jnp.float32),
        pltpu.VMEM((6, tiles + 1, window + 2 * EDGE, LANES), jnp.float32),
        pltpu.SemaphoreType.DMA((tiles,)),
        pltpu.SemaphoreType.DMA((tiles,)),
        pltpu.SemaphoreType.DMA((2,)),
    ]


def coarse_parts(sums, taps, matrix):
    window = sums.shape[2] - 2 * EDGE
    whole = lambda index, by=0: wide(sums.at[index], EDGE + by, window)
    full = whole(0)
    by_tap = [full - whole(1) + whole(1, 1), full, full - whole(2) + whole(2, -1)]
    across = [sum(taps[a][b] * by_tap[a] for a in range(3)) for b in range(3)]
    source = across[1] + roll(across[0], -1, 1) + roll(across[2], 1, 1)
    full = whole(3)
    last = (iota(full.shape, 1) & (COARSE - 1)) == COARSE - 1
    east = jnp.where(last, full + roll(full, -1, 1), 0.0)
    south = whole(5) + whole(4, 1)
    cells = split_dot(jnp.concatenate([source, east, south], axis=0), matrix)
    source, east, south = cells[:window], cells[window : 2 * window], cells[2 * window :]
    around = east + roll(east, 1, 1) + south + roll(south, 1, 0)
    return [source, east, south, around]


def edge_kernel(tiles, down, *refs):
    arguments, (send_a, send_b), (obs, cond, message, *scratch) = refs[:4], refs[4:6], refs[6:]
    height = down * COARSE
    halves = height // LANES
    window = down + 2 * EDGE
    settle = reader((0, tiles - 1), arguments, scratch, obs, cond, down)
    matrix = gather_matrix(2)
    fine = [[], []]
    for slot, begin_row in ((0, 0), (1, LANES - REACH)):
        settle(slot)
        for ref in (obs, cond):
            turned = jnp.transpose(ref[slot, 2 * EDGE : 2 * EDGE + height, :])
            turned = turned[begin_row : begin_row + REACH]
            for half in range(halves):
                fine[slot].append(turned[:, half * LANES : (half + 1) * LANES])
    parts = coarse_parts(scratch[3], read_taps(scratch[2]), matrix)
    spare = jnp.zeros((2 * LANES - 4 * window, 2 * LANES), jnp.float32)
    stack = jnp.concatenate(parts + [spare], axis=0)
    left = jnp.transpose(stack[:, :LANES])
    right = jnp.transpose(stack[:, LANES:])
    past = 2 * LANES // COARSE
    split = lambda piece: [piece[:, half * LANES : (half + 1) * LANES] for half in range(2)]
    for slot, main, over in (
        (0, left[:EDGE], right[LANES - 1 :]),
        (1, left[past - EDGE : past], left[past : past + 1]),
    ):
        rows = split(main) + fine[slot] + split(over)
        filled = sum(piece.shape[0] for piece in rows)
        rows.append(jnp.zeros((message.shape[1] - filled, LANES), jnp.float32))
        message[slot] = jnp.concatenate(rows, axis=0)
    send_a[...], send_b[...] = in_pair_order(place()[0], message[0], message[1])


def edge(observed, class_map, class_weights, taps):
    height, breadth = observed.shape
    tiles, down = breadth // LANES, height // COARSE
    window = down + 2 * EDGE
    field = (3, height + 4 * EDGE, LANES)
    rows = 2 * EDGE + 2 * REACH * (height // LANES) + 2
    strip = (-(-rows // EDGE) * EDGE, LANES)
    return pl.pallas_call(
        functools.partial(edge_kernel, tiles, down),
        in_specs=[HBM] * 4,
        out_specs=[VMEM] * 2,
        out_shape=floats(strip, strip),
        scratch_shapes=[
            pltpu.VMEM(field, jnp.float32),
            pltpu.VMEM(field, jnp.float32),
            pltpu.VMEM((2,) + strip, jnp.float32),
        ]
        + reader_scratch(2, height, window, class_weights, taps),
        compiler_params=params(),
        name="pack_east_west",
    )(*[in_hbm(array) for array in (observed, class_map, class_weights, taps)])


def pack_kernel(tiles, down, *refs):
    arguments, (obs, cond, coarse_ref), scratch = refs[:4], refs[5:8], refs[8:]
    settle = reader(range(tiles), arguments, scratch, obs, cond, down)
    matrix = gather_matrix(tiles)
    for t in range(tiles):
        settle(t)
    for index, part in enumerate(coarse_parts(scratch[3], read_taps(scratch[2]), matrix)):
        coarse_ref[index] = part


def pack(observed, class_map, class_weights, taps, after):
    height, breadth = observed.shape
    tiles, down = breadth // LANES, height // COARSE
    window = down + 2 * EDGE
    field = (tiles + 1, height + 4 * EDGE, LANES)
    pixels = height * breadth
    return pl.pallas_call(
        functools.partial(pack_kernel, tiles, down),
        in_specs=[HBM] * 4 + [VMEM],
        out_specs=[VMEM] * 3,
        out_shape=floats(field, field, (4, window, 2 * LANES)),
        scratch_shapes=reader_scratch(tiles, height, window, class_weights, taps),
        compiler_params=params(),
        cost_estimate=pl.CostEstimate(
            flops=20 * pixels, bytes_accessed=16 * pixels, transcendentals=0
        ),
        name="pack_all",
    )(*[in_hbm(array) for array in (observed, class_map, class_weights, taps)], after)


def message_rows(tiles):
    rest = EDGE
    fine = rest + 2 * tiles
    sides = fine + tiles * EDGE
    return 0, rest, fine, sides, sides + EDGE


def merge_sides(parts):
    block = iota((EDGE, LANES), 1) // (2 * EDGE)
    merged = jnp.zeros((EDGE, LANES), jnp.float32)
    for index, part in enumerate(parts):
        merged = jnp.where(block == index, roll(part, (2 * index + 1) * EDGE, 1), merged)
    return merged


def split_sides(merged, count):
    lane = iota((EDGE, LANES), 1)
    outer = (lane < EDGE) | (lane >= LANES - EDGE)
    return [
        jnp.where(outer, roll(merged, -(2 * index + 1) * EDGE, 1), 0.0) for index in range(count)
    ]


def middle_kernel(
    tiles,
    down,
    got_b,
    got_a,
    coarse_in,
    obs_in,
    cond_in,
    obs,
    cond,
    coarse_ref,
    send_a,
    send_b,
    message,
):
    height = down * COARSE
    halves = height // LANES
    at_col, at_row, _, _ = place()
    from_e, from_w = in_pair_order(at_col, got_b[...], got_a[...])
    zeros = lambda rows: jnp.zeros((rows, LANES), jnp.float32)

    def turned(low, high):
        low = [low, zeros(EDGE - low.shape[0])] if low.shape[0] < EDGE else [low]
        high = [zeros(EDGE - high.shape[0]), high] if high.shape[0] < EDGE else [high]
        return jnp.transpose(jnp.concatenate([*low, zeros(LANES - 2 * EDGE), *high], axis=0))

    for which, field in enumerate((obs, cond)):
        for half in range(halves):
            at = 2 * EDGE + REACH * (which * halves + half)
            begin_row = 2 * EDGE + half * LANES
            field[tiles, begin_row : begin_row + LANES, :] = turned(
                from_e[at : at + REACH], from_w[at : at + REACH]
            )
    main = lambda strip, half: strip[half * EDGE : (half + 1) * EDGE]

    def over(strip, half):
        at = 2 * EDGE + 2 * REACH * halves + half
        return strip[at : at + 1]

    left = [turned(over(from_w, half), over(from_e, half)) for half in range(2)]
    right = [turned(main(from_e, half), main(from_w, half)) for half in range(2)]
    left = jnp.concatenate(left, axis=0)
    right = jnp.concatenate(right, axis=0)
    window = down + 2 * EDGE
    for index in range(4):
        rows = slice(index * window, (index + 1) * window)
        coarse_ref[index, :, :LANES] = coarse_in[index, :, :LANES] + left[rows]
        coarse_ref[index, :, LANES:] = coarse_in[index, :, LANES:] + right[rows]
    row = iota((EDGE, LANES), 0)
    over_at, rest_at, fine_at, sides_at, coarse_at = message_rows(tiles)
    for slot, begin_row, reach_row, first_row, over_row in (
        (0, 2 * EDGE, 2 * EDGE, EDGE, EDGE - 1),
        (1, EDGE + height, 2 * EDGE + height - REACH, window - 2 * EDGE, window - EDGE),
    ):
        for t in range(tiles):
            at = fine_at + t * EDGE
            message[slot, at : at + EDGE, :] = jnp.where(
                row < REACH,
                obs[t, reach_row : reach_row + EDGE, :],
                cond[t, reach_row - REACH : reach_row - REACH + EDGE, :],
            )
        for begin_tile in range(0, tiles, 4):
            rest = None
            for index in range(4):
                at = reach_row + EDGE - REACH - 2 * index
                piece = cond[begin_tile + index, at : at + EDGE, :]
                rest = piece if rest is None else jnp.where(row < 2 * index, rest, piece)
            at = rest_at + begin_tile * 2
            message[slot, at : at + EDGE, :] = rest
        rows = slice(first_row, first_row + EDGE)
        for index in range(4):
            at = coarse_at + index * EDGE
            message[slot, at : at + EDGE, :] = coarse_ref[index, rows, :LANES]
        beyond = [coarse_ref[index, rows, LANES:] for index in range(4)]
        beyond += [field[tiles, begin_row : begin_row + EDGE, :] for field in (obs, cond)]
        message[slot, sides_at : sides_at + EDGE, :] = merge_sides(beyond)
        message[slot, over_at : over_at + EDGE, :] = jnp.concatenate(
            [
                coarse_ref[index, over_row : over_row + 1, half * LANES : (half + 1) * LANES]
                for index in range(4)
                for half in range(2)
            ],
            axis=0,
        )
    send_a[...], send_b[...] = in_pair_order(at_row, message[0], message[1])


def middle(got_a, got_b, coarse, obs, cond):
    tiles, height = obs.shape[0] - 1, obs.shape[1] - 4 * EDGE
    down = height // COARSE
    long = (message_rows(tiles)[-1] + 4 * EDGE, LANES)
    return pl.pallas_call(
        functools.partial(middle_kernel, tiles, down),
        in_specs=[VMEM] * 5,
        out_specs=[VMEM] * 5,
        out_shape=floats(obs.shape, cond.shape, coarse.shape, long, long),
        input_output_aliases={3: 0, 4: 1},
        scratch_shapes=[pltpu.VMEM((2,) + long, jnp.float32)],
        compiler_params=params(),
        name="pack_north_south",
    )(got_b, got_a, coarse, obs, cond)


def inner_kernel(taps, obs, cond, res_ref, east_ref, south_ref, inv_ref, u_ref, dot_ref, cells_ref):
    _, _, has_e, has_w = has_sides()
    clear_pads(east_ref, south_ref)
    taps = read_taps(taps)
    sides = side_lanes(has_e, has_w)

    tiles = obs.shape[0] - 1
    cells_ref[...] = cell_matrix(tiles)

    def work(at, start, total):
        fields = begin(obs, cond, at, taps, sides)
        flags = [jnp.where(at + by >= start, 1.0, 0.0) for by in range(0, STRIP, EDGE)]
        total = total + product_sum(fields[3], fields[4], tiles, flags)
        return list(zip((east_ref, south_ref, inv_ref, res_ref, u_ref), fields)), total

    nothing = jnp.zeros((EDGE, LANES), jnp.float32)
    dot_ref[...] = sweep(5, 3 * EDGE, obs.shape[1] - 3 * EDGE, work, nothing)


def inner(taps, obs, cond):
    field = obs.shape
    pixels = field[0] * field[1] * field[2]
    return pl.pallas_call(
        inner_kernel,
        in_specs=[SMEM] + [VMEM] * 2,
        out_specs=[VMEM] * 7,
        out_shape=floats(field, field, field, field, field, (EDGE, LANES))
        + [jax.ShapeDtypeStruct(((field[0] - 1) * LANES, LANES), jnp.bfloat16)],
        compiler_params=params(),
        cost_estimate=pl.CostEstimate(
            flops=45 * pixels, bytes_accessed=24 * pixels, transcendentals=0
        ),
        name="inner_strips",
    )(taps, obs, cond)


def first_kernel(
    tiles,
    down,
    taps,
    obs_in,
    cond_in,
    res_in,
    east_in,
    south_in,
    inv_in,
    u_in,
    got_b,
    got_a,
    coarse_in,
    dot_in,
    cells_in,
    obs,
    cond,
    res_ref,
    east_ref,
    south_ref,
    inv_ref,
    u_ref,
    p_ref,
    q_ref,
    table_ref,
    own_ref,
    chunk_ref,
    image,
    spread,
    work,
):
    height = down * COARSE
    window = down + 2 * EDGE
    at_col, at_row, n_cols, n_rows = place()
    has_n, has_s, has_e, has_w = has_sides()
    clear_pads(obs, cond, p_ref, image)
    clear_work(work)
    from_s, from_n = in_pair_order(
        at_row,
        lambda at, rows=EDGE: got_b[at : at + rows, :],
        lambda at, rows=EDGE: got_a[at : at + rows, :],
    )
    over_at, rest_at, fine_at, sides_at, coarse_at = message_rows(tiles)
    row = iota((EDGE, LANES), 0)
    short = EDGE - REACH
    for t in range(tiles):
        at = fine_at + t * EDGE
        rest = rest_at + 2 * t
        begin_row = 2 * EDGE + height
        obs[t, EDGE : 2 * EDGE, :] = jnp.where(row >= short, from_n(at - short), 0.0)
        obs[t, begin_row : begin_row + EDGE, :] = jnp.where(row < REACH, from_s(at), 0.0)
        near, far = from_n(at + REACH - short), from_n(rest - 2 * short)
        near = jnp.where(row < short, 0.0, near)
        cond[t, EDGE : 2 * EDGE, :] = jnp.where(row < 2 * short, near, far)
        near, far = from_s(at + REACH), from_s(rest - short)
        far = jnp.where(row < REACH, far, 0.0)
        cond[t, begin_row : begin_row + EDGE, :] = jnp.where(row < short, near, far)
    sides_n, sides_s = [split_sides(strip(sides_at), 6) for strip in (from_n, from_s)]
    for which, field in enumerate((obs, cond)):
        field[tiles, EDGE : 2 * EDGE, :] = sides_n[4 + which]
        field[tiles, 2 * EDGE + height : 3 * EDGE + height, :] = sides_s[4 + which]

    edge_row = iota((EDGE, 2 * LANES), 0)

    def joined(index):
        def over(strip, row):
            line = [
                jnp.broadcast_to(
                    strip(over_at + 2 * index + half, 1), (EDGE, LANES)
                )
                for half in range(2)
            ]
            return jnp.where(edge_row == row, jnp.concatenate(line, axis=1), 0.0)

        def rows(strip, beyond):
            return jnp.concatenate([strip(coarse_at + index * EDGE), beyond[index]], axis=1)

        parts = [coarse_in[index, at : at + EDGE, :] for at in range(0, window, EDGE)]
        parts[0] = parts[0] + rows(from_n, sides_n)
        parts[1] = parts[1] + over(from_n, 0)
        parts[-2] = parts[-2] + over(from_s, EDGE - 1)
        parts[-1] = parts[-1] + rows(from_s, sides_s)
        return jnp.concatenate(parts, axis=0)

    source, east, south, around = [joined(index) for index in range(4)]
    row = iota(source.shape, 0)
    lane = iota(source.shape, 1)
    inside = jnp.where(row < EDGE, has_n, jnp.where(row < window - EDGE, 1.0, has_s))
    inside = inside * jnp.where(
        lane < LANES, 1.0, jnp.where(lane < LANES + HALF, has_e, has_w)
    )
    taps = read_taps(taps)
    taps_sum = tap_total(taps, 1)
    factor = inside * OMEGA / (COARSE * COARSE * taps_sum * taps_sum + around)
    weights = (east, roll(east, 1, 1), south, roll(south, 1, 0))
    table = [factor] + [factor * weight for weight in weights]
    for index, part in enumerate([*table, source]):
        table_ref[index] = part
    sides = side_lanes(has_e, has_w)
    half = iota((STRIP, LANES), 0) // EDGE
    pending = []
    total = dot_in[...]
    for index, known in ((0, has_n), (1, has_s)):
        at = EDGE + index * height
        fields = begin(obs, cond, at, taps, sides)
        own = jnp.where(half == index, 0.0, 1.0)
        total = total + fold(own * product_sum_rows(fields[3], fields[4], tiles))
        flag = jnp.where(half == index, known, 1.0)
        inverse, start = [[part * flag for part in fields[index]] for index in (2, 4)]
        fields = (*fields[:2], inverse, fields[3], start)
        pending += [
            (ref, at, strip)
            for ref, strip in zip((east_ref, south_ref, inv_ref, res_ref, u_ref), fields)
        ]
    cells = jacobi(source, table, work)
    spread_cells(cells, spread)
    inner_cells = slice(EDGE, EDGE + down)
    total = total + fold(source[inner_cells, :LANES] * cells[inner_cells, :LANES])
    dot_rp = total
    for ref, at, strip in pending:
        store(ref, at, strip)

    def flags(at, start):
        rows = [at + by for by in range(0, STRIP, EDGE)]
        first_row = jnp.maximum(start, 2 * EDGE)
        return [
            jnp.where((row >= first_row) & (row < 2 * EDGE + height), 1.0, 0.0) for row in rows
        ]

    def begin_p(at, _, carry):
        start, cells = load(u_ref, at), cells_at(spread, at)
        return [(p_ref, [start[t] + cells[t] for t in range(tiles + 1)])], carry

    def blur(at, _, carry):
        strip = conv(p_ref, at, taps, False)
        strip[tiles] = strip[tiles] * sides
        return [(image, strip)], carry

    def finish(at, start, total):
        here, product = operate(p_ref, image, east_ref, south_ref, at, taps)
        return [(q_ref, product)], total + product_sum(here, product, tiles, flags(at, start))

    nothing = jnp.zeros((EDGE, LANES), jnp.float32)
    span = (EDGE, 3 * EDGE + height)
    sweep(3, *span, begin_p, 0)
    sweep(6, *span, blur, 0)
    mask_rows(image, has_n, has_s)
    dot_pq = sweep(3, *span, finish, nothing)

    own = cell_sums(q_ref, tiles, down, cells_in[...])
    own_ref[...] = own
    spare = jnp.zeros((LANES - down, LANES), jnp.float32)
    turned = jnp.transpose(jnp.concatenate([own, spare], axis=0))
    me = at_col * n_rows + at_row
    chunk_ref[pl.ds(me * PIECE, EDGE), 0, :] = jnp.zeros((EDGE, LANES), jnp.float32)
    for down_by in (-1, 0, 1):
        for right_by in (-1, 0, 1):
            if down_by == 0 and right_by == 0:
                continue
            if down_by == 0:
                piece = turned[:EDGE] if right_by < 0 else turned[LANES - EDGE :]
            else:
                piece = own[:EDGE] if down_by < 0 else own[down - EDGE :]
            to_row, to_col = at_row + down_by, at_col + right_by
            there = (to_row >= 0) & (to_row < n_rows) & (to_col >= 0) & (to_col < n_cols)
            slot = jnp.where(there, to_col * n_rows + to_row, me)
            chunk_ref[pl.ds(slot * PIECE, EDGE), 0, :] = piece * jnp.where(there, 1.0, 0.0)
    line = sum_line((dot_rp, dot_pq))
    for at in range(EDGE, chunk_ref.shape[0], PIECE):
        chunk_ref[at] = line


def first(taps, fields, got_a, got_b, coarse, dot, matrix):
    field = fields[0].shape
    tiles, height = field[0] - 1, field[1] - 4 * EDGE
    down = height // COARSE
    window = down + 2 * EDGE
    count = lax.axis_size("cols") * lax.axis_size("rows")
    shapes = [field] * 9 + [
        (6, window, 2 * LANES),
        (down, LANES),
        (count * PIECE, 1, LANES),
    ]
    return pl.pallas_call(
        functools.partial(first_kernel, tiles, down),
        in_specs=[SMEM] + [VMEM] * 12,
        out_specs=[VMEM] * len(shapes),
        out_shape=floats(*shapes),
        input_output_aliases={index + 1: index for index in range(7)},
        scratch_shapes=[
            pltpu.VMEM(field, jnp.float32),
            pltpu.VMEM((tiles + 1, window, LANES), jnp.float32),
            pltpu.VMEM((2, 2, window + 2 * EDGE, LANES), jnp.float32),
        ],
        compiler_params=params(),
        name="first_direction",
    )(taps, *fields, got_b, got_a, coarse, dot, matrix)[2:]


def second_kernel(
    tiles,
    down,
    taps,
    got_ref,
    own_ref,
    table_ref,
    res_ref,
    q_ref,
    east_ref,
    south_ref,
    inv_ref,
    w_ref,
    v_ref,
    out_ref,
    known_ref,
    image,
    spread,
    work,
):
    height = down * COARSE
    has_n, has_s, has_e, has_w = has_sides()
    at_col, at_row, n_cols, n_rows = place()
    me = at_col * n_rows + at_row

    def got(down_by, right_by):
        to_row, to_col = at_row + down_by, at_col + right_by
        there = (to_row >= 0) & (to_row < n_rows) & (to_col >= 0) & (to_col < n_cols)
        slot = jnp.where(there, to_col * n_rows + to_row, me)
        return got_ref[pl.ds(slot * PIECE, EDGE), 0, :]

    low = iota((EDGE, LANES), 1) < HALF
    gap = jnp.zeros((LANES - 2 * EDGE, LANES), jnp.float32)
    beside = jnp.transpose(jnp.concatenate([got(0, 1), gap, got(0, -1)], axis=0))[:down]
    source = jnp.concatenate(
        [
            jnp.concatenate([got(-1, 0), jnp.where(low, got(-1, 1), got(-1, -1))], axis=1),
            jnp.concatenate([own_ref[...], beside], axis=1),
            jnp.concatenate([got(1, 0), jnp.where(low, got(1, 1), got(1, -1))], axis=1),
        ],
        axis=0,
    )
    clear_work(work)
    rp, pq = line_totals(
        [got_ref[at] for at in range(EDGE, got_ref.shape[0], PIECE)], 2
    )
    step = rp / pq
    for index, value in enumerate((step, rp)):
        known_ref[index] = jnp.broadcast_to(value, (EDGE, LANES))
    source = table_ref[5] - jnp.broadcast_to(step, source.shape) * source
    spread_cells(jacobi(source, table_ref, work), spread)
    step = jnp.broadcast_to(step, (STRIP, LANES))
    clear_pads(w_ref, image)
    sides = side_lanes(has_e, has_w)
    taps = read_taps(taps)

    def begin_w(at, start, total):
        right, field, inverse = load(res_ref, at), load(q_ref, at), load(inv_ref, at)
        cells = cells_at(spread, at)
        span = range(tiles + 1)
        residual = [right[t] - step * field[t] for t in span]
        strip = [residual[t] * inverse[t] + cells[t] for t in span]
        first_row = jnp.maximum(start, 2 * EDGE)
        flags = [
            jnp.where((row >= first_row) & (row < 2 * EDGE + height), 1.0, 0.0)
            for row in [at + by for by in range(0, STRIP, EDGE)]
        ]
        return [(w_ref, strip)], total + product_sum(residual, strip, tiles, flags)

    def blur(at, _, carry):
        strip = conv(w_ref, at, taps, False)
        strip[tiles] = strip[tiles] * sides
        return [(image, strip)], carry

    def finish(at, _, total):
        here, product = operate(w_ref, image, east_ref, south_ref, at, taps)
        return [(v_ref, product[:tiles])], total + product_sum(here, product, tiles)

    nothing = jnp.zeros((EDGE, LANES), jnp.float32)
    span = (EDGE, 3 * EDGE + height)
    dot_rz = sweep(3, *span, begin_w, nothing)
    sweep(6, *span, blur, 0)
    mask_rows(image, has_n, has_s)
    dot_zz = sweep(4, 2 * EDGE, 2 * EDGE + height, finish, nothing)
    line = sum_line((dot_rz, dot_zz))
    for index in range(out_ref.shape[0]):
        out_ref[index] = line


def second(taps, got, own, table, r, q, east, south, inv):
    tiles, height = q.shape[0] - 1, q.shape[1] - 4 * EDGE
    down = height // COARSE
    window = down + 2 * EDGE
    count = lax.axis_size("cols") * lax.axis_size("rows")
    return pl.pallas_call(
        functools.partial(second_kernel, tiles, down),
        in_specs=[SMEM] + [VMEM] * 8,
        out_specs=[VMEM] * 4,
        out_shape=floats(q.shape, q.shape, (count, 1, LANES), (2, EDGE, LANES)),
        scratch_shapes=[
            pltpu.VMEM(q.shape, jnp.float32),
            pltpu.VMEM((tiles + 1, window, LANES), jnp.float32),
            pltpu.VMEM((2, 2, window + 2 * EDGE, LANES), jnp.float32),
        ],
        compiler_params=params(),
        name="second_direction",
    )(taps, got, own, table, r, q, east, south, inv)


def combine_kernel(
    tiles, height, sums_ref, known_ref, p_ref, w_ref, r_ref, q_ref, v_ref, sol_out, res_out, sol, res, sem
):
    rz, zz = line_totals([sums_ref[index] for index in range(sums_ref.shape[0])], 2)
    step, rp = [known_ref[index, :1, :] for index in range(2)]
    ratio = rz / rp
    step_next = rz / (zz - ratio * (rz / step))
    on_w = jnp.broadcast_to(step_next, (CHUNK, LANES))
    on_p = jnp.broadcast_to(step + step_next * ratio, (CHUNK, LANES))

    def copies(index):
        rows = pl.ds(pl.multiple_of(index * CHUNK, CHUNK), CHUNK)
        return (
            pltpu.make_async_copy(sol.at[rows, :], sol_out.at[rows, :], sem.at[0, index]),
            pltpu.make_async_copy(res.at[rows, :], res_out.at[rows, :], sem.at[1, index]),
        )

    def work(index, _):
        at = pl.multiple_of(index * CHUNK, CHUNK)
        p, w, r, q, v = [
            load(ref, at + 2 * EDGE, CHUNK) for ref in (p_ref, w_ref, r_ref, q_ref, v_ref)
        ]
        one = [on_p * p[t] + on_w * w[t] for t in range(tiles)]
        two = [r[t] - on_p * q[t] - on_w * v[t] for t in range(tiles)]
        for t in range(tiles):
            sol[pl.ds(at, CHUNK), t * LANES : (t + 1) * LANES] = one[t]
            res[pl.ds(at, CHUNK), t * LANES : (t + 1) * LANES] = two[t]
        for copy in copies(index):
            copy.start()
        return 0

    def settle(index, _):
        for copy in copies(index):
            copy.wait()
        return 0

    lax.fori_loop(0, height // CHUNK, work, 0)
    lax.fori_loop(0, height // CHUNK, settle, 0)


def combine(sums, known, p, w, r, q, v):
    tiles, height = q.shape[0] - 1, q.shape[1] - 4 * EDGE
    shape = (height, tiles * LANES)
    return pl.pallas_call(
        functools.partial(combine_kernel, tiles, height),
        in_specs=[VMEM] * 7,
        out_specs=[HBM] * 2,
        out_shape=floats(shape, shape),
        scratch_shapes=[
            pltpu.VMEM(shape, jnp.float32),
            pltpu.VMEM(shape, jnp.float32),
            pltpu.SemaphoreType.DMA((2, height // CHUNK)),
        ],
        compiler_params=params(),
        name="combine",
    )(sums, known, p, w, r, q, v)


def exchange(send_a, send_b, axis):
    count = lax.axis_size(axis)

    def pairs(begin):
        return [
            pair for i in range(begin, count - 1, 2) for pair in ((i, i + 1), (i + 1, i))
        ]

    got_b = lax.ppermute(send_b, axis, pairs(1))
    got_a = lax.ppermute(send_a, axis, pairs(0))
    return got_a, got_b


def body(observed, class_map, class_weights, blur_kernel):
    arguments = (observed, class_map, class_weights, blur_kernel)
    send_a, send_b = edge(*arguments)
    got_a, got_b = exchange(send_a, send_b, "cols")
    obs, cond, coarse = pack(*arguments, send_a)
    obs, cond, coarse, send_a, send_b = middle(got_a, got_b, coarse, obs, cond)
    got_a, got_b = exchange(send_a, send_b, "rows")
    r, east, south, inv, u, dot, matrix = inner(blur_kernel, obs, cond)
    fields = (obs, cond, r, east, south, inv, u)
    r, east, south, inv, _, p, q, table, own, chunk = first(
        blur_kernel, fields, got_a, got_b, coarse, dot, matrix
    )
    got = lax.all_to_all(chunk, AXES, 0, 0, tiled=True)
    w, v, line, known = second(blur_kernel, got, own, table, r, q, east, south, inv)
    sums = lax.all_to_all(line, AXES[::-1], 0, 0, tiled=True)
    return tuple(combine(sums, known, p, w, r, q, v))


def solution(mesh):
    return jax.shard_map(
        body,
        mesh=mesh,
        in_specs=(P("rows", "cols"), P("rows", "cols"), P(), P()),
        out_specs=(P("rows", "cols"), P("rows", "cols")),
        check_vma=False,
    )
```
